32 devices in a mesh: dp: 4 (over y, x), seq: 2 (over core), fsdp: 4 (over z).
Axes of the slice: x: 2, y: 2, z: 4, core: 2. Of those that a mesh axis runs over, the one named last changes fastest.
Arguments:
- layer_input: bfloat16 [4, 1024, 2048], P('dp', ('seq', 'fsdp')), may hold values from -6 to 6
- out_grad: bfloat16 [4, 1024, 2048], P('dp', ('seq', 'fsdp')), may hold values from -6 to 6
- norm_gain: float32 [2048], P(('dp', 'seq', 'fsdp')), may hold values from 0.4 to 1.6
- in_weight: bfloat16 [2048, 8512], P(('dp', 'seq', 'fsdp')), may hold values from -0.125 to 0.125
- conv_weight: float32 [4352, 4], P(('dp', 'seq', 'fsdp')), may hold values from -3 to 3
- conv_bias: float32 [4352], P(('dp', 'seq', 'fsdp')), may hold values from -0.5 to 0.5
- step_bias: float32 [64], replicated, may hold values from -7 to -3
- log_rate: float32 [64], replicated, may hold values from -1 to 1.5
- skip_gain: float32 [64], replicated, may hold values from 0.5 to 1.5
- gate_gain: float32 [4096], P(('dp', 'seq', 'fsdp')), may hold values from 0.25 to 1.75
- out_weight: bfloat16 [4096, 2048], P(('dp', 'seq', 'fsdp')), may hold values from -0.1875 to 0.1875
- nest_level: int32 [4], P('dp'), may hold values from 0 to 3
- doc_lengths: int32 [4, 4], P('dp'), may hold values from 1 to 512, 1024 in all within a row
Outputs:
- layer_output: bfloat16 [4, 1024, 2048], P('dp', ('seq', 'fsdp'))
- input_grad: bfloat16 [4, 1024, 2048], P('dp', ('seq', 'fsdp'))
- norm_gain_grad: float32 [2048], P(('dp', 'seq', 'fsdp'))
- in_weight_grad: float32 [2048, 8512], P(('dp', 'seq', 'fsdp'))
- conv_weight_grad: float32 [4352, 4], P(('dp', 'seq', 'fsdp'))
- conv_bias_grad: float32 [4352], P(('dp', 'seq', 'fsdp'))
- step_bias_grad: float32 [64], replicated
- log_rate_grad: float32 [64], replicated
- skip_gain_grad: float32 [64], replicated
- gate_gain_grad: float32 [4096], P(('dp', 'seq', 'fsdp'))
- out_weight_grad: float32 [4096, 2048], P(('dp', 'seq', 'fsdp'))
The draws below stay inside these ranges and needn't reach their ends.
Inputs may be any that keep to these rules, and one draw needn't show every extreme that they name: `doc_lengths`: each row holds the 4 document lengths of one sequence, which add up to 1024; the longest is 512. `nest_level`: the level of a sequence: it uses the first 64 / 2^(3 - level) heads.
All inputs are finite; a program needn't handle non-finite values.
Results may differ from the reference program's by a relative error of at most 0.011.
Values may be sent and summed in bfloat16 or wider, within the bound.
A program may use at most 192 MiB of HBM per device.

```python
import math
import jax
import jax.numpy as jnp
import numpy as np
from jax import lax

D = 2048
HEADS = 64
HEAD_DIM = 64
STATE = 128
KW = 4
NDOC = 4
SPAN = 128
INNER = 4096
CONV = 4352
EXTENT = 8512
LEN = 1024
NSEQ = 4


def place_ends(drawn, key, least, top_value):
    index_at = [jax.random.randint(jax.random.fold_in(key, axis), (), 0, length) for axis, length in enumerate(drawn.shape)]
    widest = drawn.shape.index(max(drawn.shape))
    next_to = index_at[:widest] + [(index_at[widest] + 1) % drawn.shape[widest]] + index_at[widest + 1:]
    return drawn.at[tuple(index_at)].set(least).at[tuple(next_to)].set(top_value)


def shard_levels(rng, shape, cuts, least, largest):
    gain, own = 1.0, jax.random.fold_in(rng, 6)
    for axis_at, shards_of in cuts:
        steps = jnp.exp(jax.random.uniform(jax.random.fold_in(own, axis_at), (shards_of,), jnp.float32, least / len(cuts), largest / len(cuts)))
        gain = gain * jnp.repeat(steps, shape[axis_at] // shards_of).reshape([-1 if axis == axis_at else 1 for axis in range(len(shape))])
    return gain


def profile(number_of, total, limit, slope):
    loads = [(1 << 20) // math.isqrt(standing ** slope) + 1 for standing in range(2, number_of + 1)]
    rest, holding = total - limit - (number_of - 1), [1] * (number_of - 1)
    while rest > 0:
        movable = [i for i in range(number_of - 1) if holding[i] < limit]
        pool, remaining = sum([loads[i] for i in movable]), rest
        for i in movable:
            more = min(limit - holding[i], max(1, remaining * loads[i] // pool), rest)
            holding[i] = holding[i] + more
            rest = rest - more
    return np.array([limit] + holding)


def ragged(key, count, total, reach, skew):
    if count == 2:
        one = jax.random.randint(key, (), max(1, total - reach), min(reach, total - 1) + 1)
        return jnp.stack([one, total - one])
    tallies = jnp.asarray(profile(count, total, reach, skew), jnp.int32)
    twos = (count - 1) // 2
    donor, receiver = tallies[1:1 + 2 * twos:2], tallies[2:2 + 2 * twos:2]
    margin = jnp.minimum(donor - 1, reach - receiver)
    shifted = jax.random.randint(jax.random.fold_in(key, 1), (twos,), 0, 1 << 20) % (margin + 1)
    tallies = tallies.at[1:1 + 2 * twos:2].set(donor - shifted).at[2:2 + 2 * twos:2].set(receiver + shifted)
    return tallies[jax.random.permutation(jax.random.fold_in(key, 2), count)]


def normal_values(rng, dims, scale, most, shards=(), kind=jnp.bfloat16):
    gain = shard_levels(rng, dims, shards, -0.22, 0.18) if shards else 1.0
    values = jax.random.normal(rng, dims, jnp.float32) * scale * gain
    return jnp.minimum(jnp.maximum(values, -most), most).astype(kind)


def setup_inputs(seed: int = 0) -> dict:
    streams_of = jax.random.split(jax.random.key(seed), 14)
    layer_input = normal_values(streams_of[0], (NSEQ, LEN, D), 1.0, 6.0, ((0, 4), (1, 8)))
    out_grad = normal_values(streams_of[1], (NSEQ, LEN, D), 1.0, 6.0, ((0, 4), (1, 8)))
    norm_gain = jnp.clip(1.0 + 0.12 * jax.random.normal(streams_of[2], (D,), jnp.float32), 0.4, 1.6)
    in_weight = normal_values(streams_of[3], (D, EXTENT), D ** -0.5, 0.125, ((0, 32),))
    conv_weight = normal_values(streams_of[4], (CONV, KW), 0.5, 3.0, ((0, 32),), jnp.float32)
    conv_bias = jnp.clip(jax.random.uniform(streams_of[5], (CONV,), jnp.float32, -0.5, 0.5) * shard_levels(streams_of[5], (CONV,), ((0, 32),), -0.4, 0.0), -0.5, 0.5)
    step_bias = jnp.clip(jax.random.uniform(streams_of[6], (HEADS,), jnp.float32, -7.0, -3.0), -7.0, -3.0)
    log_rate = jnp.clip(jax.random.uniform(streams_of[7], (HEADS,), jnp.float32, -1.0, 1.5), -1.0, 1.5)
    skip_gain = jnp.clip(jax.random.uniform(streams_of[8], (HEADS,), jnp.float32, 0.5, 1.5), 0.5, 1.5)
    gate_gain = jnp.clip(1.0 + 0.15 * jax.random.normal(streams_of[9], (INNER,), jnp.float32), 0.25, 1.75)
    out_weight = normal_values(streams_of[10], (INNER, D), (INNER // 4) ** -0.5, 0.1875, ((0, 32),))
    nest_level = place_ends(jax.random.randint(streams_of[11], (NSEQ,), 0, 4), jax.random.fold_in(streams_of[11], 1), 0, 3).astype(jnp.int32)
    doc_lengths = jax.vmap(lambda own: ragged(own, NDOC, LEN, LEN // 2, 2))(jax.random.split(streams_of[12], NSEQ)).reshape((NSEQ, NDOC)).astype(jnp.int32)
    return dict(layer_input=layer_input, out_grad=out_grad, norm_gain=norm_gain, in_weight=in_weight, conv_weight=conv_weight, conv_bias=conv_bias, step_bias=step_bias, log_rate=log_rate, skip_gain=skip_gain, gate_gain=gate_gain, out_weight=out_weight, nest_level=nest_level, doc_lengths=doc_lengths)


@jax.custom_vjp
def low(v):
    return lax.optimization_barrier(v.astype(jnp.bfloat16)).astype(jnp.float32)

@jax.custom_vjp
def low_back(v):
    return v

def low_keep(v):
    return (low(v), None)

def low_pass(kept, grad):
    return (grad,)

def back_keep(v):
    return (v, None)

def back_low(kept, grad):
    return (low(grad),)
low.defvjp(low_keep, low_pass)
low_back.defvjp(back_keep, back_low)
HIGH = lax.Precision.HIGHEST
EPSILON = 1e-05

def doc_begins(lengths, positions):
    endings = jnp.cumsum(lengths) - lengths
    reached = endings[None, :] <= positions[:, None]
    return lax.optimization_barrier(jnp.max(jnp.where(reached, endings[None, :], 0), axis=1)).astype(jnp.int32)

def scan_block(state, pieces):
    signal, key_side, query_side, log_decay, step, begins, block_start = pieces
    cumulative = jnp.cumsum(log_decay, axis=0)
    indices = jnp.arange(signal.shape[0])
    same_doc = (begins[:, None] == begins[None, :]) & (indices[None, :] <= indices[:, None])
    gaps = cumulative[:, None, :] - cumulative[None, :, :]
    kernel = jnp.exp(jnp.where(same_doc[:, :, None], gaps, 0.0)) * same_doc[:, :, None]
    intersection = jnp.dot(query_side, key_side.T, precision=HIGH)
    mixing = kernel * intersection[:, :, None] * step[None, :, :]
    local_out = jnp.einsum('tsh,shp->thp', mixing, signal, precision=HIGH)
    inherits = (begins < block_start).astype(jnp.float32)
    carried = jnp.exp(cumulative) * inherits[:, None]
    carry_out = carried[:, :, None] * jnp.einsum('tn,hpn->thp', query_side, state, precision=HIGH)
    last_same = begins == begins[-1]
    tail_weight = jnp.exp(jnp.where(last_same[:, None], cumulative[-1][None, :] - cumulative, 0.0)) * last_same[:, None] * step
    fresh_state = jnp.einsum('sh,shp,sn->hpn', tail_weight, signal, key_side, precision=HIGH)
    new_state = carried[-1][:, None, None] * state + fresh_state
    return (new_state, local_out + carry_out)

def layer(hidden, norm_gain, in_weight, conv_weight, conv_bias, step_bias, log_rate, skip_gain, gate_gain, out_weight, level, lengths):
    positions = jnp.arange(LEN, dtype=jnp.int32)
    begins = doc_begins(lengths, positions)
    inv_rms = lax.rsqrt(lax.optimization_barrier(jnp.mean(hidden * hidden, axis=1, keepdims=True)) + EPSILON)
    normed = low(hidden * inv_rms * norm_gain)
    projected = low(low_back(jnp.dot(normed, in_weight, precision=HIGH)))
    gate_in = projected[:, :INNER]
    conv_in = projected[:, INNER:INNER + CONV]
    rate_in = projected[:, INNER + CONV:]
    padded = jnp.concatenate([jnp.zeros((KW - 1, CONV), jnp.float32), conv_in], axis=0)
    running = conv_bias + jnp.zeros((LEN, CONV), jnp.float32)
    for tap in range(KW):
        source = positions - (KW - 1) + tap
        validity = (source >= begins).astype(jnp.float32)
        running = running + padded[tap:tap + LEN] * conv_weight[:, tap] * validity[:, None]
    activated = jax.nn.silu(running)
    signal = activated[:, :INNER].reshape(LEN, HEADS, HEAD_DIM)
    key_side = activated[:, INNER:INNER + STATE]
    query_side = activated[:, INNER + STATE:]
    step = jax.nn.softplus(rate_in + step_bias)
    log_decay = step * -jnp.exp(log_rate)
    blocks = LEN // SPAN
    pieces = (signal.reshape(blocks, SPAN, HEADS, HEAD_DIM), key_side.reshape(blocks, SPAN, STATE), query_side.reshape(blocks, SPAN, STATE), log_decay.reshape(blocks, SPAN, HEADS), step.reshape(blocks, SPAN, HEADS), begins.reshape(blocks, SPAN), (jnp.arange(blocks, dtype=jnp.int32) * SPAN).astype(jnp.int32))
    start_state = jnp.zeros((HEADS, HEAD_DIM, STATE), jnp.float32)
    unused, outputs = lax.scan(jax.checkpoint(scan_block), start_state, pieces)
    scan_out = outputs.reshape(LEN, HEADS, HEAD_DIM)
    active = jnp.right_shift(HEADS, 3 - level)
    head_mask = (jnp.arange(HEADS) < active).astype(jnp.float32)
    mixed = (scan_out + skip_gain[:, None] * signal) * head_mask[:, None]
    gated = mixed.reshape(LEN, INNER) * jax.nn.silu(gate_in)
    unit_count = (active * HEAD_DIM).astype(jnp.float32)
    mean_square = lax.optimization_barrier(jnp.sum(gated * gated, axis=1, keepdims=True)) / unit_count
    gate_normed = low(gated * lax.rsqrt(mean_square + EPSILON) * gate_gain)
    return hidden + jnp.dot(gate_normed, out_weight, precision=HIGH)

def reference(layer_input, out_grad, norm_gain, in_weight, conv_weight, conv_bias, step_bias, log_rate, skip_gain, gate_gain, out_weight, nest_level, doc_lengths):
    weights = (norm_gain, in_weight.astype(jnp.float32), conv_weight, conv_bias, step_bias, log_rate, skip_gain, gate_gain, out_weight.astype(jnp.float32))
    zero_grads = jax.tree.map(jnp.zeros_like, weights)

    def one_sequence(totals, item):
        hidden, cotangent, level, lengths = item

        def run(hidden_f, params):
            return layer(hidden_f, *params, level, lengths)
        result, pull = jax.vjp(run, hidden.astype(jnp.float32), weights)
        grad_hidden, grad_weights = pull(cotangent.astype(jnp.float32))
        totals = jax.tree.map(jnp.add, totals, grad_weights)
        return (totals, (result.astype(jnp.bfloat16), grad_hidden.astype(jnp.bfloat16)))
    totals, stacked = lax.scan(one_sequence, zero_grads, (layer_input, out_grad, nest_level, doc_lengths))
    return (stacked[0], stacked[1], totals[0], totals[1], totals[2], totals[3], totals[4], totals[5], totals[6], totals[7], totals[8])
```

```python
import functools

import jax
import jax.numpy as jnp
from jax import lax
from jax.experimental import pallas as pl
from jax.experimental.pallas import tpu as pltpu
from jax.sharding import PartitionSpec as P

HEADS = 64
HEAD_DIM = 64
STATE = 128
KW = 4
INNER = 4096
CONV = 4352
EXTENT = 8512


HIGH = lax.Precision.HIGHEST
EPSILON = 1e-05


def shifted(value, axis, steps):
    count = lax.axis_size(axis)
    leading, last = (max(0, -steps), min(count, count - steps))
    return lax.ppermute(value, axis, [(source, source + steps) for source in range(leading, last)])


def prefix(array, axis, combine, identity):
    peers, place = (lax.axis_size(axis), lax.axis_index(axis))
    everything = jax.tree.map(
        lambda part, kind: lax.all_gather(part.astype(kind), axis),
        array,
        (jnp.bfloat16, jnp.bfloat16),
    )
    start = jax.tree.map(
        lambda part, zero: jnp.broadcast_to(jnp.asarray(zero, part.dtype), part.shape),
        array,
        identity,
    )

    def prefix_lap(k, before):
        reached = k < place
        new = combine(
            before, jax.tree.map(lambda part, own: part[k].astype(own.dtype), everything, array)
        )
        return jax.tree.map(lambda a, b: jnp.where(reached, a, b), new, before)

    return lax.fori_loop(0, peers, prefix_lap, start)


def carried_in(array, axis, combine, identity):
    peers, place = (lax.axis_size(axis), lax.axis_index(axis))
    everything = jax.tree.map(
        lambda part, kind: lax.all_gather(part.astype(kind), axis),
        array,
        jax.tree.map(lambda a: jnp.bfloat16 if a.dtype == jnp.float32 else a.dtype, array),
    )
    start = jax.tree.map(
        lambda part, zero: jnp.broadcast_to(jnp.asarray(zero, part.dtype), part.shape),
        array,
        identity,
    )

    def carried_lap(k, before):
        at = peers - 1 - k
        reached = at > place
        new = combine(
            before, jax.tree.map(lambda part, own: part[at].astype(own.dtype), everything, array)
        )
        return jax.tree.map(lambda a, b: jnp.where(reached, a, b), new, before)

    return lax.fori_loop(0, peers, carried_lap, start)


def doc_begins(lengths, positions):
    places = jnp.arange(lengths.shape[1])
    ahead = places[:, None] < places[None, :]
    endings = jnp.sum(jnp.where(ahead[None], lengths[:, :, None], 0), axis=1)
    reached = endings[:, None, :] <= positions[None, :, None]
    return jnp.max(jnp.where(reached, endings[:, None, :], 0), axis=2)


def input_norm(hidden, gain):
    inv_rms = lax.rsqrt(jnp.mean(hidden * hidden, axis=1, keepdims=True) + EPSILON)
    return hidden * inv_rms * gain


def causal_conv(extended, taps, bias, validity):
    block_len = validity.shape[2]
    running = bias + jnp.zeros((extended.shape[0], block_len, extended.shape[2]), jnp.float32)
    for tap in range(taps.shape[1]):
        running = (
            running + extended[:, tap : tap + block_len] * taps[:, tap] * validity[tap][:, :, None]
        )
    return jax.nn.silu(running)


def scan_parts(signal, key_side, query_side, rate_in, step_bias, log_rate, begins, block_start):
    step = jax.nn.softplus(rate_in + step_bias)
    log_decay = step * -jnp.exp(log_rate)
    places = jnp.arange(log_decay.shape[1])
    lower = (places[None, :] <= places[:, None]).astype(jnp.float32)
    cumulative = jnp.einsum("ts,bsh->bth", lower, log_decay, precision=HIGH)
    by_head = jnp.swapaxes(cumulative, 1, 2)
    indices = jnp.arange(signal.shape[1])
    same_doc = (begins[:, :, None] == begins[:, None, :]) & (
        indices[None, None, :] <= indices[None, :, None]
    )
    gaps = by_head[:, :, :, None] - by_head[:, :, None, :]
    kernel = jnp.exp(jnp.where(same_doc[:, None], gaps, 0.0)) * same_doc[:, None]
    intersection = jnp.einsum("btn,bsn->bts", query_side, key_side, precision=HIGH)
    mixing = kernel * intersection[:, None] * jnp.swapaxes(step, 1, 2)[:, :, None, :]
    local_out = jnp.einsum("bhts,bshp->bthp", mixing, signal, precision=HIGH)
    inherits = (begins < block_start).astype(jnp.float32)
    carried = jnp.exp(cumulative) * inherits[:, :, None]
    last_same = begins == begins[:, -1:]
    tail_weight = (
        jnp.exp(jnp.where(last_same[:, :, None], cumulative[:, -1:] - cumulative, 0.0))
        * last_same[:, :, None]
        * step
    )
    fresh_state = jnp.einsum("bsh,bshp,bsn->bhpn", tail_weight, signal, key_side, precision=HIGH)
    return (local_out, carried, carried[:, -1], fresh_state)


def gated_norm(scan_out, signal, skip_gain, gate_in, gate_gain, head_mask, unit_count):
    mixed = (scan_out + skip_gain[:, None] * signal) * head_mask[:, None, :, None]
    gated = mixed.reshape(gate_in.shape) * jax.nn.silu(gate_in)
    mean_square = jnp.sum(gated * gated, axis=2, keepdims=True) / unit_count[:, None, None]
    return gated * lax.rsqrt(mean_square + EPSILON) * gate_gain


def combine_states(earlier, later):
    return (earlier[0] * later[0], later[1] + later[0][:, :, None, None] * earlier[1])


def token_split(
    layer_input,
    out_grad,
    norm_gain,
    in_weight,
    conv_weight,
    conv_bias,
    step_bias,
    log_rate,
    skip_gain,
    gate_gain,
    out_weight,
    nest_level,
    doc_lengths,
):
    seq_count, block_len, model_width = layer_input.shape
    token_count = seq_count * block_len
    gain_all, taps_all, bias_all, gate_all = (
        lax.all_gather(norm_gain, ("dp", "seq", "fsdp"), axis=0, tiled=True),
        lax.all_gather(conv_weight, ("dp", "seq", "fsdp"), axis=0, tiled=True),
        lax.all_gather(conv_bias, ("dp", "seq", "fsdp"), axis=0, tiled=True),
        lax.all_gather(gate_gain, ("dp", "seq", "fsdp"), axis=0, tiled=True),
    )
    block_start = lax.axis_index(("seq", "fsdp")) * block_len
    positions = block_start + jnp.arange(block_len, dtype=jnp.int32)
    begins = doc_begins(doc_lengths, positions)
    hidden = layer_input.reshape(token_count, model_width).astype(jnp.float32)
    normed = input_norm(hidden, gain_all).astype(jnp.bfloat16)
    columns = normed
    projected = jnp.dot(
        columns,
        lax.all_gather(in_weight, ("dp", "seq", "fsdp"), axis=0, tiled=True),
        preferred_element_type=jnp.float32,
    ).astype(jnp.bfloat16)
    projected = projected.reshape(seq_count, block_len, EXTENT)
    gate_in = projected[:, :, :INNER].astype(jnp.float32)
    conv_in = projected[:, :, INNER : INNER + CONV]
    rate_in = projected[:, :, INNER + CONV :].astype(jnp.float32)
    edge_rows = shifted(conv_in[:, block_len - (KW - 1) :], ("seq", "fsdp"), 1)
    extended = jnp.concatenate([edge_rows, conv_in], axis=1).astype(jnp.float32)
    validity = jnp.stack(
        [(positions[None, :] - (KW - 1) + tap >= begins).astype(jnp.float32) for tap in range(KW)]
    )
    activated, conv_pull = jax.vjp(
        lambda ext_in, taps, bias: causal_conv(ext_in, taps, bias, validity),
        extended,
        taps_all,
        bias_all,
    )
    signal = activated[:, :, :INNER].reshape(seq_count, block_len, HEADS, HEAD_DIM)
    key_side = activated[:, :, INNER : INNER + STATE]
    query_side = activated[:, :, INNER + STATE :]
    local_out, carried, decays, fresh_state = scan_parts(
        signal, key_side, query_side, rate_in, step_bias, log_rate, begins, block_start
    )
    identity = (jnp.ones_like(decays), jnp.zeros_like(fresh_state))
    entry_state = prefix((decays, fresh_state), ("seq", "fsdp"), combine_states, identity)[1]
    scan_out = local_out + carried[..., None] * jnp.einsum(
        "btn,bhpn->bthp", query_side, entry_state, precision=HIGH
    )
    active = jnp.right_shift(HEADS, 3 - nest_level)
    head_mask = (jnp.arange(HEADS)[None, :] < active[:, None]).astype(jnp.float32)
    unit_count = (active * HEAD_DIM).astype(jnp.float32)
    gate_normed, gate_pull = jax.vjp(
        lambda sv, xv, sk, gi, gg: gated_norm(sv, xv, sk, gi, gg, head_mask, unit_count),
        scan_out,
        signal,
        skip_gain,
        gate_in,
        gate_all,
    )
    normed_out = gate_normed.reshape(token_count, INNER).astype(jnp.bfloat16)
    columns = normed_out
    branch_out = jnp.dot(
        columns,
        lax.all_gather(out_weight, ("dp", "seq", "fsdp"), axis=0, tiled=True),
        preferred_element_type=jnp.float32,
    )
    layer_output = (
        (hidden + branch_out).astype(jnp.bfloat16).reshape(seq_count, block_len, model_width)
    )
    grad_flat = out_grad.reshape(token_count, model_width)
    grad_normed_out = lax.dot_general(
        grad_flat,
        lax.all_gather(out_weight, ("dp", "seq", "fsdp"), axis=0, tiled=True),
        (((1,), (1,)), ((), ())),
        preferred_element_type=jnp.float32,
    )
    grad_scan, grad_skip_signal, grad_skip, grad_gate_in, grad_gate_gain = gate_pull(
        grad_normed_out.reshape(seq_count, block_len, INNER)
    )
    lead_grad = jnp.einsum("bth,bthp,btn->bhpn", carried, grad_scan, query_side, precision=HIGH)
    later_grad = carried_in((decays, lead_grad), ("seq", "fsdp"), combine_states, identity)[1]

    def full_scan(signal_in, key_in, query_in, rate_values, bias_values, rate_logs):
        part_out, part_carried, part_decays, part_fresh = scan_parts(
            signal_in, key_in, query_in, rate_values, bias_values, rate_logs, begins, block_start
        )
        joined_out = part_out + part_carried[..., None] * jnp.einsum(
            "btn,bhpn->bthp", query_in, entry_state, precision=HIGH
        )
        return (joined_out, part_decays[:, :, None, None] * entry_state + part_fresh)

    scan_pull = jax.vjp(full_scan, signal, key_side, query_side, rate_in, step_bias, log_rate)[1]
    grad_signal, grad_key, grad_query, grad_rate, grad_step_bias, grad_log_rate = scan_pull(
        (grad_scan, later_grad)
    )
    grad_activated = jnp.concatenate(
        [
            (grad_signal + grad_skip_signal).reshape(seq_count, block_len, INNER),
            grad_key,
            grad_query,
        ],
        axis=2,
    )
    grad_extended, grad_taps, grad_bias = conv_pull(grad_activated)
    returned = shifted(grad_extended[:, : KW - 1].astype(jnp.bfloat16), ("seq", "fsdp"), -1).astype(
        jnp.float32
    )
    grad_conv_in = grad_extended[:, KW - 1 :] + jnp.pad(
        returned, ((0, 0), (block_len - (KW - 1), 0), (0, 0))
    )
    grad_projected = (
        jnp.concatenate([grad_gate_in, grad_conv_in, grad_rate], axis=2)
        .reshape(token_count, EXTENT)
        .astype(jnp.bfloat16)
    )
    grad_normed = lax.dot_general(
        grad_projected,
        lax.all_gather(in_weight, ("dp", "seq", "fsdp"), axis=0, tiled=True),
        (((1,), (1,)), ((), ())),
        preferred_element_type=jnp.float32,
    )
    replicas = lax.axis_size("dp")
    members = lax.axis_size(("seq", "fsdp"))
    width_in = model_width // lax.axis_size(("dp", "seq", "fsdp"))
    width_out = INNER // lax.axis_size(("dp", "seq", "fsdp"))
    in_cols, out_cols = (
        lax.all_to_all(
            normed.reshape(token_count, replicas, members, width_in),
            ("seq", "fsdp"),
            split_axis=2,
            concat_axis=0,
            tiled=True,
        ),
        lax.all_to_all(
            normed_out.reshape(token_count, replicas, members, width_out),
            ("seq", "fsdp"),
            split_axis=2,
            concat_axis=0,
            tiled=True,
        ),
    )
    in_cols = in_cols.reshape(members * token_count, replicas * width_in)
    out_cols = out_cols.reshape(members * token_count, replicas * width_out)
    in_new = lax.dot_general(
        in_cols,
        lax.all_gather(grad_projected, ("seq", "fsdp"), axis=0, tiled=True),
        (((0,), (0,)), ((), ())),
        preferred_element_type=jnp.float32,
    )
    out_new = lax.dot_general(
        out_cols,
        lax.all_gather(grad_flat, ("seq", "fsdp"), axis=0, tiled=True),
        (((0,), (0,)), ((), ())),
        preferred_element_type=jnp.float32,
    )
    in_weight_grad, out_weight_grad = (
        lax.psum_scatter(in_new.astype(jnp.bfloat16), "dp", scatter_dimension=0, tiled=True).astype(
            jnp.float32
        ),
        lax.psum_scatter(
            out_new.astype(jnp.bfloat16), "dp", scatter_dimension=0, tiled=True
        ).astype(jnp.float32),
    )
    norm_pull = jax.vjp(input_norm, hidden, gain_all)[1]
    grad_hidden, grad_gain = norm_pull(grad_normed)
    input_grad = (
        (grad_flat.astype(jnp.float32) + grad_hidden)
        .astype(jnp.bfloat16)
        .reshape(seq_count, block_len, model_width)
    )
    norm_gain_grad, conv_weight_grad, conv_bias_grad, gate_gain_grad = (
        lax.psum_scatter(grad_gain, ("dp", "seq", "fsdp"), scatter_dimension=0, tiled=True),
        lax.psum_scatter(grad_taps, ("dp", "seq", "fsdp"), scatter_dimension=0, tiled=True),
        lax.psum_scatter(grad_bias, ("dp", "seq", "fsdp"), scatter_dimension=0, tiled=True),
        lax.psum_scatter(grad_gate_gain, ("dp", "seq", "fsdp"), scatter_dimension=0, tiled=True),
    )
    step_bias_grad, log_rate_grad, skip_gain_grad = lax.psum(
        (grad_step_bias, grad_log_rate, grad_skip), ("dp", "seq", "fsdp")
    )
    return (
        layer_output,
        input_grad,
        norm_gain_grad,
        in_weight_grad,
        conv_weight_grad,
        conv_bias_grad,
        step_bias_grad,
        log_rate_grad,
        skip_gain_grad,
        gate_gain_grad,
        out_weight_grad,
    )


MESH = pl.DeviceIdType.MESH
F32 = jnp.float32
BF16 = jnp.bfloat16
TILE = 128
SPAN = 128
MODEL = 2048
COMMON = 384
NEG = -1e30
LIMIT = 56 * 2**20
VM = pl.BlockSpec(memory_space=pltpu.VMEM)
SM = pl.BlockSpec(memory_space=pltpu.SMEM)
ANY = pl.BlockSpec(memory_space=pl.ANY)
DMA = pltpu.SemaphoreType.DMA


def remote(src, dst, sends, recvs, device):
    return pltpu.make_async_remote_copy(
        src_ref=src,
        dst_ref=dst,
        send_sem=sends,
        recv_sem=recvs,
        device_id=device,
        device_id_type=MESH,
    )


def dot(a, b, over=((1,), (0,))):
    return lax.dot_general(a, b, (over, ((), ())), preferred_element_type=F32)


def exact(a, b, over=((1,), (0,))):
    return lax.dot_general(a, b, (over, ((), ())), precision=HIGH, preferred_element_type=F32)


def begin_at(place, starts, docs):
    begin = jnp.zeros_like(place)
    for doc in range(1, docs):
        begin = jnp.where(starts[0, doc] <= place, starts[0, doc], begin)
    return begin


def iota(shape, dim):
    return lax.broadcasted_iota(jnp.int32, shape, dim)


def silu_slope(value):
    gate = jax.nn.sigmoid(value)
    return gate * (1.0 + value * (1.0 - gate))


def softplus(value):
    return jnp.maximum(value, 0.0) + jnp.log1p(jnp.exp(-jnp.abs(value)))


def conv_tile(extended, taps, bias, first, starts, docs, lanes):
    place = first + iota((SPAN, TILE), 0)
    begin = begin_at(place, starts, docs)
    total = jnp.broadcast_to(bias[0:1, lanes], (SPAN, TILE))
    for tap in range(KW):
        back = KW - 1 - tap
        moved = extended if back == 0 else pltpu.roll(extended, back, 0)
        valid = place - back >= begin
        total = total + jnp.where(valid, moved[16:], 0.0) * taps[tap : tap + 1, lanes]
    return total


def tile_of(index):
    return slice(index * TILE, (index + 1) * TILE)


def head_col(values, head):
    return jnp.broadcast_to(values[:, head : head + 1], (SPAN, TILE))


class HeadSplit:
    def __init__(self, nd, nc, nz):
        self.nd, self.nc, self.nz = nd, nc, nz
        self.nm = nc * nz
        self.span = self.nm * SPAN
        self.rows_in = MODEL // (nd * self.nm)

    def fits(self):
        return INNER == self.nd * self.nm * TILE and self.rows_in % 16 == 0

    def place(self):
        return lax.axis_index("dp"), lax.axis_index("seq"), lax.axis_index("fsdp")

    def group_steps(self):
        return [(e, d) for d in range(self.nz) for e in range(self.nc) if e or d]

    def target(self, step):
        dp, c, z = self.place()
        ct, zt = lax.rem(c + step[0], self.nc), lax.rem(z + step[1], self.nz)
        return (dp, ct, zt), ct * self.nz + zt

    def source(self, step):
        dp, c, z = self.place()
        cs, zs = lax.rem(c + self.nc - step[0], self.nc), lax.rem(z + self.nz - step[1], self.nz)
        return cs * self.nz + zs

    def barrier(self, group=True, line=True):
        dp, c, z = self.place()
        sem = pltpu.get_barrier_semaphore()
        count = 0
        if group:
            for step in self.group_steps():
                pl.semaphore_signal(sem, inc=1, device_id=self.target(step)[0], device_id_type=MESH)
                count += 1
        if line:
            for k in range(1, self.nd):
                pl.semaphore_signal(
                    sem, inc=1, device_id=(lax.rem(dp + k, self.nd), c, z), device_id_type=MESH
                )
                count += 1
        pl.semaphore_wait(sem, count)

    def gather_kernel(
        self, x_ref, par_ref, g_ref, wm_ref, wc_ref, wo_ref,
        xall, gall, wall, wcall, woall, parall,
        normed, parbuf, pd_s, pd_r, pg_s, pg_r, wz_s, wz_r, wd_s, wd_r, cz_s, cz_r, cd_s, cd_r,
        xz_s, xz_r, xc_s, xc_r, gz_s, gz_r, gc_s, gc_r, wo_s, wo_r, loc,
    ):
        nd, nc, nz, nm = self.nd, self.nc, self.nz, self.nm
        dp, c, z = self.place()
        me = c * nz + z
        steps = self.group_steps()
        lines = [(k, lax.rem(dp + k, nd), lax.rem(dp + nd - k, nd)) for k in range(1, nd)]
        parbuf[dp] = par_ref[...]
        self.barrier()
        started = []

        def go(copy):
            copy.start()
            started.append(copy)

        for k, to, _ in lines:
            go(remote(parbuf.at[dp], parbuf.at[dp], pd_s.at[k], pd_r.at[k], (to, c, z)))
        for j, step in enumerate(steps):
            device, there = self.target(step)
            go(remote(wm_ref.at[there], wall.at[dp, me], wz_s.at[j], wz_r.at[j], device))
            go(remote(wc_ref, wcall.at[dp, me], cz_s.at[j], cz_r.at[j], device))
        own = [
            pltpu.make_async_copy(wm_ref.at[me], wall.at[dp, me], loc.at[0]),
            pltpu.make_async_copy(wc_ref, wcall.at[dp, me], loc.at[1]),
            pltpu.make_async_copy(g_ref, gall.at[me], loc.at[2]),
            pltpu.make_async_copy(wo_ref, woall.at[dp], loc.at[3]),
        ]
        for copy in own:
            copy.start()
        for k, to, _ in lines:
            go(remote(wo_ref, woall.at[dp], wo_s.at[k], wo_r.at[k], (to, c, z)))
            go(remote(wm_ref.at[me], wall.at[dp, me], wd_s.at[k, nm - 1], wd_r.at[k, nm - 1], (to, c, z)))
            go(remote(wc_ref, wcall.at[dp, me], cd_s.at[k, nm - 1], cd_r.at[k, nm - 1], (to, c, z)))
        for k, to, frm in lines:
            remote(parbuf.at[frm], parbuf.at[frm], pd_s.at[k], pd_r.at[k], (to, c, z)).wait_recv()
        parall[me] = parbuf[...]
        for j, step in enumerate(steps):
            device, _ = self.target(step)
            go(remote(parbuf, parall.at[me], pg_s.at[j], pg_r.at[j], device))
        for j, step in enumerate(steps):
            device, _ = self.target(step)
            remote(parbuf, parall.at[self.source(step)], pg_s.at[j], pg_r.at[j], device).wait_recv()
        gains = []
        for first in range(0, nd * nm, 2):
            left = parall[first % nm, first // nm][0:1, : self.rows_in]
            right = parall[(first + 1) % nm, (first + 1) // nm][0:1, : self.rows_in]
            gains.append(jnp.concatenate([left, right], axis=1))
        gain = jnp.concatenate(gains, axis=1)
        hidden = x_ref[...].astype(F32)
        inverse = lax.rsqrt(jnp.mean(hidden * hidden, axis=1, keepdims=True) + EPSILON)
        normed[...] = (hidden * inverse * gain).astype(BF16)
        mine = pltpu.make_async_copy(normed, xall.at[me], loc.at[4])
        mine.start()
        own.append(mine)
        other = (dp, nc - 1 - c, z)

        def spread(source, every, z_s, z_r, c_s, c_r):
            for d in range(1, nz):
                go(remote(source, every.at[me], z_s.at[d], z_r.at[d], (dp, c, lax.rem(z + d, nz))))
            go(remote(source, every.at[me], c_s.at[0], c_r.at[0], other))

        spread(normed, xall, xz_s, xz_r, xc_s, xc_r)
        spread(g_ref, gall, gz_s, gz_r, gc_s, gc_r)
        for j, step in enumerate(steps):
            device, _ = self.target(step)
            frm = self.source(step)
            block, common = wall.at[dp, frm], wcall.at[dp, frm]
            remote(block, block, wz_s.at[j], wz_r.at[j], device).wait_recv()
            remote(common, common, cz_s.at[j], cz_r.at[j], device).wait_recv()
            for k, to, _ in lines:
                go(remote(block, block, wd_s.at[k, j], wd_r.at[k, j], (to, c, z)))
                go(remote(common, common, cd_s.at[k, j], cd_r.at[k, j], (to, c, z)))

        def pass_on(every, z_s, z_r, c_s, c_r):
            for d in range(1, nz):
                block = every.at[c * nz + lax.rem(z + nz - d, nz)]
                remote(block, block, z_s.at[d], z_r.at[d], other).wait_recv()
                go(remote(block, block, c_s.at[d], c_r.at[d], other))

        pass_on(xall, xz_s, xz_r, xc_s, xc_r)
        pass_on(gall, gz_s, gz_r, gc_s, gc_r)
        for d in range(nz):
            frm = (nc - 1 - c) * nz + lax.rem(z + nz - d, nz)
            remote(xall.at[frm], xall.at[frm], xc_s.at[d], xc_r.at[d], other).wait_recv()
            remote(gall.at[frm], gall.at[frm], gc_s.at[d], gc_r.at[d], other).wait_recv()
        for k, to, frm in lines:
            remote(woall.at[frm], woall.at[frm], wo_s.at[k], wo_r.at[k], (to, c, z)).wait_recv()
            for j in range(nm):
                here = me if j == nm - 1 else self.source(steps[j])
                block, common = wall.at[frm, here], wcall.at[frm, here]
                remote(block, block, wd_s.at[k, j], wd_r.at[k, j], (to, c, z)).wait_recv()
                remote(common, common, cd_s.at[k, j], cd_r.at[k, j], (to, c, z)).wait_recv()
        for copy in own:
            copy.wait()
        for copy in started:
            copy.wait_send()

    def gather(self, x, par, g, wm, wc, wo):
        nd, nz, nm, rows = self.nd, self.nz, self.nm, self.rows_in
        out = [
            jax.ShapeDtypeStruct((nm, SPAN, MODEL), BF16),
            jax.ShapeDtypeStruct((nm, SPAN, MODEL), BF16),
            jax.ShapeDtypeStruct((nd, nm, rows, 2 * nd * TILE), BF16),
            jax.ShapeDtypeStruct((nd, nm, rows, COMMON), BF16),
            jax.ShapeDtypeStruct((nd, TILE, MODEL), BF16),
            jax.ShapeDtypeStruct((nm, nd, 8, TILE), F32),
        ]
        return pl.pallas_call(
            self.gather_kernel,
            out_shape=out,
            in_specs=[VM, VM, ANY, ANY, ANY, ANY],
            out_specs=[ANY, ANY, ANY, ANY, ANY, VM],
            scratch_shapes=[
                pltpu.VMEM((SPAN, MODEL), BF16),
                pltpu.VMEM((nd, 8, TILE), F32),
                DMA((nd,)), DMA((nd,)), DMA((nm,)), DMA((nm,)),
                DMA((nm,)), DMA((nm,)), DMA((nd, nm)), DMA((nd, nm)),
                DMA((nm,)), DMA((nm,)), DMA((nd, nm)), DMA((nd, nm)),
                DMA((nz,)), DMA((nz,)), DMA((nz,)), DMA((nz,)),
                DMA((nz,)), DMA((nz,)), DMA((nz,)), DMA((nz,)),
                DMA((nd,)), DMA((nd,)), DMA((5,)),
            ],
            compiler_params=pltpu.CompilerParams(
                collective_id=0, has_side_effects=True, vmem_limit_bytes=LIMIT
            ),
            name="gather",
        )(x, par, g, wm, wc, wo)

    def forward_kernel(
        self, docs, starts, pm, pm_prev, pc, pc_prev, g, wo, taps, bias, sel, hp, chp,
        pre_sig, pre_bc, o, sin, step_o, cum_o, dg_o, y_o, st_o, state,
    ):
        nd = self.nd
        chunk = pl.program_id(0)
        first = chunk * SPAN

        @pl.when(chunk == 0)
        def _():
            state[...] = jnp.zeros_like(state)

        lane = iota((SPAN, TILE), 1)
        row = iota((SPAN, TILE), 0)
        for i in range(nd):
            lanes = tile_of(i)
            cols = slice(nd * TILE + i * TILE, nd * TILE + (i + 1) * TILE)
            ext = jnp.concatenate([pm_prev[SPAN - 16 :, lanes], pm[:, cols]], axis=0).astype(F32)
            pre_sig[:, lanes] = conv_tile(ext, taps, bias, first, starts, docs, lanes)
        sides = []
        for i in range(2):
            lanes = tile_of(i)
            ext = jnp.concatenate([pc_prev[SPAN - 16 :, lanes], pc[:, lanes]], axis=0).astype(F32)
            value = conv_tile(ext, taps, bias, first, starts, docs, tile_of(nd + i))
            pre_bc[:, lanes] = value
            sides.append((value * jax.nn.sigmoid(value)).astype(BF16))
        key_side, query_side = sides
        rate = dot(pc[:, 2 * TILE :], sel[...])
        step = softplus(rate + hp[0:1, :])
        log_decay = step * hp[1:2, :]
        lower = (lane <= row).astype(F32)
        cum = exact(lower, log_decay)
        step_o[...] = step
        cum_o[...] = cum
        cum_t = cum.T
        begin_t = begin_at(first + row, starts, docs)
        begin_s = begin_at(first + lane, starts, docs)
        shut = jnp.where((begin_t == begin_s) & (lane <= row), 0.0, NEG)
        inherits = (begin_t < first).astype(F32)
        begin_last = begin_at(jnp.full((SPAN, TILE), first + SPAN - 1, jnp.int32), starts, docs)
        last_same = (begin_t == begin_last).astype(F32)
        meet = dot(query_side, key_side, ((1,), (1,)))
        before = state[...]
        sin[0] = before
        carried_out = dot(query_side, before.astype(BF16))
        squares = jnp.zeros((SPAN, TILE), F32)
        crosses = jnp.zeros((SPAN, TILE), F32)
        lefts, fulls = [], []
        grad = dot(g[...], wo[...], ((1,), (1,)))
        dg_o[...] = grad
        for i in range(nd):
            lanes = tile_of(i)
            low = lane < TILE // 2
            pre = pre_sig[:, lanes]
            signal = pre * jax.nn.sigmoid(pre)
            cums = [head_col(cum, 2 * i), head_col(cum, 2 * i + 1)]
            stepx = jnp.where(low, head_col(step, 2 * i), head_col(step, 2 * i + 1))
            cumx = jnp.where(low, cums[0], cums[1])
            fed = stepx * signal
            fed_low = fed.astype(BF16)
            local = []
            for e in range(2):
                head = 2 * i + e
                kernel = jnp.exp(cums[e] - cum_t[head : head + 1, :] + shut)
                local.append(dot((kernel * meet).astype(BF16), fed_low))
            entry = jnp.exp(cumx) * inherits
            out = jnp.where(low, local[0], local[1]) + entry * carried_out[:, lanes]
            o[:, lanes] = out
            last = cumx[SPAN - 1 : SPAN, :]
            tail = jnp.exp((last - cumx) * last_same) * last_same
            state[:, lanes] = entry[SPAN - 1 : SPAN, :] * before[:, lanes] + dot(
                key_side, (tail * fed).astype(BF16), ((0,), (0,))
            )
            mixed = (out + chp[0:1, lanes] * signal) * chp[1:2, lanes]
            gate_in = pm[:, lanes].astype(F32)
            gated = mixed * (gate_in * jax.nn.sigmoid(gate_in))
            scaled = gated * chp[2:3, lanes]
            squares = squares + gated * gated
            crosses = crosses + scaled * grad[:, lanes]
            fulls.append(scaled.astype(BF16))
        y_o[...] = dot(jnp.concatenate(fulls, axis=1), wo[...]).astype(BF16)
        square = jnp.broadcast_to(jnp.sum(squares, axis=1, keepdims=True), (SPAN, TILE))
        cross = jnp.broadcast_to(jnp.sum(crosses, axis=1, keepdims=True), (SPAN, TILE))
        both = jnp.where(lane == 0, square, jnp.where(lane == 1, cross, 0.0))
        st_o[0] = both.T[0:8, :]

    def forward(self, docs, starts, projm, projc, gall, wo, taps, bias, sel, hp, chp):
        nd, nm, span = self.nd, self.nm, self.span
        wide = nd * TILE
        whole = lambda shape: pl.BlockSpec(shape, lambda i: (0,) * len(shape))
        prev = lambda i: jnp.maximum(i - 1, 0)
        return pl.pallas_call(
            functools.partial(self.forward_kernel, docs),
            grid=(nm,),
            in_specs=[
                SM,
                pl.BlockSpec((SPAN, 2 * wide), lambda i: (i, 0)),
                pl.BlockSpec((SPAN, wide), lambda i: (prev(i), 1)),
                pl.BlockSpec((SPAN, COMMON), lambda i: (i, 0)),
                pl.BlockSpec((SPAN, COMMON), lambda i: (prev(i), 0)),
                pl.BlockSpec((SPAN, MODEL), lambda i: (i, 0)),
                whole((wide, MODEL)),
                whole(taps.shape),
                whole(bias.shape),
                whole(sel.shape),
                whole(hp.shape),
                whole(chp.shape),
            ],
            out_specs=[
                pl.BlockSpec((SPAN, wide), lambda i: (i, 0)),
                pl.BlockSpec((SPAN, 2 * TILE), lambda i: (i, 0)),
                pl.BlockSpec((SPAN, wide), lambda i: (i, 0)),
                pl.BlockSpec((1, STATE, wide), lambda i: (i, 0, 0)),
                pl.BlockSpec((SPAN, TILE), lambda i: (i, 0)),
                pl.BlockSpec((SPAN, TILE), lambda i: (i, 0)),
                pl.BlockSpec((SPAN, wide), lambda i: (i, 0)),
                pl.BlockSpec((SPAN, MODEL), lambda i: (i, 0)),
                pl.BlockSpec((1, 8, TILE), lambda i: (i, 0, 0)),
            ],
            out_shape=[
                jax.ShapeDtypeStruct((span, wide), F32),
                jax.ShapeDtypeStruct((span, 2 * TILE), F32),
                jax.ShapeDtypeStruct((span, wide), F32),
                jax.ShapeDtypeStruct((nm, STATE, wide), F32),
                jax.ShapeDtypeStruct((span, TILE), F32),
                jax.ShapeDtypeStruct((span, TILE), F32),
                jax.ShapeDtypeStruct((span, wide), F32),
                jax.ShapeDtypeStruct((span, MODEL), BF16),
                jax.ShapeDtypeStruct((nm, 8, TILE), F32),
            ],
            scratch_shapes=[pltpu.VMEM((STATE, wide), F32)],
            compiler_params=pltpu.CompilerParams(vmem_limit_bytes=LIMIT),
            name="forward",
        )(starts, projm, projm, projc, projc, gall, wo, taps, bias, sel, hp, chp)

    def stats_kernel(self, st, total, heard, sends, recvs):
        steps = self.group_steps()
        self.barrier(line=False)
        copies = []
        for j, step in enumerate(steps):
            device, _ = self.target(step)
            copy = remote(st, heard.at[j], sends.at[j], recvs.at[j], device)
            copy.start()
            copies.append(copy)
        value = st[...]
        for j, copy in enumerate(copies):
            copy.wait_recv()
            value = value + heard[j]
        total[...] = value
        for copy in copies:
            copy.wait_send()

    def stats(self, st):
        n = self.nm - 1
        return pl.pallas_call(
            self.stats_kernel,
            out_shape=jax.ShapeDtypeStruct(st.shape, F32),
            in_specs=[VM],
            out_specs=VM,
            scratch_shapes=[pltpu.VMEM((n, *st.shape), F32), DMA((n,)), DMA((n,))],
            compiler_params=pltpu.CompilerParams(collective_id=1, has_side_effects=True),
            name="stats",
        )(st)

    def backward_kernel(
        self, docs, starts, unit, pm, pm_prev, pre_sig, pre_bc, o, sin, step_i, cum_i, dg_i, st, taps, sel, hp, chp,
        dproj, dcom, normed_out, sums, heads, dstate, dnext,
    ):
        nd = self.nd
        chunk = self.nm - 1 - pl.program_id(0)
        first = chunk * SPAN

        @pl.when(pl.program_id(0) == 0)
        def _():
            dstate[...] = jnp.zeros_like(dstate)
            dnext[...] = jnp.zeros_like(dnext)
            sums[...] = jnp.zeros_like(sums)
            heads[...] = jnp.zeros_like(heads)

        lane = iota((SPAN, TILE), 1)
        row = iota((SPAN, TILE), 0)
        low = lane < TILE // 2
        begin_t = begin_at(first + row, starts, docs)
        begin_s = begin_at(first + lane, starts, docs)
        shut = jnp.where((begin_t == begin_s) & (lane <= row), 0.0, NEG)
        inherits = (begin_t < first).astype(F32)
        begin_last = begin_at(jnp.full((SPAN, TILE), first + SPAN - 1, jnp.int32), starts, docs)
        last_same = (begin_t == begin_last).astype(F32)
        lower = (lane <= row).astype(F32)
        key_pre, query_pre = pre_bc[:, :TILE], pre_bc[:, TILE:]
        key_side = (key_pre * jax.nn.sigmoid(key_pre)).astype(BF16)
        query_side = (query_pre * jax.nn.sigmoid(query_pre)).astype(BF16)
        meet = dot(query_side, key_side, ((1,), (1,)))
        step, cum = step_i[...], cum_i[...]
        cum_t = cum.T
        stat = jnp.concatenate([st[0], jnp.zeros((SPAN - 8, TILE), F32)], axis=0).T
        square, cross = head_col(stat, 0), head_col(stat, 1)
        root = lax.rsqrt(square * unit[0, 0] + EPSILON)
        pull = root * root * root * cross * unit[0, 0]
        before = sin[0]
        before_low = before.astype(BF16)
        after = dstate[...]
        after_low = after.astype(BF16)
        carried_out = dot(query_side, before_low)
        from_state = dot(key_side, after_low)
        meet_grad = jnp.zeros((SPAN, SPAN), F32)
        cum_cols = jnp.zeros((SPAN, TILE), F32)
        cum_rows = jnp.zeros((8, SPAN), F32)
        step_cols = jnp.zeros((SPAN, TILE), F32)
        entered, tails, lasts = [], [], []
        head_rows = iota((8, SPAN), 0)
        next_rows = first + iota((SPAN + 16, TILE), 0)
        next_begin = begin_at(next_rows, starts, docs)
        tail_row = iota((SPAN, TILE), 0) == SPAN - 1
        for i in range(nd):
            lanes = tile_of(i)
            pre = pre_sig[:, lanes]
            gate_of = jax.nn.sigmoid(pre)
            signal = pre * gate_of
            gate_in = pm[:, lanes].astype(F32)
            gate_sig = jax.nn.sigmoid(gate_in)
            opened = gate_in * gate_sig
            mask = chp[1:2, lanes]
            mixed = (o[:, lanes] + chp[0:1, lanes] * signal) * mask
            gated = mixed * opened
            grad = dg_i[:, lanes]
            gain = chp[2:3, lanes]
            normed_out[:, lanes] = (gated * root * gain).astype(BF16)
            sums[0:1, lanes] += jnp.sum(grad * gated * root, axis=0, keepdims=True)
            gated_grad = root * grad * gain - gated * pull
            mixed_grad = gated_grad * opened * mask
            dproj[:, lanes] = (
                gated_grad * mixed * (gate_sig * (1.0 + gate_in * (1.0 - gate_sig)))
            ).astype(BF16)
            sums[1:2, lanes] += jnp.sum(mixed_grad * signal, axis=0, keepdims=True)
            cums = [head_col(cum, 2 * i), head_col(cum, 2 * i + 1)]
            stepx = jnp.where(low, head_col(step, 2 * i), head_col(step, 2 * i + 1))
            cumx = jnp.where(low, cums[0], cums[1])
            fed = stepx * signal
            fed_low = fed.astype(BF16)
            out_grad = mixed_grad
            out_low = out_grad.astype(BF16)
            entry = jnp.exp(cumx) * inherits
            last = cumx[SPAN - 1 : SPAN, :]
            tail = jnp.exp((last - cumx) * last_same) * last_same
            backs = []
            for e in range(2):
                head = 2 * i + e
                kernel = jnp.exp(cums[e] - cum_t[head : head + 1, :] + shut)
                mix = kernel * meet
                half = low if e == 0 else jnp.logical_not(low)
                mix_grad = dot(jnp.where(half, out_grad, 0.0).astype(BF16), fed_low, ((1,), (1,)))
                meet_grad = meet_grad + kernel * mix_grad
                weight = mix * mix_grad
                cum_cols = cum_cols + jnp.where(
                    lane == head, jnp.broadcast_to(jnp.sum(weight, axis=1, keepdims=True), (SPAN, TILE)), 0.0
                )
                cum_rows = cum_rows + jnp.where(
                    head_rows == head, jnp.broadcast_to(jnp.sum(weight, axis=0, keepdims=True), (8, SPAN)), 0.0
                )
                backs.append(dot(mix.astype(BF16), out_low, ((0,), (0,))))
            entry_grad = entry * out_grad
            tail_fed = tail * fed
            entered.append(entry_grad.astype(BF16))
            tails.append(tail_fed.astype(BF16))
            fed_grad = jnp.where(low, backs[0], backs[1]) + tail * from_state[:, lanes]
            moved_in = entry_grad * carried_out[:, lanes]
            moved_out = tail_fed * from_state[:, lanes]
            direct = fed_grad * signal
            end = entry[SPAN - 1 : SPAN, :]
            kept = jnp.sum(after[:, lanes] * before[:, lanes], axis=0, keepdims=True) * end
            at_end = jnp.sum(moved_out, axis=0, keepdims=True) + kept
            local = moved_in - moved_out + jnp.where(tail_row, at_end, 0.0)
            for e in range(2):
                half = low if e == 0 else jnp.logical_not(low)
                place = lane == 2 * i + e
                cum_cols = cum_cols + jnp.where(
                    place,
                    jnp.broadcast_to(jnp.sum(jnp.where(half, local, 0.0), axis=1, keepdims=True), (SPAN, TILE)),
                    0.0,
                )
                step_cols = step_cols + jnp.where(
                    place,
                    jnp.broadcast_to(jnp.sum(jnp.where(half, direct, 0.0), axis=1, keepdims=True), (SPAN, TILE)),
                    0.0,
                )
            dstate[:, lanes] = end * after[:, lanes] + dot(
                query_side, entry_grad.astype(BF16), ((0,), (0,))
            )
            signal_grad = stepx * fed_grad + chp[0:1, lanes] * mixed_grad
            pre_grad = signal_grad * (gate_of * (1.0 + pre * (1.0 - gate_of)))
            sums[2:3, lanes] += jnp.sum(pre_grad, axis=0, keepdims=True)
            later = jnp.concatenate([pre_grad, dnext[:, lanes]], axis=0)
            dnext[:, lanes] = pre_grad[0:16, :]
            cols = slice(nd * TILE + i * TILE, nd * TILE + (i + 1) * TILE)
            ext = jnp.concatenate([pm_prev[SPAN - 16 :, lanes], pm[:, cols]], axis=0).astype(F32)
            back_grad = jnp.zeros((SPAN, TILE), F32)
            for tap in range(KW):
                back = KW - 1 - tap
                masked = jnp.where(next_rows - back >= next_begin, later, 0.0)
                moved = ext if back == 0 else pltpu.roll(ext, back, 0)
                sums[4 + tap : 5 + tap, lanes] += jnp.sum(
                    masked[:SPAN] * moved[16:], axis=0, keepdims=True
                )
                ahead = masked if back == 0 else pltpu.roll(masked, SPAN + 16 - back, 0)
                back_grad = back_grad + ahead[:SPAN] * taps[tap : tap + 1, lanes]
            dproj[:, cols] = back_grad.astype(BF16)
        meet_low = meet_grad.astype(BF16)
        state_rows = ((1,), (1,))
        query_grad = dot(meet_low, key_side) + dot(jnp.concatenate(entered, axis=1), before_low, state_rows)
        key_grad = dot(meet_low, query_side, ((0,), (0,))) + dot(
            jnp.concatenate(tails, axis=1), after_low, state_rows
        )
        dcom[:, :TILE] = key_grad.astype(BF16)
        dcom[:, TILE : 2 * TILE] = query_grad.astype(BF16)
        rows_t = jnp.concatenate([cum_rows, jnp.zeros((SPAN - 8, SPAN), F32)], axis=0).T
        decay_grad = exact(lower, cum_cols - rows_t, ((0,), (0,)))
        log_decay = step * hp[1:2, :]
        slope = 1.0 - jnp.exp(-step)
        rate_grad = (step_cols + decay_grad * hp[1:2, :]) * slope
        heads[0:1, :] += jnp.sum(rate_grad, axis=0, keepdims=True)
        heads[1:2, :] += jnp.sum(decay_grad * log_decay, axis=0, keepdims=True)
        dcom[:, 2 * TILE :] = dot(rate_grad.astype(BF16), sel[...], ((1,), (1,))).astype(BF16)

    def backward(
        self, docs, starts, unit, projm, pre_sig, pre_bc, o, sin, step, cum, dg, st, taps, sel, hp, chp
    ):
        nd, nm, span = self.nd, self.nm, self.span
        wide = nd * TILE
        whole = lambda shape: pl.BlockSpec(shape, lambda i: (0,) * len(shape))
        at = lambda i: nm - 1 - i
        prev = lambda i: jnp.maximum(nm - 2 - i, 0)
        return pl.pallas_call(
            functools.partial(self.backward_kernel, docs),
            grid=(nm,),
            in_specs=[
                SM,
                SM,
                pl.BlockSpec((SPAN, 2 * wide), lambda i: (at(i), 0)),
                pl.BlockSpec((SPAN, wide), lambda i: (prev(i), 1)),
                pl.BlockSpec((SPAN, wide), lambda i: (at(i), 0)),
                pl.BlockSpec((SPAN, 2 * TILE), lambda i: (at(i), 0)),
                pl.BlockSpec((SPAN, wide), lambda i: (at(i), 0)),
                pl.BlockSpec((1, STATE, wide), lambda i: (at(i), 0, 0)),
                pl.BlockSpec((SPAN, TILE), lambda i: (at(i), 0)),
                pl.BlockSpec((SPAN, TILE), lambda i: (at(i), 0)),
                pl.BlockSpec((SPAN, wide), lambda i: (at(i), 0)),
                pl.BlockSpec((1, 8, TILE), lambda i: (at(i), 0, 0)),
                whole(taps.shape),
                whole(sel.shape),
                whole(hp.shape),
                whole(chp.shape),
            ],
            out_specs=[
                pl.BlockSpec((SPAN, 2 * wide), lambda i: (at(i), 0)),
                pl.BlockSpec((SPAN, COMMON), lambda i: (at(i), 0)),
                pl.BlockSpec((SPAN, wide), lambda i: (at(i), 0)),
                whole((8, wide)),
                whole((8, TILE)),
            ],
            out_shape=[
                jax.ShapeDtypeStruct((span, 2 * wide), BF16),
                jax.ShapeDtypeStruct((span, COMMON), BF16),
                jax.ShapeDtypeStruct((span, wide), BF16),
                jax.ShapeDtypeStruct((8, wide), F32),
                jax.ShapeDtypeStruct((8, TILE), F32),
            ],
            scratch_shapes=[pltpu.VMEM((STATE, wide), F32), pltpu.VMEM((16, wide), F32)],
            compiler_params=pltpu.CompilerParams(vmem_limit_bytes=LIMIT),
            name="backward",
        )(starts, unit, projm, projm, pre_sig, pre_bc, o, sin, step, cum, dg, st, taps, sel, hp, chp)

    def common_kernel(
        self, docs, starts, dcom, pre_bc, projc, taps, every, sums, padded, heard, mine,
        sends, recvs, back_s, back_r,
    ):
        nm = self.nm
        dp, c, z = self.place()
        me = c * self.nz + z
        steps = self.group_steps()
        padded[0 : self.span, :] = dcom[...]
        padded[self.span :, :] = jnp.zeros((16, COMMON), BF16)
        self.barrier(line=False)
        copies = []
        long = SPAN + 16
        for j, step in enumerate(steps):
            device, there = self.target(step)
            src = padded.at[pl.ds(pl.multiple_of(there * SPAN, SPAN), long), :]
            copy = remote(src, heard.at[j], sends.at[j], recvs.at[j], device)
            copy.start()
            copies.append(copy)
        base = pl.multiple_of(me * SPAN, SPAN)
        total = padded[pl.ds(base, long), :].astype(F32)
        for j, copy in enumerate(copies):
            copy.wait_recv()
            total = total + heard[j].astype(F32)
        after = pl.multiple_of(lax.rem(me + 1, nm) * SPAN, SPAN)
        ahead = pl.multiple_of(lax.rem(me + nm - 1, nm) * SPAN + SPAN - 16, 16)
        rows = base + iota((long, TILE), 0)
        begin = begin_at(rows, starts, docs)
        inside = rows < self.span
        for i in range(2):
            lanes = tile_of(i)
            pre = jnp.concatenate([pre_bc[pl.ds(base, SPAN), lanes], pre_bc[pl.ds(after, 16), lanes]], axis=0)
            later = jnp.where(inside, total[:, lanes] * silu_slope(pre), 0.0)
            ext = jnp.concatenate([projc[pl.ds(ahead, 16), lanes], projc[pl.ds(base, SPAN), lanes]], axis=0)
            ext = ext.astype(F32)
            sums[i : i + 1, :] = jnp.sum(later[:SPAN], axis=0, keepdims=True)
            back_grad = jnp.zeros((SPAN, TILE), F32)
            for tap in range(KW):
                back = KW - 1 - tap
                masked = jnp.where(rows - back >= begin, later, 0.0)
                moved = ext if back == 0 else pltpu.roll(ext, back, 0)
                sums[2 + 2 * tap + i : 3 + 2 * tap + i, :] = jnp.sum(
                    masked[:SPAN] * moved[16:], axis=0, keepdims=True
                )
                shifted_up = masked if back == 0 else pltpu.roll(masked, long - back, 0)
                side = tile_of(self.nd + i)
                back_grad = back_grad + shifted_up[:SPAN] * taps[tap : tap + 1, side]
            mine[:, lanes] = back_grad.astype(BF16)
        mine[:, 2 * TILE :] = total[:SPAN, 2 * TILE :].astype(BF16)
        sums[10:16, :] = jnp.zeros((6, TILE), F32)
        every[me] = mine[...]
        outs = []
        for j, step in enumerate(steps):
            device, _ = self.target(step)
            copy = remote(mine, every.at[me], back_s.at[j], back_r.at[j], device)
            copy.start()
            outs.append(copy)
        for j, step in enumerate(steps):
            device, _ = self.target(step)
            block = every.at[self.source(step)]
            remote(mine, block, back_s.at[j], back_r.at[j], device).wait_recv()
        for copy in copies + outs:
            copy.wait_send()

    def common(self, docs, starts, dcom, pre_bc, projc, taps):
        nm = self.nm
        n = nm - 1
        return pl.pallas_call(
            functools.partial(self.common_kernel, docs),
            out_shape=[jax.ShapeDtypeStruct((nm, SPAN, COMMON), BF16), jax.ShapeDtypeStruct((16, TILE), F32)],
            in_specs=[SM, VM, VM, VM, VM],
            out_specs=[VM, VM],
            scratch_shapes=[
                pltpu.VMEM((self.span + 16, COMMON), BF16),
                pltpu.VMEM((n, SPAN + 16, COMMON), BF16),
                pltpu.VMEM((SPAN, COMMON), BF16),
                DMA((n,)), DMA((n,)), DMA((n,)), DMA((n,)),
            ],
            compiler_params=pltpu.CompilerParams(
                collective_id=2, has_side_effects=True, vmem_limit_bytes=LIMIT
            ),
            name="common",
        )(starts, dcom, pre_bc, projc, taps)

    def reduce_kernel(
        self, unit, yp, dxp, dwp, dwop, dwcp, parp, x_ref, g_ref, dxc, st, gain,
        y_out, dx_out, dw_out, dwo_out, dwc_out, par_out,
        yc, xc, ysum, xsum, yz, xz, wd, wod, wcd, wsum, pard, parbuf,
        yc_s, yc_r, xc_s, xc_r, yz_s, yz_r, xz_s, xz_r, wd_s, wd_r, wod_s, wod_r, wcd_s, wcd_r,
        wz_s, wz_r, pd_s, pd_r, pg_s, pg_r,
    ):
        nd, nc, nz, nm = self.nd, self.nc, self.nz, self.nm
        dp, c, z = self.place()
        me = c * nz + z
        steps = self.group_steps()
        lines = [(k, (lax.rem(dp + k, nd), c, z), lax.rem(dp + k, nd)) for k in range(1, nd)]
        self.barrier()
        started = []

        def go(copy):
            copy.start()
            started.append(copy)
            return copy

        other = (dp, nc - 1 - c, z)
        theirs = pl.ds((nc - 1 - c) * nz, nz)
        cores = [
            go(remote(yp.at[theirs], yc, yc_s, yc_r, other)),
            go(remote(dxp.at[theirs], xc, xc_s, xc_r, other)),
        ]
        overs = []
        for k, device, to in lines:
            overs.append(go(remote(dwp.at[to], wd.at[k - 1], wd_s.at[k], wd_r.at[k], device)))
            overs.append(go(remote(dwop.at[to], wod.at[k - 1], wod_s.at[k], wod_r.at[k], device)))
            overs.append(go(remote(dwcp.at[to], wcd.at[k - 1], wcd_s.at[k], wcd_r.at[k], device)))
        zs = []
        for part, came, total, heard, z_s, z_r, core in (
            (yp, yc, ysum, yz, yz_s, yz_r, cores[0]),
            (dxp, xc, xsum, xz, xz_s, xz_r, cores[1]),
        ):
            core.wait_recv()
            for d in range(nz):
                there = lax.rem(z + d, nz)

                def add(r, _, part=part, came=came, total=total, there=there):
                    at = pl.ds(pl.multiple_of(r * 16, 16), 16)
                    total[there, at, :] = (
                        part[c * nz + there, at, :].astype(F32) + came[there, at, :].astype(F32)
                    ).astype(BF16)
                    return 0

                lax.fori_loop(0, SPAN // 16, add, 0)
                if d:
                    zs.append(
                        go(remote(total.at[there], heard.at[d - 1], z_s.at[d], z_r.at[d], (dp, c, there)))
                    )
        for copy in overs:
            copy.wait_recv()

        def add_weight(r, _):
            at = pl.ds(pl.multiple_of(r * 16, 16), 16)
            total = dwp[dp, at, :].astype(F32)
            for k in range(nd - 1):
                total = total + wd[k, at, :].astype(F32)
            wsum[at, :] = total.astype(BF16)
            return 0

        lax.fori_loop(0, nm * self.rows_in // 16, add_weight, 0)
        block = lambda m: wsum.at[pl.ds(pl.multiple_of(m * self.rows_in, self.rows_in), self.rows_in), :]
        for j, step in enumerate(steps):
            device, there = self.target(step)
            go(remote(block(there), dw_out.at[me], wz_s.at[j], wz_r.at[j], device))
        dw_out[me] = block(me)[...]

        def add_out(r, _):
            at = pl.ds(pl.multiple_of(r * 16, 16), 16)
            total = dwop[dp, at, :].astype(F32)
            for k in range(nd - 1):
                total = total + wod[k, at, :].astype(F32)
            dwo_out[at, :] = total
            return 0

        lax.fori_loop(0, TILE // 16, add_out, 0)
        total = dwcp[dp].astype(F32)
        for k in range(nd - 1):
            total = total + wcd[k].astype(F32)
        dwc_out[...] = total
        for copy in zs:
            copy.wait_recv()
        stat = jnp.concatenate([st[me], jnp.zeros((SPAN - 8, TILE), F32)], axis=0).T
        square = stat[:, 0:1]
        root = lax.rsqrt(square * unit[0, 0] + EPSILON)
        hidden = x_ref[...].astype(F32)
        branch = ysum[z].astype(F32)
        normed_grad = xsum[z].astype(F32) + dxc[...]
        for d in range(nz - 1):
            branch = branch + yz[d].astype(F32)
            normed_grad = normed_grad + xz[d].astype(F32)
        y_out[...] = (hidden + root * branch).astype(BF16)
        inverse = lax.rsqrt(jnp.mean(hidden * hidden, axis=1, keepdims=True) + EPSILON)
        unitary = hidden * inverse
        gain_grad = jnp.sum(normed_grad * unitary, axis=0, keepdims=True)
        scaled = normed_grad * gain[0:1, :]
        middle = jnp.mean(scaled * unitary, axis=1, keepdims=True)
        dx_out[...] = (g_ref[...].astype(F32) + inverse * (scaled - unitary * middle)).astype(BF16)
        parbuf[...] = parp[...]
        for i in range(MODEL // TILE):
            parbuf[i : i + 1, :] = gain_grad[:, tile_of(i)]
        small = [
            go(remote(parbuf, pard.at[k - 1], pd_s.at[k], pd_r.at[k], device)) for k, device, _ in lines
        ]
        for copy in small:
            copy.wait_recv()
        total = parbuf[...]
        for k in range(nd - 1):
            total = total + pard[k]
        par_out[me] = total
        last = [
            go(remote(par_out.at[me], par_out.at[me], pg_s.at[j], pg_r.at[j], self.target(step)[0]))
            for j, step in enumerate(steps)
        ]
        for j, step in enumerate(steps):
            device, _ = self.target(step)
            here = par_out.at[self.source(step)]
            remote(here, here, pg_s.at[j], pg_r.at[j], device).wait_recv()
            got = dw_out.at[self.source(step)]
            remote(got, got, wz_s.at[j], wz_r.at[j], device).wait_recv()
        for copy in started:
            copy.wait_send()

    def reduce(self, unit, yp, dxp, dwp, dwop, dwcp, parp, x, g, dxc, st, gain):
        nd, nz, nm, rows = self.nd, self.nz, self.nm, self.rows_in
        wide = 2 * nd * TILE
        block = (SPAN, MODEL)
        return pl.pallas_call(
            self.reduce_kernel,
            out_shape=[
                jax.ShapeDtypeStruct(block, BF16),
                jax.ShapeDtypeStruct(block, BF16),
                jax.ShapeDtypeStruct((nm, rows, wide), BF16),
                jax.ShapeDtypeStruct((TILE, MODEL), F32),
                jax.ShapeDtypeStruct((rows, COMMON), F32),
                jax.ShapeDtypeStruct((nm, *parp.shape), F32),
            ],
            in_specs=[SM] + [VM] * 11,
            out_specs=[VM] * 6,
            scratch_shapes=[
                pltpu.VMEM((nz, *block), BF16),
                pltpu.VMEM((nz, *block), BF16),
                pltpu.VMEM((nz, *block), BF16),
                pltpu.VMEM((nz, *block), BF16),
                pltpu.VMEM((nz - 1, *block), BF16),
                pltpu.VMEM((nz - 1, *block), BF16),
                pltpu.VMEM((nd - 1, nm * rows, wide), BF16),
                pltpu.VMEM((nd - 1, TILE, MODEL), BF16),
                pltpu.VMEM((nd - 1, rows, COMMON), BF16),
                pltpu.VMEM((nm * rows, wide), BF16),
                pltpu.VMEM((nd - 1, *parp.shape), F32),
                pltpu.VMEM(parp.shape, F32),
                DMA, DMA, DMA, DMA,
                DMA((nz,)), DMA((nz,)), DMA((nz,)), DMA((nz,)),
                DMA((nd,)), DMA((nd,)), DMA((nd,)), DMA((nd,)), DMA((nd,)), DMA((nd,)),
                DMA((nm,)), DMA((nm,)), DMA((nd,)), DMA((nd,)), DMA((nm,)), DMA((nm,)),
            ],
            compiler_params=pltpu.CompilerParams(
                collective_id=3, has_side_effects=True, vmem_limit_bytes=60 * 2**20
            ),
            name="reduce",
        )(unit, yp, dxp, dwp, dwop, dwcp, parp, x, g, dxc, st, gain)

    def local(
        self, layer_input, out_grad, norm_gain, in_weight, conv_weight, conv_bias, step_bias, log_rate,
        skip_gain, gate_gain, out_weight, nest_level, doc_lengths,
    ):
        nd, nc, nz, nm, rows = self.nd, self.nc, self.nz, self.nm, self.rows_in
        span, wide = self.span, nd * TILE
        dp, c, z = self.place()
        me = c * nz + z
        docs = doc_lengths.shape[1]
        order = jnp.arange(docs)
        ahead = order[:, None] < order[None, :]
        starts = jnp.sum(jnp.where(ahead, doc_lengths[0][:, None], 0), axis=0, keepdims=True)
        starts = starts.astype(jnp.int32)
        active = jnp.right_shift(HEADS, 3 - nest_level[0])
        unit = (1.0 / (active * HEAD_DIM).astype(F32)).reshape(1, 1)
        x = layer_input.reshape(SPAN, MODEL)
        g = out_grad.reshape(SPAN, MODEL)
        wm = in_weight[:, : 2 * INNER].reshape(rows, 2 * nd, nm, TILE)
        wm = jnp.transpose(wm, (2, 0, 1, 3)).reshape(nm, rows, 2 * wide)
        wc = jnp.pad(in_weight[:, 2 * INNER :], ((0, 0), (0, COMMON - (EXTENT - 2 * INNER))))
        own_conv = conv_bias.shape[0]
        conv_pack = jnp.concatenate([conv_bias, conv_weight.reshape(-1)])
        par = jnp.concatenate(
            [
                jnp.pad(norm_gain, (0, TILE - rows)),
                gate_gain,
                jnp.pad(conv_pack, (0, 6 * TILE - conv_pack.shape[0])),
            ]
        ).reshape(8, TILE)
        xall, gall, wall, wcall, woall, parall = self.gather(x, par, g, wm, wc, out_weight)
        by_owner = jnp.swapaxes(parall, 0, 1)
        gain = by_owner[:, :, 0, :rows].reshape(1, MODEL)
        gate_mine = lax.dynamic_index_in_dim(parall, me, 0, keepdims=False)[:, 1, :].reshape(wide)
        conv_all = by_owner[:, :, 2:, :].reshape(nd * nm, 6 * TILE)
        bias_all = conv_all[:, :own_conv].reshape(CONV)
        taps_all = conv_all[:, own_conv : own_conv * (1 + KW)].reshape(CONV, KW)

        def my_channels(values):
            main = values[:INNER].reshape(nd, nm, TILE, *values.shape[1:])
            main = lax.dynamic_index_in_dim(main, me, 1, keepdims=False)
            return jnp.concatenate([main.reshape(wide, *values.shape[1:]), values[INNER:]], axis=0)

        bias = my_channels(bias_all).reshape(1, -1)
        taps = jnp.pad(my_channels(taps_all).T, ((0, 8 - KW), (0, 0)))
        per = HEADS // (nd * nm)

        def my_heads(values):
            return lax.dynamic_index_in_dim(values.reshape(nd, nm, per), me, 1, keepdims=False).reshape(-1)

        numbers = my_heads(jnp.arange(HEADS))
        mine = nd * per
        sel = (jnp.arange(TILE)[:, None] == jnp.pad(numbers, (0, TILE - mine), constant_values=-1)[None, :])
        sel = sel.astype(BF16)
        lane_pad = lambda v: jnp.pad(v, (0, TILE - mine))
        hp = jnp.stack([lane_pad(my_heads(step_bias)), lane_pad(my_heads(-jnp.exp(log_rate)))])
        hp = jnp.pad(hp, ((0, 6), (0, 0)))
        mask = (numbers < active).astype(F32)
        chp = jnp.stack(
            [jnp.repeat(my_heads(skip_gain), HEAD_DIM), jnp.repeat(mask, HEAD_DIM), gate_mine]
        )
        chp = jnp.pad(chp, ((0, 5), (0, 0)))
        xflat = xall.reshape(span, MODEL)
        gflat = gall.reshape(span, MODEL)
        wflat = wall.reshape(MODEL, 2 * wide)
        wcflat = wcall.reshape(MODEL, COMMON)
        woflat = woall.reshape(wide, MODEL)
        projm = jnp.dot(xflat, wflat, preferred_element_type=F32).astype(BF16)
        projc = jnp.dot(xflat, wcflat, preferred_element_type=F32).astype(BF16)
        pre_sig, pre_bc, o, sin, step, cum, dg, y, st = self.forward(
            docs, starts, projm, projc, gflat, woflat, taps, bias, sel, hp, chp
        )
        st = self.stats(st)
        dproj, dcom, normed_out, sums, heads = self.backward(
            docs, starts, unit, projm, pre_sig, pre_bc, o, sin, step, cum, dg, st, taps, sel, hp, chp
        )
        dcall, bc_sums = self.common(docs, starts, dcom, pre_bc, projc, taps)
        dxp = lax.dot_general(dproj, wflat, (((1,), (1,)), ((), ())), preferred_element_type=F32)
        dxp = dxp.astype(BF16).reshape(nm, SPAN, MODEL)
        dwp = lax.dot_general(xflat, dproj, (((0,), (0,)), ((), ())), preferred_element_type=F32)
        dwp = dwp.astype(BF16).reshape(nd, nm * rows, 2 * wide)
        dwop = lax.dot_general(normed_out, gflat, (((0,), (0,)), ((), ())), preferred_element_type=F32)
        dwop = dwop.astype(BF16).reshape(nd, TILE, MODEL)
        dc_mine = lax.dynamic_index_in_dim(dcall, me, 0, keepdims=False)
        dxc = lax.dot_general(dc_mine, wcflat, (((1,), (1,)), ((), ())), preferred_element_type=F32)
        x_rows = lax.dynamic_index_in_dim(xflat.reshape(span, nd, nm, rows), me, 2, keepdims=False)
        dwcp = lax.dot_general(
            x_rows.reshape(span, nd * rows), dcall.reshape(span, COMMON), (((0,), (0,)), ((), ())),
            preferred_element_type=F32,
        )
        dwcp = dwcp.astype(BF16).reshape(nd, rows, COMMON)
        parp = jnp.concatenate(
            [
                jnp.zeros((MODEL // TILE, TILE), F32),
                sums.reshape(8 * nd, TILE),
                bc_sums,
                heads,
            ]
        )
        y_out, dx_out, dw, dwo, dwc, pars = self.reduce(
            unit, y.reshape(nm, SPAN, MODEL), dxp, dwp, dwop, dwcp, parp, x, g, dxc, st, gain
        )
        dw = jnp.transpose(dw.reshape(nm, rows, 2 * nd, TILE), (1, 2, 0, 3)).reshape(rows, 2 * INNER)
        in_weight_grad = jnp.concatenate([dw.astype(F32), dwc[:, : EXTENT - 2 * INNER]], axis=1)
        owner = dp * nm + me
        gains = jnp.sum(pars[:, : MODEL // TILE], axis=0).reshape(MODEL)
        norm_gain_grad = lax.dynamic_slice_in_dim(gains, owner * rows, rows)
        base = MODEL // TILE
        mains = pars[:, base : base + 8 * nd].reshape(nm, 8, nd, TILE)
        shared = jnp.sum(pars[:, base + 8 * nd : base + 8 * nd + 16], axis=0)
        head_sums = pars[:, base + 8 * nd + 16 :]
        gate_gain_grad = lax.dynamic_index_in_dim(mains[me, 0], dp, 0, keepdims=False)
        everything = jnp.transpose(mains[:, 1:], (1, 2, 0, 3)).reshape(7, INNER)
        skip_gain_grad = jnp.sum(everything[0].reshape(HEADS, HEAD_DIM), axis=1)
        bias_sum = jnp.concatenate([everything[1], shared[:2].reshape(-1)])
        taps_sum = jnp.concatenate([everything[3:], shared[2:10].reshape(KW, 2 * TILE)], axis=1).T
        conv_bias_grad = lax.dynamic_slice_in_dim(bias_sum, owner * own_conv, own_conv)
        conv_weight_grad = lax.dynamic_slice_in_dim(taps_sum, owner * own_conv, own_conv)
        by_head = lambda v: jnp.swapaxes(v[:, :mine].reshape(nm, nd, per), 0, 1).reshape(HEADS)
        step_bias_grad, log_rate_grad = by_head(head_sums[:, 0]), by_head(head_sums[:, 1])
        return (
            y_out.reshape(1, SPAN, MODEL),
            dx_out.reshape(1, SPAN, MODEL),
            norm_gain_grad,
            in_weight_grad,
            conv_weight_grad,
            conv_bias_grad,
            step_bias_grad,
            log_rate_grad,
            skip_gain_grad,
            gate_gain_grad,
            dwo,
        )


def solution(mesh):
    shape = dict(mesh.shape)
    head_split = HeadSplit(shape["dp"], shape["seq"], shape["fsdp"])
    return jax.shard_map(
        head_split.local if head_split.fits() else token_split,
        mesh=mesh,
        in_specs=(
            P("dp", ("seq", "fsdp"), None),
            P("dp", ("seq", "fsdp"), None),
            P(("dp", "seq", "fsdp")),
            P(("dp", "seq", "fsdp"), None),
            P(("dp", "seq", "fsdp"), None),
            P(("dp", "seq", "fsdp")),
            P(),
            P(),
            P(),
            P(("dp", "seq", "fsdp")),
            P(("dp", "seq", "fsdp"), None),
            P("dp"),
            P("dp", None),
        ),
        out_specs=(
            P("dp", ("seq", "fsdp"), None),
            P("dp", ("seq", "fsdp"), None),
            P(("dp", "seq", "fsdp")),
            P(("dp", "seq", "fsdp"), None),
            P(("dp", "seq", "fsdp"), None),
            P(("dp", "seq", "fsdp")),
            P(),
            P(),
            P(),
            P(("dp", "seq", "fsdp")),
            P(("dp", "seq", "fsdp"), None),
        ),
        check_vma=False,
    )
```

```python
import functools

import jax
import jax.numpy as jnp
from jax import lax
from jax.experimental import pallas as pl
from jax.experimental.pallas import tpu as pltpu
from jax.sharding import PartitionSpec as P

HEADS = 64
HEAD_DIM = 64
STATE = 128
KW = 4
INNER = 4096
CONV = 4352
EXTENT = 8512


HIGH = lax.Precision.HIGHEST
EPSILON = 1e-05


def shifted(value, axis, steps):
    count = lax.axis_size(axis)
    leading, last = (max(0, -steps), min(count, count - steps))
    return lax.ppermute(value, axis, [(source, source + steps) for source in range(leading, last)])


def prefix(array, axis, combine, identity):
    peers, place = (lax.axis_size(axis), lax.axis_index(axis))
    everything = jax.tree.map(
        lambda part, kind: lax.all_gather(part.astype(kind), axis),
        array,
        (jnp.bfloat16, jnp.bfloat16),
    )
    start = jax.tree.map(
        lambda part, zero: jnp.broadcast_to(jnp.asarray(zero, part.dtype), part.shape),
        array,
        identity,
    )

    def prefix_lap(k, before):
        reached = k < place
        new = combine(
            before, jax.tree.map(lambda part, own: part[k].astype(own.dtype), everything, array)
        )
        return jax.tree.map(lambda a, b: jnp.where(reached, a, b), new, before)

    return lax.fori_loop(0, peers, prefix_lap, start)


def carried_in(array, axis, combine, identity):
    peers, place = (lax.axis_size(axis), lax.axis_index(axis))
    everything = jax.tree.map(
        lambda part, kind: lax.all_gather(part.astype(kind), axis),
        array,
        jax.tree.map(lambda a: jnp.bfloat16 if a.dtype == jnp.float32 else a.dtype, array),
    )
    start = jax.tree.map(
        lambda part, zero: jnp.broadcast_to(jnp.asarray(zero, part.dtype), part.shape),
        array,
        identity,
    )

    def carried_lap(k, before):
        at = peers - 1 - k
        reached = at > place
        new = combine(
            before, jax.tree.map(lambda part, own: part[at].astype(own.dtype), everything, array)
        )
        return jax.tree.map(lambda a, b: jnp.where(reached, a, b), new, before)

    return lax.fori_loop(0, peers, carried_lap, start)


def doc_begins(lengths, positions):
    places = jnp.arange(lengths.shape[1])
    ahead = places[:, None] < places[None, :]
    endings = jnp.sum(jnp.where(ahead[None], lengths[:, :, None], 0), axis=1)
    reached = endings[:, None, :] <= positions[None, :, None]
    return jnp.max(jnp.where(reached, endings[:, None, :], 0), axis=2)


def input_norm(hidden, gain):
    inv_rms = lax.rsqrt(jnp.mean(hidden * hidden, axis=1, keepdims=True) + EPSILON)
    return hidden * inv_rms * gain


def causal_conv(extended, taps, bias, validity):
    block_len = validity.shape[2]
    running = bias + jnp.zeros((extended.shape[0], block_len, extended.shape[2]), jnp.float32)
    for tap in range(taps.shape[1]):
        running = (
            running + extended[:, tap : tap + block_len] * taps[:, tap] * validity[tap][:, :, None]
        )
    return jax.nn.silu(running)


def scan_parts(signal, key_side, query_side, rate_in, step_bias, log_rate, begins, block_start):
    step = jax.nn.softplus(rate_in + step_bias)
    log_decay = step * -jnp.exp(log_rate)
    places = jnp.arange(log_decay.shape[1])
    lower = (places[None, :] <= places[:, None]).astype(jnp.float32)
    cumulative = jnp.einsum("ts,bsh->bth", lower, log_decay, precision=HIGH)
    by_head = jnp.swapaxes(cumulative, 1, 2)
    indices = jnp.arange(signal.shape[1])
    same_doc = (begins[:, :, None] == begins[:, None, :]) & (
        indices[None, None, :] <= indices[None, :, None]
    )
    gaps = by_head[:, :, :, None] - by_head[:, :, None, :]
    kernel = jnp.exp(jnp.where(same_doc[:, None], gaps, 0.0)) * same_doc[:, None]
    intersection = jnp.einsum("btn,bsn->bts", query_side, key_side, precision=HIGH)
    mixing = kernel * intersection[:, None] * jnp.swapaxes(step, 1, 2)[:, :, None, :]
    local_out = jnp.einsum("bhts,bshp->bthp", mixing, signal, precision=HIGH)
    inherits = (begins < block_start).astype(jnp.float32)
    carried = jnp.exp(cumulative) * inherits[:, :, None]
    last_same = begins == begins[:, -1:]
    tail_weight = (
        jnp.exp(jnp.where(last_same[:, :, None], cumulative[:, -1:] - cumulative, 0.0))
        * last_same[:, :, None]
        * step
    )
    fresh_state = jnp.einsum("bsh,bshp,bsn->bhpn", tail_weight, signal, key_side, precision=HIGH)
    return (local_out, carried, carried[:, -1], fresh_state)


def gated_norm(scan_out, signal, skip_gain, gate_in, gate_gain, head_mask, unit_count):
    mixed = (scan_out + skip_gain[:, None] * signal) * head_mask[:, None, :, None]
    gated = mixed.reshape(gate_in.shape) * jax.nn.silu(gate_in)
    mean_square = jnp.sum(gated * gated, axis=2, keepdims=True) / unit_count[:, None, None]
    return gated * lax.rsqrt(mean_square + EPSILON) * gate_gain


def combine_states(earlier, later):
    return (earlier[0] * later[0], later[1] + later[0][:, :, None, None] * earlier[1])


def token_split(
    layer_input,
    out_grad,
    norm_gain,
    in_weight,
    conv_weight,
    conv_bias,
    step_bias,
    log_rate,
    skip_gain,
    gate_gain,
    out_weight,
    nest_level,
    doc_lengths,
):
    seq_count, block_len, model_width = layer_input.shape
    token_count = seq_count * block_len
    gain_all, taps_all, bias_all, gate_all = (
        lax.all_gather(norm_gain, ("dp", "seq", "fsdp"), axis=0, tiled=True),
        lax.all_gather(conv_weight, ("dp", "seq", "fsdp"), axis=0, tiled=True),
        lax.all_gather(conv_bias, ("dp", "seq", "fsdp"), axis=0, tiled=True),
        lax.all_gather(gate_gain, ("dp", "seq", "fsdp"), axis=0, tiled=True),
    )
    block_start = lax.axis_index(("seq", "fsdp")) * block_len
    positions = block_start + jnp.arange(block_len, dtype=jnp.int32)
    begins = doc_begins(doc_lengths, positions)
    hidden = layer_input.reshape(token_count, model_width).astype(jnp.float32)
    normed = input_norm(hidden, gain_all).astype(jnp.bfloat16)
    columns = normed
    projected = jnp.dot(
        columns,
        lax.all_gather(in_weight, ("dp", "seq", "fsdp"), axis=0, tiled=True),
        preferred_element_type=jnp.float32,
    ).astype(jnp.bfloat16)
    projected = projected.reshape(seq_count, block_len, EXTENT)
    gate_in = projected[:, :, :INNER].astype(jnp.float32)
    conv_in = projected[:, :, INNER : INNER + CONV]
    rate_in = projected[:, :, INNER + CONV :].astype(jnp.float32)
    edge_rows = shifted(conv_in[:, block_len - (KW - 1) :], ("seq", "fsdp"), 1)
    extended = jnp.concatenate([edge_rows, conv_in], axis=1).astype(jnp.float32)
    validity = jnp.stack(
        [(positions[None, :] - (KW - 1) + tap >= begins).astype(jnp.float32) for tap in range(KW)]
    )
    activated, conv_pull = jax.vjp(
        lambda ext_in, taps, bias: causal_conv(ext_in, taps, bias, validity),
        extended,
        taps_all,
        bias_all,
    )
    signal = activated[:, :, :INNER].reshape(seq_count, block_len, HEADS, HEAD_DIM)
    key_side = activated[:, :, INNER : INNER + STATE]
    query_side = activated[:, :, INNER + STATE :]
    local_out, carried, decays, fresh_state = scan_parts(
        signal, key_side, query_side, rate_in, step_bias, log_rate, begins, block_start
    )
    identity = (jnp.ones_like(decays), jnp.zeros_like(fresh_state))
    entry_state = prefix((decays, fresh_state), ("seq", "fsdp"), combine_states, identity)[1]
    scan_out = local_out + carried[..., None] * jnp.einsum(
        "btn,bhpn->bthp", query_side, entry_state, precision=HIGH
    )
    active = jnp.right_shift(HEADS, 3 - nest_level)
    head_mask = (jnp.arange(HEADS)[None, :] < active[:, None]).astype(jnp.float32)
    unit_count = (active * HEAD_DIM).astype(jnp.float32)
    gate_normed, gate_pull = jax.vjp(
        lambda sv, xv, sk, gi, gg: gated_norm(sv, xv, sk, gi, gg, head_mask, unit_count),
        scan_out,
        signal,
        skip_gain,
        gate_in,
        gate_all,
    )
    normed_out = gate_normed.reshape(token_count, INNER).astype(jnp.bfloat16)
    columns = normed_out
    branch_out = jnp.dot(
        columns,
        lax.all_gather(out_weight, ("dp", "seq", "fsdp"), axis=0, tiled=True),
        preferred_element_type=jnp.float32,
    )
    layer_output = (
        (hidden + branch_out).astype(jnp.bfloat16).reshape(seq_count, block_len, model_width)
    )
    grad_flat = out_grad.reshape(token_count, model_width)
    grad_normed_out = lax.dot_general(
        grad_flat,
        lax.all_gather(out_weight, ("dp", "seq", "fsdp"), axis=0, tiled=True),
        (((1,), (1,)), ((), ())),
        preferred_element_type=jnp.float32,
    )
    grad_scan, grad_skip_signal, grad_skip, grad_gate_in, grad_gate_gain = gate_pull(
        grad_normed_out.reshape(seq_count, block_len, INNER)
    )
    lead_grad = jnp.einsum("bth,bthp,btn->bhpn", carried, grad_scan, query_side, precision=HIGH)
    later_grad = carried_in((decays, lead_grad), ("seq", "fsdp"), combine_states, identity)[1]

    def full_scan(signal_in, key_in, query_in, rate_values, bias_values, rate_logs):
        part_out, part_carried, part_decays, part_fresh = scan_parts(
            signal_in, key_in, query_in, rate_values, bias_values, rate_logs, begins, block_start
        )
        joined_out = part_out + part_carried[..., None] * jnp.einsum(
            "btn,bhpn->bthp", query_in, entry_state, precision=HIGH
        )
        return (joined_out, part_decays[:, :, None, None] * entry_state + part_fresh)

    scan_pull = jax.vjp(full_scan, signal, key_side, query_side, rate_in, step_bias, log_rate)[1]
    grad_signal, grad_key, grad_query, grad_rate, grad_step_bias, grad_log_rate = scan_pull(
        (grad_scan, later_grad)
    )
    grad_activated = jnp.concatenate(
        [
            (grad_signal + grad_skip_signal).reshape(seq_count, block_len, INNER),
            grad_key,
            grad_query,
        ],
        axis=2,
    )
    grad_extended, grad_taps, grad_bias = conv_pull(grad_activated)
    returned = shifted(grad_extended[:, : KW - 1].astype(jnp.bfloat16), ("seq", "fsdp"), -1).astype(
        jnp.float32
    )
    grad_conv_in = grad_extended[:, KW - 1 :] + jnp.pad(
        returned, ((0, 0), (block_len - (KW - 1), 0), (0, 0))
    )
    grad_projected = (
        jnp.concatenate([grad_gate_in, grad_conv_in, grad_rate], axis=2)
        .reshape(token_count, EXTENT)
        .astype(jnp.bfloat16)
    )
    grad_normed = lax.dot_general(
        grad_projected,
        lax.all_gather(in_weight, ("dp", "seq", "fsdp"), axis=0, tiled=True),
        (((1,), (1,)), ((), ())),
        preferred_element_type=jnp.float32,
    )
    replicas = lax.axis_size("dp")
    members = lax.axis_size(("seq", "fsdp"))
    width_in = model_width // lax.axis_size(("dp", "seq", "fsdp"))
    width_out = INNER // lax.axis_size(("dp", "seq", "fsdp"))
    in_cols, out_cols = (
        lax.all_to_all(
            normed.reshape(token_count, replicas, members, width_in),
            ("seq", "fsdp"),
            split_axis=2,
            concat_axis=0,
            tiled=True,
        ),
        lax.all_to_all(
            normed_out.reshape(token_count, replicas, members, width_out),
            ("seq", "fsdp"),
            split_axis=2,
            concat_axis=0,
            tiled=True,
        ),
    )
    in_cols = in_cols.reshape(members * token_count, replicas * width_in)
    out_cols = out_cols.reshape(members * token_count, replicas * width_out)
    in_new = lax.dot_general(
        in_cols,
        lax.all_gather(grad_projected, ("seq", "fsdp"), axis=0, tiled=True),
        (((0,), (0,)), ((), ())),
        preferred_element_type=jnp.float32,
    )
    out_new = lax.dot_general(
        out_cols,
        lax.all_gather(grad_flat, ("seq", "fsdp"), axis=0, tiled=True),
        (((0,), (0,)), ((), ())),
        preferred_element_type=jnp.float32,
    )
    in_weight_grad, out_weight_grad = (
        lax.psum_scatter(in_new.astype(jnp.bfloat16), "dp", scatter_dimension=0, tiled=True).astype(
            jnp.float32
        ),
        lax.psum_scatter(
            out_new.astype(jnp.bfloat16), "dp", scatter_dimension=0, tiled=True
        ).astype(jnp.float32),
    )
    norm_pull = jax.vjp(input_norm, hidden, gain_all)[1]
    grad_hidden, grad_gain = norm_pull(grad_normed)
    input_grad = (
        (grad_flat.astype(jnp.float32) + grad_hidden)
        .astype(jnp.bfloat16)
        .reshape(seq_count, block_len, model_width)
    )
    norm_gain_grad, conv_weight_grad, conv_bias_grad, gate_gain_grad = (
        lax.psum_scatter(grad_gain, ("dp", "seq", "fsdp"), scatter_dimension=0, tiled=True),
        lax.psum_scatter(grad_taps, ("dp", "seq", "fsdp"), scatter_dimension=0, tiled=True),
        lax.psum_scatter(grad_bias, ("dp", "seq", "fsdp"), scatter_dimension=0, tiled=True),
        lax.psum_scatter(grad_gate_gain, ("dp", "seq", "fsdp"), scatter_dimension=0, tiled=True),
    )
    step_bias_grad, log_rate_grad, skip_gain_grad = lax.psum(
        (grad_step_bias, grad_log_rate, grad_skip), ("dp", "seq", "fsdp")
    )
    return (
        layer_output,
        input_grad,
        norm_gain_grad,
        in_weight_grad,
        conv_weight_grad,
        conv_bias_grad,
        step_bias_grad,
        log_rate_grad,
        skip_gain_grad,
        gate_gain_grad,
        out_weight_grad,
    )


MESH = pl.DeviceIdType.MESH
F32 = jnp.float32
BF16 = jnp.bfloat16
TILE = 128
SPAN = 128
MODEL = 2048
COMMON = 384
PAD = 16
NEG = -1e30
VM = pl.BlockSpec(memory_space=pltpu.VMEM)
SM = pl.BlockSpec(memory_space=pltpu.SMEM)
ANY = pl.BlockSpec(memory_space=pl.ANY)
DMA = pltpu.SemaphoreType.DMA


def remote(src, dst, sends, recvs, device):
    return pltpu.make_async_remote_copy(
        src_ref=src,
        dst_ref=dst,
        send_sem=sends,
        recv_sem=recvs,
        device_id=device,
        device_id_type=MESH,
    )


def dot(a, b, over=((1,), (0,))):
    return lax.dot_general(a, b, (over, ((), ())), preferred_element_type=F32)


def exact(a, b, over=((1,), (0,))):
    return lax.dot_general(a, b, (over, ((), ())), precision=HIGH, preferred_element_type=F32)


def begin_at(place, starts, docs):
    begin = jnp.zeros_like(place)
    for doc in range(1, docs):
        begin = jnp.where(starts[0, doc] <= place, starts[0, doc], begin)
    return begin


def iota(shape, dim):
    return lax.broadcasted_iota(jnp.int32, shape, dim)


def silu_slope(value):
    gate = jax.nn.sigmoid(value)
    return gate * (1.0 + value * (1.0 - gate))


def softplus(value):
    return jnp.maximum(value, 0.0) + jnp.log1p(jnp.exp(-jnp.abs(value)))


def conv_tile(extended, taps, lanes, valid):
    total = jnp.broadcast_to(taps[KW : KW + 1, lanes], (SPAN, TILE))
    for tap in range(KW):
        back = KW - 1 - tap
        moved = extended if back == 0 else pltpu.roll(extended, back, 0)
        total = total + jnp.where(valid[tap], moved[PAD:], 0.0) * taps[tap : tap + 1, lanes]
    return total


def tile_of(index):
    return slice(index * TILE, (index + 1) * TILE)


def rows_of(index, size=SPAN):
    return pl.ds(pl.multiple_of(index * size, size), size)


def head_col(values, head):
    return jnp.broadcast_to(values[:, head : head + 1], (SPAN, TILE))


def lane_sum(values):
    return jnp.broadcast_to(jnp.sum(values, axis=1, keepdims=True), values.shape)


class Line:
    def __init__(self, place, sizes, block, sems):
        self.dp, self.c, self.z = place
        self.nc, self.nz = sizes
        self.block = block
        self.right_s, self.right_r, self.left_s, self.left_r, self.core_s, self.core_r = sems

    def right(self, s):
        block = self.block(self.c, self.z - s)
        to = (self.dp, self.c, lax.rem(self.z + 1, self.nz))
        return remote(block, block, self.right_s.at[s], self.right_r.at[s], to)

    def left(self, s):
        block = self.block(self.c, self.z + s)
        to = (self.dp, self.c, lax.rem(self.z + self.nz - 1, self.nz))
        return remote(block, block, self.left_s.at[s], self.left_r.at[s], to)

    def core(self, z):
        block = self.block(self.c, z)
        to = (self.dp, self.nc - 1 - self.c, self.z)
        return remote(block, block, self.core_s.at[z], self.core_r.at[z], to)

    def across(self):
        return (self.dp, self.nc - 1 - self.c, self.z)

    def begin(self):
        pl.when(self.z < self.nz - 1)(lambda: self.right(0).start())
        pl.when(self.z > 0)(lambda: self.left(0).start())
        self.core(self.z).start()

    def step(self, s):
        z, nz = self.z, self.nz

        @pl.when(z >= s)
        def _():
            block = self.block(self.c, z - s)
            remote(block, block, self.right_s.at[s - 1], self.right_r.at[s - 1], self.across()).wait_recv()
            if s < nz - 1:
                pl.when(z < nz - 1)(lambda: self.right(s).start())
            self.core(z - s).start()

        @pl.when(z + s < nz)
        def _():
            block = self.block(self.c, z + s)
            remote(block, block, self.left_s.at[s - 1], self.left_r.at[s - 1], self.across()).wait_recv()
            if s < nz - 1:
                pl.when(z > 0)(lambda: self.left(s).start())
            self.core(z + s).start()

    def arrive(self):
        for z in range(self.nz):
            block = self.block(self.nc - 1 - self.c, z)
            to = (self.dp, self.nc - 1 - self.c, self.z)
            remote(block, block, self.core_s.at[z], self.core_r.at[z], to).wait_recv()

    def end(self):
        z, nz = self.z, self.nz
        for s in range(nz - 1):
            pl.when((z >= s) & (z < nz - 1))(lambda s=s: self.right(s).wait_send())
            pl.when((z + s < nz) & (z > 0))(lambda s=s: self.left(s).wait_send())
        for s in range(nz):
            self.core(jnp.int32(s)).wait_send()


class Sum:
    def __init__(self, place, sizes, part, came, total, heard, sems):
        self.dp, self.c, self.z = place
        self.nc, self.nz = sizes
        self.part, self.came, self.total, self.heard = part, came, total, heard
        self.core_s, self.core_r, self.right_s, self.right_r, self.left_s, self.left_r = sems

    def core(self, t):
        to = (self.dp, self.nc - 1 - self.c, self.z)
        src = self.part.at[(self.nc - 1 - self.c) * self.nz + t]
        return remote(src, self.came.at[t], self.core_s.at[t], self.core_r.at[t], to)

    def right(self, t):
        to = (self.dp, self.c, lax.rem(self.z + 1, self.nz))
        return remote(self.total.at[t], self.heard.at[t], self.right_s.at[t], self.right_r.at[t], to)

    def left(self, t):
        to = (self.dp, self.c, lax.rem(self.z + self.nz - 1, self.nz))
        return remote(self.total.at[t], self.heard.at[self.nz + t], self.left_s.at[t], self.left_r.at[t], to)

    def add_core(self, t):
        self.core(t).wait_recv()

        def add(r, _):
            at = rows_of(r, 16)
            self.total[t, at, :] = (
                self.part[self.c * self.nz + t, at, :].astype(F32) + self.came[t, at, :].astype(F32)
            ).astype(BF16)
            return 0

        lax.fori_loop(0, SPAN // 16, add, 0)

    def add(self, t, slot):
        def add(r, _):
            at = rows_of(r, 16)
            self.total[t, at, :] = (
                self.total[t, at, :].astype(F32) + self.heard[slot, at, :].astype(F32)
            ).astype(BF16)
            return 0

        lax.fori_loop(0, SPAN // 16, add, 0)

    def begin(self):
        z, nz = self.z, self.nz
        for k in range(nz - 1):
            pl.when(z == 0)(lambda k=k: self.right(nz - 1 - k).start())
            pl.when(z == nz - 1)(lambda k=k: self.left(k).start())

    def relay(self, hops, k):
        z, nz = self.z, self.nz
        if nz - 1 - k <= hops:
            return

        @pl.when(z == hops)
        def _():
            t = nz - 1 - k
            self.right(t).wait_recv()
            self.add(t, t)
            self.right(t).start()

        @pl.when(z == nz - 1 - hops)
        def _():
            self.left(k).wait_recv()
            self.add(k, nz + k)
            self.left(k).start()

    def arrive(self):
        z, nz = self.z, self.nz
        for t in range(nz):
            pl.when((z == t) & (z > 0))(lambda t=t: self.right(t).wait_recv())
            pl.when((z == t) & (z < nz - 1))(lambda t=t: self.left(t).wait_recv())

    def own(self, rows):
        z, nz = self.z, self.nz
        value = self.total[z, rows, :].astype(F32)
        left = self.heard[z, rows, :].astype(F32)
        right = self.heard[nz + z, rows, :].astype(F32)
        value = value + jnp.where(z > 0, left, 0.0)
        return value + jnp.where(z < nz - 1, right, 0.0)

    def end(self):
        for t in range(self.nz):
            self.core(t).wait_send()
            pl.when(self.z < t)(lambda t=t: self.right(t).wait_send())
            pl.when(self.z > t)(lambda t=t: self.left(t).wait_send())


class Square:
    def __init__(self, place, block, size, sems):
        dp, c, z = place
        self.dp, self.dx, self.dy = dp, dp + 1 - 2 * lax.rem(dp, 2), lax.rem(dp + 2, 4)
        self.diag = lax.rem(self.dx + 2, 4)
        self.x, self.y = (self.dx, c, z), (self.dy, c, z)
        self.block = block
        self.half = size // 2
        self.sems = sems

    def copy(self, way, owner, piece, first, rows, to):
        block = self.block(owner, piece, first, rows)
        sends, recvs = self.sems
        return remote(block, block, sends.at[way, piece], recvs.at[way, piece], to)

    def whole(self, way, owner, piece):
        return self.copy(way, owner, piece, 0, 2 * self.half, self.x if way == 0 else self.y)

    def part(self, way, owner, piece):
        return self.copy(way, owner, piece, 0 if way == 2 else self.half, self.half, self.y if way == 2 else self.x)

    def begin(self, piece):
        self.whole(0, self.dp, piece).start()
        self.whole(1, self.dp, piece).start()

    def step(self, piece):
        self.whole(0, self.dx, piece).wait_recv()
        self.part(2, self.dx, piece).start()
        self.whole(1, self.dy, piece).wait_recv()
        self.part(3, self.dy, piece).start()

    def arrive(self, piece):
        self.part(2, self.diag, piece).wait_recv()
        self.part(3, self.diag, piece).wait_recv()

    def end(self, piece):
        self.whole(0, self.dp, piece).wait_send()
        self.whole(1, self.dp, piece).wait_send()
        self.part(2, self.dx, piece).wait_send()
        self.part(3, self.dy, piece).wait_send()


class SquareSum:
    def __init__(self, place, part, once, twice, gone, sems, pieces):
        dp, c, z = place
        self.dp, self.dx, self.dy = dp, dp + 1 - 2 * lax.rem(dp, 2), lax.rem(dp + 2, 4)
        self.diag = lax.rem(self.dx + 2, 4)
        self.x, self.y = (self.dx, c, z), (self.dy, c, z)
        self.part, self.once, self.twice, self.gone = part, once, twice, gone
        self.s1, self.r1, self.s2, self.r2 = sems
        self.pieces = pieces
        self.rows = part.shape[1] // pieces
        self.half = part.shape[2] // 2
        self.halves = (slice(0, self.half), slice(self.half, 2 * self.half))

    def first(self, p, side, k):
        owner = ((self.dx, self.diag), (self.dy, self.diag))[side][k]
        at = pl.ds(p * self.rows, self.rows)
        slot = 2 * side + k
        return remote(
            self.part.at[owner, at, self.halves[side]], self.once.at[slot, at, :],
            self.s1.at[p, slot], self.r1.at[p, slot], (self.x, self.y)[side],
        )

    def second(self, p, side):
        at = pl.ds(p * self.rows, self.rows)
        return remote(
            self.gone.at[side, at, :], self.twice.at[side, at, :], self.s2.at[p, side], self.r2.at[p, side],
            (self.y, self.x)[side],
        )

    def begin_x(self, p):
        self.first(p, 0, 1).start()
        self.first(p, 0, 0).start()

    def begin_y(self, p):
        self.first(p, 1, 1).start()
        self.first(p, 1, 0).start()

    def each(self, p, body):
        def step(r, _):
            body(pl.ds(pl.multiple_of(p * self.rows + r * 16, 16), 16))
            return 0

        lax.fori_loop(0, self.rows // 16, step, 0)

    def pass_on(self, p):
        for side in range(2):
            self.first(p, side, 1).wait_recv()
            owner = (self.dy, self.dx)[side]

            def body(at, side=side, owner=owner):
                self.gone[side, at, :] = (
                    self.part[owner, at, self.halves[side]].astype(F32)
                    + self.once[2 * side + 1, at, :].astype(F32)
                ).astype(BF16)

            self.each(p, body)
            self.second(p, side).start()

    def finish(self, p, out):
        for side in range(2):
            self.first(p, side, 0).wait_recv()
            self.second(p, side).wait_recv()

            def body(at, side=side):
                out[at, self.halves[side]] = (
                    self.part[self.dp, at, self.halves[side]].astype(F32)
                    + self.once[2 * side, at, :].astype(F32)
                    + self.twice[side, at, :].astype(F32)
                ).astype(out.dtype)

            self.each(p, body)

    def end(self):
        for p in range(self.pieces):
            for side in range(2):
                self.first(p, side, 0).wait_send()
                self.first(p, side, 1).wait_send()
                self.second(p, side).wait_send()


class HeadSplit:
    def __init__(self, nd, nc, nz):
        self.nd, self.nc, self.nz = nd, nc, nz
        self.nm = nc * nz
        self.span = self.nm * SPAN
        self.rows_in = MODEL // (nd * self.nm)
        self.wide = nd * TILE
        self.per = HEADS // (nd * self.nm)

    def fits(self):
        return (
            INNER == self.nd * self.nm * TILE and self.nd == 4 and self.nc == 2 and self.rows_in % 32 == 0
        )

    def place(self):
        return lax.axis_index("dp"), lax.axis_index("seq"), lax.axis_index("fsdp")

    def group_steps(self):
        return [(e, d) for d in range(self.nz) for e in range(self.nc) if e or d]

    def target(self, step):
        dp, c, z = self.place()
        ct, zt = lax.rem(c + step[0], self.nc), lax.rem(z + step[1], self.nz)
        return (dp, ct, zt), ct * self.nz + zt

    def source(self, step):
        dp, c, z = self.place()
        cs, zs = lax.rem(c + self.nc - step[0], self.nc), lax.rem(z + self.nz - step[1], self.nz)
        return cs * self.nz + zs

    def barrier(self):
        dp, c, z = self.place()
        sem = pltpu.get_barrier_semaphore()
        for step in self.group_steps():
            pl.semaphore_signal(sem, inc=1, device_id=self.target(step)[0], device_id_type=MESH)
        for k in range(1, self.nd):
            pl.semaphore_signal(
                sem, inc=1, device_id=(lax.rem(dp + k, self.nd), c, z), device_id_type=MESH
            )
        pl.semaphore_wait(sem, self.nm - 1 + self.nd - 1)

    def first_kernel(
        self, docs, starts, unit, x_ref, par_ref, head_ref, g_ref, wm_ref, wc_ref, wo_ref,
        y_out, x_out, g_out, w_out, wc_out, dproj, dcom, normed_out, sums, heads, pre_bc, projc, taps, gain_out, st,
        xall, gall, wall, wcall, woall, parbuf, parall, every_par, projm, pre_sig, o, states, step_s, cum_s,
        dg, scaled, sel, hp, chp, state, dnext, heard_st, ypart, ycame, ytotal, yheard,
        pd_s, pd_r, pg_s, pg_r, wz_s, wz_r, cz_s, cz_r, wq_s, wq_r, cq_s, cq_r, oq_s, oq_r, cc_s, cc_r,
        xr_s, xr_r, xl_s, xl_r, xc_s, xc_r, gr_s, gr_r, gl_s, gl_r, gc_s, gc_r,
        st_s, st_r, yc_s, yc_r, yr_s, yr_r, yl_s, yl_r, loc,
    ):
        nd, nc, nz, nm = self.nd, self.nc, self.nz, self.nm
        rows, wide = self.rows_in, self.wide
        where = dp, c, z = self.place()
        me = c * nz + z
        sizes = (nc, nz)
        steps = self.group_steps()
        other = (dp, nc - 1 - c, z)
        lines = [(k, (lax.rem(dp + k, nd), c, z), lax.rem(dp + nd - k, nd)) for k in range(1, nd)]
        started = []

        def go(copy):
            copy.start()
            started.append(copy)
            return copy

        def w_block(owner, m, first=0, count=rows):
            at = pl.multiple_of((owner * nm + m) * rows + first, rows // 2)
            return wall.at[pl.ds(at, count), :]

        def c_block(owner, m, first=0, count=rows):
            at = pl.multiple_of((owner * nm + m) * rows + first, rows // 2)
            return wcall.at[pl.ds(at, count), :]

        w_from = [me] + [self.source(step) for step in steps]
        c_from = [c * nz + lax.rem(z + nz - d, nz) for d in range(nz)]
        w_square = Square(
            where, lambda owner, j, first, count: w_block(owner, w_from[j], first, count), rows, (wq_s, wq_r)
        )
        c_square = Square(
            where, lambda owner, j, first, count: c_block(owner, c_from[j], first, count), rows, (cq_s, cq_r)
        )
        o_square = Square(
            where,
            lambda owner, j, first, count: woall.at[
                pl.ds(pl.multiple_of(owner * TILE + first, TILE // 2), count), :
            ],
            TILE,
            (oq_s, oq_r),
        )
        x_line = Line(where, sizes, lambda a, b: xall.at[rows_of(a * nz + b), :], (xr_s, xr_r, xl_s, xl_r, xc_s, xc_r))
        g_line = Line(where, sizes, lambda a, b: gall.at[rows_of(a * nz + b), :], (gr_s, gr_r, gl_s, gl_r, gc_s, gc_r))
        y_sum = Sum(where, sizes, ypart, ycame, ytotal, yheard, (yc_s, yc_r, yr_s, yr_r, yl_s, yl_r))

        st[...] = jnp.zeros_like(st)
        parbuf[dp] = par_ref[...]
        own = [
            pltpu.make_async_copy(wm_ref.at[me], w_block(dp, me), loc.at[0]),
            pltpu.make_async_copy(wc_ref, c_block(dp, me), loc.at[1]),
            pltpu.make_async_copy(wo_ref, woall.at[rows_of(dp), :], loc.at[2]),
            pltpu.make_async_copy(g_ref, gall.at[rows_of(me), :], loc.at[3]),
        ]
        for copy in own:
            copy.start()
        self.barrier()
        for k, device, _ in lines:
            go(remote(parbuf.at[dp], parbuf.at[dp], pd_s.at[k], pd_r.at[k], device))
        for j, step in enumerate(steps):
            device, there = self.target(step)
            go(remote(wm_ref.at[there], w_block(dp, me), wz_s.at[j], wz_r.at[j], device))
            if step[0] == 0:
                go(remote(wc_ref, c_block(dp, me), cz_s.at[step[1]], cz_r.at[step[1]], device))
        for copy in own[:3]:
            copy.wait()
        o_square.begin(0)
        w_square.begin(0)
        c_square.begin(0)
        for k, device, frm in lines:
            remote(parbuf.at[frm], parbuf.at[frm], pd_s.at[k], pd_r.at[k], device).wait_recv()
        parall[me] = parbuf[...]
        for j, step in enumerate(steps):
            device, _ = self.target(step)
            go(remote(parbuf, parall.at[me], pg_s.at[j], pg_r.at[j], device))
        for j, step in enumerate(steps):
            device, _ = self.target(step)
            remote(parbuf, parall.at[self.source(step)], pg_s.at[j], pg_r.at[j], device).wait_recv()
        owners = [(first // nm, first % nm) for first in range(nd * nm)]
        gain = jnp.concatenate([parall[m, d][5:6, :rows] for d, m in owners], axis=1)
        gain_out[...] = jnp.broadcast_to(gain, (8, MODEL))
        hidden = x_ref[...].astype(F32)
        inverse = lax.rsqrt(jnp.mean(hidden * hidden, axis=1, keepdims=True) + EPSILON)
        xall[rows_of(me), :] = (hidden * inverse * gain).astype(BF16)
        x_line.begin()

        for j, step in enumerate(steps):
            device, _ = self.target(step)
            block = w_block(dp, w_from[j + 1])
            remote(block, block, wz_s.at[j], wz_r.at[j], device).wait_recv()
            w_square.begin(j + 1)
            if step[0] == 0:
                d = step[1]
                block = c_block(dp, c_from[d])
                remote(block, block, cz_s.at[d], cz_r.at[d], device).wait_recv()
                c_square.begin(d)
            if j == 2:
                o_square.step(0)
                w_square.step(0)
                c_square.step(0)
        own_conv = CONV // (nd * nm)
        every_par[...] = jnp.concatenate([parall[m, d][:, :own_conv] for d, m in owners], axis=1)
        for i in range(nd):
            at = pl.ds(pl.multiple_of((i * nm + me) * TILE, TILE), TILE)
            taps[:, tile_of(i)] = every_par[:, at]
        taps[:, wide:] = every_par[:, INNER : INNER + 2 * TILE]
        head, lane = iota((TILE, TILE), 0), iota((TILE, TILE), 1)
        step_of = nm * self.per
        chosen = (head == lax.div(lane, self.per) * step_of + self.per * me + lax.rem(lane, self.per)) & (
            lane < nd * self.per
        )
        sel[...] = chosen.astype(BF16)
        hp[...] = exact(head_ref[...], chosen.astype(F32))
        for i in range(nd):
            chosen = head == i * step_of + self.per * me + lax.div(lane, HEAD_DIM)
            spread = exact(head_ref[...], chosen.astype(F32))
            chp[0:2, tile_of(i)] = spread[2:4, :]
            chp[2:3, tile_of(i)] = parbuf[i][6:7, :TILE]
        x_line.step(1)
        for j in range(1, 4):
            w_square.step(j)
        for j in range(1, nz):
            c_square.step(j)
        x_line.step(2)
        for j in range(4, nm):
            w_square.step(j)
        x_line.step(3)
        own[3].wait()
        g_line.begin()
        for j in range(nz):
            c_square.arrive(j)
        for i in range(nd):
            at = pl.ds(pl.multiple_of((i * nm + c * nz) * rows, rows), nz * rows)
            go(remote(wcall.at[at, :], wcall.at[at, :], cc_s.at[i], cc_r.at[i], other))
        x_line.arrive()
        for j in range(nm):
            w_square.arrive(j)
        for i in range(nd):
            at = pl.ds(pl.multiple_of((i * nm + (nc - 1 - c) * nz) * rows, rows), nz * rows)
            remote(wcall.at[at, :], wcall.at[at, :], cc_s.at[i], cc_r.at[i], other).wait_recv()
        outs = [
            pltpu.make_async_copy(xall, x_out, loc.at[4]),
            pltpu.make_async_copy(wall, w_out, loc.at[5]),
            pltpu.make_async_copy(wcall, wc_out, loc.at[6]),
        ]
        for copy in outs:
            copy.start()

        projm[0:PAD, :] = jnp.zeros((PAD, 2 * wide), BF16)
        projc[0:PAD, :] = jnp.zeros((PAD, COMMON), BF16)
        projc[PAD:, :] = dot(xall[...], wcall[...]).astype(BF16)

        def project(n, _):
            at = rows_of(n, 256)
            projm[PAD:, at] = dot(xall[...], wall[:, at]).astype(BF16)
            pl.when(n == 2)(lambda: g_line.step(1))
            return 0

        lax.fori_loop(0, 2 * wide // 256, project, 0)
        state[...] = jnp.zeros_like(state)

        def forward(i, _):
            self.forward_chunk(
                i, docs, starts, projm, projc, taps, sel, hp, chp,
                pre_sig, pre_bc, o, states, step_s, cum_s, scaled, st, state,
            )
            pl.when(i == 2)(lambda: g_line.step(2))
            pl.when(i == 6)(lambda: g_line.step(3))
            return 0

        lax.fori_loop(0, nm, forward, 0)

        o_square.arrive(0)

        def branch(n, _):
            turn = lax.rem(n + (nc - 1 - c) * nz, nm)
            ypart[turn] = dot(scaled[rows_of(turn), :], woall[...]).astype(BF16)
            return 0

        lax.fori_loop(0, nz, branch, 0)
        for t in range(nz):
            y_sum.core(t).start()
        lax.fori_loop(nz, nm, branch, 0)
        for t in range(nz):
            y_sum.add_core(t)
        y_sum.begin()

        g_line.arrive()
        out = pltpu.make_async_copy(gall, g_out, loc.at[7])
        out.start()
        outs.append(out)
        lanes_at = iota((SPAN, TILE), 1)

        def gate_grad(n, _):
            at = rows_of(n, 256)
            grad = dot(gall[at, :], woall[...], ((1,), (1,)))
            dg[at, :] = grad
            for half in range(2):
                product = jnp.zeros((SPAN, TILE), F32)
                for i in range(nd):
                    mine = scaled[pl.ds(pl.multiple_of(n * 256 + half * SPAN, SPAN), SPAN), tile_of(i)]
                    product = product + mine.astype(F32) * grad[half * SPAN : (half + 1) * SPAN, tile_of(i)]
                st[2 * n + half, 1:2, :] = jnp.where(lanes_at == 0, lane_sum(product), 0.0).T[0:1, :]
            return 0

        lax.fori_loop(0, nm // 2, gate_grad, 0)
        sent = []
        for j, step in enumerate(steps):
            device, _ = self.target(step)
            sent.append(go(remote(st, heard_st.at[j], st_s.at[j], st_r.at[j], device)))

        totals = st[...]
        for j, copy in enumerate(sent):
            copy.wait_recv()
            totals = totals + heard_st[j]
        for copy in sent:
            copy.wait_send()
        st[...] = totals

        dnext[...] = jnp.zeros_like(dnext)
        state[...] = jnp.zeros_like(state)
        sums[...] = jnp.zeros_like(sums)
        heads[...] = jnp.zeros_like(heads)

        def backward(n, _):
            self.backward_chunk(
                nm - 1 - n, docs, starts, unit, projm, pre_sig, pre_bc, o, states, step_s, cum_s, dg, st, taps, sel,
                hp, chp, dproj, dcom, normed_out, sums, heads, state, dnext,
            )
            pl.when(n == 1)(lambda: y_sum.relay(1, 0))

            @pl.when(n == 4)
            def _():
                y_sum.relay(1, 1)
                y_sum.relay(2, 0)

            return 0

        lax.fori_loop(0, nm, backward, 0)
        y_sum.arrive()
        stat = jnp.concatenate([st[me], jnp.zeros((SPAN - 8, TILE), F32)], axis=0).T
        root = lax.rsqrt(stat[:, 0:1] * unit[0, 0] + EPSILON)
        y_out[...] = (x_ref[...].astype(F32) + root * y_sum.own(slice(None))).astype(BF16)
        for copy in outs:
            copy.wait()
        for copy in started:
            if not any(copy is s for s in sent):
                copy.wait_send()
        for j in range(nm):
            w_square.end(j)
        for j in range(nz):
            c_square.end(j)
        o_square.end(0)
        x_line.end()
        g_line.end()
        y_sum.end()

    def forward_chunk(
        self, chunk, docs, starts, projm, projc, taps, sel, hp, chp,
        pre_sig, pre_bc, o, states, step_s, cum_s, scaled, st, state,
    ):
        nd, wide = self.nd, self.wide
        first = chunk * SPAN
        here = rows_of(chunk)
        lead = pl.ds(pl.multiple_of(chunk * SPAN, SPAN), SPAN + PAD)
        body = pl.ds(pl.multiple_of(chunk * SPAN + PAD, PAD), SPAN)
        lane = iota((SPAN, TILE), 1)
        row = iota((SPAN, TILE), 0)
        low = lane < HEAD_DIM
        begin_t = begin_at(first + row, starts, docs)
        begin_s = begin_at(first + lane, starts, docs)
        valid = [first + row - (KW - 1 - tap) >= begin_t for tap in range(KW)]
        sides = []
        for i in range(2):
            lanes = tile_of(i)
            value = conv_tile(projc[lead, lanes].astype(F32), taps, tile_of(nd + i), valid)
            pre_bc[here, lanes] = value
            sides.append((value * jax.nn.sigmoid(value)).astype(BF16))
        key_side, query_side = sides
        rate = dot(projc[body, 2 * TILE :], sel[...])
        step = softplus(rate + hp[0:1, :])
        log_decay = step * hp[1:2, :]
        cum = exact((lane <= row).astype(F32), log_decay)
        step_s[here, :] = step
        cum_s[here, :] = cum
        cum_t = cum.T
        shut = jnp.where((begin_t == begin_s) & (lane <= row), 0.0, NEG)
        inherits = (begin_t < first).astype(F32)
        begin_last = begin_at(jnp.full((SPAN, TILE), first + SPAN - 1, jnp.int32), starts, docs)
        last_same = (begin_t == begin_last).astype(F32)
        meet = dot(query_side, key_side, ((1,), (1,)))
        before = state[...]
        states[chunk] = before
        carried_out = dot(query_side, before.astype(BF16))
        squares = jnp.zeros((SPAN, TILE), F32)
        for i in range(nd):
            lanes = tile_of(i)
            pre = conv_tile(projm[lead, tile_of(nd + i)].astype(F32), taps, lanes, valid)
            pre_sig[here, lanes] = pre
            signal = pre * jax.nn.sigmoid(pre)
            cums = [head_col(cum, 2 * i), head_col(cum, 2 * i + 1)]
            stepx = jnp.where(low, head_col(step, 2 * i), head_col(step, 2 * i + 1))
            cumx = jnp.where(low, cums[0], cums[1])
            fed = stepx * signal
            fed_low = fed.astype(BF16)
            local = []
            for e in range(2):
                head = 2 * i + e
                kernel = jnp.exp(cums[e] - cum_t[head : head + 1, :] + shut)
                local.append(dot((kernel * meet).astype(BF16), fed_low))
            entry = jnp.exp(cumx) * inherits
            out = jnp.where(low, local[0], local[1]) + entry * carried_out[:, lanes]
            o[here, lanes] = out
            last = cumx[SPAN - 1 : SPAN, :]
            tail = jnp.exp((last - cumx) * last_same) * last_same
            state[:, lanes] = entry[SPAN - 1 : SPAN, :] * before[:, lanes] + dot(
                key_side, (tail * fed).astype(BF16), ((0,), (0,))
            )
            mixed = (out + chp[0:1, lanes] * signal) * chp[1:2, lanes]
            gate_in = projm[body, lanes].astype(F32)
            gated = mixed * (gate_in * jax.nn.sigmoid(gate_in))
            squares = squares + gated * gated
            scaled[here, lanes] = (gated * chp[2:3, lanes]).astype(BF16)
        st[chunk, 0:1, :] = jnp.where(lane == 0, lane_sum(squares), 0.0).T[0:1, :]

    def backward_chunk(
        self, chunk, docs, starts, unit, projm, pre_sig, pre_bc, o, states, step_s, cum_s, dg, st, taps, sel,
        hp, chp, dproj, dcom, normed_out, sums, heads, dstate, dnext,
    ):
        nd = self.nd
        first = chunk * SPAN
        here = rows_of(chunk)
        lead = pl.ds(pl.multiple_of(chunk * SPAN, SPAN), SPAN + PAD)
        body = pl.ds(pl.multiple_of(chunk * SPAN + PAD, PAD), SPAN)
        lane = iota((SPAN, TILE), 1)
        row = iota((SPAN, TILE), 0)
        low = lane < HEAD_DIM
        begin_t = begin_at(first + row, starts, docs)
        begin_s = begin_at(first + lane, starts, docs)
        shut = jnp.where((begin_t == begin_s) & (lane <= row), 0.0, NEG)
        inherits = (begin_t < first).astype(F32)
        begin_last = begin_at(jnp.full((SPAN, TILE), first + SPAN - 1, jnp.int32), starts, docs)
        last_same = (begin_t == begin_last).astype(F32)
        lower = (lane <= row).astype(F32)
        key_pre, query_pre = pre_bc[here, :TILE], pre_bc[here, TILE:]
        key_side = (key_pre * jax.nn.sigmoid(key_pre)).astype(BF16)
        query_side = (query_pre * jax.nn.sigmoid(query_pre)).astype(BF16)
        meet = dot(query_side, key_side, ((1,), (1,)))
        step, cum = step_s[here, :], cum_s[here, :]
        cum_t = cum.T
        stat = jnp.concatenate([st[chunk], jnp.zeros((SPAN - 8, TILE), F32)], axis=0).T
        square, cross = head_col(stat, 0), head_col(stat, 1)
        root = lax.rsqrt(square * unit[0, 0] + EPSILON)
        pull = root * root * root * cross * unit[0, 0]
        before = states[chunk]
        before_low = before.astype(BF16)
        after = dstate[...]
        after_low = after.astype(BF16)
        carried_out = dot(query_side, before_low)
        from_state = dot(key_side, after_low)
        meet_grad = jnp.zeros((SPAN, SPAN), F32)
        cum_cols = jnp.zeros((SPAN, TILE), F32)
        cum_rows = jnp.zeros((8, SPAN), F32)
        step_cols = jnp.zeros((SPAN, TILE), F32)
        entered, tails = [], []
        head_rows = iota((8, SPAN), 0)
        next_rows = first + iota((SPAN + PAD, TILE), 0)
        next_begin = begin_at(next_rows, starts, docs)
        valid = [next_rows - (KW - 1 - tap) >= next_begin for tap in range(KW)]
        tail_row = row == SPAN - 1
        for i in range(nd):
            lanes = tile_of(i)
            pre = pre_sig[here, lanes]
            gate_of = jax.nn.sigmoid(pre)
            signal = pre * gate_of
            gate_in = projm[body, lanes].astype(F32)
            gate_sig = jax.nn.sigmoid(gate_in)
            opened = gate_in * gate_sig
            mask = chp[1:2, lanes]
            mixed = (o[here, lanes] + chp[0:1, lanes] * signal) * mask
            gated = mixed * opened
            grad = dg[here, lanes]
            gain = chp[2:3, lanes]
            normed_out[here, lanes] = (gated * root * gain).astype(BF16)
            sums[0:1, lanes] += jnp.sum(grad * gated * root, axis=0, keepdims=True)
            gated_grad = root * grad * gain - gated * pull
            mixed_grad = gated_grad * opened * mask
            dproj[here, lanes] = (
                gated_grad * mixed * (gate_sig * (1.0 + gate_in * (1.0 - gate_sig)))
            ).astype(BF16)
            sums[1:2, lanes] += jnp.sum(mixed_grad * signal, axis=0, keepdims=True)
            cums = [head_col(cum, 2 * i), head_col(cum, 2 * i + 1)]
            stepx = jnp.where(low, head_col(step, 2 * i), head_col(step, 2 * i + 1))
            cumx = jnp.where(low, cums[0], cums[1])
            fed = stepx * signal
            fed_low = fed.astype(BF16)
            out_grad = mixed_grad
            out_low = out_grad.astype(BF16)
            entry = jnp.exp(cumx) * inherits
            last = cumx[SPAN - 1 : SPAN, :]
            tail = jnp.exp((last - cumx) * last_same) * last_same
            backs = []
            for e in range(2):
                head = 2 * i + e
                kernel = jnp.exp(cums[e] - cum_t[head : head + 1, :] + shut)
                mix = kernel * meet
                half = low if e == 0 else jnp.logical_not(low)
                mix_grad = dot(jnp.where(half, out_grad, 0.0).astype(BF16), fed_low, ((1,), (1,)))
                meet_grad = meet_grad + kernel * mix_grad
                weight = mix * mix_grad
                cum_cols = cum_cols + jnp.where(lane == head, lane_sum(weight), 0.0)
                cum_rows = cum_rows + jnp.where(
                    head_rows == head, jnp.broadcast_to(jnp.sum(weight, axis=0, keepdims=True), (8, SPAN)), 0.0
                )
                backs.append(dot(mix.astype(BF16), out_low, ((0,), (0,))))
            entry_grad = entry * out_grad
            tail_fed = tail * fed
            entered.append(entry_grad.astype(BF16))
            tails.append(tail_fed.astype(BF16))
            fed_grad = jnp.where(low, backs[0], backs[1]) + tail * from_state[:, lanes]
            moved_in = entry_grad * carried_out[:, lanes]
            moved_out = tail_fed * from_state[:, lanes]
            direct = fed_grad * signal
            end = entry[SPAN - 1 : SPAN, :]
            kept = jnp.sum(after[:, lanes] * before[:, lanes], axis=0, keepdims=True) * end
            at_end = jnp.sum(moved_out, axis=0, keepdims=True) + kept
            local = moved_in - moved_out + jnp.where(tail_row, at_end, 0.0)
            for e in range(2):
                half = low if e == 0 else jnp.logical_not(low)
                place = lane == 2 * i + e
                cum_cols = cum_cols + jnp.where(place, lane_sum(jnp.where(half, local, 0.0)), 0.0)
                step_cols = step_cols + jnp.where(place, lane_sum(jnp.where(half, direct, 0.0)), 0.0)
            dstate[:, lanes] = end * after[:, lanes] + dot(query_side, entry_grad.astype(BF16), ((0,), (0,)))
            signal_grad = stepx * fed_grad + chp[0:1, lanes] * mixed_grad
            pre_grad = signal_grad * (gate_of * (1.0 + pre * (1.0 - gate_of)))
            sums[2:3, lanes] += jnp.sum(pre_grad, axis=0, keepdims=True)
            later = jnp.concatenate([pre_grad, dnext[:, lanes]], axis=0)
            dnext[:, lanes] = pre_grad[0:PAD, :]
            cols = tile_of(nd + i)
            ext = projm[lead, cols].astype(F32)
            back_grad = jnp.zeros((SPAN, TILE), F32)
            for tap in range(KW):
                back = KW - 1 - tap
                masked = jnp.where(valid[tap], later, 0.0)
                moved = ext if back == 0 else pltpu.roll(ext, back, 0)
                sums[4 + tap : 5 + tap, lanes] += jnp.sum(masked[:SPAN] * moved[PAD:], axis=0, keepdims=True)
                ahead = masked if back == 0 else pltpu.roll(masked, SPAN + PAD - back, 0)
                back_grad = back_grad + ahead[:SPAN] * taps[tap : tap + 1, lanes]
            dproj[here, cols] = back_grad.astype(BF16)
        meet_low = meet_grad.astype(BF16)
        state_rows = ((1,), (1,))
        query_grad = dot(meet_low, key_side) + dot(jnp.concatenate(entered, axis=1), before_low, state_rows)
        key_grad = dot(meet_low, query_side, ((0,), (0,))) + dot(
            jnp.concatenate(tails, axis=1), after_low, state_rows
        )
        dcom[here, :TILE] = key_grad.astype(BF16)
        dcom[here, TILE : 2 * TILE] = query_grad.astype(BF16)
        rows_t = jnp.concatenate([cum_rows, jnp.zeros((SPAN - 8, SPAN), F32)], axis=0).T
        decay_grad = exact(lower, cum_cols - rows_t, ((0,), (0,)))
        log_decay = step * hp[1:2, :]
        slope = 1.0 - jnp.exp(-step)
        rate_grad = (step_cols + decay_grad * hp[1:2, :]) * slope
        heads[0:1, :] += jnp.sum(rate_grad, axis=0, keepdims=True)
        heads[1:2, :] += jnp.sum(decay_grad * log_decay, axis=0, keepdims=True)
        dcom[here, 2 * TILE :] = dot(rate_grad.astype(BF16), sel[...], ((1,), (1,))).astype(BF16)

    def first(self, docs, starts, unit, x, par, heads, g, wm, wc, wo):
        nd, nz, nm, rows, span, wide = self.nd, self.nz, self.nm, self.rows_in, self.span, self.wide
        like = jax.ShapeDtypeStruct
        block = (SPAN, MODEL)
        return pl.pallas_call(
            functools.partial(self.first_kernel, docs),
            out_shape=[
                like(block, BF16),
                like((span, MODEL), BF16),
                like((span, MODEL), BF16),
                like((MODEL, 2 * wide), BF16),
                like((MODEL, COMMON), BF16),
                like((span, 2 * wide), BF16),
                like((span, COMMON), BF16),
                like((span, wide), BF16),
                like((8, wide), F32),
                like((8, TILE), F32),
                like((span, 2 * TILE), F32),
                like((PAD + span, COMMON), BF16),
                like((8, wide + 2 * TILE), F32),
                like((8, MODEL), F32),
                like((nm, 8, TILE), F32),
            ],
            in_specs=[SM, SM, VM, VM, VM, ANY, ANY, ANY, ANY],
            out_specs=[VM, ANY, ANY, ANY, ANY] + [VM] * 10,
            scratch_shapes=[
                pltpu.VMEM((span, MODEL), BF16),
                pltpu.VMEM((span, MODEL), BF16),
                pltpu.VMEM((MODEL, 2 * wide), BF16),
                pltpu.VMEM((MODEL, COMMON), BF16),
                pltpu.VMEM((wide, MODEL), BF16),
                pltpu.VMEM((nd, 8, 2 * TILE), F32),
                pltpu.VMEM((nm, nd, 8, 2 * TILE), F32),
                pltpu.VMEM((8, CONV), F32),
                pltpu.VMEM((PAD + span, 2 * wide), BF16),
                pltpu.VMEM((span, wide), F32),
                pltpu.VMEM((span, wide), F32),
                pltpu.VMEM((nm, STATE, wide), F32),
                pltpu.VMEM((span, TILE), F32),
                pltpu.VMEM((span, TILE), F32),
                pltpu.VMEM((span, wide), F32),
                pltpu.VMEM((span, wide), BF16),
                pltpu.VMEM((TILE, TILE), BF16),
                pltpu.VMEM((8, TILE), F32),
                pltpu.VMEM((8, wide), F32),
                pltpu.VMEM((STATE, wide), F32),
                pltpu.VMEM((PAD, wide), F32),
                pltpu.VMEM((nm - 1, nm, 8, TILE), F32),
                pltpu.VMEM((nm, *block), BF16),
                pltpu.VMEM((nz, *block), BF16),
                pltpu.VMEM((nz, *block), BF16),
                pltpu.VMEM((2 * nz, *block), BF16),
                DMA((nd,)), DMA((nd,)), DMA((nm,)), DMA((nm,)),
                DMA((nm,)), DMA((nm,)), DMA((nz,)), DMA((nz,)),
                DMA((4, nm)), DMA((4, nm)), DMA((4, nz)), DMA((4, nz)), DMA((4, 1)), DMA((4, 1)),
                DMA((nd,)), DMA((nd,)),
                DMA((nz,)), DMA((nz,)), DMA((nz,)), DMA((nz,)), DMA((nz,)), DMA((nz,)),
                DMA((nz,)), DMA((nz,)), DMA((nz,)), DMA((nz,)), DMA((nz,)), DMA((nz,)),
                DMA((nm,)), DMA((nm,)),
                DMA((nz,)), DMA((nz,)), DMA((nz,)), DMA((nz,)), DMA((nz,)), DMA((nz,)),
                DMA((8,)),
            ],
            compiler_params=pltpu.CompilerParams(
                collective_id=0, has_side_effects=True, vmem_limit_bytes=62 * 2**20
            ),
            name="first",
        )(starts, unit, x, par, heads, g, wm, wc, wo)

    def second_kernel(
        self, docs, starts, dproj, dcom, normed_out, sums, heads, pre_bc, projc, taps, gain, x_ref, g_ref,
        x_in, g_in, w_in, wc_in,
        dx_out, dw_out, dwc_out, dwo_out, par_out,
        xall, gall, wall, wcall, xpart, xcame, xtotal, xheard,
        padded, ccame, ctotal, cheard, every, dxc, x_rows, wcpart, wccame,
        wpart, w1, w2, wgo, wsum, opart, o1, o2, ogo, pard, parbuf,
        xc_s, xc_r, xr_s, xr_r, xl_s, xl_r, cc_s, cc_r, cz_s, cz_r, ez_s, ez_r, ec_s, ec_r,
        w1_s, w1_r, w2_s, w2_r, o1_s, o1_r, o2_s, o2_r, wz_s, wz_r, wcd_s, wcd_r, pd_s, pd_r, pg_s, pg_r, loc,
    ):
        nd, nc, nz, nm = self.nd, self.nc, self.nz, self.nm
        rows, wide, span = self.rows_in, self.wide, self.span
        where = dp, c, z = self.place()
        me = c * nz + z
        sizes = (nc, nz)
        steps = self.group_steps()
        other = (dp, nc - 1 - c, z)
        long = SPAN + PAD
        started = []

        def go(copy):
            copy.start()
            started.append(copy)
            return copy

        loads = [
            pltpu.make_async_copy(w_in, wall, loc.at[0]),
            pltpu.make_async_copy(x_in, xall, loc.at[1]),
            pltpu.make_async_copy(wc_in, wcall, loc.at[2]),
            pltpu.make_async_copy(g_in, gall, loc.at[3]),
        ]
        for load in loads:
            load.start()
        padded[0:span, :] = dcom[...]
        padded[span:, :] = jnp.zeros((PAD, COMMON), BF16)
        self.barrier()
        x_sum = Sum(where, sizes, xpart, xcame, xtotal, xheard, (xc_s, xc_r, xr_s, xr_r, xl_s, xl_r))
        w_sum = SquareSum(where, wpart, w1, w2, wgo, (w1_s, w1_r, w2_s, w2_r), 2)
        o_sum = SquareSum(where, opart, o1, o2, ogo, (o1_s, o1_r, o2_s, o2_r), 1)

        def c_rows(m):
            return pl.ds(pl.multiple_of(m * SPAN, SPAN), long)

        ccopies = [
            go(remote(padded.at[c_rows((nc - 1 - c) * nz + t), :], ccame.at[t], cc_s.at[t], cc_r.at[t], other))
            for t in range(nz)
        ]
        loads[0].wait()

        def input_grad(n, _):
            at = rows_of(n, 256)
            base = rows_of(nc - 1 - c, nz * SPAN)
            part = dot(dproj[base, :], wall[at, :], ((1,), (1,))).astype(BF16)
            for t in range(nz):
                xpart[(nc - 1 - c) * nz + t, :, at] = part[t * SPAN : (t + 1) * SPAN, :]
            return 0

        lax.fori_loop(0, MODEL // 256, input_grad, 0)
        for t in range(nz):
            x_sum.core(t).start()
        for t in range(nz):
            ccopies[t].wait_recv()
            ctotal[t] = (padded[c_rows(c * nz + t), :].astype(F32) + ccame[t].astype(F32)).astype(BF16)
        for d in range(1, nz):
            to = lax.rem(z + d, nz)
            go(remote(ctotal.at[to], cheard.at[d - 1], cz_s.at[d], cz_r.at[d], (dp, c, to)))

        def own_grad(n, _):
            at = rows_of(n, 256)
            base = rows_of(c, nz * SPAN)
            part = dot(dproj[base, :], wall[at, :], ((1,), (1,))).astype(BF16)
            for t in range(nz):
                xpart[c * nz + t, :, at] = part[t * SPAN : (t + 1) * SPAN, :]
            return 0

        lax.fori_loop(0, MODEL // 256, own_grad, 0)
        for t in range(nz):
            x_sum.add_core(t)
        x_sum.begin()

        total = ctotal[z].astype(F32)
        for d in range(1, nz):
            remote(cheard.at[d - 1], cheard.at[d - 1], cz_s.at[d], cz_r.at[d], other).wait_recv()
            total = total + cheard[d - 1].astype(F32)
        base = pl.multiple_of(me * SPAN, SPAN)
        after = pl.multiple_of(lax.rem(me + 1, nm) * SPAN, SPAN)
        places = base + iota((long, TILE), 0)
        begin = begin_at(places, starts, docs)
        inside = places < span
        counts = MODEL // TILE + 8 * nd
        parbuf[counts : counts + 16, :] = jnp.zeros((16, TILE), F32)
        for i in range(2):
            lanes = tile_of(i)
            pre = jnp.concatenate([pre_bc[pl.ds(base, SPAN), lanes], pre_bc[pl.ds(after, PAD), lanes]], axis=0)
            later = jnp.where(inside, total[:, lanes] * silu_slope(pre), 0.0)
            ext = projc[pl.ds(base, long), lanes].astype(F32)
            parbuf[counts + i : counts + i + 1, :] = jnp.sum(later[:SPAN], axis=0, keepdims=True)
            back_grad = jnp.zeros((SPAN, TILE), F32)
            for tap in range(KW):
                back = KW - 1 - tap
                masked = jnp.where(places - back >= begin, later, 0.0)
                moved = ext if back == 0 else pltpu.roll(ext, back, 0)
                at = counts + 2 + 2 * tap + i
                parbuf[at : at + 1, :] = jnp.sum(masked[:SPAN] * moved[PAD:], axis=0, keepdims=True)
                ahead = masked if back == 0 else pltpu.roll(masked, long - back, 0)
                back_grad = back_grad + ahead[:SPAN] * taps[tap : tap + 1, tile_of(nd + i)]
            every[me, :, lanes] = back_grad.astype(BF16)
        every[me, :, 2 * TILE :] = total[:SPAN, 2 * TILE :].astype(BF16)
        mine = every.at[me]
        for d in range(1, nz):
            go(remote(mine, mine, ez_s.at[d], ez_r.at[d], (dp, c, lax.rem(z + d, nz))))
        go(remote(mine, mine, ec_s.at[0], ec_r.at[0], other))

        loads[1].wait()

        def weight_grad(owner):
            def piece(n, _):
                at = pl.ds(pl.multiple_of(owner * (nm * rows) + n * 256, 256), 256)
                wpart[owner, rows_of(n, 256), :] = dot(xall[:, at], dproj[...], ((0,), (0,))).astype(BF16)
                return 0

            lax.fori_loop(0, nm * rows // 256, piece, 0)

        weight_grad(w_sum.diag)
        weight_grad(w_sum.dx)
        for p in range(2):
            w_sum.begin_x(p)
        weight_grad(w_sum.dy)
        for p in range(2):
            w_sum.begin_y(p)
        x_sum.relay(1, 0)
        weight_grad(dp)
        loads[2].wait()
        dxc[...] = dot(every[me], wcall[...], ((1,), (1,)))
        loads[3].wait()

        def out_grad(n, _):
            at = rows_of(n, 512)
            part = dot(normed_out[...], gall[:, at], ((0,), (0,))).astype(BF16)
            for i in range(nd):
                opart[i, :, at] = part[tile_of(i), :]
            return 0

        lax.fori_loop(0, MODEL // 512, out_grad, 0)
        o_sum.begin_x(0)
        o_sum.begin_y(0)
        for d in range(1, nz):
            block = every.at[c * nz + lax.rem(z + nz - d, nz)]
            remote(block, block, ez_s.at[d], ez_r.at[d], other).wait_recv()
            go(remote(block, block, ec_s.at[d], ec_r.at[d], other))
        w_sum.pass_on(0)
        x_sum.relay(1, 1)
        x_sum.relay(2, 0)
        for i in range(nd):
            pair = pl.ds(pl.multiple_of(i * (nm * rows) + (me // 2) * (2 * rows), 2 * rows), 2 * rows)
            both = xall[:, pair]
            x_rows[:, i * rows : (i + 1) * rows] = jnp.where(
                lax.rem(me, 2) == 0, both[:, :rows].astype(F32), both[:, rows:].astype(F32)
            ).astype(BF16)
        for d in range(nz):
            block = every.at[(nc - 1 - c) * nz + lax.rem(z + nz - d, nz)]
            remote(block, block, ec_s.at[d], ec_r.at[d], other).wait_recv()
        shared = dot(x_rows[...], every[...].reshape(span, COMMON), ((0,), (0,))).astype(BF16)
        for i in range(nd):
            wcpart[i] = shared[i * rows : (i + 1) * rows, :]
        lines = [(k, (lax.rem(dp + k, nd), c, z), lax.rem(dp + k, nd)) for k in range(1, nd)]
        wc_copies = [
            go(remote(wcpart.at[to], wccame.at[k - 1], wcd_s.at[k], wcd_r.at[k], device)) for k, device, to in lines
        ]
        w_sum.pass_on(1)

        def send_rows(p):
            half = nm // 2
            for j in range(half):
                there = p * half + j
                block = wsum.at[there * rows : (there + 1) * rows, :]
                ct, zt = there // nz, there % nz

                @pl.when(there != me)
                def _():
                    remote(block, dw_out.at[me], wz_s.at[there], wz_r.at[me], (dp, ct, zt)).start()

                @pl.when(there == me)
                def _():
                    dw_out[there] = block[...]

        w_sum.finish(0, wsum)
        send_rows(0)
        o_sum.pass_on(0)

        x_sum.arrive()
        hidden = x_ref[...].astype(F32)
        normed_grad = x_sum.own(slice(None)) + dxc[...]
        inverse = lax.rsqrt(jnp.mean(hidden * hidden, axis=1, keepdims=True) + EPSILON)
        unitary = hidden * inverse
        gain_grad = jnp.sum(normed_grad * unitary, axis=0, keepdims=True)
        grad_scaled = normed_grad * gain[0:1, :]
        middle = jnp.mean(grad_scaled * unitary, axis=1, keepdims=True)
        dx_out[...] = (g_ref[...].astype(F32) + inverse * (grad_scaled - unitary * middle)).astype(BF16)
        base_row = MODEL // TILE
        for i in range(base_row):
            parbuf[i : i + 1, :] = gain_grad[:, tile_of(i)]
        for r in range(8):
            for i in range(nd):
                parbuf[base_row + r * nd + i : base_row + r * nd + i + 1, :] = sums[r : r + 1, tile_of(i)]
        parbuf[counts + 16 :, :] = heads[...]
        small = [
            go(remote(parbuf, pard.at[k - 1], pd_s.at[k], pd_r.at[k], device)) for k, device, _ in lines
        ]
        w_sum.finish(1, wsum)
        send_rows(1)
        for copy in small:
            copy.wait_recv()
        total = parbuf[...]
        for k in range(nd - 1):
            total = total + pard[k]
        par_out[me] = total
        for j, step in enumerate(steps):
            go(remote(par_out.at[me], par_out.at[me], pg_s.at[j], pg_r.at[j], self.target(step)[0]))
        o_sum.finish(0, dwo_out)
        for copy in wc_copies:
            copy.wait_recv()
        total = wcpart[dp].astype(F32)
        for k in range(nd - 1):
            total = total + wccame[k].astype(F32)
        dwc_out[...] = total
        for j, step in enumerate(steps):
            here = par_out.at[self.source(step)]
            remote(here, here, pg_s.at[j], pg_r.at[j], other).wait_recv()
        for m in range(nm):
            got = dw_out.at[m]

            @pl.when(m != me)
            def _():
                remote(got, got, wz_s.at[m], wz_r.at[m], other).wait_recv()
                remote(got, got, wz_s.at[m], wz_r.at[m], other).wait_send()

        for copy in started:
            copy.wait_send()
        x_sum.end()
        w_sum.end()
        o_sum.end()

    def second(self, docs, starts, dproj, dcom, normed_out, sums, heads, pre_bc, projc, taps, gain, x, g, xall, gall, w, wc):
        nd, nz, nm, rows, span, wide = self.nd, self.nz, self.nm, self.rows_in, self.span, self.wide
        like = jax.ShapeDtypeStruct
        block = (SPAN, MODEL)
        npar = MODEL // TILE + 8 * nd + 16 + 8
        long = SPAN + PAD
        return pl.pallas_call(
            functools.partial(self.second_kernel, docs),
            out_shape=[
                like(block, BF16),
                like((nm, rows, 2 * wide), BF16),
                like((rows, COMMON), F32),
                like((TILE, MODEL), F32),
                like((nm, npar, TILE), F32),
            ],
            in_specs=[SM] + [VM] * 11 + [ANY] * 4,
            out_specs=[VM] * 5,
            scratch_shapes=[
                pltpu.VMEM((span, MODEL), BF16),
                pltpu.VMEM((span, MODEL), BF16),
                pltpu.VMEM((MODEL, 2 * wide), BF16),
                pltpu.VMEM((MODEL, COMMON), BF16),
                pltpu.VMEM((nm, *block), BF16),
                pltpu.VMEM((nz, *block), BF16),
                pltpu.VMEM((nz, *block), BF16),
                pltpu.VMEM((2 * nz, *block), BF16),
                pltpu.VMEM((span + PAD, COMMON), BF16),
                pltpu.VMEM((nz, long, COMMON), BF16),
                pltpu.VMEM((nz, long, COMMON), BF16),
                pltpu.VMEM((nz - 1, long, COMMON), BF16),
                pltpu.VMEM((nm, SPAN, COMMON), BF16),
                pltpu.VMEM(block, F32),
                pltpu.VMEM((span, nd * rows), BF16),
                pltpu.VMEM((nd, rows, COMMON), BF16),
                pltpu.VMEM((nd - 1, rows, COMMON), BF16),
                pltpu.VMEM((nd, nm * rows, 2 * wide), BF16),
                pltpu.VMEM((4, nm * rows, wide), BF16),
                pltpu.VMEM((2, nm * rows, wide), BF16),
                pltpu.VMEM((2, nm * rows, wide), BF16),
                pltpu.VMEM((nm * rows, 2 * wide), BF16),
                pltpu.VMEM((nd, TILE, MODEL), BF16),
                pltpu.VMEM((4, TILE, MODEL // 2), BF16),
                pltpu.VMEM((2, TILE, MODEL // 2), BF16),
                pltpu.VMEM((2, TILE, MODEL // 2), BF16),
                pltpu.VMEM((nd - 1, npar, TILE), F32),
                pltpu.VMEM((npar, TILE), F32),
                DMA((nz,)), DMA((nz,)), DMA((nz,)), DMA((nz,)), DMA((nz,)), DMA((nz,)),
                DMA((nz,)), DMA((nz,)), DMA((nz,)), DMA((nz,)), DMA((nz,)), DMA((nz,)), DMA((nz,)), DMA((nz,)),
                DMA((2, 4)), DMA((2, 4)), DMA((2, 2)), DMA((2, 2)),
                DMA((1, 4)), DMA((1, 4)), DMA((1, 2)), DMA((1, 2)),
                DMA((nm,)), DMA((nm,)), DMA((nd,)), DMA((nd,)), DMA((nd,)), DMA((nd,)),
                DMA((nm,)), DMA((nm,)), DMA((4,)),
            ],
            compiler_params=pltpu.CompilerParams(
                collective_id=1, has_side_effects=True, vmem_limit_bytes=62 * 2**20
            ),
            name="second",
        )(starts, dproj, dcom, normed_out, sums, heads, pre_bc, projc, taps, gain, x, g, xall, gall, w, wc)

    def local(
        self, layer_input, out_grad, norm_gain, in_weight, conv_weight, conv_bias, step_bias, log_rate,
        skip_gain, gate_gain, out_weight, nest_level, doc_lengths,
    ):
        nd, nz, nm, rows, wide = self.nd, self.nz, self.nm, self.rows_in, self.wide
        dp, c, z = self.place()
        me = c * nz + z
        docs = doc_lengths.shape[1]
        order = jnp.arange(docs)
        ahead = order[:, None] < order[None, :]
        starts = jnp.sum(jnp.where(ahead, doc_lengths[0][:, None], 0), axis=0, keepdims=True)
        starts = starts.astype(jnp.int32)
        active = jnp.right_shift(HEADS, 3 - nest_level[0])
        unit = (1.0 / (active * HEAD_DIM).astype(F32)).reshape(1, 1)
        x = layer_input.reshape(SPAN, MODEL)
        g = out_grad.reshape(SPAN, MODEL)
        wm = in_weight[:, : 2 * INNER].reshape(rows, 2 * nd, nm, TILE)
        wm = jnp.transpose(wm, (2, 0, 1, 3)).reshape(nm, rows, 2 * wide)
        wc = jnp.pad(in_weight[:, 2 * INNER :], ((0, 0), (0, COMMON - (EXTENT - 2 * INNER))))
        own_conv = conv_bias.shape[0]
        widen = lambda v: jnp.pad(v, ((0, 0), (0, 2 * TILE - v.shape[1])))
        par = jnp.concatenate(
            [
                widen(conv_weight.T),
                widen(conv_bias[None]),
                widen(norm_gain[None]),
                widen(gate_gain[None]),
                jnp.zeros((1, 2 * TILE), F32),
            ]
        )
        mask = (jnp.arange(HEADS) < active).astype(F32)
        head_in = jnp.stack([step_bias, -jnp.exp(log_rate), skip_gain, mask])
        head_in = jnp.pad(head_in, ((0, 4), (0, TILE - HEADS)))
        (
            y_out, xall, gall, w, wc_all, dproj, dcom, normed_out, sums, heads, pre_bc, projc, taps, gain, _,
        ) = self.first(docs, starts, unit, x, par, head_in, g, wm, wc, out_weight)
        dx_out, dw, dwc, dwo, pars = self.second(
            docs, starts, dproj, dcom, normed_out, sums, heads, pre_bc, projc, taps, gain, x, g, xall, gall, w, wc_all
        )
        dw = jnp.transpose(dw.reshape(nm, rows, 2 * nd, TILE), (1, 2, 0, 3)).reshape(rows, 2 * INNER)
        in_weight_grad = jnp.concatenate([dw.astype(F32), dwc[:, : EXTENT - 2 * INNER]], axis=1)
        owner = dp * nm + me
        gains = jnp.sum(pars[:, : MODEL // TILE], axis=0).reshape(MODEL)
        norm_gain_grad = lax.dynamic_slice_in_dim(gains, owner * rows, rows)
        base = MODEL // TILE
        mains = pars[:, base : base + 8 * nd].reshape(nm, 8, nd, TILE)
        shared = jnp.sum(pars[:, base + 8 * nd : base + 8 * nd + 16], axis=0)
        head_sums = pars[:, base + 8 * nd + 16 :]
        gate_gain_grad = lax.dynamic_index_in_dim(mains[me, 0], dp, 0, keepdims=False)
        everything = jnp.transpose(mains[:, 1:], (1, 2, 0, 3)).reshape(7, INNER)
        skip_gain_grad = jnp.sum(everything[0].reshape(HEADS, HEAD_DIM), axis=1)
        bias_sum = jnp.concatenate([everything[1], shared[:2].reshape(-1)])
        taps_sum = jnp.concatenate([everything[3:], shared[2:10].reshape(KW, 2 * TILE)], axis=1).T
        conv_bias_grad = lax.dynamic_slice_in_dim(bias_sum, owner * own_conv, own_conv)
        conv_weight_grad = lax.dynamic_slice_in_dim(taps_sum, owner * own_conv, own_conv)
        mine = nd * self.per
        by_head = lambda v: jnp.swapaxes(v[:, :mine].reshape(nm, nd, self.per), 0, 1).reshape(HEADS)
        step_bias_grad, log_rate_grad = by_head(head_sums[:, 0]), by_head(head_sums[:, 1])
        return (
            y_out.reshape(1, SPAN, MODEL),
            dx_out.reshape(1, SPAN, MODEL),
            norm_gain_grad,
            in_weight_grad,
            conv_weight_grad,
            conv_bias_grad,
            step_bias_grad,
            log_rate_grad,
            skip_gain_grad,
            gate_gain_grad,
            dwo,
        )


def solution(mesh):
    shape = dict(mesh.shape)
    head_split = HeadSplit(shape["dp"], shape["seq"], shape["fsdp"])
    return jax.shard_map(
        head_split.local if head_split.fits() else token_split,
        mesh=mesh,
        in_specs=(
            P("dp", ("seq", "fsdp"), None),
            P("dp", ("seq", "fsdp"), None),
            P(("dp", "seq", "fsdp")),
            P(("dp", "seq", "fsdp"), None),
            P(("dp", "seq", "fsdp"), None),
            P(("dp", "seq", "fsdp")),
            P(),
            P(),
            P(),
            P(("dp", "seq", "fsdp")),
            P(("dp", "seq", "fsdp"), None),
            P("dp"),
            P("dp", None),
        ),
        out_specs=(
            P("dp", ("seq", "fsdp"), None),
            P("dp", ("seq", "fsdp"), None),
            P(("dp", "seq", "fsdp")),
            P(("dp", "seq", "fsdp"), None),
            P(("dp", "seq", "fsdp"), None),
            P(("dp", "seq", "fsdp")),
            P(),
            P(),
            P(),
            P(("dp", "seq", "fsdp")),
            P(("dp", "seq", "fsdp"), None),
        ),
        check_vma=False,
    )
```

```python
import functools

import jax
import jax.numpy as jnp
from jax import lax
from jax.experimental import pallas as pl
from jax.experimental.pallas import tpu as pltpu
from jax.sharding import PartitionSpec as P

HEADS = 64
HEAD_DIM = 64
STATE = 128
KW = 4
INNER = 4096
CONV = 4352
EXTENT = 8512


HIGH = lax.Precision.HIGHEST
EPSILON = 1e-05


def shifted(value, axis, steps):
    count = lax.axis_size(axis)
    leading, last = (max(0, -steps), min(count, count - steps))
    return lax.ppermute(value, axis, [(source, source + steps) for source in range(leading, last)])


def prefix(array, axis, combine, identity):
    peers, place = (lax.axis_size(axis), lax.axis_index(axis))
    everything = jax.tree.map(
        lambda part, kind: lax.all_gather(part.astype(kind), axis),
        array,
        (jnp.bfloat16, jnp.bfloat16),
    )
    start = jax.tree.map(
        lambda part, zero: jnp.broadcast_to(jnp.asarray(zero, part.dtype), part.shape),
        array,
        identity,
    )

    def prefix_lap(k, before):
        reached = k < place
        new = combine(
            before, jax.tree.map(lambda part, own: part[k].astype(own.dtype), everything, array)
        )
        return jax.tree.map(lambda a, b: jnp.where(reached, a, b), new, before)

    return lax.fori_loop(0, peers, prefix_lap, start)


def carried_in(array, axis, combine, identity):
    peers, place = (lax.axis_size(axis), lax.axis_index(axis))
    everything = jax.tree.map(
        lambda part, kind: lax.all_gather(part.astype(kind), axis),
        array,
        jax.tree.map(lambda a: jnp.bfloat16 if a.dtype == jnp.float32 else a.dtype, array),
    )
    start = jax.tree.map(
        lambda part, zero: jnp.broadcast_to(jnp.asarray(zero, part.dtype), part.shape),
        array,
        identity,
    )

    def carried_lap(k, before):
        at = peers - 1 - k
        reached = at > place
        new = combine(
            before, jax.tree.map(lambda part, own: part[at].astype(own.dtype), everything, array)
        )
        return jax.tree.map(lambda a, b: jnp.where(reached, a, b), new, before)

    return lax.fori_loop(0, peers, carried_lap, start)


def doc_begins(lengths, positions):
    places = jnp.arange(lengths.shape[1])
    ahead = places[:, None] < places[None, :]
    endings = jnp.sum(jnp.where(ahead[None], lengths[:, :, None], 0), axis=1)
    reached = endings[:, None, :] <= positions[None, :, None]
    return jnp.max(jnp.where(reached, endings[:, None, :], 0), axis=2)


def input_norm(hidden, gain):
    inv_rms = lax.rsqrt(jnp.mean(hidden * hidden, axis=1, keepdims=True) + EPSILON)
    return hidden * inv_rms * gain


def causal_conv(extended, taps, bias, validity):
    block_len = validity.shape[2]
    running = bias + jnp.zeros((extended.shape[0], block_len, extended.shape[2]), jnp.float32)
    for tap in range(taps.shape[1]):
        running = (
            running + extended[:, tap : tap + block_len] * taps[:, tap] * validity[tap][:, :, None]
        )
    return jax.nn.silu(running)


def scan_parts(signal, key_side, query_side, rate_in, step_bias, log_rate, begins, block_start):
    step = jax.nn.softplus(rate_in + step_bias)
    log_decay = step * -jnp.exp(log_rate)
    places = jnp.arange(log_decay.shape[1])
    lower = (places[None, :] <= places[:, None]).astype(jnp.float32)
    cumulative = jnp.einsum("ts,bsh->bth", lower, log_decay, precision=HIGH)
    by_head = jnp.swapaxes(cumulative, 1, 2)
    indices = jnp.arange(signal.shape[1])
    same_doc = (begins[:, :, None] == begins[:, None, :]) & (
        indices[None, None, :] <= indices[None, :, None]
    )
    gaps = by_head[:, :, :, None] - by_head[:, :, None, :]
    kernel = jnp.exp(jnp.where(same_doc[:, None], gaps, 0.0)) * same_doc[:, None]
    intersection = jnp.einsum("btn,bsn->bts", query_side, key_side, precision=HIGH)
    mixing = kernel * intersection[:, None] * jnp.swapaxes(step, 1, 2)[:, :, None, :]
    local_out = jnp.einsum("bhts,bshp->bthp", mixing, signal, precision=HIGH)
    inherits = (begins < block_start).astype(jnp.float32)
    carried = jnp.exp(cumulative) * inherits[:, :, None]
    last_same = begins == begins[:, -1:]
    tail_weight = (
        jnp.exp(jnp.where(last_same[:, :, None], cumulative[:, -1:] - cumulative, 0.0))
        * last_same[:, :, None]
        * step
    )
    fresh_state = jnp.einsum("bsh,bshp,bsn->bhpn", tail_weight, signal, key_side, precision=HIGH)
    return (local_out, carried, carried[:, -1], fresh_state)


def gated_norm(scan_out, signal, skip_gain, gate_in, gate_gain, head_mask, unit_count):
    mixed = (scan_out + skip_gain[:, None] * signal) * head_mask[:, None, :, None]
    gated = mixed.reshape(gate_in.shape) * jax.nn.silu(gate_in)
    mean_square = jnp.sum(gated * gated, axis=2, keepdims=True) / unit_count[:, None, None]
    return gated * lax.rsqrt(mean_square + EPSILON) * gate_gain


def combine_states(earlier, later):
    return (earlier[0] * later[0], later[1] + later[0][:, :, None, None] * earlier[1])


def token_split(
    layer_input,
    out_grad,
    norm_gain,
    in_weight,
    conv_weight,
    conv_bias,
    step_bias,
    log_rate,
    skip_gain,
    gate_gain,
    out_weight,
    nest_level,
    doc_lengths,
):
    seq_count, block_len, model_width = layer_input.shape
    token_count = seq_count * block_len
    gain_all, taps_all, bias_all, gate_all = (
        lax.all_gather(norm_gain, ("dp", "seq", "fsdp"), axis=0, tiled=True),
        lax.all_gather(conv_weight, ("dp", "seq", "fsdp"), axis=0, tiled=True),
        lax.all_gather(conv_bias, ("dp", "seq", "fsdp"), axis=0, tiled=True),
        lax.all_gather(gate_gain, ("dp", "seq", "fsdp"), axis=0, tiled=True),
    )
    block_start = lax.axis_index(("seq", "fsdp")) * block_len
    positions = block_start + jnp.arange(block_len, dtype=jnp.int32)
    begins = doc_begins(doc_lengths, positions)
    hidden = layer_input.reshape(token_count, model_width).astype(jnp.float32)
    normed = input_norm(hidden, gain_all).astype(jnp.bfloat16)
    columns = normed
    projected = jnp.dot(
        columns,
        lax.all_gather(in_weight, ("dp", "seq", "fsdp"), axis=0, tiled=True),
        preferred_element_type=jnp.float32,
    ).astype(jnp.bfloat16)
    projected = projected.reshape(seq_count, block_len, EXTENT)
    gate_in = projected[:, :, :INNER].astype(jnp.float32)
    conv_in = projected[:, :, INNER : INNER + CONV]
    rate_in = projected[:, :, INNER + CONV :].astype(jnp.float32)
    edge_rows = shifted(conv_in[:, block_len - (KW - 1) :], ("seq", "fsdp"), 1)
    extended = jnp.concatenate([edge_rows, conv_in], axis=1).astype(jnp.float32)
    validity = jnp.stack(
        [(positions[None, :] - (KW - 1) + tap >= begins).astype(jnp.float32) for tap in range(KW)]
    )
    activated, conv_pull = jax.vjp(
        lambda ext_in, taps, bias: causal_conv(ext_in, taps, bias, validity),
        extended,
        taps_all,
        bias_all,
    )
    signal = activated[:, :, :INNER].reshape(seq_count, block_len, HEADS, HEAD_DIM)
    key_side = activated[:, :, INNER : INNER + STATE]
    query_side = activated[:, :, INNER + STATE :]
    local_out, carried, decays, fresh_state = scan_parts(
        signal, key_side, query_side, rate_in, step_bias, log_rate, begins, block_start
    )
    identity = (jnp.ones_like(decays), jnp.zeros_like(fresh_state))
    entry_state = prefix((decays, fresh_state), ("seq", "fsdp"), combine_states, identity)[1]
    scan_out = local_out + carried[..., None] * jnp.einsum(
        "btn,bhpn->bthp", query_side, entry_state, precision=HIGH
    )
    active = jnp.right_shift(HEADS, 3 - nest_level)
    head_mask = (jnp.arange(HEADS)[None, :] < active[:, None]).astype(jnp.float32)
    unit_count = (active * HEAD_DIM).astype(jnp.float32)
    gate_normed, gate_pull = jax.vjp(
        lambda sv, xv, sk, gi, gg: gated_norm(sv, xv, sk, gi, gg, head_mask, unit_count),
        scan_out,
        signal,
        skip_gain,
        gate_in,
        gate_all,
    )
    normed_out = gate_normed.reshape(token_count, INNER).astype(jnp.bfloat16)
    columns = normed_out
    branch_out = jnp.dot(
        columns,
        lax.all_gather(out_weight, ("dp", "seq", "fsdp"), axis=0, tiled=True),
        preferred_element_type=jnp.float32,
    )
    layer_output = (
        (hidden + branch_out).astype(jnp.bfloat16).reshape(seq_count, block_len, model_width)
    )
    grad_flat = out_grad.reshape(token_count, model_width)
    grad_normed_out = lax.dot_general(
        grad_flat,
        lax.all_gather(out_weight, ("dp", "seq", "fsdp"), axis=0, tiled=True),
        (((1,), (1,)), ((), ())),
        preferred_element_type=jnp.float32,
    )
    grad_scan, grad_skip_signal, grad_skip, grad_gate_in, grad_gate_gain = gate_pull(
        grad_normed_out.reshape(seq_count, block_len, INNER)
    )
    lead_grad = jnp.einsum("bth,bthp,btn->bhpn", carried, grad_scan, query_side, precision=HIGH)
    later_grad = carried_in((decays, lead_grad), ("seq", "fsdp"), combine_states, identity)[1]

    def full_scan(signal_in, key_in, query_in, rate_values, bias_values, rate_logs):
        part_out, part_carried, part_decays, part_fresh = scan_parts(
            signal_in, key_in, query_in, rate_values, bias_values, rate_logs, begins, block_start
        )
        joined_out = part_out + part_carried[..., None] * jnp.einsum(
            "btn,bhpn->bthp", query_in, entry_state, precision=HIGH
        )
        return (joined_out, part_decays[:, :, None, None] * entry_state + part_fresh)

    scan_pull = jax.vjp(full_scan, signal, key_side, query_side, rate_in, step_bias, log_rate)[1]
    grad_signal, grad_key, grad_query, grad_rate, grad_step_bias, grad_log_rate = scan_pull(
        (grad_scan, later_grad)
    )
    grad_activated = jnp.concatenate(
        [
            (grad_signal + grad_skip_signal).reshape(seq_count, block_len, INNER),
            grad_key,
            grad_query,
        ],
        axis=2,
    )
    grad_extended, grad_taps, grad_bias = conv_pull(grad_activated)
    returned = shifted(grad_extended[:, : KW - 1].astype(jnp.bfloat16), ("seq", "fsdp"), -1).astype(
        jnp.float32
    )
    grad_conv_in = grad_extended[:, KW - 1 :] + jnp.pad(
        returned, ((0, 0), (block_len - (KW - 1), 0), (0, 0))
    )
    grad_projected = (
        jnp.concatenate([grad_gate_in, grad_conv_in, grad_rate], axis=2)
        .reshape(token_count, EXTENT)
        .astype(jnp.bfloat16)
    )
    grad_normed = lax.dot_general(
        grad_projected,
        lax.all_gather(in_weight, ("dp", "seq", "fsdp"), axis=0, tiled=True),
        (((1,), (1,)), ((), ())),
        preferred_element_type=jnp.float32,
    )
    replicas = lax.axis_size("dp")
    members = lax.axis_size(("seq", "fsdp"))
    width_in = model_width // lax.axis_size(("dp", "seq", "fsdp"))
    width_out = INNER // lax.axis_size(("dp", "seq", "fsdp"))
    in_cols, out_cols = (
        lax.all_to_all(
            normed.reshape(token_count, replicas, members, width_in),
            ("seq", "fsdp"),
            split_axis=2,
            concat_axis=0,
            tiled=True,
        ),
        lax.all_to_all(
            normed_out.reshape(token_count, replicas, members, width_out),
            ("seq", "fsdp"),
            split_axis=2,
            concat_axis=0,
            tiled=True,
        ),
    )
    in_cols = in_cols.reshape(members * token_count, replicas * width_in)
    out_cols = out_cols.reshape(members * token_count, replicas * width_out)
    in_new = lax.dot_general(
        in_cols,
        lax.all_gather(grad_projected, ("seq", "fsdp"), axis=0, tiled=True),
        (((0,), (0,)), ((), ())),
        preferred_element_type=jnp.float32,
    )
    out_new = lax.dot_general(
        out_cols,
        lax.all_gather(grad_flat, ("seq", "fsdp"), axis=0, tiled=True),
        (((0,), (0,)), ((), ())),
        preferred_element_type=jnp.float32,
    )
    in_weight_grad, out_weight_grad = (
        lax.psum_scatter(in_new.astype(jnp.bfloat16), "dp", scatter_dimension=0, tiled=True).astype(
            jnp.float32
        ),
        lax.psum_scatter(
            out_new.astype(jnp.bfloat16), "dp", scatter_dimension=0, tiled=True
        ).astype(jnp.float32),
    )
    norm_pull = jax.vjp(input_norm, hidden, gain_all)[1]
    grad_hidden, grad_gain = norm_pull(grad_normed)
    input_grad = (
        (grad_flat.astype(jnp.float32) + grad_hidden)
        .astype(jnp.bfloat16)
        .reshape(seq_count, block_len, model_width)
    )
    norm_gain_grad, conv_weight_grad, conv_bias_grad, gate_gain_grad = (
        lax.psum_scatter(grad_gain, ("dp", "seq", "fsdp"), scatter_dimension=0, tiled=True),
        lax.psum_scatter(grad_taps, ("dp", "seq", "fsdp"), scatter_dimension=0, tiled=True),
        lax.psum_scatter(grad_bias, ("dp", "seq", "fsdp"), scatter_dimension=0, tiled=True),
        lax.psum_scatter(grad_gate_gain, ("dp", "seq", "fsdp"), scatter_dimension=0, tiled=True),
    )
    step_bias_grad, log_rate_grad, skip_gain_grad = lax.psum(
        (grad_step_bias, grad_log_rate, grad_skip), ("dp", "seq", "fsdp")
    )
    return (
        layer_output,
        input_grad,
        norm_gain_grad,
        in_weight_grad,
        conv_weight_grad,
        conv_bias_grad,
        step_bias_grad,
        log_rate_grad,
        skip_gain_grad,
        gate_gain_grad,
        out_weight_grad,
    )


MESH = pl.DeviceIdType.MESH
F32 = jnp.float32
BF16 = jnp.bfloat16
TILE = 128
SPAN = 128
MODEL = 2048
COMMON = 384
PAD = 16
NEG = -1e30
SLOTS = (1, 4)
VM = pl.BlockSpec(memory_space=pltpu.VMEM)
SM = pl.BlockSpec(memory_space=pltpu.SMEM)
ANY = pl.BlockSpec(memory_space=pl.ANY)
DMA = pltpu.SemaphoreType.DMA


def remote(src, dst, sends, recvs, device):
    return pltpu.make_async_remote_copy(
        src_ref=src,
        dst_ref=dst,
        send_sem=sends,
        recv_sem=recvs,
        device_id=device,
        device_id_type=MESH,
    )


def dot(a, b, over=((1,), (0,))):
    return lax.dot_general(a, b, (over, ((), ())), preferred_element_type=F32)


def exact(a, b, over=((1,), (0,))):
    return lax.dot_general(a, b, (over, ((), ())), precision=HIGH, preferred_element_type=F32)


def begin_at(place, starts, docs):
    begin = jnp.zeros_like(place)
    for doc in range(1, docs):
        begin = jnp.where(starts[0, doc] <= place, starts[0, doc], begin)
    return begin


def iota(shape, dim):
    return lax.broadcasted_iota(jnp.int32, shape, dim)


def silu_slope(value):
    gate = jax.nn.sigmoid(value)
    return gate * (1.0 + value * (1.0 - gate))


def softplus(value):
    return jnp.maximum(value, 0.0) + jnp.log1p(jnp.exp(-jnp.abs(value)))


def conv_tile(extended, taps, lanes, valid):
    total = jnp.broadcast_to(taps[KW : KW + 1, lanes], (SPAN, TILE))
    for tap in range(KW):
        back = KW - 1 - tap
        moved = extended if back == 0 else pltpu.roll(extended, back, 0)
        total = total + jnp.where(valid[tap], moved[PAD:], 0.0) * taps[tap : tap + 1, lanes]
    return total


def tile_of(index):
    return slice(index * TILE, (index + 1) * TILE)


def rows_of(index, size=SPAN):
    return pl.ds(pl.multiple_of(index * size, size), size)


def head_col(values, head):
    return jnp.broadcast_to(values[:, head : head + 1], (SPAN, TILE))


def lane_sum(values):
    return jnp.broadcast_to(jnp.sum(values, axis=1, keepdims=True), values.shape)


class Line:
    def __init__(self, place, sizes, block, sems):
        self.dp, self.c, self.z = place
        self.nc, self.nz = sizes
        self.block = block
        self.right_s, self.right_r, self.left_s, self.left_r, self.core_s, self.core_r = sems

    def right(self, s):
        block = self.block(self.c, self.z - s)
        to = (self.dp, self.c, lax.rem(self.z + 1, self.nz))
        return remote(block, block, self.right_s.at[s], self.right_r.at[s], to)

    def left(self, s):
        block = self.block(self.c, self.z + s)
        to = (self.dp, self.c, lax.rem(self.z + self.nz - 1, self.nz))
        return remote(block, block, self.left_s.at[s], self.left_r.at[s], to)

    def core(self, z):
        block = self.block(self.c, z)
        to = (self.dp, self.nc - 1 - self.c, self.z)
        return remote(block, block, self.core_s.at[z], self.core_r.at[z], to)

    def across(self):
        return (self.dp, self.nc - 1 - self.c, self.z)

    def begin(self):
        pl.when(self.z < self.nz - 1)(lambda: self.right(0).start())
        pl.when(self.z > 0)(lambda: self.left(0).start())
        self.core(self.z).start()

    def step(self, s):
        z, nz = self.z, self.nz

        @pl.when(z >= s)
        def _():
            block = self.block(self.c, z - s)
            remote(block, block, self.right_s.at[s - 1], self.right_r.at[s - 1], self.across()).wait_recv()
            if s < nz - 1:
                pl.when(z < nz - 1)(lambda: self.right(s).start())
            self.core(z - s).start()

        @pl.when(z + s < nz)
        def _():
            block = self.block(self.c, z + s)
            remote(block, block, self.left_s.at[s - 1], self.left_r.at[s - 1], self.across()).wait_recv()
            if s < nz - 1:
                pl.when(z > 0)(lambda: self.left(s).start())
            self.core(z + s).start()

    def arrive(self):
        for z in range(self.nz):
            block = self.block(self.nc - 1 - self.c, z)
            to = (self.dp, self.nc - 1 - self.c, self.z)
            remote(block, block, self.core_s.at[z], self.core_r.at[z], to).wait_recv()

    def end(self):
        z, nz = self.z, self.nz
        for s in range(nz - 1):
            pl.when((z >= s) & (z < nz - 1))(lambda s=s: self.right(s).wait_send())
            pl.when((z + s < nz) & (z > 0))(lambda s=s: self.left(s).wait_send())
        for s in range(nz):
            self.core(jnp.int32(s)).wait_send()


class Sum:
    def __init__(self, place, sizes, part, came, total, heard, sems):
        self.dp, self.c, self.z = place
        self.nc, self.nz = sizes
        self.part, self.came, self.total, self.heard = part, came, total, heard
        self.core_s, self.core_r, self.right_s, self.right_r, self.left_s, self.left_r = sems

    def core(self, t):
        to = (self.dp, self.nc - 1 - self.c, self.z)
        src = self.part.at[(self.nc - 1 - self.c) * self.nz + t]
        return remote(src, self.came.at[t], self.core_s.at[t], self.core_r.at[t], to)

    def right(self, t):
        to = (self.dp, self.c, lax.rem(self.z + 1, self.nz))
        return remote(self.total.at[t], self.heard.at[t], self.right_s.at[t], self.right_r.at[t], to)

    def left(self, t):
        to = (self.dp, self.c, lax.rem(self.z + self.nz - 1, self.nz))
        return remote(self.total.at[t], self.heard.at[self.nz + t], self.left_s.at[t], self.left_r.at[t], to)

    def add_core(self, t):
        self.core(t).wait_recv()

        def add(r, _):
            at = rows_of(r, 16)
            self.total[t, at, :] = (
                self.part[self.c * self.nz + t, at, :].astype(F32) + self.came[t, at, :].astype(F32)
            ).astype(BF16)
            return 0

        lax.fori_loop(0, SPAN // 16, add, 0)

    def add(self, t, slot):
        def add(r, _):
            at = rows_of(r, 16)
            self.total[t, at, :] = (
                self.total[t, at, :].astype(F32) + self.heard[slot, at, :].astype(F32)
            ).astype(BF16)
            return 0

        lax.fori_loop(0, SPAN // 16, add, 0)

    def begin(self):
        z, nz = self.z, self.nz
        pl.when(z == 0)(lambda: self.right(nz - 1).start())
        pl.when(z == nz - 1)(lambda: self.left(0).start())

    def slot(self, k):
        z, nz = self.z, self.nz
        for hop in range(1, k + 1):
            t = nz - 1 - (k - hop)
            if t > hop:

                @pl.when(z == hop)
                def _(t=t):
                    self.right(t).wait_recv()
                    self.add(t, t)
                    self.right(t).start()

                @pl.when(z == nz - 1 - hop)
                def _(u=nz - 1 - t):
                    self.left(u).wait_recv()
                    self.add(u, nz + u)
                    self.left(u).start()

        @pl.when(z == 0)
        def _():
            self.right(nz - k).wait_send()
            self.right(nz - 1 - k).start()

        @pl.when(z == nz - 1)
        def _():
            self.left(k - 1).wait_send()
            self.left(k).start()

    def arrive(self):
        z, nz = self.z, self.nz
        for t in range(nz):
            pl.when((z == t) & (z > 0))(lambda t=t: self.right(t).wait_recv())
            pl.when((z == t) & (z < nz - 1))(lambda t=t: self.left(t).wait_recv())

    def own(self, rows):
        z, nz = self.z, self.nz
        value = self.total[z, rows, :].astype(F32)
        left = self.heard[z, rows, :].astype(F32)
        right = self.heard[nz + z, rows, :].astype(F32)
        value = value + jnp.where(z > 0, left, 0.0)
        return value + jnp.where(z < nz - 1, right, 0.0)

    def end(self):
        for t in range(self.nz):
            self.core(t).wait_send()
            if t > 1:
                pl.when((self.z < t) & (self.z > 0))(lambda t=t: self.right(t).wait_send())
            else:
                pl.when(self.z < t)(lambda t=t: self.right(t).wait_send())
            if t < self.nz - 2:
                pl.when((self.z > t) & (self.z < self.nz - 1))(lambda t=t: self.left(t).wait_send())
            else:
                pl.when(self.z > t)(lambda t=t: self.left(t).wait_send())


class Square:
    def __init__(self, place, block, size, sems):
        dp, c, z = place
        self.dp, self.dx, self.dy = dp, dp + 1 - 2 * lax.rem(dp, 2), lax.rem(dp + 2, 4)
        self.diag = lax.rem(self.dx + 2, 4)
        self.x, self.y = (self.dx, c, z), (self.dy, c, z)
        self.block = block
        self.half = size // 2
        self.sems = sems

    def copy(self, way, owner, piece, first, rows, to):
        block = self.block(owner, piece, first, rows)
        sends, recvs = self.sems
        return remote(block, block, sends.at[way, piece], recvs.at[way, piece], to)

    def whole(self, way, owner, piece):
        return self.copy(way, owner, piece, 0, 2 * self.half, self.x if way == 0 else self.y)

    def part(self, way, owner, piece):
        return self.copy(way, owner, piece, 0 if way == 2 else self.half, self.half, self.y if way == 2 else self.x)

    def begin(self, piece):
        self.whole(0, self.dp, piece).start()
        self.whole(1, self.dp, piece).start()

    def step(self, piece):
        self.whole(0, self.dx, piece).wait_recv()
        self.part(2, self.dx, piece).start()
        self.whole(1, self.dy, piece).wait_recv()
        self.part(3, self.dy, piece).start()

    def arrive(self, piece):
        self.part(2, self.diag, piece).wait_recv()
        self.part(3, self.diag, piece).wait_recv()

    def end(self, piece):
        self.whole(0, self.dp, piece).wait_send()
        self.whole(1, self.dp, piece).wait_send()
        self.part(2, self.dx, piece).wait_send()
        self.part(3, self.dy, piece).wait_send()


class SquareSum:
    def __init__(self, place, part, once, twice, gone, sems, pieces):
        dp, c, z = place
        self.dp, self.dx, self.dy = dp, dp + 1 - 2 * lax.rem(dp, 2), lax.rem(dp + 2, 4)
        self.diag = lax.rem(self.dx + 2, 4)
        self.x, self.y = (self.dx, c, z), (self.dy, c, z)
        self.part, self.once, self.twice, self.gone = part, once, twice, gone
        self.s1, self.r1, self.s2, self.r2 = sems
        self.pieces = pieces
        self.rows = part.shape[1] // pieces
        cut = (part.shape[2] // TILE + 1) // 2 * TILE
        self.halves = (slice(0, cut), slice(cut, part.shape[2]))
        self.widths = (cut, part.shape[2] - cut)

    def first(self, p, side, k):
        owner = ((self.dx, self.diag), (self.dy, self.diag))[side][k]
        at = pl.ds(p * self.rows, self.rows)
        slot = 2 * side + k
        return remote(
            self.part.at[owner, at, self.halves[side]], self.once.at[slot, at, : self.widths[side]],
            self.s1.at[p, slot], self.r1.at[p, slot], (self.x, self.y)[side],
        )

    def second(self, p, side):
        at = pl.ds(p * self.rows, self.rows)
        return remote(
            self.gone.at[side, at, : self.widths[side]], self.twice.at[side, at, : self.widths[side]],
            self.s2.at[p, side], self.r2.at[p, side], (self.y, self.x)[side],
        )

    def begin_x(self, p):
        self.first(p, 0, 1).start()
        self.first(p, 0, 0).start()

    def begin_y(self, p):
        self.first(p, 1, 1).start()
        self.first(p, 1, 0).start()

    def each(self, p, body):
        def step(r, _):
            body(pl.ds(pl.multiple_of(p * self.rows + r * 16, 16), 16))
            return 0

        lax.fori_loop(0, self.rows // 16, step, 0)

    def pass_on(self, p):
        for side in range(2):
            self.first(p, side, 1).wait_recv()
            owner = (self.dy, self.dx)[side]

            def body(at, side=side, owner=owner):
                self.gone[side, at, : self.widths[side]] = (
                    self.part[owner, at, self.halves[side]].astype(F32)
                    + self.once[2 * side + 1, at, : self.widths[side]].astype(F32)
                ).astype(BF16)

            self.each(p, body)
            self.second(p, side).start()

    def finish(self, p, out):
        for side in range(2):
            self.first(p, side, 0).wait_recv()
            self.second(p, side).wait_recv()

            def body(at, side=side):
                out[at, self.halves[side]] = (
                    self.part[self.dp, at, self.halves[side]].astype(F32)
                    + self.once[2 * side, at, : self.widths[side]].astype(F32)
                    + self.twice[side, at, : self.widths[side]].astype(F32)
                ).astype(out.dtype)

            self.each(p, body)

    def end(self):
        for p in range(self.pieces):
            for side in range(2):
                self.first(p, side, 0).wait_send()
                self.first(p, side, 1).wait_send()
                self.second(p, side).wait_send()


class HeadSplit:
    def __init__(self, nd, nc, nz):
        self.nd, self.nc, self.nz = nd, nc, nz
        self.nm = nc * nz
        self.span = self.nm * SPAN
        self.rows_in = MODEL // (nd * self.nm)
        self.wide = nd * TILE
        self.per = HEADS // (nd * self.nm)

    def fits(self):
        return (
            INNER == self.nd * self.nm * TILE and self.nd == 4 and self.nc == 2 and self.rows_in % 32 == 0
        )

    def place(self):
        return lax.axis_index("dp"), lax.axis_index("seq"), lax.axis_index("fsdp")

    def group_steps(self):
        return [(e, d) for d in range(self.nz) for e in range(self.nc) if e or d]

    def target(self, step):
        dp, c, z = self.place()
        ct, zt = lax.rem(c + step[0], self.nc), lax.rem(z + step[1], self.nz)
        return (dp, ct, zt), ct * self.nz + zt

    def source(self, step):
        dp, c, z = self.place()
        cs, zs = lax.rem(c + self.nc - step[0], self.nc), lax.rem(z + self.nz - step[1], self.nz)
        return cs * self.nz + zs

    def barrier(self):
        dp, c, z = self.place()
        sem = pltpu.get_barrier_semaphore()
        for step in self.group_steps():
            pl.semaphore_signal(sem, inc=1, device_id=self.target(step)[0], device_id_type=MESH)
        for k in range(1, self.nd):
            pl.semaphore_signal(
                sem, inc=1, device_id=(lax.rem(dp + k, self.nd), c, z), device_id_type=MESH
            )
        pl.semaphore_wait(sem, self.nm - 1 + self.nd - 1)

    def first_kernel(
        self, docs, starts, unit, x_ref, par_ref, head_ref, g_ref, wm_ref, wc_ref, wo_ref,
        y_out, x_out, g_out, w_out, wc_out, dproj, dcom, normed_out, sums, heads, gain_out,
        xall, gall, wall, wcall, woall, parbuf, parall, every_par, projm, pre_sig, o, states, step_s, cum_s,
        dg, scaled, sel, hp, chp, state, dnext, heard_st, st, pre_bc, projc, taps, ypart, ycame, ytotal, yheard,
        pd_s, pd_r, pg_s, pg_r, wz_s, wz_r, cz_s, cz_r, wq_s, wq_r, cq_s, cq_r, oq_s, oq_r, cc_s, cc_r,
        xr_s, xr_r, xl_s, xl_r, xc_s, xc_r, gr_s, gr_r, gl_s, gl_r, gc_s, gc_r,
        st_s, st_r, yc_s, yc_r, yr_s, yr_r, yl_s, yl_r, loc,
    ):
        nd, nc, nz, nm = self.nd, self.nc, self.nz, self.nm
        rows, wide = self.rows_in, self.wide
        where = dp, c, z = self.place()
        me = c * nz + z
        sizes = (nc, nz)
        steps = self.group_steps()
        other = (dp, nc - 1 - c, z)
        lines = [(k, (lax.rem(dp + k, nd), c, z), lax.rem(dp + nd - k, nd)) for k in range(1, nd)]
        started = []

        def go(copy):
            copy.start()
            started.append(copy)
            return copy

        def w_block(owner, m, first=0, count=rows):
            at = pl.multiple_of((owner * nm + m) * rows + first, rows // 2)
            return wall.at[pl.ds(at, count), :]

        def c_block(owner, m, first=0, count=rows):
            at = pl.multiple_of((owner * nm + m) * rows + first, rows // 2)
            return wcall.at[pl.ds(at, count), :]

        w_from = [me] + [self.source(step) for step in steps]
        c_from = [c * nz + lax.rem(z + nz - d, nz) for d in range(nz)]
        w_square = Square(
            where, lambda owner, j, first, count: w_block(owner, w_from[j], first, count), rows, (wq_s, wq_r)
        )
        c_square = Square(
            where, lambda owner, j, first, count: c_block(owner, c_from[j], first, count), rows, (cq_s, cq_r)
        )
        o_square = Square(
            where,
            lambda owner, j, first, count: woall.at[
                pl.ds(pl.multiple_of(owner * TILE + first, TILE // 2), count), :
            ],
            TILE,
            (oq_s, oq_r),
        )
        x_line = Line(where, sizes, lambda a, b: xall.at[rows_of(a * nz + b), :], (xr_s, xr_r, xl_s, xl_r, xc_s, xc_r))
        g_line = Line(where, sizes, lambda a, b: gall.at[rows_of(a * nz + b), :], (gr_s, gr_r, gl_s, gl_r, gc_s, gc_r))
        y_sum = Sum(where, sizes, ypart, ycame, ytotal, yheard, (yc_s, yc_r, yr_s, yr_r, yl_s, yl_r))

        st[...] = jnp.zeros_like(st)
        parbuf[dp] = par_ref[...]
        own = [
            pltpu.make_async_copy(wm_ref.at[me], w_block(dp, me), loc.at[0]),
            pltpu.make_async_copy(wc_ref, c_block(dp, me), loc.at[1]),
            pltpu.make_async_copy(wo_ref, woall.at[rows_of(dp), :], loc.at[2]),
            pltpu.make_async_copy(g_ref, gall.at[rows_of(me), :], loc.at[3]),
        ]
        for copy in own:
            copy.start()
        self.barrier()
        for k, device, _ in lines:
            go(remote(parbuf.at[dp], parbuf.at[dp], pd_s.at[k], pd_r.at[k], device))
        for j, step in enumerate(steps):
            device, there = self.target(step)
            go(remote(wm_ref.at[there], w_block(dp, me), wz_s.at[j], wz_r.at[j], device))
            if step[0] == 0:
                go(remote(wc_ref, c_block(dp, me), cz_s.at[step[1]], cz_r.at[step[1]], device))
        for copy in own[:3]:
            copy.wait()
        o_square.begin(0)
        w_square.begin(0)
        c_square.begin(0)
        for k, device, frm in lines:
            remote(parbuf.at[frm], parbuf.at[frm], pd_s.at[k], pd_r.at[k], device).wait_recv()
        parall[me] = parbuf[...]
        for j, step in enumerate(steps):
            device, _ = self.target(step)
            go(remote(parbuf, parall.at[me], pg_s.at[j], pg_r.at[j], device))
        for j, step in enumerate(steps):
            device, _ = self.target(step)
            remote(parbuf, parall.at[self.source(step)], pg_s.at[j], pg_r.at[j], device).wait_recv()
        owners = [(first // nm, first % nm) for first in range(nd * nm)]
        gain = jnp.concatenate([parall[m, d][5:6, :rows] for d, m in owners], axis=1)
        gain_out[...] = jnp.broadcast_to(gain, (8, MODEL))
        hidden = x_ref[...].astype(F32)
        inverse = lax.rsqrt(jnp.mean(hidden * hidden, axis=1, keepdims=True) + EPSILON)
        xall[rows_of(me), :] = (hidden * inverse * gain).astype(BF16)
        x_line.begin()

        for j, step in enumerate(steps):
            device, _ = self.target(step)
            block = w_block(dp, w_from[j + 1])
            remote(block, block, wz_s.at[j], wz_r.at[j], device).wait_recv()
            w_square.begin(j + 1)
            if step[0] == 0:
                d = step[1]
                block = c_block(dp, c_from[d])
                remote(block, block, cz_s.at[d], cz_r.at[d], device).wait_recv()
                c_square.begin(d)
            if j == 2:
                o_square.step(0)
                w_square.step(0)
                c_square.step(0)
        own_conv = CONV // (nd * nm)
        every_par[...] = jnp.concatenate([parall[m, d][:, :own_conv] for d, m in owners], axis=1)
        for i in range(nd):
            at = pl.ds(pl.multiple_of((i * nm + me) * TILE, TILE), TILE)
            taps[:, tile_of(i)] = every_par[:, at]
        taps[:, wide:] = every_par[:, INNER : INNER + 2 * TILE]
        head, lane = iota((TILE, TILE), 0), iota((TILE, TILE), 1)
        step_of = nm * self.per
        chosen = (head == lax.div(lane, self.per) * step_of + self.per * me + lax.rem(lane, self.per)) & (
            lane < nd * self.per
        )
        sel[...] = chosen.astype(BF16)
        hp[...] = exact(head_ref[...], chosen.astype(F32))
        for i in range(nd):
            chosen = head == i * step_of + self.per * me + lax.div(lane, HEAD_DIM)
            spread = exact(head_ref[...], chosen.astype(F32))
            chp[0:2, tile_of(i)] = spread[2:4, :]
            chp[2:3, tile_of(i)] = parbuf[i][6:7, :TILE]
        x_line.step(1)
        for j in range(1, 4):
            w_square.step(j)
        for j in range(1, nz):
            c_square.step(j)
        x_line.step(2)
        for j in range(4, nm):
            w_square.step(j)
        x_line.step(3)
        own[3].wait()
        g_line.begin()
        for j in range(nz):
            c_square.arrive(j)
        for i in range(nd):
            at = pl.ds(pl.multiple_of((i * nm + c * nz) * rows, rows), nz * rows)
            go(remote(wcall.at[at, :], wcall.at[at, :], cc_s.at[i], cc_r.at[i], other))
        x_line.arrive()
        for j in range(nm):
            w_square.arrive(j)
        for i in range(nd):
            at = pl.ds(pl.multiple_of((i * nm + (nc - 1 - c) * nz) * rows, rows), nz * rows)
            remote(wcall.at[at, :], wcall.at[at, :], cc_s.at[i], cc_r.at[i], other).wait_recv()
        outs = [
            pltpu.make_async_copy(xall, x_out, loc.at[4]),
            pltpu.make_async_copy(wall, w_out, loc.at[5]),
            pltpu.make_async_copy(wcall, wc_out, loc.at[6]),
        ]
        for copy in outs:
            copy.start()

        projm[0:PAD, :] = jnp.zeros((PAD, 2 * wide), BF16)
        projc[0:PAD, :] = jnp.zeros((PAD, COMMON), BF16)
        projc[PAD:, :] = dot(xall[...], wcall[...]).astype(BF16)

        def project(n, _):
            at = rows_of(n, 256)
            projm[PAD:, at] = dot(xall[...], wall[:, at]).astype(BF16)
            pl.when(n == 2)(lambda: g_line.step(1))
            return 0

        lax.fori_loop(0, 2 * wide // 256, project, 0)
        state[...] = jnp.zeros_like(state)

        def forward(i, _):
            self.forward_chunk(
                i, docs, starts, projm, projc, taps, sel, hp, chp,
                pre_sig, pre_bc, o, states, step_s, cum_s, scaled, st, state,
            )
            pl.when(i == 2)(lambda: g_line.step(2))
            pl.when(i == 6)(lambda: g_line.step(3))
            return 0

        lax.fori_loop(0, nm, forward, 0)

        o_square.arrive(0)

        def branch(n, _):
            turn = lax.rem(n + (nc - 1 - c) * nz, nm)
            ypart[turn] = dot(scaled[rows_of(turn), :], woall[...]).astype(BF16)
            return 0

        lax.fori_loop(0, nz, branch, 0)
        for t in range(nz):
            y_sum.core(t).start()
        lax.fori_loop(nz, nm, branch, 0)
        for t in range(nz):
            y_sum.add_core(t)
        y_sum.begin()

        g_line.arrive()
        out = pltpu.make_async_copy(gall, g_out, loc.at[7])
        out.start()
        outs.append(out)
        lanes_at = iota((SPAN, TILE), 1)

        def gate_grad(n, _):
            at = rows_of(n, 256)
            grad = dot(gall[at, :], woall[...], ((1,), (1,)))
            dg[at, :] = grad
            for half in range(2):
                product = jnp.zeros((SPAN, TILE), F32)
                for i in range(nd):
                    mine = scaled[pl.ds(pl.multiple_of(n * 256 + half * SPAN, SPAN), SPAN), tile_of(i)]
                    product = product + mine.astype(F32) * grad[half * SPAN : (half + 1) * SPAN, tile_of(i)]
                st[1, pl.ds(2 * n + half, 1), :] = lane_sum(product).T[0:1, :]
            return 0

        lax.fori_loop(0, nm // 2, gate_grad, 0)
        sent = []
        for j, step in enumerate(steps):
            device, _ = self.target(step)
            sent.append(go(remote(st, heard_st.at[j], st_s.at[j], st_r.at[j], device)))

        totals = st[...]
        for j, copy in enumerate(sent):
            copy.wait_recv()
            totals = totals + heard_st[j]
        for copy in sent:
            copy.wait_send()
        st[...] = totals

        dnext[...] = jnp.zeros_like(dnext)
        state[...] = jnp.zeros_like(state)
        sums[...] = jnp.zeros_like(sums)
        heads[...] = jnp.zeros_like(heads)

        def backward(n, _):
            self.backward_chunk(
                nm - 1 - n, docs, starts, unit, projm, pre_sig, pre_bc, o, states, step_s, cum_s, dg, st, taps, sel,
                hp, chp, dproj, dcom, normed_out, sums, heads, state, dnext, projc,
            )
            for k in range(1, nz - 1):
                pl.when(n == SLOTS[k - 1])(lambda k=k: y_sum.slot(k))
            return 0

        lax.fori_loop(0, nm, backward, 0)
        y_sum.arrive()
        stat = jnp.broadcast_to(st[0, pl.ds(me, 1), :], (SPAN, TILE)).T
        root = lax.rsqrt(stat[:, 0:1] * unit[0, 0] + EPSILON)
        y_out[...] = (x_ref[...].astype(F32) + root * y_sum.own(slice(None))).astype(BF16)
        for copy in outs:
            copy.wait()
        for copy in started:
            if not any(copy is s for s in sent):
                copy.wait_send()
        for j in range(nm):
            w_square.end(j)
        for j in range(nz):
            c_square.end(j)
        o_square.end(0)
        x_line.end()
        g_line.end()
        y_sum.end()

    def forward_chunk(
        self, chunk, docs, starts, projm, projc, taps, sel, hp, chp,
        pre_sig, pre_bc, o, states, step_s, cum_s, scaled, st, state,
    ):
        nd, wide = self.nd, self.wide
        first = chunk * SPAN
        here = rows_of(chunk)
        lead = pl.ds(pl.multiple_of(chunk * SPAN, SPAN), SPAN + PAD)
        body = pl.ds(pl.multiple_of(chunk * SPAN + PAD, PAD), SPAN)
        lane = iota((SPAN, TILE), 1)
        row = iota((SPAN, TILE), 0)
        low = lane < HEAD_DIM
        begin_t = begin_at(first + row, starts, docs)
        begin_s = begin_at(first + lane, starts, docs)
        valid = [first + row - (KW - 1 - tap) >= begin_t for tap in range(KW)]
        sides = []
        for i in range(2):
            lanes = tile_of(i)
            value = conv_tile(projc[lead, lanes].astype(F32), taps, tile_of(nd + i), valid)
            pre_bc[here, lanes] = value
            sides.append((value * jax.nn.sigmoid(value)).astype(BF16))
        key_side, query_side = sides
        rate = dot(projc[body, 2 * TILE :], sel[...])
        step = softplus(rate + hp[0:1, :])
        log_decay = step * hp[1:2, :]
        cum = exact((lane <= row).astype(F32), log_decay)
        step_s[here, :] = step
        cum_s[here, :] = cum
        cum_t = cum.T
        shut = jnp.where((begin_t == begin_s) & (lane <= row), 0.0, NEG)
        inherits = (begin_t < first).astype(F32)
        begin_last = begin_at(jnp.full((SPAN, TILE), first + SPAN - 1, jnp.int32), starts, docs)
        last_same = (begin_t == begin_last).astype(F32)
        meet = dot(query_side, key_side, ((1,), (1,)))
        before = state[...]
        states[chunk] = before
        carried_out = dot(query_side, before.astype(BF16))
        squares = jnp.zeros((SPAN, TILE), F32)
        for i in range(nd):
            lanes = tile_of(i)
            pre = conv_tile(projm[lead, tile_of(nd + i)].astype(F32), taps, lanes, valid)
            pre_sig[here, lanes] = pre
            signal = pre * jax.nn.sigmoid(pre)
            cums = [head_col(cum, 2 * i), head_col(cum, 2 * i + 1)]
            stepx = jnp.where(low, head_col(step, 2 * i), head_col(step, 2 * i + 1))
            cumx = jnp.where(low, cums[0], cums[1])
            fed = stepx * signal
            fed_low = fed.astype(BF16)
            local = []
            for e in range(2):
                head = 2 * i + e
                kernel = jnp.exp(cums[e] - cum_t[head : head + 1, :] + shut)
                local.append(dot((kernel * meet).astype(BF16), fed_low))
            entry = jnp.exp(cumx) * inherits
            out = jnp.where(low, local[0], local[1]) + entry * carried_out[:, lanes]
            o[here, lanes] = out
            last = cumx[SPAN - 1 : SPAN, :]
            tail = jnp.exp((last - cumx) * last_same) * last_same
            state[:, lanes] = entry[SPAN - 1 : SPAN, :] * before[:, lanes] + dot(
                key_side, (tail * fed).astype(BF16), ((0,), (0,))
            )
            mixed = (out + chp[0:1, lanes] * signal) * chp[1:2, lanes]
            gate_in = projm[body, lanes].astype(F32)
            gated = mixed * (gate_in * jax.nn.sigmoid(gate_in))
            squares = squares + gated * gated
            scaled[here, lanes] = (gated * chp[2:3, lanes]).astype(BF16)
        st[0, pl.ds(chunk, 1), :] = lane_sum(squares).T[0:1, :]

    def backward_chunk(
        self, chunk, docs, starts, unit, projm, pre_sig, pre_bc, o, states, step_s, cum_s, dg, st, taps, sel,
        hp, chp, dproj, dcom, normed_out, sums, heads, dstate, dnext, projc,
    ):
        nd = self.nd
        first = chunk * SPAN
        here = rows_of(chunk)
        lead = pl.ds(pl.multiple_of(chunk * SPAN, SPAN), SPAN + PAD)
        body = pl.ds(pl.multiple_of(chunk * SPAN + PAD, PAD), SPAN)
        lane = iota((SPAN, TILE), 1)
        row = iota((SPAN, TILE), 0)
        low = lane < HEAD_DIM
        begin_t = begin_at(first + row, starts, docs)
        begin_s = begin_at(first + lane, starts, docs)
        shut = jnp.where((begin_t == begin_s) & (lane <= row), 0.0, NEG)
        inherits = (begin_t < first).astype(F32)
        begin_last = begin_at(jnp.full((SPAN, TILE), first + SPAN - 1, jnp.int32), starts, docs)
        last_same = (begin_t == begin_last).astype(F32)
        lower = (lane <= row).astype(F32)
        key_pre, query_pre = pre_bc[here, :TILE], pre_bc[here, TILE:]
        key_side = (key_pre * jax.nn.sigmoid(key_pre)).astype(BF16)
        query_side = (query_pre * jax.nn.sigmoid(query_pre)).astype(BF16)
        meet = dot(query_side, key_side, ((1,), (1,)))
        step, cum = step_s[here, :], cum_s[here, :]
        cum_t = cum.T
        square = jnp.broadcast_to(st[0, pl.ds(chunk, 1), :], (SPAN, TILE)).T
        cross = jnp.broadcast_to(st[1, pl.ds(chunk, 1), :], (SPAN, TILE)).T
        root = lax.rsqrt(square * unit[0, 0] + EPSILON)
        pull = root * root * root * cross * unit[0, 0]
        before = states[chunk]
        before_low = before.astype(BF16)
        after = dstate[...]
        after_low = after.astype(BF16)
        carried_out = dot(query_side, before_low)
        from_state = dot(key_side, after_low)
        meet_grad = jnp.zeros((SPAN, SPAN), F32)
        cum_cols = jnp.zeros((SPAN, TILE), F32)
        cum_rows = jnp.zeros((8, SPAN), F32)
        step_cols = jnp.zeros((SPAN, TILE), F32)
        entered, tails = [], []
        head_rows = iota((8, SPAN), 0)
        next_rows = first + iota((SPAN + PAD, TILE), 0)
        next_begin = begin_at(next_rows, starts, docs)
        valid = [next_rows - (KW - 1 - tap) >= next_begin for tap in range(KW)]
        tail_row = row == SPAN - 1

        def conv_back(pre_grad, ext, lanes):
            sums[2:3, lanes] += jnp.sum(pre_grad, axis=0, keepdims=True)
            later = jnp.concatenate([pre_grad, dnext[:, lanes]], axis=0)
            dnext[:, lanes] = pre_grad[0:PAD, :]
            back_grad = jnp.zeros((SPAN, TILE), F32)
            for tap in range(KW):
                back = KW - 1 - tap
                masked = jnp.where(valid[tap], later, 0.0)
                moved = ext if back == 0 else pltpu.roll(ext, back, 0)
                sums[4 + tap : 5 + tap, lanes] += jnp.sum(masked[:SPAN] * moved[PAD:], axis=0, keepdims=True)
                ahead = masked if back == 0 else pltpu.roll(masked, SPAN + PAD - back, 0)
                back_grad = back_grad + ahead[:SPAN] * taps[tap : tap + 1, lanes]
            return back_grad

        for i in range(nd):
            lanes = tile_of(i)
            pre = pre_sig[here, lanes]
            gate_of = jax.nn.sigmoid(pre)
            signal = pre * gate_of
            gate_in = projm[body, lanes].astype(F32)
            gate_sig = jax.nn.sigmoid(gate_in)
            opened = gate_in * gate_sig
            mask = chp[1:2, lanes]
            mixed = (o[here, lanes] + chp[0:1, lanes] * signal) * mask
            gated = mixed * opened
            grad = dg[here, lanes]
            gain = chp[2:3, lanes]
            normed_out[here, lanes] = (gated * root * gain).astype(BF16)
            sums[0:1, lanes] += jnp.sum(grad * gated * root, axis=0, keepdims=True)
            gated_grad = root * grad * gain - gated * pull
            mixed_grad = gated_grad * opened * mask
            dproj[here, lanes] = (
                gated_grad * mixed * (gate_sig * (1.0 + gate_in * (1.0 - gate_sig)))
            ).astype(BF16)
            sums[1:2, lanes] += jnp.sum(mixed_grad * signal, axis=0, keepdims=True)
            cums = [head_col(cum, 2 * i), head_col(cum, 2 * i + 1)]
            stepx = jnp.where(low, head_col(step, 2 * i), head_col(step, 2 * i + 1))
            cumx = jnp.where(low, cums[0], cums[1])
            fed = stepx * signal
            fed_low = fed.astype(BF16)
            out_grad = mixed_grad
            out_low = out_grad.astype(BF16)
            entry = jnp.exp(cumx) * inherits
            last = cumx[SPAN - 1 : SPAN, :]
            tail = jnp.exp((last - cumx) * last_same) * last_same
            backs = []
            for e in range(2):
                head = 2 * i + e
                kernel = jnp.exp(cums[e] - cum_t[head : head + 1, :] + shut)
                mix = kernel * meet
                half = low if e == 0 else jnp.logical_not(low)
                mix_grad = dot(jnp.where(half, out_grad, 0.0).astype(BF16), fed_low, ((1,), (1,)))
                meet_grad = meet_grad + kernel * mix_grad
                weight = mix * mix_grad
                cum_cols = cum_cols + jnp.where(lane == head, lane_sum(weight), 0.0)
                cum_rows = cum_rows + jnp.where(
                    head_rows == head, jnp.broadcast_to(jnp.sum(weight, axis=0, keepdims=True), (8, SPAN)), 0.0
                )
                backs.append(dot(mix.astype(BF16), out_low, ((0,), (0,))))
            entry_grad = entry * out_grad
            tail_fed = tail * fed
            entered.append(entry_grad.astype(BF16))
            tails.append(tail_fed.astype(BF16))
            fed_grad = jnp.where(low, backs[0], backs[1]) + tail * from_state[:, lanes]
            moved_in = entry_grad * carried_out[:, lanes]
            moved_out = tail_fed * from_state[:, lanes]
            direct = fed_grad * signal
            end = entry[SPAN - 1 : SPAN, :]
            kept = jnp.sum(after[:, lanes] * before[:, lanes], axis=0, keepdims=True) * end
            at_end = jnp.sum(moved_out, axis=0, keepdims=True) + kept
            local = moved_in - moved_out + jnp.where(tail_row, at_end, 0.0)
            for e in range(2):
                half = low if e == 0 else jnp.logical_not(low)
                place = lane == 2 * i + e
                cum_cols = cum_cols + jnp.where(place, lane_sum(jnp.where(half, local, 0.0)), 0.0)
                step_cols = step_cols + jnp.where(place, lane_sum(jnp.where(half, direct, 0.0)), 0.0)
            dstate[:, lanes] = end * after[:, lanes] + dot(query_side, entry_grad.astype(BF16), ((0,), (0,)))
            signal_grad = stepx * fed_grad + chp[0:1, lanes] * mixed_grad
            pre_grad = signal_grad * (gate_of * (1.0 + pre * (1.0 - gate_of)))
            cols = tile_of(nd + i)
            dproj[here, cols] = conv_back(pre_grad, projm[lead, cols].astype(F32), lanes).astype(BF16)
        meet_low = meet_grad.astype(BF16)
        state_rows = ((1,), (1,))
        query_grad = dot(meet_low, key_side) + dot(jnp.concatenate(entered, axis=1), before_low, state_rows)
        key_grad = dot(meet_low, query_side, ((0,), (0,))) + dot(
            jnp.concatenate(tails, axis=1), after_low, state_rows
        )
        for i, (side_grad, side_pre) in enumerate(((key_grad, key_pre), (query_grad, query_pre))):
            back_grad = conv_back(side_grad * silu_slope(side_pre), projc[lead, tile_of(i)].astype(F32), tile_of(nd + i))
            dcom[here, tile_of(i)] = back_grad.astype(BF16)
        rows_t = jnp.concatenate([cum_rows, jnp.zeros((SPAN - 8, SPAN), F32)], axis=0).T
        decay_grad = exact(lower, cum_cols - rows_t, ((0,), (0,)))
        log_decay = step * hp[1:2, :]
        slope = 1.0 - jnp.exp(-step)
        rate_grad = (step_cols + decay_grad * hp[1:2, :]) * slope
        heads[0:1, :] += jnp.sum(rate_grad, axis=0, keepdims=True)
        heads[1:2, :] += jnp.sum(decay_grad * log_decay, axis=0, keepdims=True)
        dcom[here, 2 * TILE :] = dot(rate_grad.astype(BF16), sel[...], ((1,), (1,))).astype(BF16)

    def first(self, docs, starts, unit, x, par, heads, g, wm, wc, wo):
        nd, nz, nm, rows, span, wide = self.nd, self.nz, self.nm, self.rows_in, self.span, self.wide
        like = jax.ShapeDtypeStruct
        block = (SPAN, MODEL)
        return pl.pallas_call(
            functools.partial(self.first_kernel, docs),
            out_shape=[
                like(block, BF16),
                like((span, MODEL), BF16),
                like((span, MODEL), BF16),
                like((MODEL, 2 * wide), BF16),
                like((MODEL, COMMON), BF16),
                like((span, 2 * wide), BF16),
                like((span, COMMON), BF16),
                like((span, wide), BF16),
                like((8, wide + 2 * TILE), F32),
                like((8, TILE), F32),
                like((8, MODEL), F32),
            ],
            in_specs=[SM, SM, VM, VM, VM, ANY, ANY, ANY, ANY],
            out_specs=[VM, ANY, ANY, ANY, ANY] + [VM] * 6,
            scratch_shapes=[
                pltpu.VMEM((span, MODEL), BF16),
                pltpu.VMEM((span, MODEL), BF16),
                pltpu.VMEM((MODEL, 2 * wide), BF16),
                pltpu.VMEM((MODEL, COMMON), BF16),
                pltpu.VMEM((wide, MODEL), BF16),
                pltpu.VMEM((nd, 8, 2 * TILE), F32),
                pltpu.VMEM((nm, nd, 8, 2 * TILE), F32),
                pltpu.VMEM((8, CONV), F32),
                pltpu.VMEM((PAD + span, 2 * wide), BF16),
                pltpu.VMEM((span, wide), F32),
                pltpu.VMEM((span, wide), F32),
                pltpu.VMEM((nm, STATE, wide), F32),
                pltpu.VMEM((span, TILE), F32),
                pltpu.VMEM((span, TILE), F32),
                pltpu.VMEM((span, wide), F32),
                pltpu.VMEM((span, wide), BF16),
                pltpu.VMEM((TILE, TILE), BF16),
                pltpu.VMEM((8, TILE), F32),
                pltpu.VMEM((8, wide), F32),
                pltpu.VMEM((STATE, wide), F32),
                pltpu.VMEM((PAD, wide + 2 * TILE), F32),
                pltpu.VMEM((nm - 1, 2, nm, TILE), F32),
                pltpu.VMEM((2, nm, TILE), F32),
                pltpu.VMEM((span, 2 * TILE), F32),
                pltpu.VMEM((PAD + span, COMMON), BF16),
                pltpu.VMEM((8, wide + 2 * TILE), F32),
                pltpu.VMEM((nm, *block), BF16),
                pltpu.VMEM((nz, *block), BF16),
                pltpu.VMEM((nz, *block), BF16),
                pltpu.VMEM((2 * nz, *block), BF16),
                DMA((nd,)), DMA((nd,)), DMA((nm,)), DMA((nm,)),
                DMA((nm,)), DMA((nm,)), DMA((nz,)), DMA((nz,)),
                DMA((4, nm)), DMA((4, nm)), DMA((4, nz)), DMA((4, nz)), DMA((4, 1)), DMA((4, 1)),
                DMA((nd,)), DMA((nd,)),
                DMA((nz,)), DMA((nz,)), DMA((nz,)), DMA((nz,)), DMA((nz,)), DMA((nz,)),
                DMA((nz,)), DMA((nz,)), DMA((nz,)), DMA((nz,)), DMA((nz,)), DMA((nz,)),
                DMA((nm,)), DMA((nm,)),
                DMA((nz,)), DMA((nz,)), DMA((nz,)), DMA((nz,)), DMA((nz,)), DMA((nz,)),
                DMA((8,)),
            ],
            compiler_params=pltpu.CompilerParams(
                collective_id=0, has_side_effects=True, vmem_limit_bytes=62 * 2**20
            ),
            name="first",
        )(starts, unit, x, par, heads, g, wm, wc, wo)

    def second_kernel(
        self, dproj, dcom, normed_out, sums, heads, gain, x_ref, g_ref, x_in, g_in, w_in, wc_in,
        dx_out, dw_out, dwc_out, dwo_out, par_out,
        xall, gall, wall, wcall, xpart, xcame, xtotal, xheard,
        cpart, ccame, csum, c1, c2, cgo, crows, cheard,
        wpart, w1, w2, wgo, wsum, opart, o1, o2, ogo, pard, parbuf,
        xc_s, xc_r, xr_s, xr_r, xl_s, xl_r, cc_s, cc_r, c1_s, c1_r, c2_s, c2_r, cz_s, cz_r,
        w1_s, w1_r, w2_s, w2_r, o1_s, o1_r, o2_s, o2_r, wz_s, wz_r, pd_s, pd_r, pg_s, pg_r, loc,
    ):
        nd, nc, nz, nm = self.nd, self.nc, self.nz, self.nm
        rows, wide, span = self.rows_in, self.wide, self.span
        where = dp, c, z = self.place()
        me = c * nz + z
        sizes = (nc, nz)
        steps = self.group_steps()
        other = (dp, nc - 1 - c, z)
        lines = [(k, (lax.rem(dp + k, nd), c, z), lax.rem(dp + k, nd)) for k in range(1, nd)]
        started = []

        def go(copy):
            copy.start()
            started.append(copy)
            return copy

        loads = [
            pltpu.make_async_copy(w_in, wall, loc.at[0]),
            pltpu.make_async_copy(wc_in, wcall, loc.at[1]),
            pltpu.make_async_copy(x_in, xall, loc.at[2]),
            pltpu.make_async_copy(g_in, gall, loc.at[3]),
        ]
        for load in loads:
            load.start()
        self.barrier()
        x_sum = Sum(where, sizes, xpart, xcame, xtotal, xheard, (xc_s, xc_r, xr_s, xr_r, xl_s, xl_r))
        w_sum = SquareSum(where, wpart, w1, w2, wgo, (w1_s, w1_r, w2_s, w2_r), 2)
        o_sum = SquareSum(where, opart, o1, o2, ogo, (o1_s, o1_r, o2_s, o2_r), 1)
        c_sum = SquareSum(where, csum, c1, c2, cgo, (c1_s, c1_r, c2_s, c2_r), 1)
        loads[0].wait()
        loads[1].wait()

        def input_grad(core):
            base = rows_of(core, nz * SPAN)

            def piece(n, _):
                at = rows_of(n, 256)
                part = dot(dproj[base, :], wall[at, :], ((1,), (1,)))
                part = (part + dot(dcom[base, :], wcall[at, :], ((1,), (1,)))).astype(BF16)
                for t in range(nz):
                    xpart[core * nz + t, :, at] = part[t * SPAN : (t + 1) * SPAN, :]
                return 0

            lax.fori_loop(0, MODEL // 256, piece, 0)

        input_grad(nc - 1 - c)
        for t in range(nz):
            x_sum.core(t).start()
        input_grad(c)
        for t in range(nz):
            x_sum.add_core(t)
        x_sum.begin()

        loads[2].wait()

        def weight_grad(owner):
            def piece(n, _):
                at = pl.ds(pl.multiple_of(owner * (nm * rows) + n * 256, 256), 256)
                wpart[owner, rows_of(n, 256), :] = dot(xall[:, at], dproj[...], ((0,), (0,))).astype(BF16)
                return 0

            lax.fori_loop(0, nm * rows // 256, piece, 0)

        weight_grad(w_sum.diag)
        weight_grad(w_sum.dx)
        for p in range(2):
            w_sum.begin_x(p)
        weight_grad(w_sum.dy)
        for p in range(2):
            w_sum.begin_y(p)
        weight_grad(dp)

        def shared_grad(n, _):
            at = rows_of(n, 256)
            cpart[n] = dot(xall[:, at], dcom[...], ((0,), (0,))).astype(BF16)
            return 0

        lax.fori_loop(0, nd * nc, shared_grad, 0)
        ccopies = [
            go(remote(cpart.at[i * nc + nc - 1 - c], ccame.at[i], cc_s.at[i], cc_r.at[i], other)) for i in range(nd)
        ]
        x_sum.slot(1)
        loads[3].wait()

        def out_grad(n, _):
            at = rows_of(n, 512)
            part = dot(normed_out[...], gall[:, at], ((0,), (0,))).astype(BF16)
            for i in range(nd):
                opart[i, :, at] = part[tile_of(i), :]
            return 0

        lax.fori_loop(0, MODEL // 512, out_grad, 0)
        for i in range(nd):
            ccopies[i].wait_recv()
            csum[i] = (cpart[i * nc + c].astype(F32) + ccame[i].astype(F32)).astype(BF16)
        c_sum.begin_x(0)
        c_sum.begin_y(0)
        o_sum.begin_x(0)
        o_sum.begin_y(0)
        w_sum.pass_on(0)
        x_sum.slot(2)
        w_sum.pass_on(1)

        def send_rows(p):
            half = nm // 2
            for j in range(half):
                there = p * half + j
                block = wsum.at[there * rows : (there + 1) * rows, :]
                ct, zt = there // nz, there % nz

                @pl.when(there != me)
                def _():
                    remote(block, dw_out.at[me], wz_s.at[there], wz_r.at[me], (dp, ct, zt)).start()

                @pl.when(there == me)
                def _():
                    dw_out[there] = block[...]

        w_sum.finish(0, wsum)
        send_rows(0)
        c_sum.pass_on(0)
        o_sum.pass_on(0)

        x_sum.arrive()
        hidden = x_ref[...].astype(F32)
        normed_grad = x_sum.own(slice(None))
        inverse = lax.rsqrt(jnp.mean(hidden * hidden, axis=1, keepdims=True) + EPSILON)
        unitary = hidden * inverse
        gain_grad = jnp.sum(normed_grad * unitary, axis=0, keepdims=True)
        grad_scaled = normed_grad * gain[0:1, :]
        middle = jnp.mean(grad_scaled * unitary, axis=1, keepdims=True)
        dx_out[...] = (g_ref[...].astype(F32) + inverse * (grad_scaled - unitary * middle)).astype(BF16)
        base_row = MODEL // TILE
        for i in range(base_row):
            parbuf[i : i + 1, :] = gain_grad[:, tile_of(i)]
        count = nd + 2
        for r in range(8):
            for i in range(count):
                at = base_row + r * count + i
                parbuf[at : at + 1, :] = sums[r : r + 1, tile_of(i)]
        parbuf[base_row + 8 * count :, :] = heads[...]
        small = [
            go(remote(parbuf, pard.at[k - 1], pd_s.at[k], pd_r.at[k], device)) for k, device, _ in lines
        ]
        w_sum.finish(1, wsum)
        send_rows(1)
        c_sum.finish(0, crows)
        for d in range(1, nz):
            to = lax.rem(z + d, nz)
            go(remote(crows.at[rows_of(to, rows), :], cheard.at[d - 1], cz_s.at[d], cz_r.at[d], (dp, c, to)))
        for copy in small:
            copy.wait_recv()
        total = parbuf[...]
        for k in range(nd - 1):
            total = total + pard[k]
        par_out[me] = total
        for j, step in enumerate(steps):
            go(remote(par_out.at[me], par_out.at[me], pg_s.at[j], pg_r.at[j], self.target(step)[0]))
        o_sum.finish(0, dwo_out)
        total = crows[rows_of(z, rows), :].astype(F32)
        for d in range(1, nz):
            remote(cheard.at[d - 1], cheard.at[d - 1], cz_s.at[d], cz_r.at[d], other).wait_recv()
            total = total + cheard[d - 1].astype(F32)
        dwc_out[...] = total
        for j, step in enumerate(steps):
            here = par_out.at[self.source(step)]
            remote(here, here, pg_s.at[j], pg_r.at[j], other).wait_recv()
        for m in range(nm):
            got = dw_out.at[m]

            @pl.when(m != me)
            def _():
                remote(got, got, wz_s.at[m], wz_r.at[m], other).wait_recv()
                remote(got, got, wz_s.at[m], wz_r.at[m], other).wait_send()

        for copy in started:
            copy.wait_send()
        x_sum.end()
        w_sum.end()
        o_sum.end()
        c_sum.end()

    def second(self, dproj, dcom, normed_out, sums, heads, gain, x, g, xall, gall, w, wc):
        nd, nc, nz, nm, rows, span, wide = self.nd, self.nc, self.nz, self.nm, self.rows_in, self.span, self.wide
        like = jax.ShapeDtypeStruct
        block = (SPAN, MODEL)
        npar = MODEL // TILE + 8 * (nd + 2) + 8
        return pl.pallas_call(
            self.second_kernel,
            out_shape=[
                like(block, BF16),
                like((nm, rows, 2 * wide), BF16),
                like((rows, COMMON), F32),
                like((TILE, MODEL), F32),
                like((nm, npar, TILE), F32),
            ],
            in_specs=[VM] * 8 + [ANY] * 4,
            out_specs=[VM] * 5,
            scratch_shapes=[
                pltpu.VMEM((span, MODEL), BF16),
                pltpu.VMEM((span, MODEL), BF16),
                pltpu.VMEM((MODEL, 2 * wide), BF16),
                pltpu.VMEM((MODEL, COMMON), BF16),
                pltpu.VMEM((nm, *block), BF16),
                pltpu.VMEM((nz, *block), BF16),
                pltpu.VMEM((nz, *block), BF16),
                pltpu.VMEM((2 * nz, *block), BF16),
                pltpu.VMEM((nd * nc, nz * rows, COMMON), BF16),
                pltpu.VMEM((nd, nz * rows, COMMON), BF16),
                pltpu.VMEM((nd, nz * rows, COMMON), BF16),
                pltpu.VMEM((4, nz * rows, 2 * TILE), BF16),
                pltpu.VMEM((2, nz * rows, 2 * TILE), BF16),
                pltpu.VMEM((2, nz * rows, 2 * TILE), BF16),
                pltpu.VMEM((nz * rows, COMMON), BF16),
                pltpu.VMEM((nz - 1, rows, COMMON), BF16),
                pltpu.VMEM((nd, nm * rows, 2 * wide), BF16),
                pltpu.VMEM((4, nm * rows, wide), BF16),
                pltpu.VMEM((2, nm * rows, wide), BF16),
                pltpu.VMEM((2, nm * rows, wide), BF16),
                pltpu.VMEM((nm * rows, 2 * wide), BF16),
                pltpu.VMEM((nd, TILE, MODEL), BF16),
                pltpu.VMEM((4, TILE, MODEL // 2), BF16),
                pltpu.VMEM((2, TILE, MODEL // 2), BF16),
                pltpu.VMEM((2, TILE, MODEL // 2), BF16),
                pltpu.VMEM((nd - 1, npar, TILE), F32),
                pltpu.VMEM((npar, TILE), F32),
                DMA((nz,)), DMA((nz,)), DMA((nz,)), DMA((nz,)), DMA((nz,)), DMA((nz,)),
                DMA((nd,)), DMA((nd,)), DMA((1, 4)), DMA((1, 4)), DMA((1, 2)), DMA((1, 2)), DMA((nz,)), DMA((nz,)),
                DMA((2, 4)), DMA((2, 4)), DMA((2, 2)), DMA((2, 2)),
                DMA((1, 4)), DMA((1, 4)), DMA((1, 2)), DMA((1, 2)),
                DMA((nm,)), DMA((nm,)), DMA((nd,)), DMA((nd,)),
                DMA((nm,)), DMA((nm,)), DMA((4,)),
            ],
            compiler_params=pltpu.CompilerParams(
                collective_id=1, has_side_effects=True, vmem_limit_bytes=62 * 2**20
            ),
            name="second",
        )(dproj, dcom, normed_out, sums, heads, gain, x, g, xall, gall, w, wc)

    def local(
        self, layer_input, out_grad, norm_gain, in_weight, conv_weight, conv_bias, step_bias, log_rate,
        skip_gain, gate_gain, out_weight, nest_level, doc_lengths,
    ):
        nd, nz, nm, rows, wide = self.nd, self.nz, self.nm, self.rows_in, self.wide
        dp, c, z = self.place()
        me = c * nz + z
        docs = doc_lengths.shape[1]
        order = jnp.arange(docs)
        ahead = order[:, None] < order[None, :]
        starts = jnp.sum(jnp.where(ahead, doc_lengths[0][:, None], 0), axis=0, keepdims=True)
        starts = starts.astype(jnp.int32)
        active = jnp.right_shift(HEADS, 3 - nest_level[0])
        unit = (1.0 / (active * HEAD_DIM).astype(F32)).reshape(1, 1)
        x = layer_input.reshape(SPAN, MODEL)
        g = out_grad.reshape(SPAN, MODEL)
        wm = in_weight[:, : 2 * INNER].reshape(rows, 2 * nd, nm, TILE)
        wm = jnp.transpose(wm, (2, 0, 1, 3)).reshape(nm, rows, 2 * wide)
        wc = jnp.pad(in_weight[:, 2 * INNER :], ((0, 0), (0, COMMON - (EXTENT - 2 * INNER))))
        own_conv = conv_bias.shape[0]
        widen = lambda v: jnp.pad(v, ((0, 0), (0, 2 * TILE - v.shape[1])))
        par = jnp.concatenate(
            [
                widen(conv_weight.T),
                widen(conv_bias[None]),
                widen(norm_gain[None]),
                widen(gate_gain[None]),
                jnp.zeros((1, 2 * TILE), F32),
            ]
        )
        mask = (jnp.arange(HEADS) < active).astype(F32)
        head_in = jnp.stack([step_bias, -jnp.exp(log_rate), skip_gain, mask])
        head_in = jnp.pad(head_in, ((0, 4), (0, TILE - HEADS)))
        y_out, xall, gall, w, wc_all, dproj, dcom, normed_out, sums, heads, gain = self.first(
            docs, starts, unit, x, par, head_in, g, wm, wc, out_weight
        )
        dx_out, dw, dwc, dwo, pars = self.second(
            dproj, dcom, normed_out, sums, heads, gain, x, g, xall, gall, w, wc_all
        )
        dw = jnp.transpose(dw.reshape(nm, rows, 2 * nd, TILE), (1, 2, 0, 3)).reshape(rows, 2 * INNER)
        in_weight_grad = jnp.concatenate([dw.astype(F32), dwc[:, : EXTENT - 2 * INNER]], axis=1)
        owner = dp * nm + me
        gains = jnp.sum(pars[:, : MODEL // TILE], axis=0).reshape(MODEL)
        norm_gain_grad = lax.dynamic_slice_in_dim(gains, owner * rows, rows)
        base = MODEL // TILE
        per_row = pars[:, base : base + 8 * (nd + 2)].reshape(nm, 8, nd + 2, TILE)
        mains = per_row[:, :, :nd]
        shared = jnp.sum(per_row[:, :, nd:], axis=0).reshape(8, 2 * TILE)
        head_sums = pars[:, base + 8 * (nd + 2) :]
        gate_gain_grad = lax.dynamic_index_in_dim(mains[me, 0], dp, 0, keepdims=False)
        everything = jnp.transpose(mains[:, 1:], (1, 2, 0, 3)).reshape(7, INNER)
        skip_gain_grad = jnp.sum(everything[0].reshape(HEADS, HEAD_DIM), axis=1)
        bias_sum = jnp.concatenate([everything[1], shared[2]])
        taps_sum = jnp.concatenate([everything[3:], shared[4:]], axis=1).T
        conv_bias_grad = lax.dynamic_slice_in_dim(bias_sum, owner * own_conv, own_conv)
        conv_weight_grad = lax.dynamic_slice_in_dim(taps_sum, owner * own_conv, own_conv)
        mine = nd * self.per
        by_head = lambda v: jnp.swapaxes(v[:, :mine].reshape(nm, nd, self.per), 0, 1).reshape(HEADS)
        step_bias_grad, log_rate_grad = by_head(head_sums[:, 0]), by_head(head_sums[:, 1])
        return (
            y_out.reshape(1, SPAN, MODEL),
            dx_out.reshape(1, SPAN, MODEL),
            norm_gain_grad,
            in_weight_grad,
            conv_weight_grad,
            conv_bias_grad,
            step_bias_grad,
            log_rate_grad,
            skip_gain_grad,
            gate_gain_grad,
            dwo,
        )


def solution(mesh):
    shape = dict(mesh.shape)
    head_split = HeadSplit(shape["dp"], shape["seq"], shape["fsdp"])
    return jax.shard_map(
        head_split.local if head_split.fits() else token_split,
        mesh=mesh,
        in_specs=(
            P("dp", ("seq", "fsdp"), None),
            P("dp", ("seq", "fsdp"), None),
            P(("dp", "seq", "fsdp")),
            P(("dp", "seq", "fsdp"), None),
            P(("dp", "seq", "fsdp"), None),
            P(("dp", "seq", "fsdp")),
            P(),
            P(),
            P(),
            P(("dp", "seq", "fsdp")),
            P(("dp", "seq", "fsdp"), None),
            P("dp"),
            P("dp", None),
        ),
        out_specs=(
            P("dp", ("seq", "fsdp"), None),
            P("dp", ("seq", "fsdp"), None),
            P(("dp", "seq", "fsdp")),
            P(("dp", "seq", "fsdp"), None),
            P(("dp", "seq", "fsdp"), None),
            P(("dp", "seq", "fsdp")),
            P(),
            P(),
            P(),
            P(("dp", "seq", "fsdp")),
            P(("dp", "seq", "fsdp"), None),
        ),
        check_vma=False,
    )
```

```python
import functools

import jax
import jax.numpy as jnp
from jax import lax
from jax.experimental import pallas as pl
from jax.experimental.pallas import tpu as pltpu
from jax.sharding import PartitionSpec as P

HEADS = 64
HEAD_DIM = 64
STATE = 128
KW = 4
INNER = 4096
CONV = 4352
EXTENT = 8512


HIGH = lax.Precision.HIGHEST
EPSILON = 1e-05


def shifted(value, axis, steps):
    count = lax.axis_size(axis)
    leading, last = (max(0, -steps), min(count, count - steps))
    return lax.ppermute(value, axis, [(source, source + steps) for source in range(leading, last)])


def prefix(array, axis, combine, identity):
    peers, place = (lax.axis_size(axis), lax.axis_index(axis))
    everything = jax.tree.map(
        lambda part, kind: lax.all_gather(part.astype(kind), axis),
        array,
        (jnp.bfloat16, jnp.bfloat16),
    )
    start = jax.tree.map(
        lambda part, zero: jnp.broadcast_to(jnp.asarray(zero, part.dtype), part.shape),
        array,
        identity,
    )

    def prefix_lap(k, before):
        reached = k < place
        new = combine(
            before, jax.tree.map(lambda part, own: part[k].astype(own.dtype), everything, array)
        )
        return jax.tree.map(lambda a, b: jnp.where(reached, a, b), new, before)

    return lax.fori_loop(0, peers, prefix_lap, start)


def carried_in(array, axis, combine, identity):
    peers, place = (lax.axis_size(axis), lax.axis_index(axis))
    everything = jax.tree.map(
        lambda part, kind: lax.all_gather(part.astype(kind), axis),
        array,
        jax.tree.map(lambda a: jnp.bfloat16 if a.dtype == jnp.float32 else a.dtype, array),
    )
    start = jax.tree.map(
        lambda part, zero: jnp.broadcast_to(jnp.asarray(zero, part.dtype), part.shape),
        array,
        identity,
    )

    def carried_lap(k, before):
        at = peers - 1 - k
        reached = at > place
        new = combine(
            before, jax.tree.map(lambda part, own: part[at].astype(own.dtype), everything, array)
        )
        return jax.tree.map(lambda a, b: jnp.where(reached, a, b), new, before)

    return lax.fori_loop(0, peers, carried_lap, start)


def doc_begins(lengths, positions):
    places = jnp.arange(lengths.shape[1])
    ahead = places[:, None] < places[None, :]
    endings = jnp.sum(jnp.where(ahead[None], lengths[:, :, None], 0), axis=1)
    reached = endings[:, None, :] <= positions[None, :, None]
    return jnp.max(jnp.where(reached, endings[:, None, :], 0), axis=2)


def input_norm(hidden, gain):
    inv_rms = lax.rsqrt(jnp.mean(hidden * hidden, axis=1, keepdims=True) + EPSILON)
    return hidden * inv_rms * gain


def causal_conv(extended, taps, bias, validity):
    block_len = validity.shape[2]
    running = bias + jnp.zeros((extended.shape[0], block_len, extended.shape[2]), jnp.float32)
    for tap in range(taps.shape[1]):
        running = (
            running + extended[:, tap : tap + block_len] * taps[:, tap] * validity[tap][:, :, None]
        )
    return jax.nn.silu(running)


def scan_parts(signal, key_side, query_side, rate_in, step_bias, log_rate, begins, block_start):
    step = jax.nn.softplus(rate_in + step_bias)
    log_decay = step * -jnp.exp(log_rate)
    places = jnp.arange(log_decay.shape[1])
    lower = (places[None, :] <= places[:, None]).astype(jnp.float32)
    cumulative = jnp.einsum("ts,bsh->bth", lower, log_decay, precision=HIGH)
    by_head = jnp.swapaxes(cumulative, 1, 2)
    indices = jnp.arange(signal.shape[1])
    same_doc = (begins[:, :, None] == begins[:, None, :]) & (
        indices[None, None, :] <= indices[None, :, None]
    )
    gaps = by_head[:, :, :, None] - by_head[:, :, None, :]
    kernel = jnp.exp(jnp.where(same_doc[:, None], gaps, 0.0)) * same_doc[:, None]
    intersection = jnp.einsum("btn,bsn->bts", query_side, key_side, precision=HIGH)
    mixing = kernel * intersection[:, None] * jnp.swapaxes(step, 1, 2)[:, :, None, :]
    local_out = jnp.einsum("bhts,bshp->bthp", mixing, signal, precision=HIGH)
    inherits = (begins < block_start).astype(jnp.float32)
    carried = jnp.exp(cumulative) * inherits[:, :, None]
    last_same = begins == begins[:, -1:]
    tail_weight = (
        jnp.exp(jnp.where(last_same[:, :, None], cumulative[:, -1:] - cumulative, 0.0))
        * last_same[:, :, None]
        * step
    )
    fresh_state = jnp.einsum("bsh,bshp,bsn->bhpn", tail_weight, signal, key_side, precision=HIGH)
    return (local_out, carried, carried[:, -1], fresh_state)


def gated_norm(scan_out, signal, skip_gain, gate_in, gate_gain, head_mask, unit_count):
    mixed = (scan_out + skip_gain[:, None] * signal) * head_mask[:, None, :, None]
    gated = mixed.reshape(gate_in.shape) * jax.nn.silu(gate_in)
    mean_square = jnp.sum(gated * gated, axis=2, keepdims=True) / unit_count[:, None, None]
    return gated * lax.rsqrt(mean_square + EPSILON) * gate_gain


def combine_states(earlier, later):
    return (earlier[0] * later[0], later[1] + later[0][:, :, None, None] * earlier[1])


def token_split(
    layer_input,
    out_grad,
    norm_gain,
    in_weight,
    conv_weight,
    conv_bias,
    step_bias,
    log_rate,
    skip_gain,
    gate_gain,
    out_weight,
    nest_level,
    doc_lengths,
):
    seq_count, block_len, model_width = layer_input.shape
    token_count = seq_count * block_len
    gain_all, taps_all, bias_all, gate_all = (
        lax.all_gather(norm_gain, ("dp", "seq", "fsdp"), axis=0, tiled=True),
        lax.all_gather(conv_weight, ("dp", "seq", "fsdp"), axis=0, tiled=True),
        lax.all_gather(conv_bias, ("dp", "seq", "fsdp"), axis=0, tiled=True),
        lax.all_gather(gate_gain, ("dp", "seq", "fsdp"), axis=0, tiled=True),
    )
    block_start = lax.axis_index(("seq", "fsdp")) * block_len
    positions = block_start + jnp.arange(block_len, dtype=jnp.int32)
    begins = doc_begins(doc_lengths, positions)
    hidden = layer_input.reshape(token_count, model_width).astype(jnp.float32)
    normed = input_norm(hidden, gain_all).astype(jnp.bfloat16)
    columns = normed
    projected = jnp.dot(
        columns,
        lax.all_gather(in_weight, ("dp", "seq", "fsdp"), axis=0, tiled=True),
        preferred_element_type=jnp.float32,
    ).astype(jnp.bfloat16)
    projected = projected.reshape(seq_count, block_len, EXTENT)
    gate_in = projected[:, :, :INNER].astype(jnp.float32)
    conv_in = projected[:, :, INNER : INNER + CONV]
    rate_in = projected[:, :, INNER + CONV :].astype(jnp.float32)
    edge_rows = shifted(conv_in[:, block_len - (KW - 1) :], ("seq", "fsdp"), 1)
    extended = jnp.concatenate([edge_rows, conv_in], axis=1).astype(jnp.float32)
    validity = jnp.stack(
        [(positions[None, :] - (KW - 1) + tap >= begins).astype(jnp.float32) for tap in range(KW)]
    )
    activated, conv_pull = jax.vjp(
        lambda ext_in, taps, bias: causal_conv(ext_in, taps, bias, validity),
        extended,
        taps_all,
        bias_all,
    )
    signal = activated[:, :, :INNER].reshape(seq_count, block_len, HEADS, HEAD_DIM)
    key_side = activated[:, :, INNER : INNER + STATE]
    query_side = activated[:, :, INNER + STATE :]
    local_out, carried, decays, fresh_state = scan_parts(
        signal, key_side, query_side, rate_in, step_bias, log_rate, begins, block_start
    )
    identity = (jnp.ones_like(decays), jnp.zeros_like(fresh_state))
    entry_state = prefix((decays, fresh_state), ("seq", "fsdp"), combine_states, identity)[1]
    scan_out = local_out + carried[..., None] * jnp.einsum(
        "btn,bhpn->bthp", query_side, entry_state, precision=HIGH
    )
    active = jnp.right_shift(HEADS, 3 - nest_level)
    head_mask = (jnp.arange(HEADS)[None, :] < active[:, None]).astype(jnp.float32)
    unit_count = (active * HEAD_DIM).astype(jnp.float32)
    gate_normed, gate_pull = jax.vjp(
        lambda sv, xv, sk, gi, gg: gated_norm(sv, xv, sk, gi, gg, head_mask, unit_count),
        scan_out,
        signal,
        skip_gain,
        gate_in,
        gate_all,
    )
    normed_out = gate_normed.reshape(token_count, INNER).astype(jnp.bfloat16)
    columns = normed_out
    branch_out = jnp.dot(
        columns,
        lax.all_gather(out_weight, ("dp", "seq", "fsdp"), axis=0, tiled=True),
        preferred_element_type=jnp.float32,
    )
    layer_output = (
        (hidden + branch_out).astype(jnp.bfloat16).reshape(seq_count, block_len, model_width)
    )
    grad_flat = out_grad.reshape(token_count, model_width)
    grad_normed_out = lax.dot_general(
        grad_flat,
        lax.all_gather(out_weight, ("dp", "seq", "fsdp"), axis=0, tiled=True),
        (((1,), (1,)), ((), ())),
        preferred_element_type=jnp.float32,
    )
    grad_scan, grad_skip_signal, grad_skip, grad_gate_in, grad_gate_gain = gate_pull(
        grad_normed_out.reshape(seq_count, block_len, INNER)
    )
    lead_grad = jnp.einsum("bth,bthp,btn->bhpn", carried, grad_scan, query_side, precision=HIGH)
    later_grad = carried_in((decays, lead_grad), ("seq", "fsdp"), combine_states, identity)[1]

    def full_scan(signal_in, key_in, query_in, rate_values, bias_values, rate_logs):
        part_out, part_carried, part_decays, part_fresh = scan_parts(
            signal_in, key_in, query_in, rate_values, bias_values, rate_logs, begins, block_start
        )
        joined_out = part_out + part_carried[..., None] * jnp.einsum(
            "btn,bhpn->bthp", query_in, entry_state, precision=HIGH
        )
        return (joined_out, part_decays[:, :, None, None] * entry_state + part_fresh)

    scan_pull = jax.vjp(full_scan, signal, key_side, query_side, rate_in, step_bias, log_rate)[1]
    grad_signal, grad_key, grad_query, grad_rate, grad_step_bias, grad_log_rate = scan_pull(
        (grad_scan, later_grad)
    )
    grad_activated = jnp.concatenate(
        [
            (grad_signal + grad_skip_signal).reshape(seq_count, block_len, INNER),
            grad_key,
            grad_query,
        ],
        axis=2,
    )
    grad_extended, grad_taps, grad_bias = conv_pull(grad_activated)
    returned = shifted(grad_extended[:, : KW - 1].astype(jnp.bfloat16), ("seq", "fsdp"), -1).astype(
        jnp.float32
    )
    grad_conv_in = grad_extended[:, KW - 1 :] + jnp.pad(
        returned, ((0, 0), (block_len - (KW - 1), 0), (0, 0))
    )
    grad_projected = (
        jnp.concatenate([grad_gate_in, grad_conv_in, grad_rate], axis=2)
        .reshape(token_count, EXTENT)
        .astype(jnp.bfloat16)
    )
    grad_normed = lax.dot_general(
        grad_projected,
        lax.all_gather(in_weight, ("dp", "seq", "fsdp"), axis=0, tiled=True),
        (((1,), (1,)), ((), ())),
        preferred_element_type=jnp.float32,
    )
    replicas = lax.axis_size("dp")
    members = lax.axis_size(("seq", "fsdp"))
    width_in = model_width // lax.axis_size(("dp", "seq", "fsdp"))
    width_out = INNER // lax.axis_size(("dp", "seq", "fsdp"))
    in_cols, out_cols = (
        lax.all_to_all(
            normed.reshape(token_count, replicas, members, width_in),
            ("seq", "fsdp"),
            split_axis=2,
            concat_axis=0,
            tiled=True,
        ),
        lax.all_to_all(
            normed_out.reshape(token_count, replicas, members, width_out),
            ("seq", "fsdp"),
            split_axis=2,
            concat_axis=0,
            tiled=True,
        ),
    )
    in_cols = in_cols.reshape(members * token_count, replicas * width_in)
    out_cols = out_cols.reshape(members * token_count, replicas * width_out)
    in_new = lax.dot_general(
        in_cols,
        lax.all_gather(grad_projected, ("seq", "fsdp"), axis=0, tiled=True),
        (((0,), (0,)), ((), ())),
        preferred_element_type=jnp.float32,
    )
    out_new = lax.dot_general(
        out_cols,
        lax.all_gather(grad_flat, ("seq", "fsdp"), axis=0, tiled=True),
        (((0,), (0,)), ((), ())),
        preferred_element_type=jnp.float32,
    )
    in_weight_grad, out_weight_grad = (
        lax.psum_scatter(in_new.astype(jnp.bfloat16), "dp", scatter_dimension=0, tiled=True).astype(
            jnp.float32
        ),
        lax.psum_scatter(
            out_new.astype(jnp.bfloat16), "dp", scatter_dimension=0, tiled=True
        ).astype(jnp.float32),
    )
    norm_pull = jax.vjp(input_norm, hidden, gain_all)[1]
    grad_hidden, grad_gain = norm_pull(grad_normed)
    input_grad = (
        (grad_flat.astype(jnp.float32) + grad_hidden)
        .astype(jnp.bfloat16)
        .reshape(seq_count, block_len, model_width)
    )
    norm_gain_grad, conv_weight_grad, conv_bias_grad, gate_gain_grad = (
        lax.psum_scatter(grad_gain, ("dp", "seq", "fsdp"), scatter_dimension=0, tiled=True),
        lax.psum_scatter(grad_taps, ("dp", "seq", "fsdp"), scatter_dimension=0, tiled=True),
        lax.psum_scatter(grad_bias, ("dp", "seq", "fsdp"), scatter_dimension=0, tiled=True),
        lax.psum_scatter(grad_gate_gain, ("dp", "seq", "fsdp"), scatter_dimension=0, tiled=True),
    )
    step_bias_grad, log_rate_grad, skip_gain_grad = lax.psum(
        (grad_step_bias, grad_log_rate, grad_skip), ("dp", "seq", "fsdp")
    )
    return (
        layer_output,
        input_grad,
        norm_gain_grad,
        in_weight_grad,
        conv_weight_grad,
        conv_bias_grad,
        step_bias_grad,
        log_rate_grad,
        skip_gain_grad,
        gate_gain_grad,
        out_weight_grad,
    )


MESH = pl.DeviceIdType.MESH
F32 = jnp.float32
BF16 = jnp.bfloat16
TILE = 128
SPAN = 128
MODEL = 2048
COMMON = 384
PAD = 16
NEG = -1e30
SLOTS = (1, 4)
VM = pl.BlockSpec(memory_space=pltpu.VMEM)
SM = pl.BlockSpec(memory_space=pltpu.SMEM)
ANY = pl.BlockSpec(memory_space=pl.ANY)
DMA = pltpu.SemaphoreType.DMA


def remote(src, dst, sends, recvs, device):
    return pltpu.make_async_remote_copy(
        src_ref=src,
        dst_ref=dst,
        send_sem=sends,
        recv_sem=recvs,
        device_id=device,
        device_id_type=MESH,
    )


def dot(a, b, over=((1,), (0,))):
    return lax.dot_general(a, b, (over, ((), ())), preferred_element_type=F32)


def exact(a, b, over=((1,), (0,))):
    return lax.dot_general(a, b, (over, ((), ())), precision=HIGH, preferred_element_type=F32)


def begin_at(place, starts, docs):
    begin = jnp.zeros_like(place)
    for doc in range(1, docs):
        begin = jnp.where(starts[doc] <= place, starts[doc], begin)
    return begin


def iota(shape, dim):
    return lax.broadcasted_iota(jnp.int32, shape, dim)


def silu_slope(value):
    gate = jax.nn.sigmoid(value)
    return gate * (1.0 + value * (1.0 - gate))


def softplus(value):
    return jnp.maximum(value, 0.0) + jnp.log1p(jnp.exp(-jnp.abs(value)))


def conv_tile(extended, taps, lanes, valid):
    total = jnp.broadcast_to(taps[KW : KW + 1, lanes], (SPAN, TILE))
    for tap in range(KW):
        back = KW - 1 - tap
        moved = extended if back == 0 else pltpu.roll(extended, back, 0)
        total = total + jnp.where(valid[tap], moved[PAD:], 0.0) * taps[tap : tap + 1, lanes]
    return total


def tile_of(index):
    return slice(index * TILE, (index + 1) * TILE)


def rows_of(index, size=SPAN):
    return pl.ds(pl.multiple_of(index * size, size), size)


def head_col(values, head):
    return jnp.broadcast_to(values[:, head : head + 1], (SPAN, TILE))


def lane_sum(values):
    return jnp.broadcast_to(jnp.sum(values, axis=1, keepdims=True), values.shape)


class Line:
    def __init__(self, place, sizes, block, sems):
        self.dp, self.c, self.z = place
        self.nc, self.nz = sizes
        self.block = block
        self.right_s, self.right_r, self.left_s, self.left_r, self.core_s, self.core_r = sems

    def right(self, s):
        block = self.block(self.c, self.z - s)
        to = (self.dp, self.c, lax.rem(self.z + 1, self.nz))
        return remote(block, block, self.right_s.at[s], self.right_r.at[s], to)

    def left(self, s):
        block = self.block(self.c, self.z + s)
        to = (self.dp, self.c, lax.rem(self.z + self.nz - 1, self.nz))
        return remote(block, block, self.left_s.at[s], self.left_r.at[s], to)

    def core(self, z):
        block = self.block(self.c, z)
        to = (self.dp, self.nc - 1 - self.c, self.z)
        return remote(block, block, self.core_s.at[z], self.core_r.at[z], to)

    def across(self):
        return (self.dp, self.nc - 1 - self.c, self.z)

    def begin(self):
        pl.when(self.z < self.nz - 1)(lambda: self.right(0).start())
        pl.when(self.z > 0)(lambda: self.left(0).start())
        self.core(self.z).start()

    def step(self, s):
        z, nz = self.z, self.nz

        @pl.when(z >= s)
        def _():
            block = self.block(self.c, z - s)
            remote(block, block, self.right_s.at[s - 1], self.right_r.at[s - 1], self.across()).wait_recv()
            if s < nz - 1:
                pl.when(z < nz - 1)(lambda: self.right(s).start())
            self.core(z - s).start()

        @pl.when(z + s < nz)
        def _():
            block = self.block(self.c, z + s)
            remote(block, block, self.left_s.at[s - 1], self.left_r.at[s - 1], self.across()).wait_recv()
            if s < nz - 1:
                pl.when(z > 0)(lambda: self.left(s).start())
            self.core(z + s).start()

    def arrive(self):
        for z in range(self.nz):
            block = self.block(self.nc - 1 - self.c, z)
            to = (self.dp, self.nc - 1 - self.c, self.z)
            remote(block, block, self.core_s.at[z], self.core_r.at[z], to).wait_recv()

    def end(self):
        z, nz = self.z, self.nz
        for s in range(nz - 1):
            pl.when((z >= s) & (z < nz - 1))(lambda s=s: self.right(s).wait_send())
            pl.when((z + s < nz) & (z > 0))(lambda s=s: self.left(s).wait_send())
        for s in range(nz):
            self.core(jnp.int32(s)).wait_send()


class Sum:
    def __init__(self, place, sizes, part, came, total, heard, sems):
        self.dp, self.c, self.z = place
        self.nc, self.nz = sizes
        self.part, self.came, self.total, self.heard = part, came, total, heard
        self.core_s, self.core_r, self.right_s, self.right_r, self.left_s, self.left_r = sems

    def core(self, t):
        to = (self.dp, self.nc - 1 - self.c, self.z)
        src = self.part.at[(self.nc - 1 - self.c) * self.nz + t]
        return remote(src, self.came.at[t], self.core_s.at[t], self.core_r.at[t], to)

    def right(self, t):
        to = (self.dp, self.c, lax.rem(self.z + 1, self.nz))
        return remote(self.total.at[t], self.heard.at[t], self.right_s.at[t], self.right_r.at[t], to)

    def left(self, t, stops):
        slot = self.nz if stops else t
        to = (self.dp, self.c, lax.rem(self.z + self.nz - 1, self.nz))
        return remote(self.total.at[t], self.heard.at[slot], self.left_s.at[t], self.left_r.at[t], to)

    def add_core(self, t):
        self.core(t).wait_recv()

        def add(r, _):
            at = rows_of(r, 16)
            self.total[t, at, :] = (
                self.part[self.c * self.nz + t, at, :].astype(F32) + self.came[t, at, :].astype(F32)
            ).astype(BF16)
            return 0

        lax.fori_loop(0, SPAN // 16, add, 0)

    def add(self, t, slot):
        def add(r, _):
            at = rows_of(r, 16)
            self.total[t, at, :] = (
                self.total[t, at, :].astype(F32) + self.heard[slot, at, :].astype(F32)
            ).astype(BF16)
            return 0

        lax.fori_loop(0, SPAN // 16, add, 0)

    def begin(self):
        z, nz = self.z, self.nz
        pl.when(z == 0)(lambda: self.right(nz - 1).start())
        pl.when(z == nz - 1)(lambda: self.left(0, nz == 2).start())

    def slot(self, k):
        z, nz = self.z, self.nz
        for hop in range(1, k + 1):
            t = nz - 1 - (k - hop)
            if t > hop:

                @pl.when(z == hop)
                def _(t=t):
                    self.right(t).wait_recv()
                    self.add(t, t)
                    self.right(t).start()

                @pl.when(z == nz - 1 - hop)
                def _(u=nz - 1 - t, hop=hop):
                    self.left(u, False).wait_recv()
                    self.add(u, u)
                    self.left(u, u == nz - 2 - hop).start()

        @pl.when(z == 0)
        def _():
            self.right(nz - k).wait_send()
            self.right(nz - 1 - k).start()

        @pl.when(z == nz - 1)
        def _():
            self.left(k - 1, False).wait_send()
            self.left(k, k == nz - 2).start()

    def arrive(self):
        z, nz = self.z, self.nz
        for t in range(nz):
            pl.when((z == t) & (z > 0))(lambda t=t: self.right(t).wait_recv())
            pl.when((z == t) & (z < nz - 1))(lambda t=t: self.left(t, True).wait_recv())

    def own(self, rows):
        z, nz = self.z, self.nz
        value = self.total[z, rows, :].astype(F32)
        left = self.heard[z, rows, :].astype(F32)
        right = self.heard[nz, rows, :].astype(F32)
        value = value + jnp.where(z > 0, left, 0.0)
        return value + jnp.where(z < nz - 1, right, 0.0)

    def end_core(self):
        for t in range(self.nz):
            self.core(t).wait_send()

    def end(self):
        z, nz = self.z, self.nz
        for t in range(nz):
            right = (z < t) if t == 1 else (z < t) & (z > 0)
            left = (z > t) if t == nz - 2 else (z > t) & (z < nz - 1)
            pl.when(right)(lambda t=t: self.right(t).wait_send())
            pl.when(left)(lambda t=t: self.left(t, False).wait_send())


class Square:
    def __init__(self, place, block, size, sems):
        dp, c, z = place
        self.dp, self.dx, self.dy = dp, dp + 1 - 2 * lax.rem(dp, 2), lax.rem(dp + 2, 4)
        self.diag = lax.rem(self.dx + 2, 4)
        self.x, self.y = (self.dx, c, z), (self.dy, c, z)
        self.block = block
        self.half = size // 2
        self.sems = sems

    def copy(self, way, owner, piece, first, rows, to):
        block = self.block(owner, piece, first, rows)
        sends, recvs = self.sems
        return remote(block, block, sends.at[way, piece], recvs.at[way, piece], to)

    def whole(self, way, owner, piece):
        return self.copy(way, owner, piece, 0, 2 * self.half, self.x if way == 0 else self.y)

    def part(self, way, owner, piece):
        return self.copy(way, owner, piece, 0 if way == 2 else self.half, self.half, self.y if way == 2 else self.x)

    def begin(self, piece):
        self.whole(0, self.dp, piece).start()
        self.whole(1, self.dp, piece).start()

    def step(self, piece):
        self.whole(0, self.dx, piece).wait_recv()
        self.part(2, self.dx, piece).start()
        self.whole(1, self.dy, piece).wait_recv()
        self.part(3, self.dy, piece).start()

    def arrive(self, piece):
        self.part(2, self.diag, piece).wait_recv()
        self.part(3, self.diag, piece).wait_recv()

    def end(self, piece):
        self.whole(0, self.dp, piece).wait_send()
        self.whole(1, self.dp, piece).wait_send()
        self.part(2, self.dx, piece).wait_send()
        self.part(3, self.dy, piece).wait_send()


class SquareSum:
    def __init__(self, place, part, once, twice, gone, sems, pieces, index=lambda owner: owner, base=None):
        dp, c, z = place
        self.dp, self.dx, self.dy = dp, dp + 1 - 2 * lax.rem(dp, 2), lax.rem(dp + 2, 4)
        self.diag = lax.rem(self.dx + 2, 4)
        self.x, self.y = (self.dx, c, z), (self.dy, c, z)
        self.part, self.once, self.twice, self.gone = part, once, twice, gone
        self.s1, self.r1, self.s2, self.r2 = sems
        self.pieces, self.index, self.base = pieces, index, base
        self.rows = part.shape[1] // pieces
        cut = (part.shape[2] // TILE + 1) // 2 * TILE
        self.halves = (slice(0, cut), slice(cut, part.shape[2]))
        self.widths = (cut, part.shape[2] - cut)

    def heard(self, slot, start, size):
        width = self.widths[slot // 2]
        if self.base is None:
            return self.once.at[slot, pl.ds(start, size), :width]
        at = pl.multiple_of(self.base + slot * self.part.shape[1] + start, 16)
        return self.once.at[pl.ds(at, size), :width]

    def first(self, p, side, k):
        owner = ((self.dx, self.diag), (self.dy, self.diag))[side][k]
        at = pl.ds(p * self.rows, self.rows)
        slot = 2 * side + k
        return remote(
            self.part.at[self.index(owner), at, self.halves[side]], self.heard(slot, p * self.rows, self.rows),
            self.s1.at[p, slot], self.r1.at[p, slot], (self.x, self.y)[side],
        )

    def second(self, p, side):
        at = pl.ds(p * self.rows, self.rows)
        return remote(
            self.gone.at[at, self.halves[side]], self.twice.at[side, at, : self.widths[side]],
            self.s2.at[p, side], self.r2.at[p, side], (self.y, self.x)[side],
        )

    def begin_x(self, p):
        self.first(p, 0, 1).start()
        self.first(p, 0, 0).start()

    def begin_y(self, p):
        self.first(p, 1, 1).start()
        self.first(p, 1, 0).start()

    def each(self, p, body):
        def step(r, _):
            start = pl.multiple_of(p * self.rows + r * 16, 16)
            body(pl.ds(start, 16), start)
            return 0

        lax.fori_loop(0, self.rows // 16, step, 0)

    def pass_on(self, p):
        for side in range(2):
            self.first(p, side, 1).wait_recv()
            owner = (self.dy, self.dx)[side]

            def body(at, start, side=side, owner=owner):
                self.gone[at, self.halves[side]] = (
                    self.part[self.index(owner), at, self.halves[side]].astype(F32)
                    + self.heard(2 * side + 1, start, 16)[...].astype(F32)
                ).astype(BF16)

            self.each(p, body)
            self.second(p, side).start()

    def finish(self, p, out):
        for side in range(2):
            self.first(p, side, 0).wait_recv()
            self.second(p, side).wait_recv()

            def body(at, start, side=side):
                out[at, self.halves[side]] = (
                    self.part[self.index(self.dp), at, self.halves[side]].astype(F32)
                    + self.heard(2 * side, start, 16)[...].astype(F32)
                    + self.twice[side, at, : self.widths[side]].astype(F32)
                ).astype(out.dtype)

            self.each(p, body)

    def end(self):
        for p in range(self.pieces):
            for side in range(2):
                self.first(p, side, 0).wait_send()
                self.first(p, side, 1).wait_send()
                self.second(p, side).wait_send()


class HeadSplit:
    def __init__(self, nd, nc, nz):
        self.nd, self.nc, self.nz = nd, nc, nz
        self.nm = nc * nz
        self.span = self.nm * SPAN
        self.rows_in = MODEL // (nd * self.nm)
        self.wide = nd * TILE
        self.per = HEADS // (nd * self.nm)

    def fits(self):
        return (
            INNER == self.nd * self.nm * TILE and self.nd == 4 and self.nc == 2 and self.rows_in % 32 == 0
        )

    def place(self):
        return lax.axis_index("dp"), lax.axis_index("seq"), lax.axis_index("fsdp")

    def group_steps(self):
        return [(e, d) for d in range(self.nz) for e in range(self.nc) if e or d]

    def target(self, step):
        dp, c, z = self.place()
        ct, zt = lax.rem(c + step[0], self.nc), lax.rem(z + step[1], self.nz)
        return (dp, ct, zt), ct * self.nz + zt

    def source(self, step):
        dp, c, z = self.place()
        cs, zs = lax.rem(c + self.nc - step[0], self.nc), lax.rem(z + self.nz - step[1], self.nz)
        return cs * self.nz + zs

    def barrier(self):
        dp, c, z = self.place()
        sem = pltpu.get_barrier_semaphore()
        for step in self.group_steps():
            pl.semaphore_signal(sem, inc=1, device_id=self.target(step)[0], device_id_type=MESH)
        for k in range(1, self.nd):
            pl.semaphore_signal(
                sem, inc=1, device_id=(lax.rem(dp + k, self.nd), c, z), device_id_type=MESH
            )
        pl.semaphore_wait(sem, self.nm - 1 + self.nd - 1)

    def kernel(
        self, docs, lengths, level, x_ref, tap_ref, bias_ref, norm_ref, gain_ref, step_ref, rate_ref, skip_ref, in_ref, g_ref, wo_ref,
        y_out, dx_out, dw_out, dwc_out, dwo_out, par_out,
        xall, gall, wall, wcall, woall, wm_ref, wc_ref, head_ref, parbuf_, parall, every_par, projm, pre_sig, o, states,
        step_s, cum_s, dg, scaled, sel, hp, chp, state, dnext, heard_st, st, pre_bc, projc, taps,
        ypart, ycame, ytotal, yheard, xheard, dcom, sums, heads, gain_out,
        cpart, c1, c2, crows, cheard, w1, w2, o2, pard, parbuf,
        pd_s, pd_r, pg_s, pg_r, wz_s, wz_r, cz_s, cz_r, wq_s, wq_r, cq_s, cq_r, oq_s, oq_r, cc_s, cc_r,
        xr_s, xr_r, xl_s, xl_r, xc_s, xc_r, gr_s, gr_r, gl_s, gl_r, gc_s, gc_r,
        st_s, st_r, yc_s, yc_r, yr_s, yr_r, yl_s, yl_r,
        uc_s, uc_r, ur_s, ur_r, ul_s, ul_r, sc_s, sc_r, c1_s, c1_r, c2_s, c2_r, sz_s, sz_r,
        w1_s, w1_r, w2_s, w2_r, o1_s, o1_r, o2_s, o2_r, vz_s, vz_r, qd_s, qd_r, qg_s, qg_r, loc,
    ):
        nd, nc, nz, nm = self.nd, self.nc, self.nz, self.nm
        rows, wide = self.rows_in, self.wide
        where = dp, c, z = self.place()
        me = c * nz + z
        sizes = (nc, nz)
        steps = self.group_steps()
        other = (dp, nc - 1 - c, z)
        lines = [(k, (lax.rem(dp + k, nd), c, z), lax.rem(dp + nd - k, nd)) for k in range(1, nd)]
        started = []

        def go(copy):
            copy.start()
            started.append(copy)
            return copy

        def w_block(owner, m, first=0, count=rows):
            at = pl.multiple_of(m * rows + first, rows // 2)
            return wall.at[owner, pl.ds(at, count), :]

        def c_block(owner, m, first=0, count=rows):
            at = pl.multiple_of((owner * nm + m) * rows + first, rows // 2)
            return wcall.at[pl.ds(at, count), :]

        w_from = [me] + [self.source(step) for step in steps]
        c_from = [c * nz + lax.rem(z + nz - d, nz) for d in range(nz)]
        w_square = Square(
            where, lambda owner, j, first, count: w_block(owner, w_from[j], first, count), rows, (wq_s, wq_r)
        )
        c_square = Square(
            where, lambda owner, j, first, count: c_block(owner, c_from[j], first, count), rows, (cq_s, cq_r)
        )
        o_square = Square(
            where,
            lambda owner, j, first, count: woall.at[owner, pl.ds(first, count), :],
            TILE,
            (oq_s, oq_r),
        )
        x_line = Line(where, sizes, lambda a, b: xall.at[rows_of(a * nz + b), :], (xr_s, xr_r, xl_s, xl_r, xc_s, xc_r))
        g_line = Line(where, sizes, lambda a, b: gall.at[rows_of(a * nz + b), :], (gr_s, gr_r, gl_s, gl_r, gc_s, gc_r))
        y_sum = Sum(where, sizes, ypart, ycame, ytotal, yheard, (yc_s, yc_r, yr_s, yr_r, yl_s, yl_r))

        starts = [jnp.int32(0)]
        for doc in range(1, docs):
            starts.append(starts[-1] + lengths[0, doc - 1])
        active = jnp.right_shift(HEADS, 3 - level[0])
        unit = jnp.float32(1.0 / INNER)
        for smaller in range(3):
            unit = jnp.where(level[0] == smaller, jnp.float32(2.0 ** (3 - smaller) / INNER), unit)
        own_conv = CONV // (nd * nm)
        parbuf_[dp, 0:KW, :own_conv] = tap_ref[...]
        parbuf_[dp, KW : KW + 1, :own_conv] = bias_ref[...]
        parbuf_[dp, 5:6, :rows] = norm_ref[...]
        parbuf_[dp, 6:7, :TILE] = gain_ref[...]
        head_ref[...] = jnp.zeros_like(head_ref)
        head_ref[0:1, :HEADS] = step_ref[...]
        head_ref[1:2, :HEADS] = -jnp.exp(rate_ref[...])
        head_ref[2:3, :HEADS] = skip_ref[...]
        head_ref[3:4, :] = (iota((1, TILE), 1) < active).astype(F32)
        for m in range(nm):
            for i in range(2 * nd):
                wm_ref[m * rows : (m + 1) * rows, tile_of(i)] = in_ref[:, tile_of(i * nm + m)]
        shared = EXTENT - 2 * INNER
        wc_ref[:, 2 * TILE :] = jnp.zeros((rows, COMMON - 2 * TILE), BF16)
        wc_ref[:, : 2 * TILE] = in_ref[:, 2 * INNER : 2 * INNER + 2 * TILE]
        wc_ref[:, 2 * TILE : shared] = in_ref[:, 2 * INNER + 2 * TILE :]
        own = [
            pltpu.make_async_copy(wm_ref.at[rows_of(me, rows), :], w_block(dp, me), loc.at[0]),
            pltpu.make_async_copy(wc_ref, c_block(dp, me), loc.at[1]),
            pltpu.make_async_copy(wo_ref, woall.at[dp], loc.at[2]),
            pltpu.make_async_copy(g_ref, gall.at[rows_of(me), :], loc.at[3]),
        ]
        for copy in own:
            copy.start()
        self.barrier()
        for k, device, _ in lines:
            go(remote(parbuf_.at[dp], parbuf_.at[dp], pd_s.at[k], pd_r.at[k], device))
        for j, step in enumerate(steps):
            device, there = self.target(step)
            go(remote(wm_ref.at[rows_of(there, rows), :], w_block(dp, me), wz_s.at[j], wz_r.at[j], device))
            if step[0] == 0:
                go(remote(wc_ref, c_block(dp, me), cz_s.at[step[1]], cz_r.at[step[1]], device))
        for copy in own[:3]:
            copy.wait()
        o_square.begin(0)
        w_square.begin(0)
        c_square.begin(0)
        for k, device, frm in lines:
            remote(parbuf_.at[frm], parbuf_.at[frm], pd_s.at[k], pd_r.at[k], device).wait_recv()
        parall[me] = parbuf_[...]
        for j, step in enumerate(steps):
            device, _ = self.target(step)
            go(remote(parbuf_, parall.at[me], pg_s.at[j], pg_r.at[j], device))
        for j, step in enumerate(steps):
            device, _ = self.target(step)
            remote(parbuf_, parall.at[self.source(step)], pg_s.at[j], pg_r.at[j], device).wait_recv()
        owners = [(first // nm, first % nm) for first in range(nd * nm)]
        gain = jnp.concatenate([parall[m, d][5:6, :rows] for d, m in owners], axis=1)
        gain_out[...] = jnp.broadcast_to(gain, (8, MODEL))
        hidden = x_ref[...].astype(F32)
        inverse = lax.rsqrt(jnp.mean(hidden * hidden, axis=1, keepdims=True) + EPSILON)
        xall[rows_of(me), :] = (hidden * inverse * gain).astype(BF16)
        x_line.begin()

        for j, step in enumerate(steps):
            device, _ = self.target(step)
            block = w_block(dp, w_from[j + 1])
            remote(block, block, wz_s.at[j], wz_r.at[j], device).wait_recv()
            w_square.begin(j + 1)
            if step[0] == 0:
                d = step[1]
                block = c_block(dp, c_from[d])
                remote(block, block, cz_s.at[d], cz_r.at[d], device).wait_recv()
                c_square.begin(d)
            if j == 2:
                o_square.step(0)
                w_square.step(0)
                c_square.step(0)
        every_par[...] = jnp.concatenate([parall[m, d][:, :own_conv] for d, m in owners], axis=1)
        for i in range(nd):
            at = pl.ds(pl.multiple_of((i * nm + me) * TILE, TILE), TILE)
            taps[:, tile_of(i)] = every_par[:, at]
        taps[:, wide:] = every_par[:, INNER : INNER + 2 * TILE]
        head, lane = iota((TILE, TILE), 0), iota((TILE, TILE), 1)
        step_of = nm * self.per
        chosen = (head == lax.div(lane, self.per) * step_of + self.per * me + lax.rem(lane, self.per)) & (
            lane < nd * self.per
        )
        sel[...] = chosen.astype(BF16)
        hp[...] = exact(head_ref[...], chosen.astype(F32))
        for i in range(nd):
            chosen = head == i * step_of + self.per * me + lax.div(lane, HEAD_DIM)
            spread = exact(head_ref[...], chosen.astype(F32))
            chp[0:2, tile_of(i)] = spread[2:4, :]
            chp[2:3, tile_of(i)] = parbuf_[i][6:7, :TILE]
        x_line.step(1)
        for j in range(1, 4):
            w_square.step(j)
        for j in range(1, nz):
            c_square.step(j)
        x_line.step(2)
        for j in range(4, nm):
            w_square.step(j)
        x_line.step(3)
        own[3].wait()
        g_line.begin()
        for j in range(nz):
            c_square.arrive(j)
        for i in range(nd):
            at = pl.ds(pl.multiple_of((i * nm + c * nz) * rows, rows), nz * rows)
            go(remote(wcall.at[at, :], wcall.at[at, :], cc_s.at[i], cc_r.at[i], other))
        x_line.arrive()
        for j in range(nm):
            w_square.arrive(j)
        for i in range(nd):
            at = pl.ds(pl.multiple_of((i * nm + (nc - 1 - c) * nz) * rows, rows), nz * rows)
            remote(wcall.at[at, :], wcall.at[at, :], cc_s.at[i], cc_r.at[i], other).wait_recv()
        projm[0:PAD, :] = jnp.zeros((PAD, 2 * wide), BF16)
        projc[0:PAD, :] = jnp.zeros((PAD, COMMON), BF16)
        projc[PAD:, :] = dot(xall[...], wcall[...]).astype(BF16)

        def project(n, _):
            at = rows_of(n, 256)
            projm[PAD:, at] = dot(xall[...], wall[:, :, at].reshape(MODEL, 256)).astype(BF16)
            pl.when(n == 2)(lambda: g_line.step(1))
            return 0

        lax.fori_loop(0, 2 * wide // 256, project, 0)
        state[...] = jnp.zeros_like(state)

        def forward(i, _):
            self.forward_chunk(
                i, docs, starts, projm, projc, taps, sel, hp, chp,
                pre_sig, pre_bc, o, states, step_s, cum_s, scaled, st, state,
            )
            pl.when(i == 2)(lambda: g_line.step(2))
            pl.when(i == 6)(lambda: g_line.step(3))
            return 0

        lax.fori_loop(0, nm, forward, 0)

        o_square.arrive(0)

        def branch(pair):
            def some(n, _):
                t = pair + lax.rem(n, 2) * (nz - 1 - 2 * pair)
                turn = t + lax.rem(nc - 1 - c + lax.div(n, 2), nc) * nz
                ypart[turn] = dot(scaled[rows_of(turn), :], woall[...].reshape(wide, MODEL)).astype(BF16)
                pl.when(n < 2)(lambda: y_sum.core(t).start())
                return 0

            lax.fori_loop(0, 4, some, 0)

        branch(0)
        y_sum.add_core(0)
        y_sum.add_core(nz - 1)
        y_sum.begin()
        for pair in range(1, nz // 2):
            branch(pair)
            y_sum.add_core(pair)
            y_sum.add_core(nz - 1 - pair)

        g_line.arrive()
        lanes_at = iota((SPAN, TILE), 1)

        def gate_grad(n, _):
            at = rows_of(n, 256)
            grad = dot(gall[at, :], woall[...].reshape(wide, MODEL), ((1,), (1,)))
            dg[at, :] = grad
            for half in range(2):
                product = jnp.zeros((SPAN, TILE), F32)
                for i in range(nd):
                    mine = scaled[pl.ds(pl.multiple_of(n * 256 + half * SPAN, SPAN), SPAN), tile_of(i)]
                    product = product + mine.astype(F32) * grad[half * SPAN : (half + 1) * SPAN, tile_of(i)]
                st[1, pl.ds(2 * n + half, 1), :] = lane_sum(product).T[0:1, :]
            return 0

        lax.fori_loop(0, nm // 2, gate_grad, 0)
        sent = []
        for j, step in enumerate(steps):
            device, _ = self.target(step)
            sent.append(go(remote(st, heard_st.at[j], st_s.at[j], st_r.at[j], device)))

        totals = st[...]
        for j, copy in enumerate(sent):
            copy.wait_recv()
            totals = totals + heard_st[j]
        for copy in sent:
            copy.wait_send()
        st[...] = totals

        dnext[...] = jnp.zeros_like(dnext)
        state[...] = jnp.zeros_like(state)
        sums[...] = jnp.zeros_like(sums)
        heads[...] = jnp.zeros_like(heads)

        def backward(n, _):
            self.backward_chunk(
                nm - 1 - n, docs, starts, unit, projm, pre_sig, pre_bc, o, states, step_s, cum_s, dg, st, taps, sel,
                hp, chp, dcom, scaled, sums, heads, state, dnext, projc,
            )
            for k in range(1, nz - 1):
                pl.when(n == SLOTS[k - 1])(lambda k=k: y_sum.slot(k))
            return 0

        lax.fori_loop(0, nm, backward, 0)
        for copy in started:
            if not any(copy is s for s in sent):
                copy.wait_send()
        started.clear()
        for j in range(nm):
            w_square.end(j)
        for j in range(nz):
            c_square.end(j)
        o_square.end(0)
        x_line.end()
        g_line.end()

        x_sum = Sum(where, sizes, ypart, ycame, ytotal, xheard, (uc_s, uc_r, ur_s, ur_r, ul_s, ul_r))
        w_sum = SquareSum(where, wall, w1, w2, projm, (w1_s, w1_r, w2_s, w2_r), 2)
        o_sum = SquareSum(where, woall, xall, o2, xall, (o1_s, o1_r, o2_s, o2_r), 1, base=4 * TILE)
        c_sum = SquareSum(where, cpart, c1, c2, dcom, (c1_s, c1_r, c2_s, c2_r), 1, lambda owner: owner * nc + c)
        def input_grad(core):
            base = rows_of(core, nz * SPAN)
            lead = pl.ds(pl.multiple_of(core * nz * SPAN + PAD, PAD), nz * SPAN)

            def piece(n, _):
                at = rows_of(n, 256)
                part = dot(projm[lead, :], wall[lax.div(n, 2), rows_of(lax.rem(n, 2), 256), :], ((1,), (1,)))
                part = (part + dot(dcom[base, :], wcall[at, :], ((1,), (1,)))).astype(BF16)
                for t in range(nz):
                    ypart[core * nz + t, :, at] = part[t * SPAN : (t + 1) * SPAN, :]
                return 0

            lax.fori_loop(0, MODEL // 256, piece, 0)

        y_sum.end_core()
        input_grad(nc - 1 - c)
        for t in range(nz):
            x_sum.core(t).start()
        input_grad(c)
        y_sum.arrive()
        stat = jnp.broadcast_to(st[0, pl.ds(me, 1), :], (SPAN, TILE)).T
        root = lax.rsqrt(stat[:, 0:1] * unit + EPSILON)
        y_out[...] = (x_ref[...].astype(F32) + root * y_sum.own(slice(None))).astype(BF16)
        y_sum.end()
        x_sum.add_core(0)
        x_sum.add_core(nz - 1)
        x_sum.begin()
        for t in range(1, nz - 1):
            x_sum.add_core(t)

        def weight_grad(owner):
            def piece(n, _):
                at = pl.ds(pl.multiple_of(owner * (nm * rows) + n * 256, 256), 256)
                wall[owner, rows_of(n, 256), :] = dot(xall[:, at], projm[PAD:, :], ((0,), (0,))).astype(BF16)
                return 0

            lax.fori_loop(0, nm * rows // 256, piece, 0)

        weight_grad(w_sum.diag)
        weight_grad(w_sum.dx)
        w_sum.begin_x(0)
        weight_grad(w_sum.dy)
        w_sum.begin_y(0)
        weight_grad(dp)

        def shared_grad(n, _):
            at = rows_of(n, 256)
            cpart[n] = dot(xall[:, at], dcom[...], ((0,), (0,))).astype(BF16)
            return 0

        lax.fori_loop(0, nd * nc, shared_grad, 0)
        ccopies = [
            go(remote(cpart.at[i * nc + nc - 1 - c], projc.at[rows_of(i, nz * rows), :], sc_s.at[i], sc_r.at[i], other)) for i in range(nd)
        ]
        x_sum.slot(1)

        def out_grad(n, _):
            at = rows_of(n, 512)
            part = dot(scaled[...], gall[:, at], ((0,), (0,))).astype(BF16)
            for i in range(nd):
                woall[i, :, at] = part[tile_of(i), :]
            return 0

        lax.fori_loop(0, MODEL // 512, out_grad, 0)
        w_sum.pass_on(0)
        w_sum.begin_x(1)
        w_sum.begin_y(1)
        for i in range(nd):
            ccopies[i].wait_recv()
            cpart[i * nc + c] = (cpart[i * nc + c].astype(F32) + projc[rows_of(i, nz * rows), :].astype(F32)).astype(BF16)
        x_sum.slot(2)

        def send_rows(p):
            half = nm // 2
            for j in range(half):
                there = p * half + j
                block = wm_ref.at[there * rows : (there + 1) * rows, :]
                ct, zt = there // nz, there % nz

                @pl.when(there != me)
                def _():
                    remote(block, dw_out.at[me], vz_s.at[there], vz_r.at[me], (dp, ct, zt)).start()

                @pl.when(there == me)
                def _():
                    dw_out[there] = block[...]

        w_sum.finish(0, wm_ref)
        send_rows(0)
        w_sum.pass_on(1)
        c_sum.begin_x(0)
        c_sum.begin_y(0)
        o_sum.begin_x(0)
        o_sum.begin_y(0)

        x_sum.arrive()
        hidden = x_ref[...].astype(F32)
        normed_grad = x_sum.own(slice(None))
        inverse = lax.rsqrt(jnp.mean(hidden * hidden, axis=1, keepdims=True) + EPSILON)
        unitary = hidden * inverse
        gain_grad = jnp.sum(normed_grad * unitary, axis=0, keepdims=True)
        grad_scaled = normed_grad * gain_out[0:1, :]
        middle = jnp.mean(grad_scaled * unitary, axis=1, keepdims=True)
        dx_out[...] = (gall[rows_of(me), :].astype(F32) + inverse * (grad_scaled - unitary * middle)).astype(BF16)
        base_row = MODEL // TILE
        for i in range(base_row):
            parbuf[i : i + 1, :] = gain_grad[:, tile_of(i)]
        count = nd + 2
        for r in range(8):
            for i in range(count):
                at = base_row + r * count + i
                parbuf[at : at + 1, :] = sums[r : r + 1, tile_of(i)]
        parbuf[base_row + 8 * count :, :] = heads[...]
        small = [
            go(remote(parbuf, pard.at[k - 1], qd_s.at[k], qd_r.at[k], device)) for k, device, _ in lines
        ]
        w_sum.finish(1, wm_ref)
        send_rows(1)
        c_sum.pass_on(0)
        o_sum.pass_on(0)
        c_sum.finish(0, crows)
        for d in range(1, nz):
            to = lax.rem(z + d, nz)
            go(remote(crows.at[rows_of(to, rows), :], cheard.at[d - 1], sz_s.at[d], sz_r.at[d], (dp, c, to)))
        for copy in small:
            copy.wait_recv()
        total = parbuf[...]
        for k in range(nd - 1):
            total = total + pard[k]
        par_out[me] = total
        for j, step in enumerate(steps):
            go(remote(par_out.at[me], par_out.at[me], qg_s.at[j], qg_r.at[j], self.target(step)[0]))
        o_sum.finish(0, dwo_out)
        total = crows[rows_of(z, rows), :].astype(F32)
        for d in range(1, nz):
            remote(cheard.at[d - 1], cheard.at[d - 1], sz_s.at[d], sz_r.at[d], other).wait_recv()
            total = total + cheard[d - 1].astype(F32)
        dwc_out[...] = total
        for j, step in enumerate(steps):
            here = par_out.at[self.source(step)]
            remote(here, here, qg_s.at[j], qg_r.at[j], other).wait_recv()
        for m in range(nm):
            got = dw_out.at[m]

            @pl.when(m != me)
            def _():
                remote(got, got, vz_s.at[m], vz_r.at[m], other).wait_recv()
                remote(got, got, vz_s.at[m], vz_r.at[m], other).wait_send()

        for copy in started:
            copy.wait_send()
        x_sum.end_core()
        x_sum.end()
        w_sum.end()
        o_sum.end()
        c_sum.end()

    def forward_chunk(
        self, chunk, docs, starts, projm, projc, taps, sel, hp, chp,
        pre_sig, pre_bc, o, states, step_s, cum_s, scaled, st, state,
    ):
        nd, wide = self.nd, self.wide
        first = chunk * SPAN
        here = rows_of(chunk)
        lead = pl.ds(pl.multiple_of(chunk * SPAN, SPAN), SPAN + PAD)
        body = pl.ds(pl.multiple_of(chunk * SPAN + PAD, PAD), SPAN)
        lane = iota((SPAN, TILE), 1)
        row = iota((SPAN, TILE), 0)
        low = lane < HEAD_DIM
        begin_t = begin_at(first + row, starts, docs)
        begin_s = begin_at(first + lane, starts, docs)
        valid = [first + row - (KW - 1 - tap) >= begin_t for tap in range(KW)]
        sides = []
        for i in range(2):
            lanes = tile_of(i)
            value = conv_tile(projc[lead, lanes].astype(F32), taps, tile_of(nd + i), valid)
            pre_bc[here, lanes] = value
            sides.append((value * jax.nn.sigmoid(value)).astype(BF16))
        key_side, query_side = sides
        rate = dot(projc[body, 2 * TILE :], sel[...])
        step = softplus(rate + hp[0:1, :])
        log_decay = step * hp[1:2, :]
        cum = exact((lane <= row).astype(F32), log_decay)
        step_s[here, :] = step
        cum_s[here, :] = cum
        cum_t = cum.T
        shut = jnp.where((begin_t == begin_s) & (lane <= row), 0.0, NEG)
        inherits = (begin_t < first).astype(F32)
        begin_last = begin_at(jnp.full((SPAN, TILE), first + SPAN - 1, jnp.int32), starts, docs)
        last_same = (begin_t == begin_last).astype(F32)
        meet = dot(query_side, key_side, ((1,), (1,)))
        before = state[...]
        before_low = before.astype(BF16)
        states[chunk] = before_low
        carried_out = dot(query_side, before_low)
        squares = jnp.zeros((SPAN, TILE), F32)
        for i in range(nd):
            lanes = tile_of(i)
            pre = conv_tile(projm[lead, tile_of(nd + i)].astype(F32), taps, lanes, valid)
            pre_sig[here, lanes] = pre
            signal = pre * jax.nn.sigmoid(pre)
            cums = [head_col(cum, 2 * i), head_col(cum, 2 * i + 1)]
            stepx = jnp.where(low, head_col(step, 2 * i), head_col(step, 2 * i + 1))
            cumx = jnp.where(low, cums[0], cums[1])
            fed = stepx * signal
            fed_low = fed.astype(BF16)
            local = []
            for e in range(2):
                head = 2 * i + e
                kernel = jnp.exp(cums[e] - cum_t[head : head + 1, :] + shut)
                local.append(dot((kernel * meet).astype(BF16), fed_low))
            entry = jnp.exp(cumx) * inherits
            out = jnp.where(low, local[0], local[1]) + entry * carried_out[:, lanes]
            o[here, lanes] = out
            last = cumx[SPAN - 1 : SPAN, :]
            tail = jnp.exp((last - cumx) * last_same) * last_same
            state[:, lanes] = entry[SPAN - 1 : SPAN, :] * before[:, lanes] + dot(
                key_side, (tail * fed).astype(BF16), ((0,), (0,))
            )
            mixed = (out + chp[0:1, lanes] * signal) * chp[1:2, lanes]
            gate_in = projm[body, lanes].astype(F32)
            gated = mixed * (gate_in * jax.nn.sigmoid(gate_in))
            squares = squares + gated * gated
            scaled[here, lanes] = (gated * chp[2:3, lanes]).astype(BF16)
        st[0, pl.ds(chunk, 1), :] = lane_sum(squares).T[0:1, :]

    def backward_chunk(
        self, chunk, docs, starts, unit, projm, pre_sig, pre_bc, o, states, step_s, cum_s, dg, st, taps, sel,
        hp, chp, dcom, normed_out, sums, heads, dstate, dnext, projc,
    ):
        nd = self.nd
        first = chunk * SPAN
        here = rows_of(chunk)
        lead = pl.ds(pl.multiple_of(chunk * SPAN, SPAN), SPAN + PAD)
        body = pl.ds(pl.multiple_of(chunk * SPAN + PAD, PAD), SPAN)
        lane = iota((SPAN, TILE), 1)
        row = iota((SPAN, TILE), 0)
        low = lane < HEAD_DIM
        begin_t = begin_at(first + row, starts, docs)
        begin_s = begin_at(first + lane, starts, docs)
        shut = jnp.where((begin_t == begin_s) & (lane <= row), 0.0, NEG)
        inherits = (begin_t < first).astype(F32)
        begin_last = begin_at(jnp.full((SPAN, TILE), first + SPAN - 1, jnp.int32), starts, docs)
        last_same = (begin_t == begin_last).astype(F32)
        lower = (lane <= row).astype(F32)
        key_pre, query_pre = pre_bc[here, :TILE], pre_bc[here, TILE:]
        key_side = (key_pre * jax.nn.sigmoid(key_pre)).astype(BF16)
        query_side = (query_pre * jax.nn.sigmoid(query_pre)).astype(BF16)
        meet = dot(query_side, key_side, ((1,), (1,)))
        step, cum = step_s[here, :], cum_s[here, :]
        cum_t = cum.T
        square = jnp.broadcast_to(st[0, pl.ds(chunk, 1), :], (SPAN, TILE)).T
        cross = jnp.broadcast_to(st[1, pl.ds(chunk, 1), :], (SPAN, TILE)).T
        root = lax.rsqrt(square * unit + EPSILON)
        pull = root * root * root * cross * unit
        before_low = states[chunk]
        before = before_low.astype(F32)
        after = dstate[...]
        after_low = after.astype(BF16)
        carried_out = dot(query_side, before_low)
        from_state = dot(key_side, after_low)
        meet_grad = jnp.zeros((SPAN, SPAN), F32)
        cum_cols = jnp.zeros((SPAN, TILE), F32)
        cum_rows = jnp.zeros((8, SPAN), F32)
        step_cols = jnp.zeros((SPAN, TILE), F32)
        entered, tails = [], []
        head_rows = iota((8, SPAN), 0)
        next_rows = first + iota((SPAN + PAD, TILE), 0)
        next_begin = begin_at(next_rows, starts, docs)
        valid = [next_rows - (KW - 1 - tap) >= next_begin for tap in range(KW)]
        tail_row = row == SPAN - 1

        def conv_back(pre_grad, ext, lanes):
            sums[2:3, lanes] += jnp.sum(pre_grad, axis=0, keepdims=True)
            later = jnp.concatenate([pre_grad, dnext[:, lanes]], axis=0)
            dnext[:, lanes] = pre_grad[0:PAD, :]
            back_grad = jnp.zeros((SPAN, TILE), F32)
            for tap in range(KW):
                back = KW - 1 - tap
                masked = jnp.where(valid[tap], later, 0.0)
                moved = ext if back == 0 else pltpu.roll(ext, back, 0)
                sums[4 + tap : 5 + tap, lanes] += jnp.sum(masked[:SPAN] * moved[PAD:], axis=0, keepdims=True)
                ahead = masked if back == 0 else pltpu.roll(masked, SPAN + PAD - back, 0)
                back_grad = back_grad + ahead[:SPAN] * taps[tap : tap + 1, lanes]
            return back_grad

        for i in range(nd):
            lanes = tile_of(i)
            pre = pre_sig[here, lanes]
            gate_of = jax.nn.sigmoid(pre)
            signal = pre * gate_of
            gate_in = projm[body, lanes].astype(F32)
            gate_sig = jax.nn.sigmoid(gate_in)
            opened = gate_in * gate_sig
            mask = chp[1:2, lanes]
            mixed = (o[here, lanes] + chp[0:1, lanes] * signal) * mask
            gated = mixed * opened
            grad = dg[here, lanes]
            gain = chp[2:3, lanes]
            normed_out[here, lanes] = (gated * root * gain).astype(BF16)
            sums[0:1, lanes] += jnp.sum(grad * gated * root, axis=0, keepdims=True)
            gated_grad = root * grad * gain - gated * pull
            mixed_grad = gated_grad * opened * mask
            projm[body, lanes] = (
                gated_grad * mixed * (gate_sig * (1.0 + gate_in * (1.0 - gate_sig)))
            ).astype(BF16)
            sums[1:2, lanes] += jnp.sum(mixed_grad * signal, axis=0, keepdims=True)
            cums = [head_col(cum, 2 * i), head_col(cum, 2 * i + 1)]
            stepx = jnp.where(low, head_col(step, 2 * i), head_col(step, 2 * i + 1))
            cumx = jnp.where(low, cums[0], cums[1])
            fed = stepx * signal
            fed_low = fed.astype(BF16)
            out_grad = mixed_grad
            out_low = out_grad.astype(BF16)
            entry = jnp.exp(cumx) * inherits
            last = cumx[SPAN - 1 : SPAN, :]
            tail = jnp.exp((last - cumx) * last_same) * last_same
            backs = []
            for e in range(2):
                head = 2 * i + e
                kernel = jnp.exp(cums[e] - cum_t[head : head + 1, :] + shut)
                mix = kernel * meet
                half = low if e == 0 else jnp.logical_not(low)
                mix_grad = dot(jnp.where(half, out_grad, 0.0).astype(BF16), fed_low, ((1,), (1,)))
                meet_grad = meet_grad + kernel * mix_grad
                weight = mix * mix_grad
                cum_cols = cum_cols + jnp.where(lane == head, lane_sum(weight), 0.0)
                cum_rows = cum_rows + jnp.where(
                    head_rows == head, jnp.broadcast_to(jnp.sum(weight, axis=0, keepdims=True), (8, SPAN)), 0.0
                )
                backs.append(dot(mix.astype(BF16), out_low, ((0,), (0,))))
            entry_grad = entry * out_grad
            tail_fed = tail * fed
            entered.append(entry_grad.astype(BF16))
            tails.append(tail_fed.astype(BF16))
            fed_grad = jnp.where(low, backs[0], backs[1]) + tail * from_state[:, lanes]
            moved_in = entry_grad * carried_out[:, lanes]
            moved_out = tail_fed * from_state[:, lanes]
            direct = fed_grad * signal
            end = entry[SPAN - 1 : SPAN, :]
            kept = jnp.sum(after[:, lanes] * before[:, lanes], axis=0, keepdims=True) * end
            at_end = jnp.sum(moved_out, axis=0, keepdims=True) + kept
            local = moved_in - moved_out + jnp.where(tail_row, at_end, 0.0)
            for e in range(2):
                half = low if e == 0 else jnp.logical_not(low)
                place = lane == 2 * i + e
                cum_cols = cum_cols + jnp.where(place, lane_sum(jnp.where(half, local, 0.0)), 0.0)
                step_cols = step_cols + jnp.where(place, lane_sum(jnp.where(half, direct, 0.0)), 0.0)
            dstate[:, lanes] = end * after[:, lanes] + dot(query_side, entry_grad.astype(BF16), ((0,), (0,)))
            signal_grad = stepx * fed_grad + chp[0:1, lanes] * mixed_grad
            pre_grad = signal_grad * (gate_of * (1.0 + pre * (1.0 - gate_of)))
            cols = tile_of(nd + i)
            projm[body, cols] = conv_back(pre_grad, projm[lead, cols].astype(F32), lanes).astype(BF16)
        meet_low = meet_grad.astype(BF16)
        state_rows = ((1,), (1,))
        query_grad = dot(meet_low, key_side) + dot(jnp.concatenate(entered, axis=1), before_low, state_rows)
        key_grad = dot(meet_low, query_side, ((0,), (0,))) + dot(
            jnp.concatenate(tails, axis=1), after_low, state_rows
        )
        for i, (side_grad, side_pre) in enumerate(((key_grad, key_pre), (query_grad, query_pre))):
            back_grad = conv_back(side_grad * silu_slope(side_pre), projc[lead, tile_of(i)].astype(F32), tile_of(nd + i))
            dcom[here, tile_of(i)] = back_grad.astype(BF16)
        rows_t = jnp.concatenate([cum_rows, jnp.zeros((SPAN - 8, SPAN), F32)], axis=0).T
        decay_grad = exact(lower, cum_cols - rows_t, ((0,), (0,)))
        log_decay = step * hp[1:2, :]
        slope = 1.0 - jnp.exp(-step)
        rate_grad = (step_cols + decay_grad * hp[1:2, :]) * slope
        heads[0:1, :] += jnp.sum(rate_grad, axis=0, keepdims=True)
        heads[1:2, :] += jnp.sum(decay_grad * log_decay, axis=0, keepdims=True)
        dcom[here, 2 * TILE :] = dot(rate_grad.astype(BF16), sel[...], ((1,), (1,))).astype(BF16)

    def run(self, docs, *args):
        nd, nc, nz, nm, rows, span, wide = self.nd, self.nc, self.nz, self.nm, self.rows_in, self.span, self.wide
        like = jax.ShapeDtypeStruct
        block = (SPAN, MODEL)
        npar = MODEL // TILE + 8 * (nd + 2) + 8

        def low(*shape):
            return pltpu.VMEM(shape, BF16)

        def full(*shape):
            return pltpu.VMEM(shape, F32)

        pair = lambda *shape: [DMA(shape), DMA(shape)]
        return pl.pallas_call(
            functools.partial(self.kernel, docs),
            out_shape=[
                like(block, BF16),
                like(block, BF16),
                like((nm, rows, 2 * wide), BF16),
                like((rows, COMMON), F32),
                like((TILE, MODEL), BF16),
                like((nm, npar, TILE), F32),
            ],
            in_specs=[SM, SM] + [VM] * 9 + [ANY, ANY],
            out_specs=[VM] * 6,
            scratch_shapes=[
                low(span, MODEL), low(span, MODEL), low(nd, nm * rows, 2 * wide), low(MODEL, COMMON),
                low(nd, TILE, MODEL), low(nm * rows, 2 * wide), low(rows, COMMON), full(8, TILE),
                full(nd, 8, 2 * TILE), full(nm, nd, 8, 2 * TILE), full(8, CONV), low(PAD + span, 2 * wide),
                full(span, wide), full(span, wide), low(nm, STATE, wide),
                full(span, TILE), full(span, TILE), full(span, wide), low(span, wide), low(TILE, TILE),
                full(8, TILE), full(8, wide), full(STATE, wide), full(PAD, wide + 2 * TILE),
                full(nm - 1, 2, nm, TILE), full(2, nm, TILE), full(span, 2 * TILE), low(PAD + span, COMMON),
                full(8, wide + 2 * TILE),
                low(nm, *block), low(nz, *block), low(nz, *block), low(nz + 1, *block), low(nz + 1, *block),
                low(span, COMMON), full(8, wide + 2 * TILE), full(8, TILE), full(8, MODEL),
                low(nd * nc, nz * rows, COMMON), low(4, nz * rows, 2 * TILE),
                low(2, nz * rows, 2 * TILE), low(nz * rows, COMMON), low(nz - 1, rows, COMMON),
                low(4, nm * rows, wide), low(2, nm * rows, wide),
                low(2, TILE, MODEL // 2),
                full(nd - 1, npar, TILE), full(npar, TILE),
                *pair(nd), *pair(nm), *pair(nm), *pair(nz), *pair(4, nm), *pair(4, nz), *pair(4, 1), *pair(nd),
                *pair(nz), *pair(nz), *pair(nz), *pair(nz), *pair(nz), *pair(nz),
                *pair(nm), *pair(nz), *pair(nz), *pair(nz),
                *pair(nz), *pair(nz), *pair(nz), *pair(nd), *pair(1, 4), *pair(1, 2), *pair(nz),
                *pair(2, 4), *pair(2, 2), *pair(1, 4), *pair(1, 2), *pair(nm), *pair(nd), *pair(nm), DMA((4,)),
            ],
            compiler_params=pltpu.CompilerParams(
                collective_id=0, has_side_effects=True, vmem_limit_bytes=63 * 2**20
            ),
            name="first",
        )(*args)

    def local(
        self, layer_input, out_grad, norm_gain, in_weight, conv_weight, conv_bias, step_bias, log_rate,
        skip_gain, gate_gain, out_weight, nest_level, doc_lengths,
    ):
        nd, nz, nm, rows, wide = self.nd, self.nz, self.nm, self.rows_in, self.wide
        dp, c, z = self.place()
        me = c * nz + z
        docs = doc_lengths.shape[1]
        x = layer_input.reshape(SPAN, MODEL)
        g = out_grad.reshape(SPAN, MODEL)
        own_conv = conv_bias.shape[0]
        y_out, dx_out, dw, dwc, dwo, pars = self.run(
            docs, doc_lengths, nest_level, x, conv_weight.T, conv_bias[None], norm_gain[None], gate_gain[None],
            step_bias[None], log_rate[None], skip_gain[None], in_weight, g, out_weight,
        )
        dw = jnp.transpose(dw.reshape(nm, rows, 2 * nd, TILE), (1, 2, 0, 3)).reshape(rows, 2 * INNER)
        in_weight_grad = jnp.concatenate([dw.astype(F32), dwc[:, : EXTENT - 2 * INNER]], axis=1)
        owner = dp * nm + me
        gains = jnp.sum(pars[:, : MODEL // TILE], axis=0).reshape(MODEL)
        norm_gain_grad = lax.dynamic_slice_in_dim(gains, owner * rows, rows)
        base = MODEL // TILE
        per_row = pars[:, base : base + 8 * (nd + 2)].reshape(nm, 8, nd + 2, TILE)
        mains = per_row[:, :, :nd]
        shared = jnp.sum(per_row[:, :, nd:], axis=0).reshape(8, 2 * TILE)
        head_sums = pars[:, base + 8 * (nd + 2) :]
        gate_gain_grad = lax.dynamic_index_in_dim(mains[me, 0], dp, 0, keepdims=False)
        everything = jnp.transpose(mains[:, 1:], (1, 2, 0, 3)).reshape(7, INNER)
        skip_gain_grad = jnp.sum(everything[0].reshape(HEADS, HEAD_DIM), axis=1)
        bias_sum = jnp.concatenate([everything[1], shared[2]])
        taps_sum = jnp.concatenate([everything[3:], shared[4:]], axis=1).T
        conv_bias_grad = lax.dynamic_slice_in_dim(bias_sum, owner * own_conv, own_conv)
        conv_weight_grad = lax.dynamic_slice_in_dim(taps_sum, owner * own_conv, own_conv)
        mine = nd * self.per
        by_head = lambda v: jnp.swapaxes(v[:, :mine].reshape(nm, nd, self.per), 0, 1).reshape(HEADS)
        step_bias_grad, log_rate_grad = by_head(head_sums[:, 0]), by_head(head_sums[:, 1])
        return (
            y_out.reshape(1, SPAN, MODEL),
            dx_out.reshape(1, SPAN, MODEL),
            norm_gain_grad,
            in_weight_grad,
            conv_weight_grad,
            conv_bias_grad,
            step_bias_grad,
            log_rate_grad,
            skip_gain_grad,
            gate_gain_grad,
            dwo.astype(F32),
        )


def solution(mesh):
    shape = dict(mesh.shape)
    head_split = HeadSplit(shape["dp"], shape["seq"], shape["fsdp"])
    return jax.shard_map(
        head_split.local if head_split.fits() else token_split,
        mesh=mesh,
        in_specs=(
            P("dp", ("seq", "fsdp"), None),
            P("dp", ("seq", "fsdp"), None),
            P(("dp", "seq", "fsdp")),
            P(("dp", "seq", "fsdp"), None),
            P(("dp", "seq", "fsdp"), None),
            P(("dp", "seq", "fsdp")),
            P(),
            P(),
            P(),
            P(("dp", "seq", "fsdp")),
            P(("dp", "seq", "fsdp"), None),
            P("dp"),
            P("dp", None),
        ),
        out_specs=(
            P("dp", ("seq", "fsdp"), None),
            P("dp", ("seq", "fsdp"), None),
            P(("dp", "seq", "fsdp")),
            P(("dp", "seq", "fsdp"), None),
            P(("dp", "seq", "fsdp"), None),
            P(("dp", "seq", "fsdp")),
            P(),
            P(),
            P(),
            P(("dp", "seq", "fsdp")),
            P(("dp", "seq", "fsdp"), None),
        ),
        check_vma=False,
    )
```

```python
import functools

import jax
import jax.numpy as jnp
from jax import lax
from jax.experimental import pallas as pl
from jax.experimental.pallas import tpu as pltpu
from jax.sharding import PartitionSpec as P

HEADS = 64
HEAD_DIM = 64
STATE = 128
KW = 4
INNER = 4096
CONV = 4352
EXTENT = 8512


HIGH = lax.Precision.HIGHEST
EPSILON = 1e-05


def shifted(value, axis, steps):
    count = lax.axis_size(axis)
    leading, last = (max(0, -steps), min(count, count - steps))
    return lax.ppermute(value, axis, [(source, source + steps) for source in range(leading, last)])


def prefix(array, axis, combine, identity):
    peers, place = (lax.axis_size(axis), lax.axis_index(axis))
    everything = jax.tree.map(
        lambda part, kind: lax.all_gather(part.astype(kind), axis),
        array,
        (jnp.bfloat16, jnp.bfloat16),
    )
    start = jax.tree.map(
        lambda part, zero: jnp.broadcast_to(jnp.asarray(zero, part.dtype), part.shape),
        array,
        identity,
    )

    def prefix_lap(k, before):
        reached = k < place
        new = combine(
            before, jax.tree.map(lambda part, own: part[k].astype(own.dtype), everything, array)
        )
        return jax.tree.map(lambda a, b: jnp.where(reached, a, b), new, before)

    return lax.fori_loop(0, peers, prefix_lap, start)


def carried_in(array, axis, combine, identity):
    peers, place = (lax.axis_size(axis), lax.axis_index(axis))
    everything = jax.tree.map(
        lambda part, kind: lax.all_gather(part.astype(kind), axis),
        array,
        jax.tree.map(lambda a: jnp.bfloat16 if a.dtype == jnp.float32 else a.dtype, array),
    )
    start = jax.tree.map(
        lambda part, zero: jnp.broadcast_to(jnp.asarray(zero, part.dtype), part.shape),
        array,
        identity,
    )

    def carried_lap(k, before):
        at = peers - 1 - k
        reached = at > place
        new = combine(
            before, jax.tree.map(lambda part, own: part[at].astype(own.dtype), everything, array)
        )
        return jax.tree.map(lambda a, b: jnp.where(reached, a, b), new, before)

    return lax.fori_loop(0, peers, carried_lap, start)


def doc_begins(lengths, positions):
    places = jnp.arange(lengths.shape[1])
    ahead = places[:, None] < places[None, :]
    endings = jnp.sum(jnp.where(ahead[None], lengths[:, :, None], 0), axis=1)
    reached = endings[:, None, :] <= positions[None, :, None]
    return jnp.max(jnp.where(reached, endings[:, None, :], 0), axis=2)


def input_norm(hidden, gain):
    inv_rms = lax.rsqrt(jnp.mean(hidden * hidden, axis=1, keepdims=True) + EPSILON)
    return hidden * inv_rms * gain


def causal_conv(extended, taps, bias, validity):
    block_len = validity.shape[2]
    running = bias + jnp.zeros((extended.shape[0], block_len, extended.shape[2]), jnp.float32)
    for tap in range(taps.shape[1]):
        running = (
            running + extended[:, tap : tap + block_len] * taps[:, tap] * validity[tap][:, :, None]
        )
    return jax.nn.silu(running)


def scan_parts(signal, key_side, query_side, rate_in, step_bias, log_rate, begins, block_start):
    step = jax.nn.softplus(rate_in + step_bias)
    log_decay = step * -jnp.exp(log_rate)
    places = jnp.arange(log_decay.shape[1])
    lower = (places[None, :] <= places[:, None]).astype(jnp.float32)
    cumulative = jnp.einsum("ts,bsh->bth", lower, log_decay, precision=HIGH)
    by_head = jnp.swapaxes(cumulative, 1, 2)
    indices = jnp.arange(signal.shape[1])
    same_doc = (begins[:, :, None] == begins[:, None, :]) & (
        indices[None, None, :] <= indices[None, :, None]
    )
    gaps = by_head[:, :, :, None] - by_head[:, :, None, :]
    kernel = jnp.exp(jnp.where(same_doc[:, None], gaps, 0.0)) * same_doc[:, None]
    intersection = jnp.einsum("btn,bsn->bts", query_side, key_side, precision=HIGH)
    mixing = kernel * intersection[:, None] * jnp.swapaxes(step, 1, 2)[:, :, None, :]
    local_out = jnp.einsum("bhts,bshp->bthp", mixing, signal, precision=HIGH)
    inherits = (begins < block_start).astype(jnp.float32)
    carried = jnp.exp(cumulative) * inherits[:, :, None]
    last_same = begins == begins[:, -1:]
    tail_weight = (
        jnp.exp(jnp.where(last_same[:, :, None], cumulative[:, -1:] - cumulative, 0.0))
        * last_same[:, :, None]
        * step
    )
    fresh_state = jnp.einsum("bsh,bshp,bsn->bhpn", tail_weight, signal, key_side, precision=HIGH)
    return (local_out, carried, carried[:, -1], fresh_state)


def gated_norm(scan_out, signal, skip_gain, gate_in, gate_gain, head_mask, unit_count):
    mixed = (scan_out + skip_gain[:, None] * signal) * head_mask[:, None, :, None]
    gated = mixed.reshape(gate_in.shape) * jax.nn.silu(gate_in)
    mean_square = jnp.sum(gated * gated, axis=2, keepdims=True) / unit_count[:, None, None]
    return gated * lax.rsqrt(mean_square + EPSILON) * gate_gain


def combine_states(earlier, later):
    return (earlier[0] * later[0], later[1] + later[0][:, :, None, None] * earlier[1])


def token_split(
    layer_input,
    out_grad,
    norm_gain,
    in_weight,
    conv_weight,
    conv_bias,
    step_bias,
    log_rate,
    skip_gain,
    gate_gain,
    out_weight,
    nest_level,
    doc_lengths,
):
    seq_count, block_len, model_width = layer_input.shape
    token_count = seq_count * block_len
    gain_all, taps_all, bias_all, gate_all = (
        lax.all_gather(norm_gain, ("dp", "seq", "fsdp"), axis=0, tiled=True),
        lax.all_gather(conv_weight, ("dp", "seq", "fsdp"), axis=0, tiled=True),
        lax.all_gather(conv_bias, ("dp", "seq", "fsdp"), axis=0, tiled=True),
        lax.all_gather(gate_gain, ("dp", "seq", "fsdp"), axis=0, tiled=True),
    )
    block_start = lax.axis_index(("seq", "fsdp")) * block_len
    positions = block_start + jnp.arange(block_len, dtype=jnp.int32)
    begins = doc_begins(doc_lengths, positions)
    hidden = layer_input.reshape(token_count, model_width).astype(jnp.float32)
    normed = input_norm(hidden, gain_all).astype(jnp.bfloat16)
    columns = normed
    projected = jnp.dot(
        columns,
        lax.all_gather(in_weight, ("dp", "seq", "fsdp"), axis=0, tiled=True),
        preferred_element_type=jnp.float32,
    ).astype(jnp.bfloat16)
    projected = projected.reshape(seq_count, block_len, EXTENT)
    gate_in = projected[:, :, :INNER].astype(jnp.float32)
    conv_in = projected[:, :, INNER : INNER + CONV]
    rate_in = projected[:, :, INNER + CONV :].astype(jnp.float32)
    edge_rows = shifted(conv_in[:, block_len - (KW - 1) :], ("seq", "fsdp"), 1)
    extended = jnp.concatenate([edge_rows, conv_in], axis=1).astype(jnp.float32)
    validity = jnp.stack(
        [(positions[None, :] - (KW - 1) + tap >= begins).astype(jnp.float32) for tap in range(KW)]
    )
    activated, conv_pull = jax.vjp(
        lambda ext_in, taps, bias: causal_conv(ext_in, taps, bias, validity),
        extended,
        taps_all,
        bias_all,
    )
    signal = activated[:, :, :INNER].reshape(seq_count, block_len, HEADS, HEAD_DIM)
    key_side = activated[:, :, INNER : INNER + STATE]
    query_side = activated[:, :, INNER + STATE :]
    local_out, carried, decays, fresh_state = scan_parts(
        signal, key_side, query_side, rate_in, step_bias, log_rate, begins, block_start
    )
    identity = (jnp.ones_like(decays), jnp.zeros_like(fresh_state))
    entry_state = prefix((decays, fresh_state), ("seq", "fsdp"), combine_states, identity)[1]
    scan_out = local_out + carried[..., None] * jnp.einsum(
        "btn,bhpn->bthp", query_side, entry_state, precision=HIGH
    )
    active = jnp.right_shift(HEADS, 3 - nest_level)
    head_mask = (jnp.arange(HEADS)[None, :] < active[:, None]).astype(jnp.float32)
    unit_count = (active * HEAD_DIM).astype(jnp.float32)
    gate_normed, gate_pull = jax.vjp(
        lambda sv, xv, sk, gi, gg: gated_norm(sv, xv, sk, gi, gg, head_mask, unit_count),
        scan_out,
        signal,
        skip_gain,
        gate_in,
        gate_all,
    )
    normed_out = gate_normed.reshape(token_count, INNER).astype(jnp.bfloat16)
    columns = normed_out
    branch_out = jnp.dot(
        columns,
        lax.all_gather(out_weight, ("dp", "seq", "fsdp"), axis=0, tiled=True),
        preferred_element_type=jnp.float32,
    )
    layer_output = (
        (hidden + branch_out).astype(jnp.bfloat16).reshape(seq_count, block_len, model_width)
    )
    grad_flat = out_grad.reshape(token_count, model_width)
    grad_normed_out = lax.dot_general(
        grad_flat,
        lax.all_gather(out_weight, ("dp", "seq", "fsdp"), axis=0, tiled=True),
        (((1,), (1,)), ((), ())),
        preferred_element_type=jnp.float32,
    )
    grad_scan, grad_skip_signal, grad_skip, grad_gate_in, grad_gate_gain = gate_pull(
        grad_normed_out.reshape(seq_count, block_len, INNER)
    )
    lead_grad = jnp.einsum("bth,bthp,btn->bhpn", carried, grad_scan, query_side, precision=HIGH)
    later_grad = carried_in((decays, lead_grad), ("seq", "fsdp"), combine_states, identity)[1]

    def full_scan(signal_in, key_in, query_in, rate_values, bias_values, rate_logs):
        part_out, part_carried, part_decays, part_fresh = scan_parts(
            signal_in, key_in, query_in, rate_values, bias_values, rate_logs, begins, block_start
        )
        joined_out = part_out + part_carried[..., None] * jnp.einsum(
            "btn,bhpn->bthp", query_in, entry_state, precision=HIGH
        )
        return (joined_out, part_decays[:, :, None, None] * entry_state + part_fresh)

    scan_pull = jax.vjp(full_scan, signal, key_side, query_side, rate_in, step_bias, log_rate)[1]
    grad_signal, grad_key, grad_query, grad_rate, grad_step_bias, grad_log_rate = scan_pull(
        (grad_scan, later_grad)
    )
    grad_activated = jnp.concatenate(
        [
            (grad_signal + grad_skip_signal).reshape(seq_count, block_len, INNER),
            grad_key,
            grad_query,
        ],
        axis=2,
    )
    grad_extended, grad_taps, grad_bias = conv_pull(grad_activated)
    returned = shifted(grad_extended[:, : KW - 1].astype(jnp.bfloat16), ("seq", "fsdp"), -1).astype(
        jnp.float32
    )
    grad_conv_in = grad_extended[:, KW - 1 :] + jnp.pad(
        returned, ((0, 0), (block_len - (KW - 1), 0), (0, 0))
    )
    grad_projected = (
        jnp.concatenate([grad_gate_in, grad_conv_in, grad_rate], axis=2)
        .reshape(token_count, EXTENT)
        .astype(jnp.bfloat16)
    )
    grad_normed = lax.dot_general(
        grad_projected,
        lax.all_gather(in_weight, ("dp", "seq", "fsdp"), axis=0, tiled=True),
        (((1,), (1,)), ((), ())),
        preferred_element_type=jnp.float32,
    )
    replicas = lax.axis_size("dp")
    members = lax.axis_size(("seq", "fsdp"))
    width_in = model_width // lax.axis_size(("dp", "seq", "fsdp"))
    width_out = INNER // lax.axis_size(("dp", "seq", "fsdp"))
    in_cols, out_cols = (
        lax.all_to_all(
            normed.reshape(token_count, replicas, members, width_in),
            ("seq", "fsdp"),
            split_axis=2,
            concat_axis=0,
            tiled=True,
        ),
        lax.all_to_all(
            normed_out.reshape(token_count, replicas, members, width_out),
            ("seq", "fsdp"),
            split_axis=2,
            concat_axis=0,
            tiled=True,
        ),
    )
    in_cols = in_cols.reshape(members * token_count, replicas * width_in)
    out_cols = out_cols.reshape(members * token_count, replicas * width_out)
    in_new = lax.dot_general(
        in_cols,
        lax.all_gather(grad_projected, ("seq", "fsdp"), axis=0, tiled=True),
        (((0,), (0,)), ((), ())),
        preferred_element_type=jnp.float32,
    )
    out_new = lax.dot_general(
        out_cols,
        lax.all_gather(grad_flat, ("seq", "fsdp"), axis=0, tiled=True),
        (((0,), (0,)), ((), ())),
        preferred_element_type=jnp.float32,
    )
    in_weight_grad, out_weight_grad = (
        lax.psum_scatter(in_new.astype(jnp.bfloat16), "dp", scatter_dimension=0, tiled=True).astype(
            jnp.float32
        ),
        lax.psum_scatter(
            out_new.astype(jnp.bfloat16), "dp", scatter_dimension=0, tiled=True
        ).astype(jnp.float32),
    )
    norm_pull = jax.vjp(input_norm, hidden, gain_all)[1]
    grad_hidden, grad_gain = norm_pull(grad_normed)
    input_grad = (
        (grad_flat.astype(jnp.float32) + grad_hidden)
        .astype(jnp.bfloat16)
        .reshape(seq_count, block_len, model_width)
    )
    norm_gain_grad, conv_weight_grad, conv_bias_grad, gate_gain_grad = (
        lax.psum_scatter(grad_gain, ("dp", "seq", "fsdp"), scatter_dimension=0, tiled=True),
        lax.psum_scatter(grad_taps, ("dp", "seq", "fsdp"), scatter_dimension=0, tiled=True),
        lax.psum_scatter(grad_bias, ("dp", "seq", "fsdp"), scatter_dimension=0, tiled=True),
        lax.psum_scatter(grad_gate_gain, ("dp", "seq", "fsdp"), scatter_dimension=0, tiled=True),
    )
    step_bias_grad, log_rate_grad, skip_gain_grad = lax.psum(
        (grad_step_bias, grad_log_rate, grad_skip), ("dp", "seq", "fsdp")
    )
    return (
        layer_output,
        input_grad,
        norm_gain_grad,
        in_weight_grad,
        conv_weight_grad,
        conv_bias_grad,
        step_bias_grad,
        log_rate_grad,
        skip_gain_grad,
        gate_gain_grad,
        out_weight_grad,
    )


MESH = pl.DeviceIdType.MESH
F32 = jnp.float32
BF16 = jnp.bfloat16
TILE = 128
SPAN = 128
MODEL = 2048
COMMON = 384
PAD = 16
NEG = -1e30
SLOTS = (1, 4)
VM = pl.BlockSpec(memory_space=pltpu.VMEM)
SM = pl.BlockSpec(memory_space=pltpu.SMEM)
ANY = pl.BlockSpec(memory_space=pl.ANY)
DMA = pltpu.SemaphoreType.DMA


def remote(src, dst, sends, recvs, device):
    return pltpu.make_async_remote_copy(
        src_ref=src,
        dst_ref=dst,
        send_sem=sends,
        recv_sem=recvs,
        device_id=device,
        device_id_type=MESH,
    )


def dot(a, b, over=((1,), (0,))):
    return lax.dot_general(a, b, (over, ((), ())), preferred_element_type=F32)


def exact(a, b, over=((1,), (0,))):
    return lax.dot_general(a, b, (over, ((), ())), precision=HIGH, preferred_element_type=F32)


def begin_at(place, starts, docs):
    begin = jnp.zeros_like(place)
    for doc in range(1, docs):
        begin = jnp.where(starts[doc] <= place, starts[doc], begin)
    return begin


def iota(shape, dim):
    return lax.broadcasted_iota(jnp.int32, shape, dim)


def silu_slope(value):
    gate = jax.nn.sigmoid(value)
    return gate * (1.0 + value * (1.0 - gate))


def softplus(value):
    return jnp.maximum(value, 0.0) + jnp.log1p(jnp.exp(-jnp.abs(value)))


def conv_tile(extended, taps, lanes, valid):
    total = jnp.broadcast_to(taps[KW : KW + 1, lanes], (SPAN, TILE))
    for tap in range(KW):
        back = KW - 1 - tap
        moved = extended if back == 0 else pltpu.roll(extended, back, 0)
        total = total + jnp.where(valid[tap], moved[PAD:], 0.0) * taps[tap : tap + 1, lanes]
    return total


def tile_of(index):
    return slice(index * TILE, (index + 1) * TILE)


def rows_of(index, size=SPAN):
    return pl.ds(pl.multiple_of(index * size, size), size)


def head_col(values, head):
    return jnp.broadcast_to(values[:, head : head + 1], (SPAN, TILE))


def lane_sum(values):
    return jnp.broadcast_to(jnp.sum(values, axis=1, keepdims=True), values.shape)


class Line:
    def __init__(self, place, sizes, block, sems):
        self.dp, self.c, self.z = place
        self.nc, self.nz = sizes
        self.block = block
        self.right_s, self.right_r, self.left_s, self.left_r, self.core_s, self.core_r = sems

    def right(self, s):
        block = self.block(self.c, self.z - s)
        to = (self.dp, self.c, lax.rem(self.z + 1, self.nz))
        return remote(block, block, self.right_s.at[s], self.right_r.at[s], to)

    def left(self, s):
        block = self.block(self.c, self.z + s)
        to = (self.dp, self.c, lax.rem(self.z + self.nz - 1, self.nz))
        return remote(block, block, self.left_s.at[s], self.left_r.at[s], to)

    def core(self, z):
        block = self.block(self.c, z)
        to = (self.dp, self.nc - 1 - self.c, self.z)
        return remote(block, block, self.core_s.at[z], self.core_r.at[z], to)

    def across(self):
        return (self.dp, self.nc - 1 - self.c, self.z)

    def begin(self):
        pl.when(self.z < self.nz - 1)(lambda: self.right(0).start())
        pl.when(self.z > 0)(lambda: self.left(0).start())
        self.core(self.z).start()

    def step(self, s):
        z, nz = self.z, self.nz

        @pl.when(z >= s)
        def _():
            block = self.block(self.c, z - s)
            remote(block, block, self.right_s.at[s - 1], self.right_r.at[s - 1], self.across()).wait_recv()
            if s < nz - 1:
                pl.when(z < nz - 1)(lambda: self.right(s).start())
            self.core(z - s).start()

        @pl.when(z + s < nz)
        def _():
            block = self.block(self.c, z + s)
            remote(block, block, self.left_s.at[s - 1], self.left_r.at[s - 1], self.across()).wait_recv()
            if s < nz - 1:
                pl.when(z > 0)(lambda: self.left(s).start())
            self.core(z + s).start()

    def arrive(self):
        for z in range(self.nz):
            block = self.block(self.nc - 1 - self.c, z)
            to = (self.dp, self.nc - 1 - self.c, self.z)
            remote(block, block, self.core_s.at[z], self.core_r.at[z], to).wait_recv()

    def end(self):
        z, nz = self.z, self.nz
        for s in range(nz - 1):
            pl.when((z >= s) & (z < nz - 1))(lambda s=s: self.right(s).wait_send())
            pl.when((z + s < nz) & (z > 0))(lambda s=s: self.left(s).wait_send())
        for s in range(nz):
            self.core(jnp.int32(s)).wait_send()


class Sum:
    def __init__(self, place, sizes, part, came, total, heard, sems):
        self.dp, self.c, self.z = place
        self.nc, self.nz = sizes
        self.part, self.came, self.total, self.heard = part, came, total, heard
        self.core_s, self.core_r, self.right_s, self.right_r, self.left_s, self.left_r = sems

    def core(self, t):
        to = (self.dp, self.nc - 1 - self.c, self.z)
        src = self.part.at[(self.nc - 1 - self.c) * self.nz + t]
        return remote(src, self.came.at[t], self.core_s.at[t], self.core_r.at[t], to)

    def right(self, t):
        to = (self.dp, self.c, lax.rem(self.z + 1, self.nz))
        return remote(self.total.at[t], self.heard.at[t], self.right_s.at[t], self.right_r.at[t], to)

    def left(self, t, stops):
        slot = self.nz if stops else t
        to = (self.dp, self.c, lax.rem(self.z + self.nz - 1, self.nz))
        return remote(self.total.at[t], self.heard.at[slot], self.left_s.at[t], self.left_r.at[t], to)

    def add_core(self, t):
        self.core(t).wait_recv()

        def add(r, _):
            at = rows_of(r, 16)
            self.total[t, at, :] = (
                self.part[self.c * self.nz + t, at, :].astype(F32) + self.came[t, at, :].astype(F32)
            ).astype(BF16)
            return 0

        lax.fori_loop(0, SPAN // 16, add, 0)

    def add(self, t, slot):
        def add(r, _):
            at = rows_of(r, 16)
            self.total[t, at, :] = (
                self.total[t, at, :].astype(F32) + self.heard[slot, at, :].astype(F32)
            ).astype(BF16)
            return 0

        lax.fori_loop(0, SPAN // 16, add, 0)

    def begin(self):
        z, nz = self.z, self.nz
        pl.when(z == 0)(lambda: self.right(nz - 1).start())
        pl.when(z == nz - 1)(lambda: self.left(0, nz == 2).start())

    def slot(self, k):
        z, nz = self.z, self.nz
        for hop in range(1, k + 1):
            t = nz - 1 - (k - hop)
            if t > hop:

                @pl.when(z == hop)
                def _(t=t):
                    self.right(t).wait_recv()
                    self.add(t, t)
                    self.right(t).start()

                @pl.when(z == nz - 1 - hop)
                def _(u=nz - 1 - t, hop=hop):
                    self.left(u, False).wait_recv()
                    self.add(u, u)
                    self.left(u, u == nz - 2 - hop).start()

        @pl.when(z == 0)
        def _():
            self.right(nz - k).wait_send()
            self.right(nz - 1 - k).start()

        @pl.when(z == nz - 1)
        def _():
            self.left(k - 1, False).wait_send()
            self.left(k, k == nz - 2).start()

    def arrive(self):
        z, nz = self.z, self.nz
        for t in range(nz):
            pl.when((z == t) & (z > 0))(lambda t=t: self.right(t).wait_recv())
            pl.when((z == t) & (z < nz - 1))(lambda t=t: self.left(t, True).wait_recv())

    def own(self, rows):
        z, nz = self.z, self.nz
        value = self.total[z, rows, :].astype(F32)
        left = self.heard[z, rows, :].astype(F32)
        right = self.heard[nz, rows, :].astype(F32)
        value = value + jnp.where(z > 0, left, 0.0)
        return value + jnp.where(z < nz - 1, right, 0.0)

    def end_core(self):
        for t in range(self.nz):
            self.core(t).wait_send()

    def end(self):
        z, nz = self.z, self.nz
        for t in range(nz):
            right = (z < t) if t == 1 else (z < t) & (z > 0)
            left = (z > t) if t == nz - 2 else (z > t) & (z < nz - 1)
            pl.when(right)(lambda t=t: self.right(t).wait_send())
            pl.when(left)(lambda t=t: self.left(t, False).wait_send())


class Square:
    def __init__(self, place, block, size, sems):
        dp, c, z = place
        self.dp, self.dx, self.dy = dp, dp + 1 - 2 * lax.rem(dp, 2), lax.rem(dp + 2, 4)
        self.diag = lax.rem(self.dx + 2, 4)
        self.x, self.y = (self.dx, c, z), (self.dy, c, z)
        self.block = block
        self.half = size // 2
        self.sems = sems

    def copy(self, way, owner, piece, first, rows, to):
        block = self.block(owner, piece, first, rows)
        sends, recvs = self.sems
        return remote(block, block, sends.at[way, piece], recvs.at[way, piece], to)

    def whole(self, way, owner, piece):
        return self.copy(way, owner, piece, 0, 2 * self.half, self.x if way == 0 else self.y)

    def part(self, way, owner, piece):
        return self.copy(way, owner, piece, 0 if way == 2 else self.half, self.half, self.y if way == 2 else self.x)

    def begin(self, piece):
        self.whole(0, self.dp, piece).start()
        self.whole(1, self.dp, piece).start()

    def step(self, piece):
        self.whole(0, self.dx, piece).wait_recv()
        self.part(2, self.dx, piece).start()
        self.whole(1, self.dy, piece).wait_recv()
        self.part(3, self.dy, piece).start()

    def arrive(self, piece):
        self.part(2, self.diag, piece).wait_recv()
        self.part(3, self.diag, piece).wait_recv()

    def end(self, piece):
        self.whole(0, self.dp, piece).wait_send()
        self.whole(1, self.dp, piece).wait_send()
        self.part(2, self.dx, piece).wait_send()
        self.part(3, self.dy, piece).wait_send()


class SquareSum:
    def __init__(self, place, part, once, twice, gone, sems, pieces, index=lambda owner: owner, base=None):
        dp, c, z = place
        self.dp, self.dx, self.dy = dp, dp + 1 - 2 * lax.rem(dp, 2), lax.rem(dp + 2, 4)
        self.diag = lax.rem(self.dx + 2, 4)
        self.x, self.y = (self.dx, c, z), (self.dy, c, z)
        self.part, self.once, self.twice, self.gone = part, once, twice, gone
        self.s1, self.r1, self.s2, self.r2 = sems
        self.pieces, self.index, self.base = pieces, index, base
        self.rows = part.shape[1] // pieces
        cut = (part.shape[2] // TILE + 1) // 2 * TILE
        self.halves = (slice(0, cut), slice(cut, part.shape[2]))
        self.widths = (cut, part.shape[2] - cut)

    def heard(self, slot, start, size):
        width = self.widths[slot // 2]
        if self.base is None:
            return self.once.at[slot, pl.ds(start, size), :width]
        at = pl.multiple_of(self.base + slot * self.part.shape[1] + start, 16)
        return self.once.at[pl.ds(at, size), :width]

    def first(self, p, side, k):
        owner = ((self.dx, self.diag), (self.dy, self.diag))[side][k]
        at = pl.ds(p * self.rows, self.rows)
        slot = 2 * side + k
        return remote(
            self.part.at[self.index(owner), at, self.halves[side]], self.heard(slot, p * self.rows, self.rows),
            self.s1.at[p, slot], self.r1.at[p, slot], (self.x, self.y)[side],
        )

    def second(self, p, side):
        at = pl.ds(p * self.rows, self.rows)
        return remote(
            self.gone.at[at, self.halves[side]], self.twice.at[side, at, : self.widths[side]],
            self.s2.at[p, side], self.r2.at[p, side], (self.y, self.x)[side],
        )

    def begin_x(self, p):
        self.first(p, 0, 1).start()
        self.first(p, 0, 0).start()

    def begin_y(self, p):
        self.first(p, 1, 1).start()
        self.first(p, 1, 0).start()

    def each(self, p, body):
        def step(r, _):
            start = pl.multiple_of(p * self.rows + r * 16, 16)
            body(pl.ds(start, 16), start)
            return 0

        lax.fori_loop(0, self.rows // 16, step, 0)

    def pass_on(self, p):
        for side in range(2):
            self.first(p, side, 1).wait_recv()
            owner = (self.dy, self.dx)[side]

            def body(at, start, side=side, owner=owner):
                self.gone[at, self.halves[side]] = (
                    self.part[self.index(owner), at, self.halves[side]].astype(F32)
                    + self.heard(2 * side + 1, start, 16)[...].astype(F32)
                ).astype(BF16)

            self.each(p, body)
            self.second(p, side).start()

    def finish(self, p, out):
        for side in range(2):
            self.first(p, side, 0).wait_recv()
            self.second(p, side).wait_recv()

            def body(at, start, side=side):
                out[at, self.halves[side]] = (
                    self.part[self.index(self.dp), at, self.halves[side]].astype(F32)
                    + self.heard(2 * side, start, 16)[...].astype(F32)
                    + self.twice[side, at, : self.widths[side]].astype(F32)
                ).astype(out.dtype)

            self.each(p, body)

    def end(self):
        for p in range(self.pieces):
            for side in range(2):
                self.first(p, side, 0).wait_send()
                self.first(p, side, 1).wait_send()
                self.second(p, side).wait_send()


class HeadSplit:
    def __init__(self, nd, nc, nz):
        self.nd, self.nc, self.nz = nd, nc, nz
        self.nm = nc * nz
        self.span = self.nm * SPAN
        self.rows_in = MODEL // (nd * self.nm)
        self.wide = nd * TILE
        self.per = HEADS // (nd * self.nm)

    def fits(self):
        return (
            INNER == self.nd * self.nm * TILE and self.nd == 4 and self.nc == 2 and self.rows_in % 32 == 0
        )

    def place(self):
        return lax.axis_index("dp"), lax.axis_index("seq"), lax.axis_index("fsdp")

    def group_steps(self):
        return [(e, d) for d in range(self.nz) for e in range(self.nc) if e or d]

    def target(self, step):
        dp, c, z = self.place()
        ct, zt = lax.rem(c + step[0], self.nc), lax.rem(z + step[1], self.nz)
        return (dp, ct, zt), ct * self.nz + zt

    def source(self, step):
        dp, c, z = self.place()
        cs, zs = lax.rem(c + self.nc - step[0], self.nc), lax.rem(z + self.nz - step[1], self.nz)
        return cs * self.nz + zs

    def barrier(self):
        dp, c, z = self.place()
        sem = pltpu.get_barrier_semaphore()
        for step in self.group_steps():
            pl.semaphore_signal(sem, inc=1, device_id=self.target(step)[0], device_id_type=MESH)
        for k in range(1, self.nd):
            pl.semaphore_signal(
                sem, inc=1, device_id=(lax.rem(dp + k, self.nd), c, z), device_id_type=MESH
            )
        pl.semaphore_wait(sem, self.nm - 1 + self.nd - 1)

    def kernel(
        self, docs, lengths, level, x_ref, tap_ref, bias_ref, norm_ref, gain_ref, step_ref, rate_ref, skip_ref, in_ref, g_ref, wo_ref,
        y_out, dx_out, dw_out, dwc_out, dwo_out, par_out,
        xall, gall, wall, wcall, woall, wm_ref, wc_ref, head_ref, parbuf_, parall, every_par, projm, pre_sig, o, states,
        step_s, cum_s, dg, scaled, sel, hp, chp, state, dnext, heard_st, st, pre_bc, projc, taps,
        ypart, ycame, ytotal, yheard, xheard, dcom, sums, heads, gain_out,
        cpart, c1, c2, crows, cheard, w1, w2, o2, pard, parbuf,
        pd_s, pd_r, pg_s, pg_r, wz_s, wz_r, cz_s, cz_r, wq_s, wq_r, cq_s, cq_r, oq_s, oq_r, cc_s, cc_r,
        xr_s, xr_r, xl_s, xl_r, xc_s, xc_r, gr_s, gr_r, gl_s, gl_r, gc_s, gc_r,
        st_s, st_r, yc_s, yc_r, yr_s, yr_r, yl_s, yl_r,
        uc_s, uc_r, ur_s, ur_r, ul_s, ul_r, sc_s, sc_r, c1_s, c1_r, c2_s, c2_r, sz_s, sz_r,
        w1_s, w1_r, w2_s, w2_r, o1_s, o1_r, o2_s, o2_r, vz_s, vz_r, qd_s, qd_r, qg_s, qg_r, loc,
    ):
        nd, nc, nz, nm = self.nd, self.nc, self.nz, self.nm
        rows, wide = self.rows_in, self.wide
        where = dp, c, z = self.place()
        me = c * nz + z
        sizes = (nc, nz)
        steps = self.group_steps()
        other = (dp, nc - 1 - c, z)
        lines = [(k, (lax.rem(dp + k, nd), c, z), lax.rem(dp + nd - k, nd)) for k in range(1, nd)]
        started = []

        def go(copy):
            copy.start()
            started.append(copy)
            return copy

        def w_block(owner, m, first=0, count=rows):
            at = pl.multiple_of(m * rows + first, rows // 2)
            return wall.at[owner, pl.ds(at, count), :]

        def c_block(owner, m, first=0, count=rows):
            at = pl.multiple_of((owner * nm + m) * rows + first, rows // 2)
            return wcall.at[pl.ds(at, count), :]

        w_from = [me] + [self.source(step) for step in steps]
        c_from = [c * nz + lax.rem(z + nz - d, nz) for d in range(nz)]
        w_square = Square(
            where, lambda owner, j, first, count: w_block(owner, w_from[j], first, count), rows, (wq_s, wq_r)
        )
        c_square = Square(
            where, lambda owner, j, first, count: c_block(owner, c_from[j], first, count), rows, (cq_s, cq_r)
        )
        o_square = Square(
            where,
            lambda owner, j, first, count: woall.at[owner, pl.ds(first, count), :],
            TILE,
            (oq_s, oq_r),
        )
        x_line = Line(where, sizes, lambda a, b: xall.at[rows_of(a * nz + b), :], (xr_s, xr_r, xl_s, xl_r, xc_s, xc_r))
        g_line = Line(where, sizes, lambda a, b: gall.at[rows_of(a * nz + b), :], (gr_s, gr_r, gl_s, gl_r, gc_s, gc_r))
        y_sum = Sum(where, sizes, ypart, ycame, ytotal, yheard, (yc_s, yc_r, yr_s, yr_r, yl_s, yl_r))

        starts = [jnp.int32(0)]
        for doc in range(1, docs):
            starts.append(starts[-1] + lengths[0, doc - 1])
        active = jnp.right_shift(HEADS, 3 - level[0])
        unit = jnp.float32(1.0 / INNER)
        for smaller in range(3):
            unit = jnp.where(level[0] == smaller, jnp.float32(2.0 ** (3 - smaller) / INNER), unit)
        own_conv = CONV // (nd * nm)
        parbuf_[dp, 0:KW, :own_conv] = tap_ref[...]
        parbuf_[dp, KW : KW + 1, :own_conv] = bias_ref[...]
        parbuf_[dp, 5:6, :rows] = norm_ref[...]
        parbuf_[dp, 6:7, :TILE] = gain_ref[...]
        head_ref[...] = jnp.zeros_like(head_ref)
        head_ref[0:1, :HEADS] = step_ref[...]
        head_ref[1:2, :HEADS] = -jnp.exp(rate_ref[...])
        head_ref[2:3, :HEADS] = skip_ref[...]
        head_ref[3:4, :] = (iota((1, TILE), 1) < active).astype(F32)
        for m in range(nm):
            for i in range(2 * nd):
                wm_ref[m * rows : (m + 1) * rows, tile_of(i)] = in_ref[:, tile_of(i * nm + m)]
        shared = EXTENT - 2 * INNER
        wc_ref[:, 2 * TILE :] = jnp.zeros((rows, COMMON - 2 * TILE), BF16)
        wc_ref[:, : 2 * TILE] = in_ref[:, 2 * INNER : 2 * INNER + 2 * TILE]
        wc_ref[:, 2 * TILE : shared] = in_ref[:, 2 * INNER + 2 * TILE :]
        own = [
            pltpu.make_async_copy(wm_ref.at[rows_of(me, rows), :], w_block(dp, me), loc.at[0]),
            pltpu.make_async_copy(wc_ref, c_block(dp, me), loc.at[1]),
            pltpu.make_async_copy(wo_ref, woall.at[dp], loc.at[2]),
            pltpu.make_async_copy(g_ref, gall.at[rows_of(me), :], loc.at[3]),
        ]
        for copy in own:
            copy.start()
        self.barrier()
        for k, device, _ in lines:
            go(remote(parbuf_.at[dp], parbuf_.at[dp], pd_s.at[k], pd_r.at[k], device))
        for j, step in enumerate(steps):
            device, there = self.target(step)
            go(remote(wm_ref.at[rows_of(there, rows), :], w_block(dp, me), wz_s.at[j], wz_r.at[j], device))
            if step[0] == 0:
                go(remote(wc_ref, c_block(dp, me), cz_s.at[step[1]], cz_r.at[step[1]], device))
        for copy in own[:3]:
            copy.wait()
        o_square.begin(0)
        w_square.begin(0)
        c_square.begin(0)
        for k, device, frm in lines:
            remote(parbuf_.at[frm], parbuf_.at[frm], pd_s.at[k], pd_r.at[k], device).wait_recv()
        parall[me] = parbuf_[...]
        for j, step in enumerate(steps):
            device, _ = self.target(step)
            go(remote(parbuf_, parall.at[me], pg_s.at[j], pg_r.at[j], device))
        for j, step in enumerate(steps):
            device, _ = self.target(step)
            remote(parbuf_, parall.at[self.source(step)], pg_s.at[j], pg_r.at[j], device).wait_recv()
        owners = [(first // nm, first % nm) for first in range(nd * nm)]
        gain = jnp.concatenate([parall[m, d][5:6, :rows] for d, m in owners], axis=1)
        gain_out[...] = jnp.broadcast_to(gain, (8, MODEL))
        hidden = x_ref[...].astype(F32)
        inverse = lax.rsqrt(jnp.mean(hidden * hidden, axis=1, keepdims=True) + EPSILON)
        xall[rows_of(me), :] = (hidden * inverse * gain).astype(BF16)
        x_line.begin()

        for j, step in enumerate(steps):
            device, _ = self.target(step)
            block = w_block(dp, w_from[j + 1])
            remote(block, block, wz_s.at[j], wz_r.at[j], device).wait_recv()
            w_square.begin(j + 1)
            if step[0] == 0:
                d = step[1]
                block = c_block(dp, c_from[d])
                remote(block, block, cz_s.at[d], cz_r.at[d], device).wait_recv()
                c_square.begin(d)
            if j == 2:
                o_square.step(0)
                w_square.step(0)
                c_square.step(0)
        every_par[...] = jnp.concatenate([parall[m, d][:, :own_conv] for d, m in owners], axis=1)
        for i in range(nd):
            at = pl.ds(pl.multiple_of((i * nm + me) * TILE, TILE), TILE)
            taps[:, tile_of(i)] = every_par[:, at]
        taps[:, wide:] = every_par[:, INNER : INNER + 2 * TILE]
        head, lane = iota((TILE, TILE), 0), iota((TILE, TILE), 1)
        step_of = nm * self.per
        chosen = (head == lax.div(lane, self.per) * step_of + self.per * me + lax.rem(lane, self.per)) & (
            lane < nd * self.per
        )
        sel[...] = chosen.astype(BF16)
        hp[...] = exact(head_ref[...], chosen.astype(F32))
        for i in range(nd):
            chosen = head == i * step_of + self.per * me + lax.div(lane, HEAD_DIM)
            spread = exact(head_ref[...], chosen.astype(F32))
            chp[0:2, tile_of(i)] = spread[2:4, :]
            chp[2:3, tile_of(i)] = parbuf_[i][6:7, :TILE]
        x_line.step(1)
        for j in range(1, 4):
            w_square.step(j)
        for j in range(1, nz):
            c_square.step(j)
        x_line.step(2)
        for j in range(4, nm):
            w_square.step(j)
        x_line.step(3)
        own[3].wait()
        g_line.begin()
        for j in range(nz):
            c_square.arrive(j)
        for i in range(nd):
            at = pl.ds(pl.multiple_of((i * nm + c * nz) * rows, rows), nz * rows)
            go(remote(wcall.at[at, :], wcall.at[at, :], cc_s.at[i], cc_r.at[i], other))
        x_line.arrive()
        for j in range(nm):
            w_square.arrive(j)
        for i in range(nd):
            at = pl.ds(pl.multiple_of((i * nm + (nc - 1 - c) * nz) * rows, rows), nz * rows)
            remote(wcall.at[at, :], wcall.at[at, :], cc_s.at[i], cc_r.at[i], other).wait_recv()
        projm[0:PAD, :] = jnp.zeros((PAD, 2 * wide), BF16)
        projc[0:PAD, :] = jnp.zeros((PAD, COMMON), BF16)
        projc[PAD:, :] = dot(xall[...], wcall[...]).astype(BF16)

        def project(n, _):
            at = rows_of(n, 256)
            projm[PAD:, at] = dot(xall[...], wall[:, :, at].reshape(MODEL, 256)).astype(BF16)
            pl.when(n == 2)(lambda: g_line.step(1))
            return 0

        lax.fori_loop(0, 2 * wide // 256, project, 0)
        state[...] = jnp.zeros_like(state)

        def forward(i, _):
            self.forward_chunk(
                i, docs, starts, projm, projc, taps, sel, hp, chp,
                pre_sig, pre_bc, o, states, step_s, cum_s, scaled, st, state,
            )
            pl.when(i == 2)(lambda: g_line.step(2))
            pl.when(i == 6)(lambda: g_line.step(3))
            return 0

        lax.fori_loop(0, nm, forward, 0)

        o_square.arrive(0)

        def branch(pair):
            def some(n, _):
                t = pair + lax.rem(n, 2) * (nz - 1 - 2 * pair)
                turn = t + lax.rem(nc - 1 - c + lax.div(n, 2), nc) * nz
                ypart[turn] = dot(scaled[rows_of(turn), :], woall[...].reshape(wide, MODEL)).astype(BF16)
                pl.when(n < 2)(lambda: y_sum.core(t).start())
                return 0

            lax.fori_loop(0, 4, some, 0)

        branch(0)
        y_sum.add_core(0)
        y_sum.add_core(nz - 1)
        y_sum.begin()
        for pair in range(1, nz // 2):
            branch(pair)
            y_sum.add_core(pair)
            y_sum.add_core(nz - 1 - pair)

        g_line.arrive()
        lanes_at = iota((SPAN, TILE), 1)

        def gate_grad(n, _):
            at = rows_of(n, 256)
            grad = dot(gall[at, :], woall[...].reshape(wide, MODEL), ((1,), (1,)))
            dg[at, :] = grad
            for half in range(2):
                product = jnp.zeros((SPAN, TILE), F32)
                for i in range(nd):
                    mine = scaled[pl.ds(pl.multiple_of(n * 256 + half * SPAN, SPAN), SPAN), tile_of(i)]
                    product = product + mine.astype(F32) * grad[half * SPAN : (half + 1) * SPAN, tile_of(i)]
                st[1, pl.ds(2 * n + half, 1), :] = lane_sum(product).T[0:1, :]
            return 0

        lax.fori_loop(0, nm // 2, gate_grad, 0)
        sent = []
        for j, step in enumerate(steps):
            device, _ = self.target(step)
            sent.append(go(remote(st, heard_st.at[j], st_s.at[j], st_r.at[j], device)))

        totals = st[...]
        for j, copy in enumerate(sent):
            copy.wait_recv()
            totals = totals + heard_st[j]
        for copy in sent:
            copy.wait_send()
        st[...] = totals

        dnext[...] = jnp.zeros_like(dnext)
        state[...] = jnp.zeros_like(state)
        sums[...] = jnp.zeros_like(sums)
        heads[...] = jnp.zeros_like(heads)

        def backward(n, _):
            self.backward_chunk(
                nm - 1 - n, docs, starts, unit, projm, pre_sig, pre_bc, o, states, step_s, cum_s, dg, st, taps, sel,
                hp, chp, dcom, scaled, sums, heads, state, dnext, projc,
            )
            for k in range(1, nz - 1):
                pl.when(n == SLOTS[k - 1])(lambda k=k: y_sum.slot(k))
            return 0

        lax.fori_loop(0, nm, backward, 0)
        for copy in started:
            if not any(copy is s for s in sent):
                copy.wait_send()
        started.clear()
        for j in range(nm):
            w_square.end(j)
        for j in range(nz):
            c_square.end(j)
        o_square.end(0)
        x_line.end()
        g_line.end()

        x_sum = Sum(where, sizes, ypart, ycame, ytotal, xheard, (uc_s, uc_r, ur_s, ur_r, ul_s, ul_r))
        w_sum = SquareSum(where, wall, w1, w2, projm, (w1_s, w1_r, w2_s, w2_r), 2)
        o_sum = SquareSum(where, woall, xall, o2, xall, (o1_s, o1_r, o2_s, o2_r), 1, base=4 * TILE)
        c_sum = SquareSum(where, cpart, c1, c2, dcom, (c1_s, c1_r, c2_s, c2_r), 1, lambda owner: owner * nc + c)
        def input_grad(core):
            base = rows_of(core, nz * SPAN)
            lead = pl.ds(pl.multiple_of(core * nz * SPAN + PAD, PAD), nz * SPAN)

            def piece(n, _):
                at = rows_of(n, 256)
                part = dot(projm[lead, :], wall[lax.div(n, 2), rows_of(lax.rem(n, 2), 256), :], ((1,), (1,)))
                part = (part + dot(dcom[base, :], wcall[at, :], ((1,), (1,)))).astype(BF16)
                for t in range(nz):
                    ypart[core * nz + t, :, at] = part[t * SPAN : (t + 1) * SPAN, :]
                return 0

            lax.fori_loop(0, MODEL // 256, piece, 0)

        y_sum.end_core()
        input_grad(nc - 1 - c)
        for t in range(nz):
            x_sum.core(t).start()
        input_grad(c)
        y_sum.arrive()
        stat = jnp.broadcast_to(st[0, pl.ds(me, 1), :], (SPAN, TILE)).T
        root = lax.rsqrt(stat[:, 0:1] * unit + EPSILON)
        y_out[...] = (x_ref[...].astype(F32) + root * y_sum.own(slice(None))).astype(BF16)
        y_sum.end()
        x_sum.add_core(0)
        x_sum.add_core(nz - 1)
        x_sum.begin()
        for t in range(1, nz - 1):
            x_sum.add_core(t)

        def weight_grad(owner):
            def piece(n, _):
                at = pl.ds(pl.multiple_of(owner * (nm * rows) + n * 256, 256), 256)
                wall[owner, rows_of(n, 256), :] = dot(xall[:, at], projm[PAD:, :], ((0,), (0,))).astype(BF16)
                return 0

            lax.fori_loop(0, nm * rows // 256, piece, 0)

        weight_grad(w_sum.diag)
        weight_grad(w_sum.dx)
        w_sum.begin_x(0)
        weight_grad(w_sum.dy)
        w_sum.begin_y(0)
        weight_grad(dp)

        def shared_grad(n, _):
            at = rows_of(n, 256)
            cpart[n] = dot(xall[:, at], dcom[...], ((0,), (0,))).astype(BF16)
            return 0

        lax.fori_loop(0, nd * nc, shared_grad, 0)
        ccopies = [
            go(remote(cpart.at[i * nc + nc - 1 - c], projc.at[rows_of(i, nz * rows), :], sc_s.at[i], sc_r.at[i], other)) for i in range(nd)
        ]
        x_sum.slot(1)

        def out_grad(n, _):
            at = rows_of(n, 512)
            part = dot(scaled[...], gall[:, at], ((0,), (0,))).astype(BF16)
            for i in range(nd):
                woall[i, :, at] = part[tile_of(i), :]
            return 0

        lax.fori_loop(0, MODEL // 512, out_grad, 0)
        w_sum.pass_on(0)
        w_sum.begin_x(1)
        w_sum.begin_y(1)
        for i in range(nd):
            ccopies[i].wait_recv()
            cpart[i * nc + c] = (cpart[i * nc + c].astype(F32) + projc[rows_of(i, nz * rows), :].astype(F32)).astype(BF16)
        x_sum.slot(2)

        def send_rows(p):
            half = nm // 2
            for j in range(half):
                there = p * half + j
                block = wm_ref.at[there * rows : (there + 1) * rows, :]
                ct, zt = there // nz, there % nz

                @pl.when(there != me)
                def _():
                    remote(block, dw_out.at[me], vz_s.at[there], vz_r.at[me], (dp, ct, zt)).start()

                @pl.when(there == me)
                def _():
                    dw_out[there] = block[...]

        w_sum.finish(0, wm_ref)
        send_rows(0)
        w_sum.pass_on(1)
        c_sum.begin_x(0)
        c_sum.begin_y(0)
        o_sum.begin_x(0)
        o_sum.begin_y(0)

        x_sum.arrive()
        hidden = x_ref[...].astype(F32)
        normed_grad = x_sum.own(slice(None))
        inverse = lax.rsqrt(jnp.mean(hidden * hidden, axis=1, keepdims=True) + EPSILON)
        unitary = hidden * inverse
        gain_grad = jnp.sum(normed_grad * unitary, axis=0, keepdims=True)
        grad_scaled = normed_grad * gain_out[0:1, :]
        middle = jnp.mean(grad_scaled * unitary, axis=1, keepdims=True)
        dx_out[...] = (gall[rows_of(me), :].astype(F32) + inverse * (grad_scaled - unitary * middle)).astype(BF16)
        base_row = MODEL // TILE
        for i in range(base_row):
            parbuf[i : i + 1, :] = gain_grad[:, tile_of(i)]
        for i in range(nd + 2):
            parbuf[base_row + 8 * i : base_row + 8 * i + 8, :] = sums[:, tile_of(i)]
        lane_at = iota((1, TILE), 1)
        skip_row = jnp.zeros((1, TILE), F32)
        for i in range(nd):
            both = sums[1:2, tile_of(i)]
            for e in range(2):
                part = jnp.where(lax.div(lane_at, HEAD_DIM) == e, both, 0.0)
                skip_row = skip_row + jnp.where(lane_at == 2 * i + e, lane_sum(part), 0.0)
        heads[2:3, :] = skip_row
        parbuf[base_row + 8 * (nd + 2) :, :] = exact(heads[...], sel[...].astype(F32), ((1,), (1,)))
        small = [
            go(remote(parbuf, pard.at[k - 1], qd_s.at[k], qd_r.at[k], device)) for k, device, _ in lines
        ]
        w_sum.finish(1, wm_ref)
        send_rows(1)
        c_sum.pass_on(0)
        o_sum.pass_on(0)
        c_sum.finish(0, crows)
        for d in range(1, nz):
            to = lax.rem(z + d, nz)
            go(remote(crows.at[rows_of(to, rows), :], cheard.at[d - 1], sz_s.at[d], sz_r.at[d], (dp, c, to)))
        for copy in small:
            copy.wait_recv()
        total = parbuf[...]
        for k in range(nd - 1):
            total = total + pard[k]
        par_out[me] = total
        for j, step in enumerate(steps):
            go(remote(par_out.at[me], par_out.at[me], qg_s.at[j], qg_r.at[j], self.target(step)[0]))
        o_sum.finish(0, dwo_out)
        total = crows[rows_of(z, rows), :].astype(F32)
        for d in range(1, nz):
            remote(cheard.at[d - 1], cheard.at[d - 1], sz_s.at[d], sz_r.at[d], other).wait_recv()
            total = total + cheard[d - 1].astype(F32)
        dwc_out[...] = total
        for j, step in enumerate(steps):
            here = par_out.at[self.source(step)]
            remote(here, here, qg_s.at[j], qg_r.at[j], other).wait_recv()
        for m in range(nm):
            got = dw_out.at[m]

            @pl.when(m != me)
            def _():
                remote(got, got, vz_s.at[m], vz_r.at[m], other).wait_recv()
                remote(got, got, vz_s.at[m], vz_r.at[m], other).wait_send()

        for copy in started:
            copy.wait_send()
        x_sum.end_core()
        x_sum.end()
        w_sum.end()
        o_sum.end()
        c_sum.end()

    def forward_chunk(
        self, chunk, docs, starts, projm, projc, taps, sel, hp, chp,
        pre_sig, pre_bc, o, states, step_s, cum_s, scaled, st, state,
    ):
        nd, wide = self.nd, self.wide
        first = chunk * SPAN
        here = rows_of(chunk)
        lead = pl.ds(pl.multiple_of(chunk * SPAN, SPAN), SPAN + PAD)
        body = pl.ds(pl.multiple_of(chunk * SPAN + PAD, PAD), SPAN)
        lane = iota((SPAN, TILE), 1)
        row = iota((SPAN, TILE), 0)
        low = lane < HEAD_DIM
        begin_t = begin_at(first + row, starts, docs)
        begin_s = begin_at(first + lane, starts, docs)
        valid = [first + row - (KW - 1 - tap) >= begin_t for tap in range(KW)]
        sides = []
        for i in range(2):
            lanes = tile_of(i)
            value = conv_tile(projc[lead, lanes].astype(F32), taps, tile_of(nd + i), valid)
            pre_bc[here, lanes] = value
            sides.append((value * jax.nn.sigmoid(value)).astype(BF16))
        key_side, query_side = sides
        rate = dot(projc[body, 2 * TILE :], sel[...])
        step = softplus(rate + hp[0:1, :])
        log_decay = step * hp[1:2, :]
        cum = exact((lane <= row).astype(F32), log_decay)
        step_s[here, :] = step
        cum_s[here, :] = cum
        cum_t = cum.T
        shut = jnp.where((begin_t == begin_s) & (lane <= row), 0.0, NEG)
        inherits = (begin_t < first).astype(F32)
        begin_last = begin_at(jnp.full((SPAN, TILE), first + SPAN - 1, jnp.int32), starts, docs)
        last_same = (begin_t == begin_last).astype(F32)
        meet = dot(query_side, key_side, ((1,), (1,)))
        before = state[...]
        before_low = before.astype(BF16)
        states[chunk] = before_low
        carried_out = dot(query_side, before_low)
        squares = jnp.zeros((SPAN, TILE), F32)
        for i in range(nd):
            lanes = tile_of(i)
            pre = conv_tile(projm[lead, tile_of(nd + i)].astype(F32), taps, lanes, valid)
            pre_sig[here, lanes] = pre
            signal = pre * jax.nn.sigmoid(pre)
            cums = [head_col(cum, 2 * i), head_col(cum, 2 * i + 1)]
            stepx = jnp.where(low, head_col(step, 2 * i), head_col(step, 2 * i + 1))
            cumx = jnp.where(low, cums[0], cums[1])
            fed = stepx * signal
            fed_low = fed.astype(BF16)
            local = []
            for e in range(2):
                head = 2 * i + e
                kernel = jnp.exp(cums[e] - cum_t[head : head + 1, :] + shut)
                local.append(dot((kernel * meet).astype(BF16), fed_low))
            entry = jnp.exp(cumx) * inherits
            out = jnp.where(low, local[0], local[1]) + entry * carried_out[:, lanes]
            o[here, lanes] = out
            last = cumx[SPAN - 1 : SPAN, :]
            tail = jnp.exp((last - cumx) * last_same) * last_same
            state[:, lanes] = entry[SPAN - 1 : SPAN, :] * before[:, lanes] + dot(
                key_side, (tail * fed).astype(BF16), ((0,), (0,))
            )
            mixed = (out + chp[0:1, lanes] * signal) * chp[1:2, lanes]
            gate_in = projm[body, lanes].astype(F32)
            gated = mixed * (gate_in * jax.nn.sigmoid(gate_in))
            squares = squares + gated * gated
            scaled[here, lanes] = (gated * chp[2:3, lanes]).astype(BF16)
        st[0, pl.ds(chunk, 1), :] = lane_sum(squares).T[0:1, :]

    def backward_chunk(
        self, chunk, docs, starts, unit, projm, pre_sig, pre_bc, o, states, step_s, cum_s, dg, st, taps, sel,
        hp, chp, dcom, normed_out, sums, heads, dstate, dnext, projc,
    ):
        nd = self.nd
        first = chunk * SPAN
        here = rows_of(chunk)
        lead = pl.ds(pl.multiple_of(chunk * SPAN, SPAN), SPAN + PAD)
        body = pl.ds(pl.multiple_of(chunk * SPAN + PAD, PAD), SPAN)
        lane = iota((SPAN, TILE), 1)
        row = iota((SPAN, TILE), 0)
        low = lane < HEAD_DIM
        begin_t = begin_at(first + row, starts, docs)
        begin_s = begin_at(first + lane, starts, docs)
        shut = jnp.where((begin_t == begin_s) & (lane <= row), 0.0, NEG)
        inherits = (begin_t < first).astype(F32)
        begin_last = begin_at(jnp.full((SPAN, TILE), first + SPAN - 1, jnp.int32), starts, docs)
        last_same = (begin_t == begin_last).astype(F32)
        lower = (lane <= row).astype(F32)
        key_pre, query_pre = pre_bc[here, :TILE], pre_bc[here, TILE:]
        key_side = (key_pre * jax.nn.sigmoid(key_pre)).astype(BF16)
        query_side = (query_pre * jax.nn.sigmoid(query_pre)).astype(BF16)
        meet = dot(query_side, key_side, ((1,), (1,)))
        step, cum = step_s[here, :], cum_s[here, :]
        cum_t = cum.T
        square = jnp.broadcast_to(st[0, pl.ds(chunk, 1), :], (SPAN, TILE)).T
        cross = jnp.broadcast_to(st[1, pl.ds(chunk, 1), :], (SPAN, TILE)).T
        root = lax.rsqrt(square * unit + EPSILON)
        pull = root * root * root * cross * unit
        before_low = states[chunk]
        before = before_low.astype(F32)
        after = dstate[...]
        after_low = after.astype(BF16)
        carried_out = dot(query_side, before_low)
        from_state = dot(key_side, after_low)
        meet_grad = jnp.zeros((SPAN, SPAN), F32)
        cum_cols = jnp.zeros((SPAN, TILE), F32)
        cum_rows = jnp.zeros((8, SPAN), F32)
        step_cols = jnp.zeros((SPAN, TILE), F32)
        entered, tails = [], []
        head_rows = iota((8, SPAN), 0)
        next_rows = first + iota((SPAN + PAD, TILE), 0)
        next_begin = begin_at(next_rows, starts, docs)
        valid = [next_rows - (KW - 1 - tap) >= next_begin for tap in range(KW)]
        tail_row = row == SPAN - 1

        def conv_back(pre_grad, ext, lanes):
            sums[2:3, lanes] += jnp.sum(pre_grad, axis=0, keepdims=True)
            later = jnp.concatenate([pre_grad, dnext[:, lanes]], axis=0)
            dnext[:, lanes] = pre_grad[0:PAD, :]
            back_grad = jnp.zeros((SPAN, TILE), F32)
            for tap in range(KW):
                back = KW - 1 - tap
                masked = jnp.where(valid[tap], later, 0.0)
                moved = ext if back == 0 else pltpu.roll(ext, back, 0)
                sums[4 + tap : 5 + tap, lanes] += jnp.sum(masked[:SPAN] * moved[PAD:], axis=0, keepdims=True)
                ahead = masked if back == 0 else pltpu.roll(masked, SPAN + PAD - back, 0)
                back_grad = back_grad + ahead[:SPAN] * taps[tap : tap + 1, lanes]
            return back_grad

        for i in range(nd):
            lanes = tile_of(i)
            pre = pre_sig[here, lanes]
            gate_of = jax.nn.sigmoid(pre)
            signal = pre * gate_of
            gate_in = projm[body, lanes].astype(F32)
            gate_sig = jax.nn.sigmoid(gate_in)
            opened = gate_in * gate_sig
            mask = chp[1:2, lanes]
            mixed = (o[here, lanes] + chp[0:1, lanes] * signal) * mask
            gated = mixed * opened
            grad = dg[here, lanes]
            gain = chp[2:3, lanes]
            normed_out[here, lanes] = (gated * root * gain).astype(BF16)
            sums[0:1, lanes] += jnp.sum(grad * gated * root, axis=0, keepdims=True)
            gated_grad = root * grad * gain - gated * pull
            mixed_grad = gated_grad * opened * mask
            projm[body, lanes] = (
                gated_grad * mixed * (gate_sig * (1.0 + gate_in * (1.0 - gate_sig)))
            ).astype(BF16)
            sums[1:2, lanes] += jnp.sum(mixed_grad * signal, axis=0, keepdims=True)
            cums = [head_col(cum, 2 * i), head_col(cum, 2 * i + 1)]
            stepx = jnp.where(low, head_col(step, 2 * i), head_col(step, 2 * i + 1))
            cumx = jnp.where(low, cums[0], cums[1])
            fed = stepx * signal
            fed_low = fed.astype(BF16)
            out_grad = mixed_grad
            out_low = out_grad.astype(BF16)
            entry = jnp.exp(cumx) * inherits
            last = cumx[SPAN - 1 : SPAN, :]
            tail = jnp.exp((last - cumx) * last_same) * last_same
            backs = []
            for e in range(2):
                head = 2 * i + e
                kernel = jnp.exp(cums[e] - cum_t[head : head + 1, :] + shut)
                mix = kernel * meet
                half = low if e == 0 else jnp.logical_not(low)
                mix_grad = dot(jnp.where(half, out_grad, 0.0).astype(BF16), fed_low, ((1,), (1,)))
                meet_grad = meet_grad + kernel * mix_grad
                weight = mix * mix_grad
                cum_cols = cum_cols + jnp.where(lane == head, lane_sum(weight), 0.0)
                cum_rows = cum_rows + jnp.where(
                    head_rows == head, jnp.broadcast_to(jnp.sum(weight, axis=0, keepdims=True), (8, SPAN)), 0.0
                )
                backs.append(dot(mix.astype(BF16), out_low, ((0,), (0,))))
            entry_grad = entry * out_grad
            tail_fed = tail * fed
            entered.append(entry_grad.astype(BF16))
            tails.append(tail_fed.astype(BF16))
            fed_grad = jnp.where(low, backs[0], backs[1]) + tail * from_state[:, lanes]
            moved_in = entry_grad * carried_out[:, lanes]
            moved_out = tail_fed * from_state[:, lanes]
            direct = fed_grad * signal
            end = entry[SPAN - 1 : SPAN, :]
            kept = jnp.sum(after[:, lanes] * before[:, lanes], axis=0, keepdims=True) * end
            at_end = jnp.sum(moved_out, axis=0, keepdims=True) + kept
            local = moved_in - moved_out + jnp.where(tail_row, at_end, 0.0)
            for e in range(2):
                half = low if e == 0 else jnp.logical_not(low)
                place = lane == 2 * i + e
                cum_cols = cum_cols + jnp.where(place, lane_sum(jnp.where(half, local, 0.0)), 0.0)
                step_cols = step_cols + jnp.where(place, lane_sum(jnp.where(half, direct, 0.0)), 0.0)
            dstate[:, lanes] = end * after[:, lanes] + dot(query_side, entry_grad.astype(BF16), ((0,), (0,)))
            signal_grad = stepx * fed_grad + chp[0:1, lanes] * mixed_grad
            pre_grad = signal_grad * (gate_of * (1.0 + pre * (1.0 - gate_of)))
            cols = tile_of(nd + i)
            projm[body, cols] = conv_back(pre_grad, projm[lead, cols].astype(F32), lanes).astype(BF16)
        meet_low = meet_grad.astype(BF16)
        state_rows = ((1,), (1,))
        query_grad = dot(meet_low, key_side) + dot(jnp.concatenate(entered, axis=1), before_low, state_rows)
        key_grad = dot(meet_low, query_side, ((0,), (0,))) + dot(
            jnp.concatenate(tails, axis=1), after_low, state_rows
        )
        for i, (side_grad, side_pre) in enumerate(((key_grad, key_pre), (query_grad, query_pre))):
            back_grad = conv_back(side_grad * silu_slope(side_pre), projc[lead, tile_of(i)].astype(F32), tile_of(nd + i))
            dcom[here, tile_of(i)] = back_grad.astype(BF16)
        rows_t = jnp.concatenate([cum_rows, jnp.zeros((SPAN - 8, SPAN), F32)], axis=0).T
        decay_grad = exact(lower, cum_cols - rows_t, ((0,), (0,)))
        log_decay = step * hp[1:2, :]
        slope = 1.0 - jnp.exp(-step)
        rate_grad = (step_cols + decay_grad * hp[1:2, :]) * slope
        heads[0:1, :] += jnp.sum(rate_grad, axis=0, keepdims=True)
        heads[1:2, :] += jnp.sum(decay_grad * log_decay, axis=0, keepdims=True)
        dcom[here, 2 * TILE :] = dot(rate_grad.astype(BF16), sel[...], ((1,), (1,))).astype(BF16)

    def run(self, docs, *args):
        nd, nc, nz, nm, rows, span, wide = self.nd, self.nc, self.nz, self.nm, self.rows_in, self.span, self.wide
        like = jax.ShapeDtypeStruct
        block = (SPAN, MODEL)
        npar = MODEL // TILE + 8 * (nd + 2) + 8

        def low(*shape):
            return pltpu.VMEM(shape, BF16)

        def full(*shape):
            return pltpu.VMEM(shape, F32)

        pair = lambda *shape: [DMA(shape), DMA(shape)]
        return pl.pallas_call(
            functools.partial(self.kernel, docs),
            out_shape=[
                like(block, BF16),
                like(block, BF16),
                like((nm, rows, 2 * wide), BF16),
                like((rows, COMMON), F32),
                like((TILE, MODEL), BF16),
                like((nm, npar, TILE), F32),
            ],
            in_specs=[SM, SM] + [VM] * 9 + [ANY, ANY],
            out_specs=[VM] * 6,
            scratch_shapes=[
                low(span, MODEL), low(span, MODEL), low(nd, nm * rows, 2 * wide), low(MODEL, COMMON),
                low(nd, TILE, MODEL), low(nm * rows, 2 * wide), low(rows, COMMON), full(8, TILE),
                full(nd, 8, 2 * TILE), full(nm, nd, 8, 2 * TILE), full(8, CONV), low(PAD + span, 2 * wide),
                full(span, wide), full(span, wide), low(nm, STATE, wide),
                full(span, TILE), full(span, TILE), full(span, wide), low(span, wide), low(TILE, TILE),
                full(8, TILE), full(8, wide), full(STATE, wide), full(PAD, wide + 2 * TILE),
                full(nm - 1, 2, nm, TILE), full(2, nm, TILE), full(span, 2 * TILE), low(PAD + span, COMMON),
                full(8, wide + 2 * TILE),
                low(nm, *block), low(nz, *block), low(nz, *block), low(nz + 1, *block), low(nz + 1, *block),
                low(span, COMMON), full(8, wide + 2 * TILE), full(8, TILE), full(8, MODEL),
                low(nd * nc, nz * rows, COMMON), low(4, nz * rows, 2 * TILE),
                low(2, nz * rows, 2 * TILE), low(nz * rows, COMMON), low(nz - 1, rows, COMMON),
                low(4, nm * rows, wide), low(2, nm * rows, wide),
                low(2, TILE, MODEL // 2),
                full(nd - 1, npar, TILE), full(npar, TILE),
                *pair(nd), *pair(nm), *pair(nm), *pair(nz), *pair(4, nm), *pair(4, nz), *pair(4, 1), *pair(nd),
                *pair(nz), *pair(nz), *pair(nz), *pair(nz), *pair(nz), *pair(nz),
                *pair(nm), *pair(nz), *pair(nz), *pair(nz),
                *pair(nz), *pair(nz), *pair(nz), *pair(nd), *pair(1, 4), *pair(1, 2), *pair(nz),
                *pair(2, 4), *pair(2, 2), *pair(1, 4), *pair(1, 2), *pair(nm), *pair(nd), *pair(nm), DMA((4,)),
            ],
            compiler_params=pltpu.CompilerParams(
                collective_id=0, has_side_effects=True, vmem_limit_bytes=63 * 2**20
            ),
            name="first",
        )(*args)

    def finish_kernel(
        self, y, dx, dw, dwc, dwo, pars,
        y_out, dx_out, norm_out, in_out, tap_out, bias_out, step_out, rate_out, skip_out, gain_out, out_out, every, narrow,
    ):
        nd, nm, rows = self.nd, self.nm, self.rows_in
        dp, c, z = self.place()
        owner = dp * nm + c * self.nz + z
        own_conv = CONV // (nd * nm)
        base_row = MODEL // TILE
        y_out[...] = y[...]
        dx_out[...] = dx[...]
        out_out[...] = dwo[...].astype(F32)
        for m in range(nm):
            for i in range(2 * nd):
                in_out[:, tile_of(i * nm + m)] = dw[m, :, tile_of(i)].astype(F32)
        in_out[:, 2 * INNER :] = dwc[:, : EXTENT - 2 * INNER]
        summed = pars[0]
        for m in range(1, nm):
            summed = summed + pars[m]
        narrow[...] = summed[0:base_row, :]
        row = narrow[pl.ds(lax.div(owner, 2), 1), :]
        norm_out[...] = jnp.where(lax.rem(owner, 2) == 0, row[:, :rows], row[:, rows:])
        for i in range(nd):
            for m in range(nm):
                every[:, tile_of(i * nm + m)] = pars[m, base_row + 8 * i : base_row + 8 * i + 8, :]
        for i in range(2):
            at = base_row + 8 * (nd + i)
            every[:, tile_of(nd * nm + i)] = summed[at : at + 8, :]
        start = owner * own_conv
        window = every[:, pl.ds(pl.multiple_of(lax.div(start, TILE) * TILE, TILE), 2 * TILE)]
        window = pltpu.roll(window, lax.rem(2 * TILE - lax.rem(start, TILE), 2 * TILE), 1)
        tap_out[...] = window[4 : 4 + KW, :own_conv]
        bias_out[...] = window[2:3, :own_conv]
        at = base_row + 8 * (nd + 2)
        step_out[...] = summed[at : at + 1, :HEADS]
        rate_out[...] = summed[at + 1 : at + 2, :HEADS]
        skip_out[...] = summed[at + 2 : at + 3, :HEADS]
        mine = pars[lax.rem(owner, nm), pl.ds(pl.multiple_of(base_row + 8 * dp, 8), 8), :]
        gain_out[...] = mine[0:1, :]

    def finish(self, *args):
        nd, nm, rows = self.nd, self.nm, self.rows_in
        own_conv = CONV // (nd * nm)
        like = jax.ShapeDtypeStruct
        return pl.pallas_call(
            self.finish_kernel,
            out_shape=[
                like((SPAN, MODEL), BF16),
                like((SPAN, MODEL), BF16),
                like((1, rows), F32),
                like((rows, EXTENT), F32),
                like((KW, own_conv), F32),
                like((1, own_conv), F32),
                like((1, HEADS), F32),
                like((1, HEADS), F32),
                like((1, HEADS), F32),
                like((1, TILE), F32),
                like((TILE, MODEL), F32),
            ],
            in_specs=[VM] * 6,
            out_specs=[VM] * 11,
            scratch_shapes=[pltpu.VMEM((8, CONV), F32), pltpu.VMEM((MODEL // TILE, TILE), F32)],
            compiler_params=pltpu.CompilerParams(vmem_limit_bytes=63 * 2**20),
            name="finish",
        )(*args)

    def local(
        self, layer_input, out_grad, norm_gain, in_weight, conv_weight, conv_bias, step_bias, log_rate,
        skip_gain, gate_gain, out_weight, nest_level, doc_lengths,
    ):
        docs = doc_lengths.shape[1]
        x = layer_input.reshape(SPAN, MODEL)
        g = out_grad.reshape(SPAN, MODEL)
        parts = self.run(
            docs, doc_lengths, nest_level, x, conv_weight.T, conv_bias[None], norm_gain[None], gate_gain[None],
            step_bias[None], log_rate[None], skip_gain[None], in_weight, g, out_weight,
        )
        y_out, dx_out, norm, in_weight_grad, taps, bias, step, rate, skip, gain, dwo = self.finish(*parts)
        return (
            y_out.reshape(1, SPAN, MODEL),
            dx_out.reshape(1, SPAN, MODEL),
            norm[0],
            in_weight_grad,
            taps.T,
            bias[0],
            step[0],
            rate[0],
            skip[0],
            gain[0],
            dwo,
        )


def solution(mesh):
    shape = dict(mesh.shape)
    head_split = HeadSplit(shape["dp"], shape["seq"], shape["fsdp"])
    return jax.shard_map(
        head_split.local if head_split.fits() else token_split,
        mesh=mesh,
        in_specs=(
            P("dp", ("seq", "fsdp"), None),
            P("dp", ("seq", "fsdp"), None),
            P(("dp", "seq", "fsdp")),
            P(("dp", "seq", "fsdp"), None),
            P(("dp", "seq", "fsdp"), None),
            P(("dp", "seq", "fsdp")),
            P(),
            P(),
            P(),
            P(("dp", "seq", "fsdp")),
            P(("dp", "seq", "fsdp"), None),
            P("dp"),
            P("dp", None),
        ),
        out_specs=(
            P("dp", ("seq", "fsdp"), None),
            P("dp", ("seq", "fsdp"), None),
            P(("dp", "seq", "fsdp")),
            P(("dp", "seq", "fsdp"), None),
            P(("dp", "seq", "fsdp"), None),
            P(("dp", "seq", "fsdp")),
            P(),
            P(),
            P(),
            P(("dp", "seq", "fsdp")),
            P(("dp", "seq", "fsdp"), None),
        ),
        check_vma=False,
    )
```

```python
import functools

import jax
import jax.numpy as jnp
from jax import lax
from jax.experimental import pallas as pl
from jax.experimental.pallas import tpu as pltpu
from jax.sharding import PartitionSpec as P

HEADS = 64
HEAD_DIM = 64
STATE = 128
KW = 4
INNER = 4096
CONV = 4352
EXTENT = 8512


HIGH = lax.Precision.HIGHEST
EPSILON = 1e-05


def shifted(value, axis, steps):
    count = lax.axis_size(axis)
    leading, last = (max(0, -steps), min(count, count - steps))
    return lax.ppermute(value, axis, [(source, source + steps) for source in range(leading, last)])


def prefix(array, axis, combine, identity):
    peers, place = (lax.axis_size(axis), lax.axis_index(axis))
    everything = jax.tree.map(
        lambda part, kind: lax.all_gather(part.astype(kind), axis),
        array,
        (jnp.bfloat16, jnp.bfloat16),
    )
    start = jax.tree.map(
        lambda part, zero: jnp.broadcast_to(jnp.asarray(zero, part.dtype), part.shape),
        array,
        identity,
    )

    def prefix_lap(k, before):
        reached = k < place
        new = combine(
            before, jax.tree.map(lambda part, own: part[k].astype(own.dtype), everything, array)
        )
        return jax.tree.map(lambda a, b: jnp.where(reached, a, b), new, before)

    return lax.fori_loop(0, peers, prefix_lap, start)


def carried_in(array, axis, combine, identity):
    peers, place = (lax.axis_size(axis), lax.axis_index(axis))
    everything = jax.tree.map(
        lambda part, kind: lax.all_gather(part.astype(kind), axis),
        array,
        jax.tree.map(lambda a: jnp.bfloat16 if a.dtype == jnp.float32 else a.dtype, array),
    )
    start = jax.tree.map(
        lambda part, zero: jnp.broadcast_to(jnp.asarray(zero, part.dtype), part.shape),
        array,
        identity,
    )

    def carried_lap(k, before):
        at = peers - 1 - k
        reached = at > place
        new = combine(
            before, jax.tree.map(lambda part, own: part[at].astype(own.dtype), everything, array)
        )
        return jax.tree.map(lambda a, b: jnp.where(reached, a, b), new, before)

    return lax.fori_loop(0, peers, carried_lap, start)


def doc_begins(lengths, positions):
    places = jnp.arange(lengths.shape[1])
    ahead = places[:, None] < places[None, :]
    endings = jnp.sum(jnp.where(ahead[None], lengths[:, :, None], 0), axis=1)
    reached = endings[:, None, :] <= positions[None, :, None]
    return jnp.max(jnp.where(reached, endings[:, None, :], 0), axis=2)


def input_norm(hidden, gain):
    inv_rms = lax.rsqrt(jnp.mean(hidden * hidden, axis=1, keepdims=True) + EPSILON)
    return hidden * inv_rms * gain


def causal_conv(extended, taps, bias, validity):
    block_len = validity.shape[2]
    running = bias + jnp.zeros((extended.shape[0], block_len, extended.shape[2]), jnp.float32)
    for tap in range(taps.shape[1]):
        running = (
            running + extended[:, tap : tap + block_len] * taps[:, tap] * validity[tap][:, :, None]
        )
    return jax.nn.silu(running)


def scan_parts(signal, key_side, query_side, rate_in, step_bias, log_rate, begins, block_start):
    step = jax.nn.softplus(rate_in + step_bias)
    log_decay = step * -jnp.exp(log_rate)
    places = jnp.arange(log_decay.shape[1])
    lower = (places[None, :] <= places[:, None]).astype(jnp.float32)
    cumulative = jnp.einsum("ts,bsh->bth", lower, log_decay, precision=HIGH)
    by_head = jnp.swapaxes(cumulative, 1, 2)
    indices = jnp.arange(signal.shape[1])
    same_doc = (begins[:, :, None] == begins[:, None, :]) & (
        indices[None, None, :] <= indices[None, :, None]
    )
    gaps = by_head[:, :, :, None] - by_head[:, :, None, :]
    kernel = jnp.exp(jnp.where(same_doc[:, None], gaps, 0.0)) * same_doc[:, None]
    intersection = jnp.einsum("btn,bsn->bts", query_side, key_side, precision=HIGH)
    mixing = kernel * intersection[:, None] * jnp.swapaxes(step, 1, 2)[:, :, None, :]
    local_out = jnp.einsum("bhts,bshp->bthp", mixing, signal, precision=HIGH)
    inherits = (begins < block_start).astype(jnp.float32)
    carried = jnp.exp(cumulative) * inherits[:, :, None]
    last_same = begins == begins[:, -1:]
    tail_weight = (
        jnp.exp(jnp.where(last_same[:, :, None], cumulative[:, -1:] - cumulative, 0.0))
        * last_same[:, :, None]
        * step
    )
    fresh_state = jnp.einsum("bsh,bshp,bsn->bhpn", tail_weight, signal, key_side, precision=HIGH)
    return (local_out, carried, carried[:, -1], fresh_state)


def gated_norm(scan_out, signal, skip_gain, gate_in, gate_gain, head_mask, unit_count):
    mixed = (scan_out + skip_gain[:, None] * signal) * head_mask[:, None, :, None]
    gated = mixed.reshape(gate_in.shape) * jax.nn.silu(gate_in)
    mean_square = jnp.sum(gated * gated, axis=2, keepdims=True) / unit_count[:, None, None]
    return gated * lax.rsqrt(mean_square + EPSILON) * gate_gain


def combine_states(earlier, later):
    return (earlier[0] * later[0], later[1] + later[0][:, :, None, None] * earlier[1])


def token_split(
    layer_input,
    out_grad,
    norm_gain,
    in_weight,
    conv_weight,
    conv_bias,
    step_bias,
    log_rate,
    skip_gain,
    gate_gain,
    out_weight,
    nest_level,
    doc_lengths,
):
    seq_count, block_len, model_width = layer_input.shape
    token_count = seq_count * block_len
    gain_all, taps_all, bias_all, gate_all = (
        lax.all_gather(norm_gain, ("dp", "seq", "fsdp"), axis=0, tiled=True),
        lax.all_gather(conv_weight, ("dp", "seq", "fsdp"), axis=0, tiled=True),
        lax.all_gather(conv_bias, ("dp", "seq", "fsdp"), axis=0, tiled=True),
        lax.all_gather(gate_gain, ("dp", "seq", "fsdp"), axis=0, tiled=True),
    )
    block_start = lax.axis_index(("seq", "fsdp")) * block_len
    positions = block_start + jnp.arange(block_len, dtype=jnp.int32)
    begins = doc_begins(doc_lengths, positions)
    hidden = layer_input.reshape(token_count, model_width).astype(jnp.float32)
    normed = input_norm(hidden, gain_all).astype(jnp.bfloat16)
    columns = normed
    projected = jnp.dot(
        columns,
        lax.all_gather(in_weight, ("dp", "seq", "fsdp"), axis=0, tiled=True),
        preferred_element_type=jnp.float32,
    ).astype(jnp.bfloat16)
    projected = projected.reshape(seq_count, block_len, EXTENT)
    gate_in = projected[:, :, :INNER].astype(jnp.float32)
    conv_in = projected[:, :, INNER : INNER + CONV]
    rate_in = projected[:, :, INNER + CONV :].astype(jnp.float32)
    edge_rows = shifted(conv_in[:, block_len - (KW - 1) :], ("seq", "fsdp"), 1)
    extended = jnp.concatenate([edge_rows, conv_in], axis=1).astype(jnp.float32)
    validity = jnp.stack(
        [(positions[None, :] - (KW - 1) + tap >= begins).astype(jnp.float32) for tap in range(KW)]
    )
    activated, conv_pull = jax.vjp(
        lambda ext_in, taps, bias: causal_conv(ext_in, taps, bias, validity),
        extended,
        taps_all,
        bias_all,
    )
    signal = activated[:, :, :INNER].reshape(seq_count, block_len, HEADS, HEAD_DIM)
    key_side = activated[:, :, INNER : INNER + STATE]
    query_side = activated[:, :, INNER + STATE :]
    local_out, carried, decays, fresh_state = scan_parts(
        signal, key_side, query_side, rate_in, step_bias, log_rate, begins, block_start
    )
    identity = (jnp.ones_like(decays), jnp.zeros_like(fresh_state))
    entry_state = prefix((decays, fresh_state), ("seq", "fsdp"), combine_states, identity)[1]
    scan_out = local_out + carried[..., None] * jnp.einsum(
        "btn,bhpn->bthp", query_side, entry_state, precision=HIGH
    )
    active = jnp.right_shift(HEADS, 3 - nest_level)
    head_mask = (jnp.arange(HEADS)[None, :] < active[:, None]).astype(jnp.float32)
    unit_count = (active * HEAD_DIM).astype(jnp.float32)
    gate_normed, gate_pull = jax.vjp(
        lambda sv, xv, sk, gi, gg: gated_norm(sv, xv, sk, gi, gg, head_mask, unit_count),
        scan_out,
        signal,
        skip_gain,
        gate_in,
        gate_all,
    )
    normed_out = gate_normed.reshape(token_count, INNER).astype(jnp.bfloat16)
    columns = normed_out
    branch_out = jnp.dot(
        columns,
        lax.all_gather(out_weight, ("dp", "seq", "fsdp"), axis=0, tiled=True),
        preferred_element_type=jnp.float32,
    )
    layer_output = (
        (hidden + branch_out).astype(jnp.bfloat16).reshape(seq_count, block_len, model_width)
    )
    grad_flat = out_grad.reshape(token_count, model_width)
    grad_normed_out = lax.dot_general(
        grad_flat,
        lax.all_gather(out_weight, ("dp", "seq", "fsdp"), axis=0, tiled=True),
        (((1,), (1,)), ((), ())),
        preferred_element_type=jnp.float32,
    )
    grad_scan, grad_skip_signal, grad_skip, grad_gate_in, grad_gate_gain = gate_pull(
        grad_normed_out.reshape(seq_count, block_len, INNER)
    )
    lead_grad = jnp.einsum("bth,bthp,btn->bhpn", carried, grad_scan, query_side, precision=HIGH)
    later_grad = carried_in((decays, lead_grad), ("seq", "fsdp"), combine_states, identity)[1]

    def full_scan(signal_in, key_in, query_in, rate_values, bias_values, rate_logs):
        part_out, part_carried, part_decays, part_fresh = scan_parts(
            signal_in, key_in, query_in, rate_values, bias_values, rate_logs, begins, block_start
        )
        joined_out = part_out + part_carried[..., None] * jnp.einsum(
            "btn,bhpn->bthp", query_in, entry_state, precision=HIGH
        )
        return (joined_out, part_decays[:, :, None, None] * entry_state + part_fresh)

    scan_pull = jax.vjp(full_scan, signal, key_side, query_side, rate_in, step_bias, log_rate)[1]
    grad_signal, grad_key, grad_query, grad_rate, grad_step_bias, grad_log_rate = scan_pull(
        (grad_scan, later_grad)
    )
    grad_activated = jnp.concatenate(
        [
            (grad_signal + grad_skip_signal).reshape(seq_count, block_len, INNER),
            grad_key,
            grad_query,
        ],
        axis=2,
    )
    grad_extended, grad_taps, grad_bias = conv_pull(grad_activated)
    returned = shifted(grad_extended[:, : KW - 1].astype(jnp.bfloat16), ("seq", "fsdp"), -1).astype(
        jnp.float32
    )
    grad_conv_in = grad_extended[:, KW - 1 :] + jnp.pad(
        returned, ((0, 0), (block_len - (KW - 1), 0), (0, 0))
    )
    grad_projected = (
        jnp.concatenate([grad_gate_in, grad_conv_in, grad_rate], axis=2)
        .reshape(token_count, EXTENT)
        .astype(jnp.bfloat16)
    )
    grad_normed = lax.dot_general(
        grad_projected,
        lax.all_gather(in_weight, ("dp", "seq", "fsdp"), axis=0, tiled=True),
        (((1,), (1,)), ((), ())),
        preferred_element_type=jnp.float32,
    )
    replicas = lax.axis_size("dp")
    members = lax.axis_size(("seq", "fsdp"))
    width_in = model_width // lax.axis_size(("dp", "seq", "fsdp"))
    width_out = INNER // lax.axis_size(("dp", "seq", "fsdp"))
    in_cols, out_cols = (
        lax.all_to_all(
            normed.reshape(token_count, replicas, members, width_in),
            ("seq", "fsdp"),
            split_axis=2,
            concat_axis=0,
            tiled=True,
        ),
        lax.all_to_all(
            normed_out.reshape(token_count, replicas, members, width_out),
            ("seq", "fsdp"),
            split_axis=2,
            concat_axis=0,
            tiled=True,
        ),
    )
    in_cols = in_cols.reshape(members * token_count, replicas * width_in)
    out_cols = out_cols.reshape(members * token_count, replicas * width_out)
    in_new = lax.dot_general(
        in_cols,
        lax.all_gather(grad_projected, ("seq", "fsdp"), axis=0, tiled=True),
        (((0,), (0,)), ((), ())),
        preferred_element_type=jnp.float32,
    )
    out_new = lax.dot_general(
        out_cols,
        lax.all_gather(grad_flat, ("seq", "fsdp"), axis=0, tiled=True),
        (((0,), (0,)), ((), ())),
        preferred_element_type=jnp.float32,
    )
    in_weight_grad, out_weight_grad = (
        lax.psum_scatter(in_new.astype(jnp.bfloat16), "dp", scatter_dimension=0, tiled=True).astype(
            jnp.float32
        ),
        lax.psum_scatter(
            out_new.astype(jnp.bfloat16), "dp", scatter_dimension=0, tiled=True
        ).astype(jnp.float32),
    )
    norm_pull = jax.vjp(input_norm, hidden, gain_all)[1]
    grad_hidden, grad_gain = norm_pull(grad_normed)
    input_grad = (
        (grad_flat.astype(jnp.float32) + grad_hidden)
        .astype(jnp.bfloat16)
        .reshape(seq_count, block_len, model_width)
    )
    norm_gain_grad, conv_weight_grad, conv_bias_grad, gate_gain_grad = (
        lax.psum_scatter(grad_gain, ("dp", "seq", "fsdp"), scatter_dimension=0, tiled=True),
        lax.psum_scatter(grad_taps, ("dp", "seq", "fsdp"), scatter_dimension=0, tiled=True),
        lax.psum_scatter(grad_bias, ("dp", "seq", "fsdp"), scatter_dimension=0, tiled=True),
        lax.psum_scatter(grad_gate_gain, ("dp", "seq", "fsdp"), scatter_dimension=0, tiled=True),
    )
    step_bias_grad, log_rate_grad, skip_gain_grad = lax.psum(
        (grad_step_bias, grad_log_rate, grad_skip), ("dp", "seq", "fsdp")
    )
    return (
        layer_output,
        input_grad,
        norm_gain_grad,
        in_weight_grad,
        conv_weight_grad,
        conv_bias_grad,
        step_bias_grad,
        log_rate_grad,
        skip_gain_grad,
        gate_gain_grad,
        out_weight_grad,
    )


MESH = pl.DeviceIdType.MESH
F32 = jnp.float32
BF16 = jnp.bfloat16
TILE = 128
SPAN = 128
MODEL = 2048
COMMON = 384
PAD = 16
NEG = -1e30
SLOTS = (1, 4)
VM = pl.BlockSpec(memory_space=pltpu.VMEM)
SM = pl.BlockSpec(memory_space=pltpu.SMEM)
ANY = pl.BlockSpec(memory_space=pl.ANY)
DMA = pltpu.SemaphoreType.DMA


def remote(src, dst, sends, recvs, device):
    return pltpu.make_async_remote_copy(
        src_ref=src,
        dst_ref=dst,
        send_sem=sends,
        recv_sem=recvs,
        device_id=device,
        device_id_type=MESH,
    )


def dot(a, b, over=((1,), (0,))):
    return lax.dot_general(a, b, (over, ((), ())), preferred_element_type=F32)


def exact(a, b, over=((1,), (0,))):
    return lax.dot_general(a, b, (over, ((), ())), precision=HIGH, preferred_element_type=F32)


def begin_at(place, starts, docs):
    begin = jnp.zeros_like(place)
    for doc in range(1, docs):
        begin = jnp.where(starts[doc] <= place, starts[doc], begin)
    return begin


def iota(shape, dim):
    return lax.broadcasted_iota(jnp.int32, shape, dim)


def silu_slope(value):
    gate = jax.nn.sigmoid(value)
    return gate * (1.0 + value * (1.0 - gate))


def softplus(value):
    return jnp.maximum(value, 0.0) + jnp.log1p(jnp.exp(-jnp.abs(value)))


def conv_tile(extended, taps, lanes, valid):
    total = jnp.broadcast_to(taps[KW : KW + 1, lanes], (SPAN, TILE))
    for tap in range(KW):
        back = KW - 1 - tap
        moved = extended if back == 0 else pltpu.roll(extended, back, 0)
        total = total + jnp.where(valid[tap], moved[PAD:], 0.0) * taps[tap : tap + 1, lanes]
    return total


def tile_of(index):
    return slice(index * TILE, (index + 1) * TILE)


def rows_of(index, size=SPAN):
    return pl.ds(pl.multiple_of(index * size, size), size)


def head_col(values, head):
    return jnp.broadcast_to(values[:, head : head + 1], (SPAN, TILE))


def lane_sum(values):
    return jnp.broadcast_to(jnp.sum(values, axis=1, keepdims=True), values.shape)


class Line:
    def __init__(self, place, sizes, block, sems):
        self.dp, self.c, self.z = place
        self.nc, self.nz = sizes
        self.block = block
        self.right_s, self.right_r, self.left_s, self.left_r, self.core_s, self.core_r = sems

    def right(self, s):
        block = self.block(self.c, self.z - s)
        to = (self.dp, self.c, lax.rem(self.z + 1, self.nz))
        return remote(block, block, self.right_s.at[s], self.right_r.at[s], to)

    def left(self, s):
        block = self.block(self.c, self.z + s)
        to = (self.dp, self.c, lax.rem(self.z + self.nz - 1, self.nz))
        return remote(block, block, self.left_s.at[s], self.left_r.at[s], to)

    def core(self, z):
        block = self.block(self.c, z)
        to = (self.dp, self.nc - 1 - self.c, self.z)
        return remote(block, block, self.core_s.at[z], self.core_r.at[z], to)

    def across(self):
        return (self.dp, self.nc - 1 - self.c, self.z)

    def begin(self):
        pl.when(self.z < self.nz - 1)(lambda: self.right(0).start())
        pl.when(self.z > 0)(lambda: self.left(0).start())
        self.core(self.z).start()

    def step(self, s):
        z, nz = self.z, self.nz

        @pl.when(z >= s)
        def _():
            block = self.block(self.c, z - s)
            remote(block, block, self.right_s.at[s - 1], self.right_r.at[s - 1], self.across()).wait_recv()
            if s < nz - 1:
                pl.when(z < nz - 1)(lambda: self.right(s).start())
            self.core(z - s).start()

        @pl.when(z + s < nz)
        def _():
            block = self.block(self.c, z + s)
            remote(block, block, self.left_s.at[s - 1], self.left_r.at[s - 1], self.across()).wait_recv()
            if s < nz - 1:
                pl.when(z > 0)(lambda: self.left(s).start())
            self.core(z + s).start()

    def arrive(self):
        for z in range(self.nz):
            block = self.block(self.nc - 1 - self.c, z)
            to = (self.dp, self.nc - 1 - self.c, self.z)
            remote(block, block, self.core_s.at[z], self.core_r.at[z], to).wait_recv()

    def end(self):
        z, nz = self.z, self.nz
        for s in range(nz - 1):
            pl.when((z >= s) & (z < nz - 1))(lambda s=s: self.right(s).wait_send())
            pl.when((z + s < nz) & (z > 0))(lambda s=s: self.left(s).wait_send())
        for s in range(nz):
            self.core(jnp.int32(s)).wait_send()


class Sum:
    def __init__(self, place, sizes, part, came, total, heard, sems):
        self.dp, self.c, self.z = place
        self.nc, self.nz = sizes
        self.part, self.came, self.total, self.heard = part, came, total, heard
        self.core_s, self.core_r, self.right_s, self.right_r, self.left_s, self.left_r = sems

    def core(self, t):
        to = (self.dp, self.nc - 1 - self.c, self.z)
        src = self.part.at[(self.nc - 1 - self.c) * self.nz + t]
        return remote(src, self.came.at[t], self.core_s.at[t], self.core_r.at[t], to)

    def right(self, t):
        to = (self.dp, self.c, lax.rem(self.z + 1, self.nz))
        return remote(self.total.at[t], self.heard.at[t], self.right_s.at[t], self.right_r.at[t], to)

    def left(self, t, stops):
        slot = self.nz if stops else t
        to = (self.dp, self.c, lax.rem(self.z + self.nz - 1, self.nz))
        return remote(self.total.at[t], self.heard.at[slot], self.left_s.at[t], self.left_r.at[t], to)

    def add_core(self, t):
        self.core(t).wait_recv()

        def add(r, _):
            at = rows_of(r, 16)
            self.total[t, at, :] = (
                self.part[self.c * self.nz + t, at, :].astype(F32) + self.came[t, at, :].astype(F32)
            ).astype(BF16)
            return 0

        lax.fori_loop(0, SPAN // 16, add, 0)

    def add(self, t, slot):
        def add(r, _):
            at = rows_of(r, 16)
            self.total[t, at, :] = (
                self.total[t, at, :].astype(F32) + self.heard[slot, at, :].astype(F32)
            ).astype(BF16)
            return 0

        lax.fori_loop(0, SPAN // 16, add, 0)

    def begin(self):
        z, nz = self.z, self.nz
        pl.when(z == 0)(lambda: self.right(nz - 1).start())
        pl.when(z == nz - 1)(lambda: self.left(0, nz == 2).start())

    def slot(self, k):
        z, nz = self.z, self.nz
        for hop in range(1, k + 1):
            t = nz - 1 - (k - hop)
            if t > hop:

                @pl.when(z == hop)
                def _(t=t):
                    self.right(t).wait_recv()
                    self.add(t, t)
                    self.right(t).start()

                @pl.when(z == nz - 1 - hop)
                def _(u=nz - 1 - t, hop=hop):
                    self.left(u, False).wait_recv()
                    self.add(u, u)
                    self.left(u, u == nz - 2 - hop).start()

        @pl.when(z == 0)
        def _():
            self.right(nz - k).wait_send()
            self.right(nz - 1 - k).start()

        @pl.when(z == nz - 1)
        def _():
            self.left(k - 1, False).wait_send()
            self.left(k, k == nz - 2).start()

    def arrive(self):
        z, nz = self.z, self.nz
        for t in range(nz):
            pl.when((z == t) & (z > 0))(lambda t=t: self.right(t).wait_recv())
            pl.when((z == t) & (z < nz - 1))(lambda t=t: self.left(t, True).wait_recv())

    def own(self, rows):
        z, nz = self.z, self.nz
        value = self.total[z, rows, :].astype(F32)
        left = self.heard[z, rows, :].astype(F32)
        right = self.heard[nz, rows, :].astype(F32)
        value = value + jnp.where(z > 0, left, 0.0)
        return value + jnp.where(z < nz - 1, right, 0.0)

    def end_core(self):
        for t in range(self.nz):
            self.core(t).wait_send()

    def end(self):
        z, nz = self.z, self.nz
        for t in range(nz):
            right = (z < t) if t == 1 else (z < t) & (z > 0)
            left = (z > t) if t == nz - 2 else (z > t) & (z < nz - 1)
            pl.when(right)(lambda t=t: self.right(t).wait_send())
            pl.when(left)(lambda t=t: self.left(t, False).wait_send())


class Square:
    def __init__(self, place, block, size, sems):
        dp, c, z = place
        self.dp, self.dx, self.dy = dp, dp + 1 - 2 * lax.rem(dp, 2), lax.rem(dp + 2, 4)
        self.diag = lax.rem(self.dx + 2, 4)
        self.x, self.y = (self.dx, c, z), (self.dy, c, z)
        self.block = block
        self.half = size // 2
        self.sems = sems

    def copy(self, way, owner, piece, first, rows, to):
        block = self.block(owner, piece, first, rows)
        sends, recvs = self.sems
        return remote(block, block, sends.at[way, piece], recvs.at[way, piece], to)

    def whole(self, way, owner, piece):
        return self.copy(way, owner, piece, 0, 2 * self.half, self.x if way == 0 else self.y)

    def part(self, way, owner, piece):
        return self.copy(way, owner, piece, 0 if way == 2 else self.half, self.half, self.y if way == 2 else self.x)

    def begin(self, piece):
        self.whole(0, self.dp, piece).start()
        self.whole(1, self.dp, piece).start()

    def step(self, piece):
        self.whole(0, self.dx, piece).wait_recv()
        self.part(2, self.dx, piece).start()
        self.whole(1, self.dy, piece).wait_recv()
        self.part(3, self.dy, piece).start()

    def arrive(self, piece):
        self.part(2, self.diag, piece).wait_recv()
        self.part(3, self.diag, piece).wait_recv()

    def end(self, piece):
        self.whole(0, self.dp, piece).wait_send()
        self.whole(1, self.dp, piece).wait_send()
        self.part(2, self.dx, piece).wait_send()
        self.part(3, self.dy, piece).wait_send()


class SquareSum:
    def __init__(self, place, part, once, twice, gone, sems, pieces, index=lambda owner: owner, base=None):
        dp, c, z = place
        self.dp, self.dx, self.dy = dp, dp + 1 - 2 * lax.rem(dp, 2), lax.rem(dp + 2, 4)
        self.diag = lax.rem(self.dx + 2, 4)
        self.x, self.y = (self.dx, c, z), (self.dy, c, z)
        self.part, self.once, self.twice, self.gone = part, once, twice, gone
        self.s1, self.r1, self.s2, self.r2 = sems
        self.pieces, self.index, self.base = pieces, index, base
        self.rows = part.shape[1] // pieces
        cut = (part.shape[2] // TILE + 1) // 2 * TILE
        self.halves = (slice(0, cut), slice(cut, part.shape[2]))
        self.widths = (cut, part.shape[2] - cut)

    def heard(self, slot, start, size):
        width = self.widths[slot // 2]
        if self.base is None:
            return self.once.at[slot, pl.ds(start, size), :width]
        at = pl.multiple_of(self.base + slot * self.part.shape[1] + start, 16)
        return self.once.at[pl.ds(at, size), :width]

    def first(self, p, side, k):
        owner = ((self.dx, self.diag), (self.dy, self.diag))[side][k]
        at = pl.ds(p * self.rows, self.rows)
        slot = 2 * side + k
        return remote(
            self.part.at[self.index(owner), at, self.halves[side]], self.heard(slot, p * self.rows, self.rows),
            self.s1.at[p, slot], self.r1.at[p, slot], (self.x, self.y)[side],
        )

    def second(self, p, side):
        at = pl.ds(p * self.rows, self.rows)
        return remote(
            self.gone.at[at, self.halves[side]], self.twice.at[side, at, : self.widths[side]],
            self.s2.at[p, side], self.r2.at[p, side], (self.y, self.x)[side],
        )

    def begin_x(self, p):
        self.first(p, 0, 1).start()
        self.first(p, 0, 0).start()

    def begin_y(self, p):
        self.first(p, 1, 1).start()
        self.first(p, 1, 0).start()

    def each(self, p, body):
        def step(r, _):
            start = pl.multiple_of(p * self.rows + r * 16, 16)
            body(pl.ds(start, 16), start)
            return 0

        lax.fori_loop(0, self.rows // 16, step, 0)

    def pass_on(self, p):
        for side in range(2):
            self.first(p, side, 1).wait_recv()
            owner = (self.dy, self.dx)[side]

            def body(at, start, side=side, owner=owner):
                self.gone[at, self.halves[side]] = (
                    self.part[self.index(owner), at, self.halves[side]].astype(F32)
                    + self.heard(2 * side + 1, start, 16)[...].astype(F32)
                ).astype(BF16)

            self.each(p, body)
            self.second(p, side).start()

    def finish(self, p, out):
        for side in range(2):
            self.first(p, side, 0).wait_recv()
            self.second(p, side).wait_recv()

            def body(at, start, side=side):
                out[at, self.halves[side]] = (
                    self.part[self.index(self.dp), at, self.halves[side]].astype(F32)
                    + self.heard(2 * side, start, 16)[...].astype(F32)
                    + self.twice[side, at, : self.widths[side]].astype(F32)
                ).astype(out.dtype)

            self.each(p, body)

    def end(self):
        for p in range(self.pieces):
            for side in range(2):
                self.first(p, side, 0).wait_send()
                self.first(p, side, 1).wait_send()
                self.second(p, side).wait_send()


class HeadSplit:
    def __init__(self, nd, nc, nz):
        self.nd, self.nc, self.nz = nd, nc, nz
        self.nm = nc * nz
        self.span = self.nm * SPAN
        self.rows_in = MODEL // (nd * self.nm)
        self.wide = nd * TILE
        self.per = HEADS // (nd * self.nm)

    def fits(self):
        return (
            INNER == self.nd * self.nm * TILE and self.nd == 4 and self.nc == 2 and self.rows_in % 32 == 0
        )

    def place(self):
        return lax.axis_index("dp"), lax.axis_index("seq"), lax.axis_index("fsdp")

    def group_steps(self):
        return [(e, d) for d in range(self.nz) for e in range(self.nc) if e or d]

    def target(self, step):
        dp, c, z = self.place()
        ct, zt = lax.rem(c + step[0], self.nc), lax.rem(z + step[1], self.nz)
        return (dp, ct, zt), ct * self.nz + zt

    def source(self, step):
        dp, c, z = self.place()
        cs, zs = lax.rem(c + self.nc - step[0], self.nc), lax.rem(z + self.nz - step[1], self.nz)
        return cs * self.nz + zs

    def barrier(self):
        dp, c, z = self.place()
        sem = pltpu.get_barrier_semaphore()
        for step in self.group_steps():
            pl.semaphore_signal(sem, inc=1, device_id=self.target(step)[0], device_id_type=MESH)
        for k in range(1, self.nd):
            pl.semaphore_signal(
                sem, inc=1, device_id=(lax.rem(dp + k, self.nd), c, z), device_id_type=MESH
            )
        pl.semaphore_wait(sem, self.nm - 1 + self.nd - 1)

    def kernel(
        self, docs, lengths, level, x_ref, tap_ref, bias_ref, norm_ref, gain_ref, step_ref, rate_ref, skip_ref, in_ref, g_ref, wo_ref,
        y_out, dx_out, dw_out, dwc_out, dwo_out, par_out,
        xall, gall, wall, wcall, woall, wm_ref, wc_ref, head_ref, parbuf_, parall, every_par, projm, pre_sig, o, states,
        step_s, cum_s, dg, scaled, sel, hp, chp, state, dnext, heard_st, st, pre_bc, projc, taps,
        ypart, ycame, ytotal, yheard, xheard, dcom, sums, heads, gain_out,
        cpart, c1, c2, crows, cheard, w1, w2, o2, pard, parbuf,
        pd_s, pd_r, pg_s, pg_r, wz_s, wz_r, cz_s, cz_r, wq_s, wq_r, cq_s, cq_r, oq_s, oq_r, cc_s, cc_r,
        xr_s, xr_r, xl_s, xl_r, xc_s, xc_r, gr_s, gr_r, gl_s, gl_r, gc_s, gc_r,
        st_s, st_r, yc_s, yc_r, yr_s, yr_r, yl_s, yl_r,
        uc_s, uc_r, ur_s, ur_r, ul_s, ul_r, sc_s, sc_r, c1_s, c1_r, c2_s, c2_r, sz_s, sz_r,
        w1_s, w1_r, w2_s, w2_r, o1_s, o1_r, o2_s, o2_r, vz_s, vz_r, qd_s, qd_r, qg_s, qg_r, loc,
    ):
        nd, nc, nz, nm = self.nd, self.nc, self.nz, self.nm
        rows, wide = self.rows_in, self.wide
        where = dp, c, z = self.place()
        me = c * nz + z
        sizes = (nc, nz)
        steps = self.group_steps()
        other = (dp, nc - 1 - c, z)
        lines = [(k, (lax.rem(dp + k, nd), c, z), lax.rem(dp + nd - k, nd)) for k in range(1, nd)]
        started = []

        def go(copy):
            copy.start()
            started.append(copy)
            return copy

        def w_block(owner, m, first=0, count=rows):
            at = pl.multiple_of(m * rows + first, rows // 2)
            return wall.at[owner, pl.ds(at, count), :]

        def c_block(owner, m, first=0, count=rows):
            at = pl.multiple_of((owner * nm + m) * rows + first, rows // 2)
            return wcall.at[pl.ds(at, count), :]

        w_from = [me] + [self.source(step) for step in steps]
        c_from = [c * nz + lax.rem(z + nz - d, nz) for d in range(nz)]
        w_square = Square(
            where, lambda owner, j, first, count: w_block(owner, w_from[j], first, count), rows, (wq_s, wq_r)
        )
        c_square = Square(
            where, lambda owner, j, first, count: c_block(owner, c_from[j], first, count), rows, (cq_s, cq_r)
        )
        o_square = Square(
            where,
            lambda owner, j, first, count: woall.at[owner, pl.ds(first, count), :],
            TILE,
            (oq_s, oq_r),
        )
        x_line = Line(where, sizes, lambda a, b: xall.at[rows_of(a * nz + b), :], (xr_s, xr_r, xl_s, xl_r, xc_s, xc_r))
        g_line = Line(where, sizes, lambda a, b: gall.at[rows_of(a * nz + b), :], (gr_s, gr_r, gl_s, gl_r, gc_s, gc_r))
        y_sum = Sum(where, sizes, ypart, ycame, ytotal, yheard, (yc_s, yc_r, yr_s, yr_r, yl_s, yl_r))

        starts = [jnp.int32(0)]
        for doc in range(1, docs):
            starts.append(starts[-1] + lengths[0, doc - 1])
        active = jnp.right_shift(HEADS, 3 - level[0])
        unit = jnp.float32(1.0 / INNER)
        for smaller in range(3):
            unit = jnp.where(level[0] == smaller, jnp.float32(2.0 ** (3 - smaller) / INNER), unit)
        own_conv = CONV // (nd * nm)
        parbuf_[dp, 0:KW, :own_conv] = tap_ref[...]
        parbuf_[dp, KW : KW + 1, :own_conv] = bias_ref[...]
        parbuf_[dp, 5:6, :rows] = norm_ref[...]
        parbuf_[dp, 6:7, :TILE] = gain_ref[...]
        head_ref[...] = jnp.zeros_like(head_ref)
        head_ref[0:1, :HEADS] = step_ref[...]
        head_ref[1:2, :HEADS] = -jnp.exp(rate_ref[...])
        head_ref[2:3, :HEADS] = skip_ref[...]
        head_ref[3:4, :] = (iota((1, TILE), 1) < active).astype(F32)
        for m in range(nm):
            for i in range(2 * nd):
                wm_ref[m * rows : (m + 1) * rows, tile_of(i)] = in_ref[:, tile_of(i * nm + m)]
        shared = EXTENT - 2 * INNER
        wc_ref[:, 2 * TILE :] = jnp.zeros((rows, COMMON - 2 * TILE), BF16)
        wc_ref[:, : 2 * TILE] = in_ref[:, 2 * INNER : 2 * INNER + 2 * TILE]
        wc_ref[:, 2 * TILE : shared] = in_ref[:, 2 * INNER + 2 * TILE :]
        own = [
            pltpu.make_async_copy(wm_ref.at[rows_of(me, rows), :], w_block(dp, me), loc.at[0]),
            pltpu.make_async_copy(wc_ref, c_block(dp, me), loc.at[1]),
            pltpu.make_async_copy(wo_ref, woall.at[dp], loc.at[2]),
            pltpu.make_async_copy(g_ref, gall.at[rows_of(me), :], loc.at[3]),
        ]
        for copy in own:
            copy.start()
        self.barrier()
        for k, device, _ in lines:
            go(remote(parbuf_.at[dp], parbuf_.at[dp], pd_s.at[k], pd_r.at[k], device))
        for j, step in enumerate(steps):
            device, there = self.target(step)
            go(remote(wm_ref.at[rows_of(there, rows), :], w_block(dp, me), wz_s.at[j], wz_r.at[j], device))
            if step[0] == 0:
                go(remote(wc_ref, c_block(dp, me), cz_s.at[step[1]], cz_r.at[step[1]], device))
        for copy in own[:3]:
            copy.wait()
        o_square.begin(0)
        w_square.begin(0)
        c_square.begin(0)
        for k, device, frm in lines:
            remote(parbuf_.at[frm], parbuf_.at[frm], pd_s.at[k], pd_r.at[k], device).wait_recv()
        parall[me] = parbuf_[...]
        for j, step in enumerate(steps):
            device, _ = self.target(step)
            go(remote(parbuf_, parall.at[me], pg_s.at[j], pg_r.at[j], device))
        for j, step in enumerate(steps):
            device, _ = self.target(step)
            remote(parbuf_, parall.at[self.source(step)], pg_s.at[j], pg_r.at[j], device).wait_recv()
        owners = [(first // nm, first % nm) for first in range(nd * nm)]
        gain = jnp.concatenate([parall[m, d][5:6, :rows] for d, m in owners], axis=1)
        gain_out[...] = jnp.broadcast_to(gain, (8, MODEL))
        hidden = x_ref[...].astype(F32)
        inverse = lax.rsqrt(jnp.mean(hidden * hidden, axis=1, keepdims=True) + EPSILON)
        xall[rows_of(me), :] = (hidden * inverse * gain).astype(BF16)
        x_line.begin()

        for j, step in enumerate(steps):
            device, _ = self.target(step)
            block = w_block(dp, w_from[j + 1])
            remote(block, block, wz_s.at[j], wz_r.at[j], device).wait_recv()
            w_square.begin(j + 1)
            if step[0] == 0:
                d = step[1]
                block = c_block(dp, c_from[d])
                remote(block, block, cz_s.at[d], cz_r.at[d], device).wait_recv()
                c_square.begin(d)
            if j == 2:
                o_square.step(0)
                w_square.step(0)
                c_square.step(0)
        every_par[...] = jnp.concatenate([parall[m, d][:, :own_conv] for d, m in owners], axis=1)
        for i in range(nd):
            at = pl.ds(pl.multiple_of((i * nm + me) * TILE, TILE), TILE)
            taps[:, tile_of(i)] = every_par[:, at]
        taps[:, wide:] = every_par[:, INNER : INNER + 2 * TILE]
        head, lane = iota((TILE, TILE), 0), iota((TILE, TILE), 1)
        step_of = nm * self.per
        chosen = (head == lax.div(lane, self.per) * step_of + self.per * me + lax.rem(lane, self.per)) & (
            lane < nd * self.per
        )
        sel[...] = chosen.astype(BF16)
        hp[...] = exact(head_ref[...], chosen.astype(F32))
        for i in range(nd):
            chosen = head == i * step_of + self.per * me + lax.div(lane, HEAD_DIM)
            spread = exact(head_ref[...], chosen.astype(F32))
            chp[0:2, tile_of(i)] = spread[2:4, :]
            chp[2:3, tile_of(i)] = parbuf_[i][6:7, :TILE]
        x_line.step(1)
        own[3].wait()
        g_line.begin()
        for j in range(1, 4):
            w_square.step(j)
        for j in range(1, nz):
            c_square.step(j)
        x_line.step(2)
        for j in range(4, nm):
            w_square.step(j)
        x_line.step(3)
        for j in range(nz):
            c_square.arrive(j)
        for i in range(nd):
            at = pl.ds(pl.multiple_of((i * nm + c * nz) * rows, rows), nz * rows)
            go(remote(wcall.at[at, :], wcall.at[at, :], cc_s.at[i], cc_r.at[i], other))
        x_line.arrive()
        for j in range(nm):
            w_square.arrive(j)
        for i in range(nd):
            at = pl.ds(pl.multiple_of((i * nm + (nc - 1 - c) * nz) * rows, rows), nz * rows)
            remote(wcall.at[at, :], wcall.at[at, :], cc_s.at[i], cc_r.at[i], other).wait_recv()
        projm[0:PAD, :] = jnp.zeros((PAD, 2 * wide), BF16)
        projc[0:PAD, :] = jnp.zeros((PAD, COMMON), BF16)
        projc[PAD:, :] = dot(xall[...], wcall[...]).astype(BF16)

        def project(n, _):
            at = rows_of(n, 256)
            projm[PAD:, at] = dot(xall[...], wall[:, :, at].reshape(MODEL, 256)).astype(BF16)
            pl.when(n == 2)(lambda: g_line.step(1))
            return 0

        lax.fori_loop(0, 2 * wide // 256, project, 0)
        state[...] = jnp.zeros_like(state)

        def forward(i, _):
            self.forward_chunk(
                i, docs, starts, projm, projc, taps, sel, hp, chp,
                pre_sig, pre_bc, o, states, step_s, cum_s, scaled, st, state,
            )
            pl.when(i == 2)(lambda: g_line.step(2))
            pl.when(i == 6)(lambda: g_line.step(3))
            return 0

        lax.fori_loop(0, nm, forward, 0)

        o_square.arrive(0)

        def branch(pair):
            def some(n, _):
                t = pair + lax.rem(n, 2) * (nz - 1 - 2 * pair)
                turn = t + lax.rem(nc - 1 - c + lax.div(n, 2), nc) * nz
                ypart[turn] = dot(scaled[rows_of(turn), :], woall[...].reshape(wide, MODEL)).astype(BF16)
                pl.when(n < 2)(lambda: y_sum.core(t).start())
                return 0

            lax.fori_loop(0, 4, some, 0)

        branch(0)
        y_sum.add_core(0)
        y_sum.add_core(nz - 1)
        y_sum.begin()
        for pair in range(1, nz // 2):
            branch(pair)
            y_sum.add_core(pair)
            y_sum.add_core(nz - 1 - pair)

        g_line.arrive()
        lanes_at = iota((SPAN, TILE), 1)

        def gate_grad(n, _):
            at = rows_of(n, 512)
            grad = dot(gall[at, :], woall[...].reshape(wide, MODEL), ((1,), (1,)))
            dg[at, :] = grad
            for half in range(4):
                product = jnp.zeros((SPAN, TILE), F32)
                for i in range(nd):
                    mine = scaled[pl.ds(pl.multiple_of(n * 512 + half * SPAN, SPAN), SPAN), tile_of(i)]
                    product = product + mine.astype(F32) * grad[half * SPAN : (half + 1) * SPAN, tile_of(i)]
                st[1, pl.ds(4 * n + half, 1), :] = lane_sum(product).T[0:1, :]
            return 0

        lax.fori_loop(0, nm // 4, gate_grad, 0)
        sent = []
        for j, step in enumerate(steps):
            device, _ = self.target(step)
            sent.append(go(remote(st, heard_st.at[j], st_s.at[j], st_r.at[j], device)))

        totals = st[...]
        for j, copy in enumerate(sent):
            copy.wait_recv()
            totals = totals + heard_st[j]
        for copy in sent:
            copy.wait_send()
        st[...] = totals

        dnext[...] = jnp.zeros_like(dnext)
        state[...] = jnp.zeros_like(state)
        sums[...] = jnp.zeros_like(sums)
        heads[...] = jnp.zeros_like(heads)

        def backward(n, _):
            self.backward_chunk(
                nm - 1 - n, docs, starts, unit, projm, pre_sig, pre_bc, o, states, step_s, cum_s, dg, st, taps, sel,
                hp, chp, dcom, scaled, sums, heads, state, dnext, projc,
            )
            for k in range(1, nz - 1):
                pl.when(n == SLOTS[k - 1])(lambda k=k: y_sum.slot(k))
            return 0

        lax.fori_loop(0, nm, backward, 0)
        for copy in started:
            if not any(copy is s for s in sent):
                copy.wait_send()
        started.clear()
        for j in range(nm):
            w_square.end(j)
        for j in range(nz):
            c_square.end(j)
        o_square.end(0)
        x_line.end()
        g_line.end()

        x_sum = Sum(where, sizes, ypart, ycame, ytotal, xheard, (uc_s, uc_r, ur_s, ur_r, ul_s, ul_r))
        w_sum = SquareSum(where, wall, w1, w2, projm, (w1_s, w1_r, w2_s, w2_r), 2)
        o_sum = SquareSum(where, woall, xall, o2, xall, (o1_s, o1_r, o2_s, o2_r), 1, base=4 * TILE)
        c_sum = SquareSum(where, cpart, c1, c2, dcom, (c1_s, c1_r, c2_s, c2_r), 1, lambda owner: owner * nc + c)
        def input_grad(core):
            base = rows_of(core, nz * SPAN)
            lead = pl.ds(pl.multiple_of(core * nz * SPAN + PAD, PAD), nz * SPAN)

            def piece(n, _):
                at = rows_of(n, 256)
                part = dot(projm[lead, :], wall[lax.div(n, 2), rows_of(lax.rem(n, 2), 256), :], ((1,), (1,)))
                part = (part + dot(dcom[base, :], wcall[at, :], ((1,), (1,)))).astype(BF16)
                for t in range(nz):
                    ypart[core * nz + t, :, at] = part[t * SPAN : (t + 1) * SPAN, :]
                return 0

            lax.fori_loop(0, MODEL // 256, piece, 0)

        y_sum.end_core()
        input_grad(nc - 1 - c)
        for t in range(nz):
            x_sum.core(t).start()
        input_grad(c)
        y_sum.arrive()
        stat = jnp.broadcast_to(st[0, pl.ds(me, 1), :], (SPAN, TILE)).T
        root = lax.rsqrt(stat[:, 0:1] * unit + EPSILON)
        y_out[...] = (x_ref[...].astype(F32) + root * y_sum.own(slice(None))).astype(BF16)
        y_sum.end()
        x_sum.add_core(0)
        x_sum.add_core(nz - 1)
        x_sum.begin()
        for t in range(1, nz - 1):
            x_sum.add_core(t)

        def weight_grad(owner):
            def piece(n, _):
                at = pl.ds(pl.multiple_of(owner * (nm * rows) + n * 512, 512), 512)
                wall[owner, rows_of(n, 512), :] = dot(xall[:, at], projm[PAD:, :], ((0,), (0,))).astype(BF16)
                return 0

            lax.fori_loop(0, nm * rows // 512, piece, 0)

        weight_grad(w_sum.diag)
        weight_grad(w_sum.dx)
        w_sum.begin_x(0)
        weight_grad(w_sum.dy)
        w_sum.begin_y(0)
        weight_grad(dp)

        def shared_grad(n, _):
            at = rows_of(n, 256)
            cpart[n] = dot(xall[:, at], dcom[...], ((0,), (0,))).astype(BF16)
            return 0

        lax.fori_loop(0, nd * nc, shared_grad, 0)
        ccopies = [
            go(remote(cpart.at[i * nc + nc - 1 - c], projc.at[rows_of(i, nz * rows), :], sc_s.at[i], sc_r.at[i], other)) for i in range(nd)
        ]
        x_sum.slot(1)

        def out_grad(n, _):
            at = rows_of(n, 512)
            part = dot(scaled[...], gall[:, at], ((0,), (0,))).astype(BF16)
            for i in range(nd):
                woall[i, :, at] = part[tile_of(i), :]
            return 0

        lax.fori_loop(0, MODEL // 512, out_grad, 0)
        w_sum.pass_on(0)
        w_sum.begin_x(1)
        w_sum.begin_y(1)
        for i in range(nd):
            ccopies[i].wait_recv()
            cpart[i * nc + c] = (cpart[i * nc + c].astype(F32) + projc[rows_of(i, nz * rows), :].astype(F32)).astype(BF16)
        x_sum.slot(2)

        def send_rows(p):
            half = nm // 2
            for j in range(half):
                there = p * half + j
                block = wm_ref.at[there * rows : (there + 1) * rows, :]
                ct, zt = there // nz, there % nz

                @pl.when(there != me)
                def _():
                    remote(block, dw_out.at[me], vz_s.at[there], vz_r.at[me], (dp, ct, zt)).start()

                @pl.when(there == me)
                def _():
                    dw_out[there] = block[...]

        w_sum.finish(0, wm_ref)
        send_rows(0)
        w_sum.pass_on(1)
        c_sum.begin_x(0)
        c_sum.begin_y(0)
        o_sum.begin_x(0)
        o_sum.begin_y(0)

        x_sum.arrive()
        hidden = x_ref[...].astype(F32)
        normed_grad = x_sum.own(slice(None))
        inverse = lax.rsqrt(jnp.mean(hidden * hidden, axis=1, keepdims=True) + EPSILON)
        unitary = hidden * inverse
        gain_grad = jnp.sum(normed_grad * unitary, axis=0, keepdims=True)
        grad_scaled = normed_grad * gain_out[0:1, :]
        middle = jnp.mean(grad_scaled * unitary, axis=1, keepdims=True)
        dx_out[...] = (gall[rows_of(me), :].astype(F32) + inverse * (grad_scaled - unitary * middle)).astype(BF16)
        base_row = MODEL // TILE
        for i in range(base_row):
            parbuf[i : i + 1, :] = gain_grad[:, tile_of(i)]
        for i in range(nd + 2):
            parbuf[base_row + 8 * i : base_row + 8 * i + 8, :] = sums[:, tile_of(i)]
        lane_at = iota((1, TILE), 1)
        skip_row = jnp.zeros((1, TILE), F32)
        for i in range(nd):
            both = sums[1:2, tile_of(i)]
            for e in range(2):
                part = jnp.where(lax.div(lane_at, HEAD_DIM) == e, both, 0.0)
                skip_row = skip_row + jnp.where(lane_at == 2 * i + e, lane_sum(part), 0.0)
        heads[2:3, :] = skip_row
        parbuf[base_row + 8 * (nd + 2) :, :] = exact(heads[...], sel[...].astype(F32), ((1,), (1,)))
        small = [
            go(remote(parbuf, pard.at[k - 1], qd_s.at[k], qd_r.at[k], device)) for k, device, _ in lines
        ]
        w_sum.finish(1, wm_ref)
        send_rows(1)
        c_sum.pass_on(0)
        o_sum.pass_on(0)
        c_sum.finish(0, crows)
        for d in range(1, nz):
            to = lax.rem(z + d, nz)
            go(remote(crows.at[rows_of(to, rows), :], cheard.at[d - 1], sz_s.at[d], sz_r.at[d], (dp, c, to)))
        for copy in small:
            copy.wait_recv()
        total = parbuf[...]
        for k in range(nd - 1):
            total = total + pard[k]
        par_out[me] = total
        for j, step in enumerate(steps):
            go(remote(par_out.at[me], par_out.at[me], qg_s.at[j], qg_r.at[j], self.target(step)[0]))
        o_sum.finish(0, dwo_out)
        total = crows[rows_of(z, rows), :].astype(F32)
        for d in range(1, nz):
            remote(cheard.at[d - 1], cheard.at[d - 1], sz_s.at[d], sz_r.at[d], other).wait_recv()
            total = total + cheard[d - 1].astype(F32)
        dwc_out[...] = total
        for j, step in enumerate(steps):
            here = par_out.at[self.source(step)]
            remote(here, here, qg_s.at[j], qg_r.at[j], other).wait_recv()
        for m in range(nm):
            got = dw_out.at[m]

            @pl.when(m != me)
            def _():
                remote(got, got, vz_s.at[m], vz_r.at[m], other).wait_recv()
                remote(got, got, vz_s.at[m], vz_r.at[m], other).wait_send()

        for copy in started:
            copy.wait_send()
        x_sum.end_core()
        x_sum.end()
        w_sum.end()
        o_sum.end()
        c_sum.end()

    def forward_chunk(
        self, chunk, docs, starts, projm, projc, taps, sel, hp, chp,
        pre_sig, pre_bc, o, states, step_s, cum_s, scaled, st, state,
    ):
        nd, wide = self.nd, self.wide
        first = chunk * SPAN
        here = rows_of(chunk)
        lead = pl.ds(pl.multiple_of(chunk * SPAN, SPAN), SPAN + PAD)
        body = pl.ds(pl.multiple_of(chunk * SPAN + PAD, PAD), SPAN)
        lane = iota((SPAN, TILE), 1)
        row = iota((SPAN, TILE), 0)
        low = lane < HEAD_DIM
        begin_t = begin_at(first + row, starts, docs)
        begin_s = begin_at(first + lane, starts, docs)
        valid = [first + row - (KW - 1 - tap) >= begin_t for tap in range(KW)]
        sides = []
        for i in range(2):
            lanes = tile_of(i)
            value = conv_tile(projc[lead, lanes].astype(F32), taps, tile_of(nd + i), valid)
            pre_bc[here, lanes] = value
            sides.append((value * jax.nn.sigmoid(value)).astype(BF16))
        key_side, query_side = sides
        rate = dot(projc[body, 2 * TILE :], sel[...])
        step = softplus(rate + hp[0:1, :])
        log_decay = step * hp[1:2, :]
        cum = exact((lane <= row).astype(F32), log_decay)
        step_s[here, :] = step
        cum_s[here, :] = cum
        cum_t = cum.T
        shut = jnp.where((begin_t == begin_s) & (lane <= row), 0.0, NEG)
        inherits = (begin_t < first).astype(F32)
        begin_last = begin_at(jnp.full((SPAN, TILE), first + SPAN - 1, jnp.int32), starts, docs)
        last_same = (begin_t == begin_last).astype(F32)
        meet = dot(query_side, key_side, ((1,), (1,)))
        before = state[...]
        before_low = before.astype(BF16)
        states[chunk] = before_low
        carried_out = dot(query_side, before_low)
        squares = jnp.zeros((SPAN, TILE), F32)
        for i in range(nd):
            lanes = tile_of(i)
            pre = conv_tile(projm[lead, tile_of(nd + i)].astype(F32), taps, lanes, valid)
            pre_sig[here, lanes] = pre
            signal = pre * jax.nn.sigmoid(pre)
            cums = [head_col(cum, 2 * i), head_col(cum, 2 * i + 1)]
            stepx = jnp.where(low, head_col(step, 2 * i), head_col(step, 2 * i + 1))
            cumx = jnp.where(low, cums[0], cums[1])
            fed = stepx * signal
            fed_low = fed.astype(BF16)
            local = []
            for e in range(2):
                head = 2 * i + e
                kernel = jnp.exp(cums[e] - cum_t[head : head + 1, :] + shut)
                local.append(dot((kernel * meet).astype(BF16), fed_low))
            entry = jnp.exp(cumx) * inherits
            out = jnp.where(low, local[0], local[1]) + entry * carried_out[:, lanes]
            o[here, lanes] = out
            last = cumx[SPAN - 1 : SPAN, :]
            tail = jnp.exp((last - cumx) * last_same) * last_same
            state[:, lanes] = entry[SPAN - 1 : SPAN, :] * before[:, lanes] + dot(
                key_side, (tail * fed).astype(BF16), ((0,), (0,))
            )
            mixed = (out + chp[0:1, lanes] * signal) * chp[1:2, lanes]
            gate_in = projm[body, lanes].astype(F32)
            gated = mixed * (gate_in * jax.nn.sigmoid(gate_in))
            squares = squares + gated * gated
            scaled[here, lanes] = (gated * chp[2:3, lanes]).astype(BF16)
        st[0, pl.ds(chunk, 1), :] = lane_sum(squares).T[0:1, :]

    def backward_chunk(
        self, chunk, docs, starts, unit, projm, pre_sig, pre_bc, o, states, step_s, cum_s, dg, st, taps, sel,
        hp, chp, dcom, normed_out, sums, heads, dstate, dnext, projc,
    ):
        nd = self.nd
        first = chunk * SPAN
        here = rows_of(chunk)
        lead = pl.ds(pl.multiple_of(chunk * SPAN, SPAN), SPAN + PAD)
        body = pl.ds(pl.multiple_of(chunk * SPAN + PAD, PAD), SPAN)
        lane = iota((SPAN, TILE), 1)
        row = iota((SPAN, TILE), 0)
        low = lane < HEAD_DIM
        begin_t = begin_at(first + row, starts, docs)
        begin_s = begin_at(first + lane, starts, docs)
        shut = jnp.where((begin_t == begin_s) & (lane <= row), 0.0, NEG)
        inherits = (begin_t < first).astype(F32)
        begin_last = begin_at(jnp.full((SPAN, TILE), first + SPAN - 1, jnp.int32), starts, docs)
        last_same = (begin_t == begin_last).astype(F32)
        lower = (lane <= row).astype(F32)
        key_pre, query_pre = pre_bc[here, :TILE], pre_bc[here, TILE:]
        key_side = (key_pre * jax.nn.sigmoid(key_pre)).astype(BF16)
        query_side = (query_pre * jax.nn.sigmoid(query_pre)).astype(BF16)
        meet = dot(query_side, key_side, ((1,), (1,)))
        step, cum = step_s[here, :], cum_s[here, :]
        cum_t = cum.T
        square = jnp.broadcast_to(st[0, pl.ds(chunk, 1), :], (SPAN, TILE)).T
        cross = jnp.broadcast_to(st[1, pl.ds(chunk, 1), :], (SPAN, TILE)).T
        root = lax.rsqrt(square * unit + EPSILON)
        pull = root * root * root * cross * unit
        before_low = states[chunk]
        before = before_low.astype(F32)
        after = dstate[...]
        after_low = after.astype(BF16)
        carried_out = dot(query_side, before_low)
        from_state = dot(key_side, after_low)
        meet_grad = jnp.zeros((SPAN, SPAN), F32)
        cum_cols = jnp.zeros((SPAN, TILE), F32)
        cum_rows = jnp.zeros((8, SPAN), F32)
        step_cols = jnp.zeros((SPAN, TILE), F32)
        entered, tails = [], []
        head_rows = iota((8, SPAN), 0)
        next_rows = first + iota((SPAN + PAD, TILE), 0)
        next_begin = begin_at(next_rows, starts, docs)
        valid = [next_rows - (KW - 1 - tap) >= next_begin for tap in range(KW)]
        tail_row = row == SPAN - 1

        def conv_back(pre_grad, ext, lanes):
            sums[2:3, lanes] += jnp.sum(pre_grad, axis=0, keepdims=True)
            later = jnp.concatenate([pre_grad, dnext[:, lanes]], axis=0)
            dnext[:, lanes] = pre_grad[0:PAD, :]
            back_grad = jnp.zeros((SPAN, TILE), F32)
            for tap in range(KW):
                back = KW - 1 - tap
                masked = jnp.where(valid[tap], later, 0.0)
                moved = ext if back == 0 else pltpu.roll(ext, back, 0)
                sums[4 + tap : 5 + tap, lanes] += jnp.sum(masked[:SPAN] * moved[PAD:], axis=0, keepdims=True)
                ahead = masked if back == 0 else pltpu.roll(masked, SPAN + PAD - back, 0)
                back_grad = back_grad + ahead[:SPAN] * taps[tap : tap + 1, lanes]
            return back_grad

        for i in range(nd):
            lanes = tile_of(i)
            pre = pre_sig[here, lanes]
            gate_of = jax.nn.sigmoid(pre)
            signal = pre * gate_of
            gate_in = projm[body, lanes].astype(F32)
            gate_sig = jax.nn.sigmoid(gate_in)
            opened = gate_in * gate_sig
            mask = chp[1:2, lanes]
            mixed = (o[here, lanes] + chp[0:1, lanes] * signal) * mask
            gated = mixed * opened
            grad = dg[here, lanes]
            gain = chp[2:3, lanes]
            normed_out[here, lanes] = (gated * root * gain).astype(BF16)
            sums[0:1, lanes] += jnp.sum(grad * gated * root, axis=0, keepdims=True)
            gated_grad = root * grad * gain - gated * pull
            mixed_grad = gated_grad * opened * mask
            projm[body, lanes] = (
                gated_grad * mixed * (gate_sig * (1.0 + gate_in * (1.0 - gate_sig)))
            ).astype(BF16)
            sums[1:2, lanes] += jnp.sum(mixed_grad * signal, axis=0, keepdims=True)
            cums = [head_col(cum, 2 * i), head_col(cum, 2 * i + 1)]
            stepx = jnp.where(low, head_col(step, 2 * i), head_col(step, 2 * i + 1))
            cumx = jnp.where(low, cums[0], cums[1])
            fed = stepx * signal
            fed_low = fed.astype(BF16)
            out_grad = mixed_grad
            out_low = out_grad.astype(BF16)
            entry = jnp.exp(cumx) * inherits
            last = cumx[SPAN - 1 : SPAN, :]
            tail = jnp.exp((last - cumx) * last_same) * last_same
            backs = []
            for e in range(2):
                head = 2 * i + e
                kernel = jnp.exp(cums[e] - cum_t[head : head + 1, :] + shut)
                mix = kernel * meet
                half = low if e == 0 else jnp.logical_not(low)
                mix_grad = dot(jnp.where(half, out_grad, 0.0).astype(BF16), fed_low, ((1,), (1,)))
                meet_grad = meet_grad + kernel * mix_grad
                weight = mix * mix_grad
                cum_cols = cum_cols + jnp.where(lane == head, lane_sum(weight), 0.0)
                cum_rows = cum_rows + jnp.where(
                    head_rows == head, jnp.broadcast_to(jnp.sum(weight, axis=0, keepdims=True), (8, SPAN)), 0.0
                )
                backs.append(dot(mix.astype(BF16), out_low, ((0,), (0,))))
            entry_grad = entry * out_grad
            tail_fed = tail * fed
            entered.append(entry_grad.astype(BF16))
            tails.append(tail_fed.astype(BF16))
            fed_grad = jnp.where(low, backs[0], backs[1]) + tail * from_state[:, lanes]
            moved_in = entry_grad * carried_out[:, lanes]
            moved_out = tail_fed * from_state[:, lanes]
            direct = fed_grad * signal
            end = entry[SPAN - 1 : SPAN, :]
            kept = jnp.sum(after[:, lanes] * before[:, lanes], axis=0, keepdims=True) * end
            at_end = jnp.sum(moved_out, axis=0, keepdims=True) + kept
            local = moved_in - moved_out + jnp.where(tail_row, at_end, 0.0)
            for e in range(2):
                half = low if e == 0 else jnp.logical_not(low)
                place = lane == 2 * i + e
                cum_cols = cum_cols + jnp.where(place, lane_sum(jnp.where(half, local, 0.0)), 0.0)
                step_cols = step_cols + jnp.where(place, lane_sum(jnp.where(half, direct, 0.0)), 0.0)
            dstate[:, lanes] = end * after[:, lanes] + dot(query_side, entry_grad.astype(BF16), ((0,), (0,)))
            signal_grad = stepx * fed_grad + chp[0:1, lanes] * mixed_grad
            pre_grad = signal_grad * (gate_of * (1.0 + pre * (1.0 - gate_of)))
            cols = tile_of(nd + i)
            projm[body, cols] = conv_back(pre_grad, projm[lead, cols].astype(F32), lanes).astype(BF16)
        meet_low = meet_grad.astype(BF16)
        state_rows = ((1,), (1,))
        query_grad = dot(meet_low, key_side) + dot(jnp.concatenate(entered, axis=1), before_low, state_rows)
        key_grad = dot(meet_low, query_side, ((0,), (0,))) + dot(
            jnp.concatenate(tails, axis=1), after_low, state_rows
        )
        for i, (side_grad, side_pre) in enumerate(((key_grad, key_pre), (query_grad, query_pre))):
            back_grad = conv_back(side_grad * silu_slope(side_pre), projc[lead, tile_of(i)].astype(F32), tile_of(nd + i))
            dcom[here, tile_of(i)] = back_grad.astype(BF16)
        rows_t = jnp.concatenate([cum_rows, jnp.zeros((SPAN - 8, SPAN), F32)], axis=0).T
        decay_grad = exact(lower, cum_cols - rows_t, ((0,), (0,)))
        log_decay = step * hp[1:2, :]
        slope = 1.0 - jnp.exp(-step)
        rate_grad = (step_cols + decay_grad * hp[1:2, :]) * slope
        heads[0:1, :] += jnp.sum(rate_grad, axis=0, keepdims=True)
        heads[1:2, :] += jnp.sum(decay_grad * log_decay, axis=0, keepdims=True)
        dcom[here, 2 * TILE :] = dot(rate_grad.astype(BF16), sel[...], ((1,), (1,))).astype(BF16)

    def run(self, docs, *args):
        nd, nc, nz, nm, rows, span, wide = self.nd, self.nc, self.nz, self.nm, self.rows_in, self.span, self.wide
        like = jax.ShapeDtypeStruct
        block = (SPAN, MODEL)
        npar = MODEL // TILE + 8 * (nd + 2) + 8

        def low(*shape):
            return pltpu.VMEM(shape, BF16)

        def full(*shape):
            return pltpu.VMEM(shape, F32)

        pair = lambda *shape: [DMA(shape), DMA(shape)]
        return pl.pallas_call(
            functools.partial(self.kernel, docs),
            out_shape=[
                like(block, BF16),
                like(block, BF16),
                like((nm, rows, 2 * wide), BF16),
                like((rows, COMMON), F32),
                like((TILE, MODEL), BF16),
                like((nm, npar, TILE), F32),
            ],
            in_specs=[SM, SM] + [VM] * 9 + [ANY, ANY],
            out_specs=[VM] * 6,
            scratch_shapes=[
                low(span, MODEL), low(span, MODEL), low(nd, nm * rows, 2 * wide), low(MODEL, COMMON),
                low(nd, TILE, MODEL), low(nm * rows, 2 * wide), low(rows, COMMON), full(8, TILE),
                full(nd, 8, 2 * TILE), full(nm, nd, 8, 2 * TILE), full(8, CONV), low(PAD + span, 2 * wide),
                full(span, wide), full(span, wide), low(nm, STATE, wide),
                full(span, TILE), full(span, TILE), full(span, wide), low(span, wide), low(TILE, TILE),
                full(8, TILE), full(8, wide), full(STATE, wide), full(PAD, wide + 2 * TILE),
                full(nm - 1, 2, nm, TILE), full(2, nm, TILE), full(span, 2 * TILE), low(PAD + span, COMMON),
                full(8, wide + 2 * TILE),
                low(nm, *block), low(nz, *block), low(nz, *block), low(nz + 1, *block), low(nz + 1, *block),
                low(span, COMMON), full(8, wide + 2 * TILE), full(8, TILE), full(8, MODEL),
                low(nd * nc, nz * rows, COMMON), low(4, nz * rows, 2 * TILE),
                low(2, nz * rows, 2 * TILE), low(nz * rows, COMMON), low(nz - 1, rows, COMMON),
                low(4, nm * rows, wide), low(2, nm * rows, wide),
                low(2, TILE, MODEL // 2),
                full(nd - 1, npar, TILE), full(npar, TILE),
                *pair(nd), *pair(nm), *pair(nm), *pair(nz), *pair(4, nm), *pair(4, nz), *pair(4, 1), *pair(nd),
                *pair(nz), *pair(nz), *pair(nz), *pair(nz), *pair(nz), *pair(nz),
                *pair(nm), *pair(nz), *pair(nz), *pair(nz),
                *pair(nz), *pair(nz), *pair(nz), *pair(nd), *pair(1, 4), *pair(1, 2), *pair(nz),
                *pair(2, 4), *pair(2, 2), *pair(1, 4), *pair(1, 2), *pair(nm), *pair(nd), *pair(nm), DMA((4,)),
            ],
            compiler_params=pltpu.CompilerParams(
                collective_id=0, has_side_effects=True, vmem_limit_bytes=63 * 2**20
            ),
            name="first",
        )(*args)

    def finish_kernel(
        self, y, dx, dw, dwc, dwo, pars,
        y_out, dx_out, norm_out, in_out, tap_out, bias_out, step_out, rate_out, skip_out, gain_out, out_out, every, narrow,
    ):
        nd, nm, rows = self.nd, self.nm, self.rows_in
        dp, c, z = self.place()
        owner = dp * nm + c * self.nz + z
        own_conv = CONV // (nd * nm)
        base_row = MODEL // TILE
        y_out[...] = y[...]
        dx_out[...] = dx[...]
        out_out[...] = dwo[...].astype(F32)
        for m in range(nm):
            for i in range(2 * nd):
                in_out[:, tile_of(i * nm + m)] = dw[m, :, tile_of(i)].astype(F32)
        in_out[:, 2 * INNER :] = dwc[:, : EXTENT - 2 * INNER]
        summed = pars[0]
        for m in range(1, nm):
            summed = summed + pars[m]
        narrow[...] = summed[0:base_row, :]
        row = narrow[pl.ds(lax.div(owner, 2), 1), :]
        norm_out[...] = jnp.where(lax.rem(owner, 2) == 0, row[:, :rows], row[:, rows:])
        for i in range(nd):
            for m in range(nm):
                every[:, tile_of(i * nm + m)] = pars[m, base_row + 8 * i : base_row + 8 * i + 8, :]
        for i in range(2):
            at = base_row + 8 * (nd + i)
            every[:, tile_of(nd * nm + i)] = summed[at : at + 8, :]
        start = owner * own_conv
        window = every[:, pl.ds(pl.multiple_of(lax.div(start, TILE) * TILE, TILE), 2 * TILE)]
        window = pltpu.roll(window, lax.rem(2 * TILE - lax.rem(start, TILE), 2 * TILE), 1)
        tap_out[...] = window[4 : 4 + KW, :own_conv]
        bias_out[...] = window[2:3, :own_conv]
        at = base_row + 8 * (nd + 2)
        step_out[...] = summed[at : at + 1, :HEADS]
        rate_out[...] = summed[at + 1 : at + 2, :HEADS]
        skip_out[...] = summed[at + 2 : at + 3, :HEADS]
        mine = pars[lax.rem(owner, nm), pl.ds(pl.multiple_of(base_row + 8 * dp, 8), 8), :]
        gain_out[...] = mine[0:1, :]

    def finish(self, *args):
        nd, nm, rows = self.nd, self.nm, self.rows_in
        own_conv = CONV // (nd * nm)
        like = jax.ShapeDtypeStruct
        return pl.pallas_call(
            self.finish_kernel,
            out_shape=[
                like((SPAN, MODEL), BF16),
                like((SPAN, MODEL), BF16),
                like((1, rows), F32),
                like((rows, EXTENT), F32),
                like((KW, own_conv), F32),
                like((1, own_conv), F32),
                like((1, HEADS), F32),
                like((1, HEADS), F32),
                like((1, HEADS), F32),
                like((1, TILE), F32),
                like((TILE, MODEL), F32),
            ],
            in_specs=[VM] * 6,
            out_specs=[VM] * 11,
            scratch_shapes=[pltpu.VMEM((8, CONV), F32), pltpu.VMEM((MODEL // TILE, TILE), F32)],
            compiler_params=pltpu.CompilerParams(vmem_limit_bytes=63 * 2**20),
            name="finish",
        )(*args)

    def local(
        self, layer_input, out_grad, norm_gain, in_weight, conv_weight, conv_bias, step_bias, log_rate,
        skip_gain, gate_gain, out_weight, nest_level, doc_lengths,
    ):
        docs = doc_lengths.shape[1]
        x = layer_input.reshape(SPAN, MODEL)
        g = out_grad.reshape(SPAN, MODEL)
        parts = self.run(
            docs, doc_lengths, nest_level, x, conv_weight.T, conv_bias[None], norm_gain[None], gate_gain[None],
            step_bias[None], log_rate[None], skip_gain[None], in_weight, g, out_weight,
        )
        y_out, dx_out, norm, in_weight_grad, taps, bias, step, rate, skip, gain, dwo = self.finish(*parts)
        return (
            y_out.reshape(1, SPAN, MODEL),
            dx_out.reshape(1, SPAN, MODEL),
            norm[0],
            in_weight_grad,
            taps.T,
            bias[0],
            step[0],
            rate[0],
            skip[0],
            gain[0],
            dwo,
        )


def solution(mesh):
    shape = dict(mesh.shape)
    head_split = HeadSplit(shape["dp"], shape["seq"], shape["fsdp"])
    return jax.shard_map(
        head_split.local if head_split.fits() else token_split,
        mesh=mesh,
        in_specs=(
            P("dp", ("seq", "fsdp"), None),
            P("dp", ("seq", "fsdp"), None),
            P(("dp", "seq", "fsdp")),
            P(("dp", "seq", "fsdp"), None),
            P(("dp", "seq", "fsdp"), None),
            P(("dp", "seq", "fsdp")),
            P(),
            P(),
            P(),
            P(("dp", "seq", "fsdp")),
            P(("dp", "seq", "fsdp"), None),
            P("dp"),
            P("dp", None),
        ),
        out_specs=(
            P("dp", ("seq", "fsdp"), None),
            P("dp", ("seq", "fsdp"), None),
            P(("dp", "seq", "fsdp")),
            P(("dp", "seq", "fsdp"), None),
            P(("dp", "seq", "fsdp"), None),
            P(("dp", "seq", "fsdp")),
            P(),
            P(),
            P(),
            P(("dp", "seq", "fsdp")),
            P(("dp", "seq", "fsdp"), None),
        ),
        check_vma=False,
    )
```

```python
import functools

import jax
import jax.numpy as jnp
from jax import lax
from jax.experimental import pallas as pl
from jax.experimental.pallas import tpu as pltpu
from jax.sharding import PartitionSpec as P

HEADS = 64
HEAD_DIM = 64
STATE = 128
KW = 4
INNER = 4096
CONV = 4352
EXTENT = 8512


HIGH = lax.Precision.HIGHEST
EPSILON = 1e-05


def shifted(value, axis, steps):
    count = lax.axis_size(axis)
    leading, last = (max(0, -steps), min(count, count - steps))
    return lax.ppermute(value, axis, [(source, source + steps) for source in range(leading, last)])


def prefix(array, axis, combine, identity):
    peers, place = (lax.axis_size(axis), lax.axis_index(axis))
    everything = jax.tree.map(
        lambda part, kind: lax.all_gather(part.astype(kind), axis),
        array,
        (jnp.bfloat16, jnp.bfloat16),
    )
    start = jax.tree.map(
        lambda part, zero: jnp.broadcast_to(jnp.asarray(zero, part.dtype), part.shape),
        array,
        identity,
    )

    def prefix_lap(k, before):
        reached = k < place
        new = combine(
            before, jax.tree.map(lambda part, own: part[k].astype(own.dtype), everything, array)
        )
        return jax.tree.map(lambda a, b: jnp.where(reached, a, b), new, before)

    return lax.fori_loop(0, peers, prefix_lap, start)


def carried_in(array, axis, combine, identity):
    peers, place = (lax.axis_size(axis), lax.axis_index(axis))
    everything = jax.tree.map(
        lambda part, kind: lax.all_gather(part.astype(kind), axis),
        array,
        jax.tree.map(lambda a: jnp.bfloat16 if a.dtype == jnp.float32 else a.dtype, array),
    )
    start = jax.tree.map(
        lambda part, zero: jnp.broadcast_to(jnp.asarray(zero, part.dtype), part.shape),
        array,
        identity,
    )

    def carried_lap(k, before):
        at = peers - 1 - k
        reached = at > place
        new = combine(
            before, jax.tree.map(lambda part, own: part[at].astype(own.dtype), everything, array)
        )
        return jax.tree.map(lambda a, b: jnp.where(reached, a, b), new, before)

    return lax.fori_loop(0, peers, carried_lap, start)


def doc_begins(lengths, positions):
    places = jnp.arange(lengths.shape[1])
    ahead = places[:, None] < places[None, :]
    endings = jnp.sum(jnp.where(ahead[None], lengths[:, :, None], 0), axis=1)
    reached = endings[:, None, :] <= positions[None, :, None]
    return jnp.max(jnp.where(reached, endings[:, None, :], 0), axis=2)


def input_norm(hidden, gain):
    inv_rms = lax.rsqrt(jnp.mean(hidden * hidden, axis=1, keepdims=True) + EPSILON)
    return hidden * inv_rms * gain


def causal_conv(extended, taps, bias, validity):
    block_len = validity.shape[2]
    running = bias + jnp.zeros((extended.shape[0], block_len, extended.shape[2]), jnp.float32)
    for tap in range(taps.shape[1]):
        running = (
            running + extended[:, tap : tap + block_len] * taps[:, tap] * validity[tap][:, :, None]
        )
    return jax.nn.silu(running)


def scan_parts(signal, key_side, query_side, rate_in, step_bias, log_rate, begins, block_start):
    step = jax.nn.softplus(rate_in + step_bias)
    log_decay = step * -jnp.exp(log_rate)
    places = jnp.arange(log_decay.shape[1])
    lower = (places[None, :] <= places[:, None]).astype(jnp.float32)
    cumulative = jnp.einsum("ts,bsh->bth", lower, log_decay, precision=HIGH)
    by_head = jnp.swapaxes(cumulative, 1, 2)
    indices = jnp.arange(signal.shape[1])
    same_doc = (begins[:, :, None] == begins[:, None, :]) & (
        indices[None, None, :] <= indices[None, :, None]
    )
    gaps = by_head[:, :, :, None] - by_head[:, :, None, :]
    kernel = jnp.exp(jnp.where(same_doc[:, None], gaps, 0.0)) * same_doc[:, None]
    intersection = jnp.einsum("btn,bsn->bts", query_side, key_side, precision=HIGH)
    mixing = kernel * intersection[:, None] * jnp.swapaxes(step, 1, 2)[:, :, None, :]
    local_out = jnp.einsum("bhts,bshp->bthp", mixing, signal, precision=HIGH)
    inherits = (begins < block_start).astype(jnp.float32)
    carried = jnp.exp(cumulative) * inherits[:, :, None]
    last_same = begins == begins[:, -1:]
    tail_weight = (
        jnp.exp(jnp.where(last_same[:, :, None], cumulative[:, -1:] - cumulative, 0.0))
        * last_same[:, :, None]
        * step
    )
    fresh_state = jnp.einsum("bsh,bshp,bsn->bhpn", tail_weight, signal, key_side, precision=HIGH)
    return (local_out, carried, carried[:, -1], fresh_state)


def gated_norm(scan_out, signal, skip_gain, gate_in, gate_gain, head_mask, unit_count):
    mixed = (scan_out + skip_gain[:, None] * signal) * head_mask[:, None, :, None]
    gated = mixed.reshape(gate_in.shape) * jax.nn.silu(gate_in)
    mean_square = jnp.sum(gated * gated, axis=2, keepdims=True) / unit_count[:, None, None]
    return gated * lax.rsqrt(mean_square + EPSILON) * gate_gain


def combine_states(earlier, later):
    return (earlier[0] * later[0], later[1] + later[0][:, :, None, None] * earlier[1])


def token_split(
    layer_input,
    out_grad,
    norm_gain,
    in_weight,
    conv_weight,
    conv_bias,
    step_bias,
    log_rate,
    skip_gain,
    gate_gain,
    out_weight,
    nest_level,
    doc_lengths,
):
    seq_count, block_len, model_width = layer_input.shape
    token_count = seq_count * block_len
    gain_all, taps_all, bias_all, gate_all = (
        lax.all_gather(norm_gain, ("dp", "seq", "fsdp"), axis=0, tiled=True),
        lax.all_gather(conv_weight, ("dp", "seq", "fsdp"), axis=0, tiled=True),
        lax.all_gather(conv_bias, ("dp", "seq", "fsdp"), axis=0, tiled=True),
        lax.all_gather(gate_gain, ("dp", "seq", "fsdp"), axis=0, tiled=True),
    )
    block_start = lax.axis_index(("seq", "fsdp")) * block_len
    positions = block_start + jnp.arange(block_len, dtype=jnp.int32)
    begins = doc_begins(doc_lengths, positions)
    hidden = layer_input.reshape(token_count, model_width).astype(jnp.float32)
    normed = input_norm(hidden, gain_all).astype(jnp.bfloat16)
    columns = normed
    projected = jnp.dot(
        columns,
        lax.all_gather(in_weight, ("dp", "seq", "fsdp"), axis=0, tiled=True),
        preferred_element_type=jnp.float32,
    ).astype(jnp.bfloat16)
    projected = projected.reshape(seq_count, block_len, EXTENT)
    gate_in = projected[:, :, :INNER].astype(jnp.float32)
    conv_in = projected[:, :, INNER : INNER + CONV]
    rate_in = projected[:, :, INNER + CONV :].astype(jnp.float32)
    edge_rows = shifted(conv_in[:, block_len - (KW - 1) :], ("seq", "fsdp"), 1)
    extended = jnp.concatenate([edge_rows, conv_in], axis=1).astype(jnp.float32)
    validity = jnp.stack(
        [(positions[None, :] - (KW - 1) + tap >= begins).astype(jnp.float32) for tap in range(KW)]
    )
    activated, conv_pull = jax.vjp(
        lambda ext_in, taps, bias: causal_conv(ext_in, taps, bias, validity),
        extended,
        taps_all,
        bias_all,
    )
    signal = activated[:, :, :INNER].reshape(seq_count, block_len, HEADS, HEAD_DIM)
    key_side = activated[:, :, INNER : INNER + STATE]
    query_side = activated[:, :, INNER + STATE :]
    local_out, carried, decays, fresh_state = scan_parts(
        signal, key_side, query_side, rate_in, step_bias, log_rate, begins, block_start
    )
    identity = (jnp.ones_like(decays), jnp.zeros_like(fresh_state))
    entry_state = prefix((decays, fresh_state), ("seq", "fsdp"), combine_states, identity)[1]
    scan_out = local_out + carried[..., None] * jnp.einsum(
        "btn,bhpn->bthp", query_side, entry_state, precision=HIGH
    )
    active = jnp.right_shift(HEADS, 3 - nest_level)
    head_mask = (jnp.arange(HEADS)[None, :] < active[:, None]).astype(jnp.float32)
    unit_count = (active * HEAD_DIM).astype(jnp.float32)
    gate_normed, gate_pull = jax.vjp(
        lambda sv, xv, sk, gi, gg: gated_norm(sv, xv, sk, gi, gg, head_mask, unit_count),
        scan_out,
        signal,
        skip_gain,
        gate_in,
        gate_all,
    )
    normed_out = gate_normed.reshape(token_count, INNER).astype(jnp.bfloat16)
    columns = normed_out
    branch_out = jnp.dot(
        columns,
        lax.all_gather(out_weight, ("dp", "seq", "fsdp"), axis=0, tiled=True),
        preferred_element_type=jnp.float32,
    )
    layer_output = (
        (hidden + branch_out).astype(jnp.bfloat16).reshape(seq_count, block_len, model_width)
    )
    grad_flat = out_grad.reshape(token_count, model_width)
    grad_normed_out = lax.dot_general(
        grad_flat,
        lax.all_gather(out_weight, ("dp", "seq", "fsdp"), axis=0, tiled=True),
        (((1,), (1,)), ((), ())),
        preferred_element_type=jnp.float32,
    )
    grad_scan, grad_skip_signal, grad_skip, grad_gate_in, grad_gate_gain = gate_pull(
        grad_normed_out.reshape(seq_count, block_len, INNER)
    )
    lead_grad = jnp.einsum("bth,bthp,btn->bhpn", carried, grad_scan, query_side, precision=HIGH)
    later_grad = carried_in((decays, lead_grad), ("seq", "fsdp"), combine_states, identity)[1]

    def full_scan(signal_in, key_in, query_in, rate_values, bias_values, rate_logs):
        part_out, part_carried, part_decays, part_fresh = scan_parts(
            signal_in, key_in, query_in, rate_values, bias_values, rate_logs, begins, block_start
        )
        joined_out = part_out + part_carried[..., None] * jnp.einsum(
            "btn,bhpn->bthp", query_in, entry_state, precision=HIGH
        )
        return (joined_out, part_decays[:, :, None, None] * entry_state + part_fresh)

    scan_pull = jax.vjp(full_scan, signal, key_side, query_side, rate_in, step_bias, log_rate)[1]
    grad_signal, grad_key, grad_query, grad_rate, grad_step_bias, grad_log_rate = scan_pull(
        (grad_scan, later_grad)
    )
    grad_activated = jnp.concatenate(
        [
            (grad_signal + grad_skip_signal).reshape(seq_count, block_len, INNER),
            grad_key,
            grad_query,
        ],
        axis=2,
    )
    grad_extended, grad_taps, grad_bias = conv_pull(grad_activated)
    returned = shifted(grad_extended[:, : KW - 1].astype(jnp.bfloat16), ("seq", "fsdp"), -1).astype(
        jnp.float32
    )
    grad_conv_in = grad_extended[:, KW - 1 :] + jnp.pad(
        returned, ((0, 0), (block_len - (KW - 1), 0), (0, 0))
    )
    grad_projected = (
        jnp.concatenate([grad_gate_in, grad_conv_in, grad_rate], axis=2)
        .reshape(token_count, EXTENT)
        .astype(jnp.bfloat16)
    )
    grad_normed = lax.dot_general(
        grad_projected,
        lax.all_gather(in_weight, ("dp", "seq", "fsdp"), axis=0, tiled=True),
        (((1,), (1,)), ((), ())),
        preferred_element_type=jnp.float32,
    )
    replicas = lax.axis_size("dp")
    members = lax.axis_size(("seq", "fsdp"))
    width_in = model_width // lax.axis_size(("dp", "seq", "fsdp"))
    width_out = INNER // lax.axis_size(("dp", "seq", "fsdp"))
    in_cols, out_cols = (
        lax.all_to_all(
            normed.reshape(token_count, replicas, members, width_in),
            ("seq", "fsdp"),
            split_axis=2,
            concat_axis=0,
            tiled=True,
        ),
        lax.all_to_all(
            normed_out.reshape(token_count, replicas, members, width_out),
            ("seq", "fsdp"),
            split_axis=2,
            concat_axis=0,
            tiled=True,
        ),
    )
    in_cols = in_cols.reshape(members * token_count, replicas * width_in)
    out_cols = out_cols.reshape(members * token_count, replicas * width_out)
    in_new = lax.dot_general(
        in_cols,
        lax.all_gather(grad_projected, ("seq", "fsdp"), axis=0, tiled=True),
        (((0,), (0,)), ((), ())),
        preferred_element_type=jnp.float32,
    )
    out_new = lax.dot_general(
        out_cols,
        lax.all_gather(grad_flat, ("seq", "fsdp"), axis=0, tiled=True),
        (((0,), (0,)), ((), ())),
        preferred_element_type=jnp.float32,
    )
    in_weight_grad, out_weight_grad = (
        lax.psum_scatter(in_new.astype(jnp.bfloat16), "dp", scatter_dimension=0, tiled=True).astype(
            jnp.float32
        ),
        lax.psum_scatter(
            out_new.astype(jnp.bfloat16), "dp", scatter_dimension=0, tiled=True
        ).astype(jnp.float32),
    )
    norm_pull = jax.vjp(input_norm, hidden, gain_all)[1]
    grad_hidden, grad_gain = norm_pull(grad_normed)
    input_grad = (
        (grad_flat.astype(jnp.float32) + grad_hidden)
        .astype(jnp.bfloat16)
        .reshape(seq_count, block_len, model_width)
    )
    norm_gain_grad, conv_weight_grad, conv_bias_grad, gate_gain_grad = (
        lax.psum_scatter(grad_gain, ("dp", "seq", "fsdp"), scatter_dimension=0, tiled=True),
        lax.psum_scatter(grad_taps, ("dp", "seq", "fsdp"), scatter_dimension=0, tiled=True),
        lax.psum_scatter(grad_bias, ("dp", "seq", "fsdp"), scatter_dimension=0, tiled=True),
        lax.psum_scatter(grad_gate_gain, ("dp", "seq", "fsdp"), scatter_dimension=0, tiled=True),
    )
    step_bias_grad, log_rate_grad, skip_gain_grad = lax.psum(
        (grad_step_bias, grad_log_rate, grad_skip), ("dp", "seq", "fsdp")
    )
    return (
        layer_output,
        input_grad,
        norm_gain_grad,
        in_weight_grad,
        conv_weight_grad,
        conv_bias_grad,
        step_bias_grad,
        log_rate_grad,
        skip_gain_grad,
        gate_gain_grad,
        out_weight_grad,
    )


MESH = pl.DeviceIdType.MESH
F32 = jnp.float32
BF16 = jnp.bfloat16
TILE = 128
SPAN = 128
MODEL = 2048
COMMON = 384
PAD = 16
NEG = -1e30
SLOTS = (0, 3)
VM = pl.BlockSpec(memory_space=pltpu.VMEM)
SM = pl.BlockSpec(memory_space=pltpu.SMEM)
ANY = pl.BlockSpec(memory_space=pl.ANY)
DMA = pltpu.SemaphoreType.DMA


def remote(src, dst, sends, recvs, device):
    return pltpu.make_async_remote_copy(
        src_ref=src,
        dst_ref=dst,
        send_sem=sends,
        recv_sem=recvs,
        device_id=device,
        device_id_type=MESH,
    )


def dot(a, b, over=((1,), (0,))):
    return lax.dot_general(a, b, (over, ((), ())), preferred_element_type=F32)


def exact(a, b, over=((1,), (0,))):
    return lax.dot_general(a, b, (over, ((), ())), precision=HIGH, preferred_element_type=F32)


def begin_at(place, starts, docs):
    begin = jnp.zeros_like(place)
    for doc in range(1, docs):
        begin = jnp.where(starts[doc] <= place, starts[doc], begin)
    return begin


def iota(shape, dim):
    return lax.broadcasted_iota(jnp.int32, shape, dim)


def silu_slope(value):
    gate = jax.nn.sigmoid(value)
    return gate * (1.0 + value * (1.0 - gate))


def softplus(value):
    return jnp.maximum(value, 0.0) + jnp.log1p(jnp.exp(-jnp.abs(value)))


def conv_tile(extended, taps, lanes, valid):
    total = jnp.broadcast_to(taps[KW : KW + 1, lanes], (SPAN, TILE))
    for tap in range(KW):
        back = KW - 1 - tap
        moved = extended if back == 0 else pltpu.roll(extended, back, 0)
        total = total + jnp.where(valid[tap], moved[PAD:], 0.0) * taps[tap : tap + 1, lanes]
    return total


def tile_of(index):
    return slice(index * TILE, (index + 1) * TILE)


def rows_of(index, size=SPAN):
    return pl.ds(pl.multiple_of(index * size, size), size)


def head_col(values, head):
    return jnp.broadcast_to(values[:, head : head + 1], (SPAN, TILE))


def lane_sum(values):
    return jnp.broadcast_to(jnp.sum(values, axis=1, keepdims=True), values.shape)


class Line:
    def __init__(self, place, sizes, block, sems):
        self.dp, self.c, self.z = place
        self.nc, self.nz = sizes
        self.block = block
        self.right_s, self.right_r, self.left_s, self.left_r, self.core_s, self.core_r = sems

    def right(self, s):
        block = self.block(self.c, self.z - s)
        to = (self.dp, self.c, lax.rem(self.z + 1, self.nz))
        return remote(block, block, self.right_s.at[s], self.right_r.at[s], to)

    def left(self, s):
        block = self.block(self.c, self.z + s)
        to = (self.dp, self.c, lax.rem(self.z + self.nz - 1, self.nz))
        return remote(block, block, self.left_s.at[s], self.left_r.at[s], to)

    def core(self, z):
        block = self.block(self.c, z)
        to = (self.dp, self.nc - 1 - self.c, self.z)
        return remote(block, block, self.core_s.at[z], self.core_r.at[z], to)

    def across(self):
        return (self.dp, self.nc - 1 - self.c, self.z)

    def begin(self):
        pl.when(self.z < self.nz - 1)(lambda: self.right(0).start())
        pl.when(self.z > 0)(lambda: self.left(0).start())
        self.core(self.z).start()

    def step(self, s):
        z, nz = self.z, self.nz

        @pl.when(z >= s)
        def _():
            block = self.block(self.c, z - s)
            remote(block, block, self.right_s.at[s - 1], self.right_r.at[s - 1], self.across()).wait_recv()
            if s < nz - 1:
                pl.when(z < nz - 1)(lambda: self.right(s).start())
            self.core(z - s).start()

        @pl.when(z + s < nz)
        def _():
            block = self.block(self.c, z + s)
            remote(block, block, self.left_s.at[s - 1], self.left_r.at[s - 1], self.across()).wait_recv()
            if s < nz - 1:
                pl.when(z > 0)(lambda: self.left(s).start())
            self.core(z + s).start()

    def arrive(self):
        for z in range(self.nz):
            block = self.block(self.nc - 1 - self.c, z)
            to = (self.dp, self.nc - 1 - self.c, self.z)
            remote(block, block, self.core_s.at[z], self.core_r.at[z], to).wait_recv()

    def end(self):
        z, nz = self.z, self.nz
        for s in range(nz - 1):
            pl.when((z >= s) & (z < nz - 1))(lambda s=s: self.right(s).wait_send())
            pl.when((z + s < nz) & (z > 0))(lambda s=s: self.left(s).wait_send())
        for s in range(nz):
            self.core(jnp.int32(s)).wait_send()


class Sum:
    def __init__(self, place, sizes, part, came, total, heard, sems):
        self.dp, self.c, self.z = place
        self.nc, self.nz = sizes
        self.part, self.came, self.total, self.heard = part, came, total, heard
        self.core_s, self.core_r, self.right_s, self.right_r, self.left_s, self.left_r = sems

    def core(self, t):
        to = (self.dp, self.nc - 1 - self.c, self.z)
        src = self.part.at[(self.nc - 1 - self.c) * self.nz + t]
        return remote(src, self.came.at[t], self.core_s.at[t], self.core_r.at[t], to)

    def right(self, t):
        to = (self.dp, self.c, lax.rem(self.z + 1, self.nz))
        return remote(self.total.at[t], self.heard.at[t], self.right_s.at[t], self.right_r.at[t], to)

    def left(self, t, stops):
        slot = self.nz if stops else t
        to = (self.dp, self.c, lax.rem(self.z + self.nz - 1, self.nz))
        return remote(self.total.at[t], self.heard.at[slot], self.left_s.at[t], self.left_r.at[t], to)

    def add_core(self, t):
        self.core(t).wait_recv()

        def add(r, _):
            at = rows_of(r, 16)
            self.total[t, at, :] = (
                self.part[self.c * self.nz + t, at, :].astype(F32) + self.came[t, at, :].astype(F32)
            ).astype(BF16)
            return 0

        lax.fori_loop(0, SPAN // 16, add, 0)

    def add(self, t, slot):
        def add(r, _):
            at = rows_of(r, 16)
            self.total[t, at, :] = (
                self.total[t, at, :].astype(F32) + self.heard[slot, at, :].astype(F32)
            ).astype(BF16)
            return 0

        lax.fori_loop(0, SPAN // 16, add, 0)

    def begin(self):
        z, nz = self.z, self.nz
        pl.when(z == 0)(lambda: self.right(nz - 1).start())
        pl.when(z == nz - 1)(lambda: self.left(0, nz == 2).start())

    def slot(self, k):
        z, nz = self.z, self.nz
        for hop in range(1, k + 1):
            t = nz - 1 - (k - hop)
            if t > hop:

                @pl.when(z == hop)
                def _(t=t):
                    self.right(t).wait_recv()
                    self.add(t, t)
                    self.right(t).start()

                @pl.when(z == nz - 1 - hop)
                def _(u=nz - 1 - t, hop=hop):
                    self.left(u, False).wait_recv()
                    self.add(u, u)
                    self.left(u, u == nz - 2 - hop).start()

        @pl.when(z == 0)
        def _():
            self.right(nz - k).wait_send()
            self.right(nz - 1 - k).start()

        @pl.when(z == nz - 1)
        def _():
            self.left(k - 1, False).wait_send()
            self.left(k, k == nz - 2).start()

    def arrive(self):
        z, nz = self.z, self.nz
        for t in range(nz):
            pl.when((z == t) & (z > 0))(lambda t=t: self.right(t).wait_recv())
            pl.when((z == t) & (z < nz - 1))(lambda t=t: self.left(t, True).wait_recv())

    def own(self, rows):
        z, nz = self.z, self.nz
        value = self.total[z, rows, :].astype(F32)
        left = self.heard[z, rows, :].astype(F32)
        right = self.heard[nz, rows, :].astype(F32)
        value = value + jnp.where(z > 0, left, 0.0)
        return value + jnp.where(z < nz - 1, right, 0.0)

    def end_core(self):
        for t in range(self.nz):
            self.core(t).wait_send()

    def end(self):
        z, nz = self.z, self.nz
        for t in range(nz):
            right = (z < t) if t == 1 else (z < t) & (z > 0)
            left = (z > t) if t == nz - 2 else (z > t) & (z < nz - 1)
            pl.when(right)(lambda t=t: self.right(t).wait_send())
            pl.when(left)(lambda t=t: self.left(t, False).wait_send())


class Square:
    def __init__(self, place, block, size, sems):
        dp, c, z = place
        self.dp, self.dx, self.dy = dp, dp + 1 - 2 * lax.rem(dp, 2), lax.rem(dp + 2, 4)
        self.diag = lax.rem(self.dx + 2, 4)
        self.x, self.y = (self.dx, c, z), (self.dy, c, z)
        self.block = block
        self.half = size // 2
        self.sems = sems

    def copy(self, way, owner, piece, first, rows, to):
        block = self.block(owner, piece, first, rows)
        sends, recvs = self.sems
        return remote(block, block, sends.at[way, piece], recvs.at[way, piece], to)

    def whole(self, way, owner, piece):
        return self.copy(way, owner, piece, 0, 2 * self.half, self.x if way == 0 else self.y)

    def part(self, way, owner, piece):
        return self.copy(way, owner, piece, 0 if way == 2 else self.half, self.half, self.y if way == 2 else self.x)

    def begin(self, piece):
        self.whole(0, self.dp, piece).start()
        self.whole(1, self.dp, piece).start()

    def step(self, piece):
        self.whole(0, self.dx, piece).wait_recv()
        self.part(2, self.dx, piece).start()
        self.whole(1, self.dy, piece).wait_recv()
        self.part(3, self.dy, piece).start()

    def arrive(self, piece):
        self.part(2, self.diag, piece).wait_recv()
        self.part(3, self.diag, piece).wait_recv()

    def end(self, piece):
        self.whole(0, self.dp, piece).wait_send()
        self.whole(1, self.dp, piece).wait_send()
        self.part(2, self.dx, piece).wait_send()
        self.part(3, self.dy, piece).wait_send()


class SquareSum:
    def __init__(self, place, part, once, twice, gone, sems, pieces, index=lambda owner: owner, base=None):
        dp, c, z = place
        self.dp, self.dx, self.dy = dp, dp + 1 - 2 * lax.rem(dp, 2), lax.rem(dp + 2, 4)
        self.diag = lax.rem(self.dx + 2, 4)
        self.x, self.y = (self.dx, c, z), (self.dy, c, z)
        self.part, self.once, self.twice, self.gone = part, once, twice, gone
        self.s1, self.r1, self.s2, self.r2 = sems
        self.pieces, self.index, self.base = pieces, index, base
        self.rows = part.shape[1] // pieces
        cut = (part.shape[2] // TILE + 1) // 2 * TILE
        self.halves = (slice(0, cut), slice(cut, part.shape[2]))
        self.widths = (cut, part.shape[2] - cut)

    def heard(self, slot, start, size):
        width = self.widths[slot // 2]
        if self.base is None:
            return self.once.at[slot, pl.ds(start, size), :width]
        at = pl.multiple_of(self.base + slot * self.part.shape[1] + start, 16)
        return self.once.at[pl.ds(at, size), :width]

    def first(self, p, side, k):
        owner = ((self.dx, self.diag), (self.dy, self.diag))[side][k]
        at = pl.ds(p * self.rows, self.rows)
        slot = 2 * side + k
        return remote(
            self.part.at[self.index(owner), at, self.halves[side]], self.heard(slot, p * self.rows, self.rows),
            self.s1.at[p, slot], self.r1.at[p, slot], (self.x, self.y)[side],
        )

    def second(self, p, side):
        at = pl.ds(p * self.rows, self.rows)
        return remote(
            self.gone.at[at, self.halves[side]], self.twice.at[side, at, : self.widths[side]],
            self.s2.at[p, side], self.r2.at[p, side], (self.y, self.x)[side],
        )

    def begin_x(self, p):
        self.first(p, 0, 1).start()
        self.first(p, 0, 0).start()

    def begin_y(self, p):
        self.first(p, 1, 1).start()
        self.first(p, 1, 0).start()

    def each(self, p, body):
        def step(r, _):
            start = pl.multiple_of(p * self.rows + r * 16, 16)
            body(pl.ds(start, 16), start)
            return 0

        lax.fori_loop(0, self.rows // 16, step, 0)

    def pass_on(self, p):
        for side in range(2):
            self.first(p, side, 1).wait_recv()
            owner = (self.dy, self.dx)[side]

            def body(at, start, side=side, owner=owner):
                self.gone[at, self.halves[side]] = (
                    self.part[self.index(owner), at, self.halves[side]].astype(F32)
                    + self.heard(2 * side + 1, start, 16)[...].astype(F32)
                ).astype(BF16)

            self.each(p, body)
            self.second(p, side).start()

    def finish(self, p, out):
        for side in range(2):
            self.first(p, side, 0).wait_recv()
            self.second(p, side).wait_recv()

            def body(at, start, side=side):
                out[at, self.halves[side]] = (
                    self.part[self.index(self.dp), at, self.halves[side]].astype(F32)
                    + self.heard(2 * side, start, 16)[...].astype(F32)
                    + self.twice[side, at, : self.widths[side]].astype(F32)
                ).astype(out.dtype)

            self.each(p, body)

    def end(self):
        for p in range(self.pieces):
            for side in range(2):
                self.first(p, side, 0).wait_send()
                self.first(p, side, 1).wait_send()
                self.second(p, side).wait_send()


class HeadSplit:
    def __init__(self, nd, nc, nz):
        self.nd, self.nc, self.nz = nd, nc, nz
        self.nm = nc * nz
        self.span = self.nm * SPAN
        self.rows_in = MODEL // (nd * self.nm)
        self.wide = nd * TILE
        self.per = HEADS // (nd * self.nm)

    def fits(self):
        return (
            INNER == self.nd * self.nm * TILE and self.nd == 4 and self.nc == 2 and self.rows_in % 32 == 0
        )

    def place(self):
        return lax.axis_index("dp"), lax.axis_index("seq"), lax.axis_index("fsdp")

    def group_steps(self):
        return [(e, d) for d in range(self.nz) for e in range(self.nc) if e or d]

    def target(self, step):
        dp, c, z = self.place()
        ct, zt = lax.rem(c + step[0], self.nc), lax.rem(z + step[1], self.nz)
        return (dp, ct, zt), ct * self.nz + zt

    def source(self, step):
        dp, c, z = self.place()
        cs, zs = lax.rem(c + self.nc - step[0], self.nc), lax.rem(z + self.nz - step[1], self.nz)
        return cs * self.nz + zs

    def barrier(self):
        dp, c, z = self.place()
        sem = pltpu.get_barrier_semaphore()
        for step in self.group_steps():
            pl.semaphore_signal(sem, inc=1, device_id=self.target(step)[0], device_id_type=MESH)
        for k in range(1, self.nd):
            pl.semaphore_signal(
                sem, inc=1, device_id=(lax.rem(dp + k, self.nd), c, z), device_id_type=MESH
            )
        pl.semaphore_wait(sem, self.nm - 1 + self.nd - 1)

    def kernel(
        self, docs, lengths, level, x_ref, tap_ref, bias_ref, norm_ref, gain_ref, step_ref, rate_ref, skip_ref, in_ref, g_ref, wo_ref,
        y_out, dx_out, dw_out, dwc_out, dwo_out, par_out,
        xall, gall, wall, wcall, woall, wm_ref, wc_ref, head_ref, parbuf_, parall, every_par, projm, pre_sig, o, states,
        step_s, cum_s, dg, scaled, sel, hp, chp, state, dnext, heard_st, st, pre_bc, projc, taps,
        ypart, ycame, ytotal, yheard, xheard, dcom, sums, heads, gain_out,
        cpart, c1, c2, crows, cheard, w1, w2, o2, pard, parbuf,
        pd_s, pd_r, pg_s, pg_r, wz_s, wz_r, cz_s, cz_r, wq_s, wq_r, cq_s, cq_r, oq_s, oq_r, cc_s, cc_r,
        xr_s, xr_r, xl_s, xl_r, xc_s, xc_r, gr_s, gr_r, gl_s, gl_r, gc_s, gc_r,
        st_s, st_r, yc_s, yc_r, yr_s, yr_r, yl_s, yl_r,
        uc_s, uc_r, ur_s, ur_r, ul_s, ul_r, sc_s, sc_r, c1_s, c1_r, c2_s, c2_r, sz_s, sz_r,
        w1_s, w1_r, w2_s, w2_r, o1_s, o1_r, o2_s, o2_r, vz_s, vz_r, qd_s, qd_r, qg_s, qg_r, loc,
    ):
        nd, nc, nz, nm = self.nd, self.nc, self.nz, self.nm
        rows, wide = self.rows_in, self.wide
        where = dp, c, z = self.place()
        me = c * nz + z
        sizes = (nc, nz)
        steps = self.group_steps()
        other = (dp, nc - 1 - c, z)
        lines = [(k, (lax.rem(dp + k, nd), c, z), lax.rem(dp + nd - k, nd)) for k in range(1, nd)]
        started = []

        def go(copy):
            copy.start()
            started.append(copy)
            return copy

        def w_block(owner, m, first=0, count=rows):
            at = pl.multiple_of(m * rows + first, rows // 2)
            return wall.at[owner, pl.ds(at, count), :]

        def c_block(owner, m, first=0, count=rows):
            at = pl.multiple_of((owner * nm + m) * rows + first, rows // 2)
            return wcall.at[pl.ds(at, count), :]

        w_from = [me] + [self.source(step) for step in steps]
        c_from = [c * nz + lax.rem(z + nz - d, nz) for d in range(nz)]
        w_square = Square(
            where, lambda owner, j, first, count: w_block(owner, w_from[j], first, count), rows, (wq_s, wq_r)
        )
        c_square = Square(
            where, lambda owner, j, first, count: c_block(owner, c_from[j], first, count), rows, (cq_s, cq_r)
        )
        o_square = Square(
            where,
            lambda owner, j, first, count: woall.at[owner, pl.ds(first, count), :],
            TILE,
            (oq_s, oq_r),
        )
        x_line = Line(where, sizes, lambda a, b: xall.at[rows_of(a * nz + b), :], (xr_s, xr_r, xl_s, xl_r, xc_s, xc_r))
        g_line = Line(where, sizes, lambda a, b: gall.at[rows_of(a * nz + b), :], (gr_s, gr_r, gl_s, gl_r, gc_s, gc_r))
        y_sum = Sum(where, sizes, ypart, ycame, ytotal, yheard, (yc_s, yc_r, yr_s, yr_r, yl_s, yl_r))

        starts = [jnp.int32(0)]
        for doc in range(1, docs):
            starts.append(starts[-1] + lengths[0, doc - 1])
        active = jnp.right_shift(HEADS, 3 - level[0])
        unit = jnp.float32(1.0 / INNER)
        for smaller in range(3):
            unit = jnp.where(level[0] == smaller, jnp.float32(2.0 ** (3 - smaller) / INNER), unit)
        own_conv = CONV // (nd * nm)
        parbuf_[dp, 0:KW, :own_conv] = tap_ref[...]
        parbuf_[dp, KW : KW + 1, :own_conv] = bias_ref[...]
        parbuf_[dp, 5:6, :rows] = norm_ref[...]
        parbuf_[dp, 6:7, :TILE] = gain_ref[...]
        head_ref[...] = jnp.zeros_like(head_ref)
        head_ref[0:1, :HEADS] = step_ref[...]
        head_ref[1:2, :HEADS] = -jnp.exp(rate_ref[...])
        head_ref[2:3, :HEADS] = skip_ref[...]
        head_ref[3:4, :] = (iota((1, TILE), 1) < active).astype(F32)
        for m in range(nm):
            for i in range(2 * nd):
                wm_ref[m * rows : (m + 1) * rows, tile_of(i)] = in_ref[:, tile_of(i * nm + m)]
        shared = EXTENT - 2 * INNER
        wc_ref[:, 2 * TILE :] = jnp.zeros((rows, COMMON - 2 * TILE), BF16)
        wc_ref[:, : 2 * TILE] = in_ref[:, 2 * INNER : 2 * INNER + 2 * TILE]
        wc_ref[:, 2 * TILE : shared] = in_ref[:, 2 * INNER + 2 * TILE :]
        own = [
            pltpu.make_async_copy(wm_ref.at[rows_of(me, rows), :], w_block(dp, me), loc.at[0]),
            pltpu.make_async_copy(wc_ref, c_block(dp, me), loc.at[1]),
            pltpu.make_async_copy(wo_ref, woall.at[dp], loc.at[2]),
            pltpu.make_async_copy(g_ref, gall.at[rows_of(me), :], loc.at[3]),
        ]
        for copy in own:
            copy.start()
        self.barrier()
        for k, device, _ in lines:
            go(remote(parbuf_.at[dp], parbuf_.at[dp], pd_s.at[k], pd_r.at[k], device))
        for j, step in enumerate(steps):
            device, there = self.target(step)
            go(remote(wm_ref.at[rows_of(there, rows), :], w_block(dp, me), wz_s.at[j], wz_r.at[j], device))
            if step[0] == 0:
                go(remote(wc_ref, c_block(dp, me), cz_s.at[step[1]], cz_r.at[step[1]], device))
        for copy in own[:3]:
            copy.wait()
        o_square.begin(0)
        w_square.begin(0)
        c_square.begin(0)
        for k, device, frm in lines:
            remote(parbuf_.at[frm], parbuf_.at[frm], pd_s.at[k], pd_r.at[k], device).wait_recv()
        parall[me] = parbuf_[...]
        for j, step in enumerate(steps):
            device, _ = self.target(step)
            go(remote(parbuf_, parall.at[me], pg_s.at[j], pg_r.at[j], device))
        for j, step in enumerate(steps):
            device, _ = self.target(step)
            remote(parbuf_, parall.at[self.source(step)], pg_s.at[j], pg_r.at[j], device).wait_recv()
        owners = [(first // nm, first % nm) for first in range(nd * nm)]
        gain = jnp.concatenate([parall[m, d][5:6, :rows] for d, m in owners], axis=1)
        gain_out[...] = jnp.broadcast_to(gain, (8, MODEL))
        hidden = x_ref[...].astype(F32)
        inverse = lax.rsqrt(jnp.mean(hidden * hidden, axis=1, keepdims=True) + EPSILON)
        xall[rows_of(me), :] = (hidden * inverse * gain).astype(BF16)
        x_line.begin()

        for j, step in enumerate(steps):
            device, _ = self.target(step)
            block = w_block(dp, w_from[j + 1])
            remote(block, block, wz_s.at[j], wz_r.at[j], device).wait_recv()
            w_square.begin(j + 1)
            if step[0] == 0:
                d = step[1]
                block = c_block(dp, c_from[d])
                remote(block, block, cz_s.at[d], cz_r.at[d], device).wait_recv()
                c_square.begin(d)
            if j == 2:
                o_square.step(0)
                w_square.step(0)
                c_square.step(0)
        every_par[...] = jnp.concatenate([parall[m, d][:, :own_conv] for d, m in owners], axis=1)
        for i in range(nd):
            at = pl.ds(pl.multiple_of((i * nm + me) * TILE, TILE), TILE)
            taps[:, tile_of(i)] = every_par[:, at]
        taps[:, wide:] = every_par[:, INNER : INNER + 2 * TILE]
        head, lane = iota((TILE, TILE), 0), iota((TILE, TILE), 1)
        step_of = nm * self.per
        chosen = (head == lax.div(lane, self.per) * step_of + self.per * me + lax.rem(lane, self.per)) & (
            lane < nd * self.per
        )
        sel[...] = chosen.astype(BF16)
        hp[...] = exact(head_ref[...], chosen.astype(F32))
        for i in range(nd):
            chosen = head == i * step_of + self.per * me + lax.div(lane, HEAD_DIM)
            spread = exact(head_ref[...], chosen.astype(F32))
            chp[0:2, tile_of(i)] = spread[2:4, :]
            chp[2:3, tile_of(i)] = parbuf_[i][6:7, :TILE]
        x_line.step(1)
        own[3].wait()
        g_line.begin()
        for j in range(1, 4):
            w_square.step(j)
        for j in range(1, nz):
            c_square.step(j)
        x_line.step(2)
        for j in range(4, nm):
            w_square.step(j)
        x_line.step(3)
        for j in range(nz):
            c_square.arrive(j)
        for i in range(nd):
            at = pl.ds(pl.multiple_of((i * nm + c * nz) * rows, rows), nz * rows)
            go(remote(wcall.at[at, :], wcall.at[at, :], cc_s.at[i], cc_r.at[i], other))
        x_line.arrive()
        for j in range(nm):
            w_square.arrive(j)
        for i in range(nd):
            at = pl.ds(pl.multiple_of((i * nm + (nc - 1 - c) * nz) * rows, rows), nz * rows)
            remote(wcall.at[at, :], wcall.at[at, :], cc_s.at[i], cc_r.at[i], other).wait_recv()
        projm[0:PAD, :] = jnp.zeros((PAD, 2 * wide), BF16)
        projc[0:PAD, :] = jnp.zeros((PAD, COMMON), BF16)
        projc[PAD:, :] = dot(xall[...], wcall[...]).astype(BF16)

        def project(n, _):
            at = rows_of(n, 256)
            projm[PAD:, at] = dot(xall[...], wall[:, :, at].reshape(MODEL, 256)).astype(BF16)
            pl.when(n == 2)(lambda: g_line.step(1))
            return 0

        lax.fori_loop(0, 2 * wide // 256, project, 0)
        state[...] = jnp.zeros_like(state)

        def forward(i, _):
            self.forward_chunk(
                i, docs, starts, projm, projc, taps, sel, hp, chp,
                pre_sig, pre_bc, o, states, step_s, cum_s, scaled, st, state,
            )
            pl.when(i == 2)(lambda: g_line.step(2))
            pl.when(i == 6)(lambda: g_line.step(3))
            return 0

        lax.fori_loop(0, nm, forward, 0)

        o_square.arrive(0)

        def branch(pair):
            def some(n, _):
                t = pair + lax.rem(n, 2) * (nz - 1 - 2 * pair)
                turn = t + lax.rem(nc - 1 - c + lax.div(n, 2), nc) * nz
                ypart[turn] = dot(scaled[rows_of(turn), :], woall[...].reshape(wide, MODEL)).astype(BF16)
                pl.when(n < 2)(lambda: y_sum.core(t).start())
                return 0

            lax.fori_loop(0, 4, some, 0)

        branch(0)
        y_sum.add_core(0)
        y_sum.add_core(nz - 1)
        y_sum.begin()
        for pair in range(1, nz // 2):
            branch(pair)
            y_sum.add_core(pair)
            y_sum.add_core(nz - 1 - pair)

        g_line.arrive()
        lanes_at = iota((SPAN, TILE), 1)

        def gate_grad(n, _):
            at = rows_of(n, 512)
            grad = dot(gall[at, :], woall[...].reshape(wide, MODEL), ((1,), (1,)))
            dg[at, :] = grad
            for half in range(4):
                product = jnp.zeros((SPAN, TILE), F32)
                for i in range(nd):
                    mine = scaled[pl.ds(pl.multiple_of(n * 512 + half * SPAN, SPAN), SPAN), tile_of(i)]
                    product = product + mine.astype(F32) * grad[half * SPAN : (half + 1) * SPAN, tile_of(i)]
                st[1, pl.ds(4 * n + half, 1), :] = lane_sum(product).T[0:1, :]
            return 0

        lax.fori_loop(0, nm // 4, gate_grad, 0)
        sent = []
        for j, step in enumerate(steps):
            device, _ = self.target(step)
            sent.append(go(remote(st, heard_st.at[j], st_s.at[j], st_r.at[j], device)))

        totals = st[...]
        for j, copy in enumerate(sent):
            copy.wait_recv()
            totals = totals + heard_st[j]
        for copy in sent:
            copy.wait_send()
        st[...] = totals

        dnext[...] = jnp.zeros_like(dnext)
        state[...] = jnp.zeros_like(state)
        sums[...] = jnp.zeros_like(sums)
        heads[...] = jnp.zeros_like(heads)

        def backward(n, _):
            self.backward_chunk(
                nm - 1 - n, docs, starts, unit, projm, pre_sig, pre_bc, o, states, step_s, cum_s, dg, st, taps, sel,
                hp, chp, dcom, scaled, sums, heads, state, dnext, projc,
            )
            for k in range(1, nz - 1):
                pl.when(n == SLOTS[k - 1])(lambda k=k: y_sum.slot(k))
            return 0

        lax.fori_loop(0, nm, backward, 0)
        for copy in started:
            if not any(copy is s for s in sent):
                copy.wait_send()
        started.clear()
        for j in range(nm):
            w_square.end(j)
        for j in range(nz):
            c_square.end(j)
        o_square.end(0)
        x_line.end()
        g_line.end()

        x_sum = Sum(where, sizes, ypart, ycame, ytotal, xheard, (uc_s, uc_r, ur_s, ur_r, ul_s, ul_r))
        w_sum = SquareSum(where, wall, w1, w2, projm, (w1_s, w1_r, w2_s, w2_r), 2)
        o_sum = SquareSum(where, woall, xall, o2, xall, (o1_s, o1_r, o2_s, o2_r), 1, base=4 * TILE)
        c_sum = SquareSum(where, cpart, c1, c2, dcom, (c1_s, c1_r, c2_s, c2_r), 1, lambda owner: owner * nc + c)
        def input_grad(core):
            base = rows_of(core, nz * SPAN)
            lead = pl.ds(pl.multiple_of(core * nz * SPAN + PAD, PAD), nz * SPAN)

            def piece(n, _):
                at = rows_of(n, 256)
                part = dot(projm[lead, :], wall[lax.div(n, 2), rows_of(lax.rem(n, 2), 256), :], ((1,), (1,)))
                part = (part + dot(dcom[base, :], wcall[at, :], ((1,), (1,)))).astype(BF16)
                for t in range(nz):
                    ypart[core * nz + t, :, at] = part[t * SPAN : (t + 1) * SPAN, :]
                return 0

            lax.fori_loop(0, MODEL // 256, piece, 0)

        y_sum.end_core()
        input_grad(nc - 1 - c)
        for t in range(nz):
            x_sum.core(t).start()
        input_grad(c)
        y_sum.arrive()
        stat = jnp.broadcast_to(st[0, pl.ds(me, 1), :], (SPAN, TILE)).T
        root = lax.rsqrt(stat[:, 0:1] * unit + EPSILON)
        y_out[...] = (x_ref[...].astype(F32) + root * y_sum.own(slice(None))).astype(BF16)
        y_sum.end()
        x_sum.add_core(0)
        x_sum.add_core(nz - 1)
        x_sum.begin()
        for t in range(1, nz - 1):
            x_sum.add_core(t)

        def weight_grad(owner):
            def piece(n, _):
                at = pl.ds(pl.multiple_of(owner * (nm * rows) + n * 512, 512), 512)
                wall[owner, rows_of(n, 512), :] = dot(xall[:, at], projm[PAD:, :], ((0,), (0,))).astype(BF16)
                return 0

            lax.fori_loop(0, nm * rows // 512, piece, 0)

        weight_grad(w_sum.diag)
        weight_grad(w_sum.dx)
        w_sum.begin_x(0)
        weight_grad(w_sum.dy)
        w_sum.begin_y(0)
        weight_grad(dp)

        def shared_grad(n, _):
            at = rows_of(n, 256)
            cpart[n] = dot(xall[:, at], dcom[...], ((0,), (0,))).astype(BF16)
            return 0

        lax.fori_loop(0, nd * nc, shared_grad, 0)
        ccopies = [
            go(remote(cpart.at[i * nc + nc - 1 - c], projc.at[rows_of(i, nz * rows), :], sc_s.at[i], sc_r.at[i], other)) for i in range(nd)
        ]
        x_sum.slot(1)

        def out_grad(n, _):
            at = rows_of(n, 512)
            part = dot(scaled[...], gall[:, at], ((0,), (0,))).astype(BF16)
            for i in range(nd):
                woall[i, :, at] = part[tile_of(i), :]
            return 0

        lax.fori_loop(0, MODEL // 512, out_grad, 0)
        w_sum.pass_on(0)
        w_sum.begin_x(1)
        w_sum.begin_y(1)
        for i in range(nd):
            ccopies[i].wait_recv()
            cpart[i * nc + c] = (cpart[i * nc + c].astype(F32) + projc[rows_of(i, nz * rows), :].astype(F32)).astype(BF16)
        x_sum.slot(2)

        def send_rows(p):
            half = nm // 2
            for j in range(half):
                there = p * half + j
                block = wm_ref.at[there * rows : (there + 1) * rows, :]
                ct, zt = there // nz, there % nz

                @pl.when(there != me)
                def _():
                    remote(block, dw_out.at[me], vz_s.at[there], vz_r.at[me], (dp, ct, zt)).start()

                @pl.when(there == me)
                def _():
                    dw_out[there] = block[...]

        w_sum.finish(0, wm_ref)
        send_rows(0)
        w_sum.pass_on(1)
        c_sum.begin_x(0)
        c_sum.begin_y(0)
        o_sum.begin_x(0)
        o_sum.begin_y(0)

        x_sum.arrive()
        hidden = x_ref[...].astype(F32)
        normed_grad = x_sum.own(slice(None))
        inverse = lax.rsqrt(jnp.mean(hidden * hidden, axis=1, keepdims=True) + EPSILON)
        unitary = hidden * inverse
        gain_grad = jnp.sum(normed_grad * unitary, axis=0, keepdims=True)
        grad_scaled = normed_grad * gain_out[0:1, :]
        middle = jnp.mean(grad_scaled * unitary, axis=1, keepdims=True)
        dx_out[...] = (gall[rows_of(me), :].astype(F32) + inverse * (grad_scaled - unitary * middle)).astype(BF16)
        base_row = MODEL // TILE
        for i in range(base_row):
            parbuf[i : i + 1, :] = gain_grad[:, tile_of(i)]
        for i in range(nd + 2):
            parbuf[base_row + 8 * i : base_row + 8 * i + 8, :] = sums[:, tile_of(i)]
        lane_at = iota((1, TILE), 1)
        skip_row = jnp.zeros((1, TILE), F32)
        for i in range(nd):
            both = sums[1:2, tile_of(i)]
            for e in range(2):
                part = jnp.where(lax.div(lane_at, HEAD_DIM) == e, both, 0.0)
                skip_row = skip_row + jnp.where(lane_at == 2 * i + e, lane_sum(part), 0.0)
        heads[2:3, :] = skip_row
        parbuf[base_row + 8 * (nd + 2) :, :] = exact(heads[...], sel[...].astype(F32), ((1,), (1,)))
        small = [
            go(remote(parbuf, pard.at[k - 1], qd_s.at[k], qd_r.at[k], device)) for k, device, _ in lines
        ]
        w_sum.finish(1, wm_ref)
        send_rows(1)
        c_sum.pass_on(0)
        o_sum.pass_on(0)
        c_sum.finish(0, crows)
        for d in range(1, nz):
            to = lax.rem(z + d, nz)
            go(remote(crows.at[rows_of(to, rows), :], cheard.at[d - 1], sz_s.at[d], sz_r.at[d], (dp, c, to)))
        for copy in small:
            copy.wait_recv()
        total = parbuf[...]
        for k in range(nd - 1):
            total = total + pard[k]
        par_out[me] = total
        for j, step in enumerate(steps):
            go(remote(par_out.at[me], par_out.at[me], qg_s.at[j], qg_r.at[j], self.target(step)[0]))
        o_sum.finish(0, dwo_out)
        total = crows[rows_of(z, rows), :].astype(F32)
        for d in range(1, nz):
            remote(cheard.at[d - 1], cheard.at[d - 1], sz_s.at[d], sz_r.at[d], other).wait_recv()
            total = total + cheard[d - 1].astype(F32)
        dwc_out[...] = total
        for j, step in enumerate(steps):
            here = par_out.at[self.source(step)]
            remote(here, here, qg_s.at[j], qg_r.at[j], other).wait_recv()
        for m in range(nm):
            got = dw_out.at[m]

            @pl.when(m != me)
            def _():
                remote(got, got, vz_s.at[m], vz_r.at[m], other).wait_recv()
                remote(got, got, vz_s.at[m], vz_r.at[m], other).wait_send()

        for copy in started:
            copy.wait_send()
        x_sum.end_core()
        x_sum.end()
        w_sum.end()
        o_sum.end()
        c_sum.end()

    def forward_chunk(
        self, chunk, docs, starts, projm, projc, taps, sel, hp, chp,
        pre_sig, pre_bc, o, states, step_s, cum_s, scaled, st, state,
    ):
        nd, wide = self.nd, self.wide
        first = chunk * SPAN
        here = rows_of(chunk)
        lead = pl.ds(pl.multiple_of(chunk * SPAN, SPAN), SPAN + PAD)
        body = pl.ds(pl.multiple_of(chunk * SPAN + PAD, PAD), SPAN)
        lane = iota((SPAN, TILE), 1)
        row = iota((SPAN, TILE), 0)
        low = lane < HEAD_DIM
        begin_t = begin_at(first + row, starts, docs)
        begin_s = begin_at(first + lane, starts, docs)
        valid = [first + row - (KW - 1 - tap) >= begin_t for tap in range(KW)]
        sides = []
        for i in range(2):
            lanes = tile_of(i)
            value = conv_tile(projc[lead, lanes].astype(F32), taps, tile_of(nd + i), valid)
            pre_bc[here, lanes] = value
            sides.append((value * jax.nn.sigmoid(value)).astype(BF16))
        key_side, query_side = sides
        rate = dot(projc[body, 2 * TILE :], sel[...])
        step = softplus(rate + hp[0:1, :])
        log_decay = step * hp[1:2, :]
        cum = exact((lane <= row).astype(F32), log_decay)
        step_s[here, :] = step
        cum_s[here, :] = cum
        cum_t = cum.T
        shut = jnp.where((begin_t == begin_s) & (lane <= row), 0.0, NEG)
        inherits = (begin_t < first).astype(F32)
        begin_last = begin_at(jnp.full((SPAN, TILE), first + SPAN - 1, jnp.int32), starts, docs)
        last_same = (begin_t == begin_last).astype(F32)
        meet = dot(query_side, key_side, ((1,), (1,)))
        before = state[...]
        before_low = before.astype(BF16)
        states[chunk] = before_low
        carried_out = dot(query_side, before_low)
        squares = jnp.zeros((SPAN, TILE), F32)
        for i in range(nd):
            lanes = tile_of(i)
            pre = conv_tile(projm[lead, tile_of(nd + i)].astype(F32), taps, lanes, valid)
            pre_sig[here, lanes] = pre
            signal = pre * jax.nn.sigmoid(pre)
            cums = [head_col(cum, 2 * i), head_col(cum, 2 * i + 1)]
            stepx = jnp.where(low, head_col(step, 2 * i), head_col(step, 2 * i + 1))
            cumx = jnp.where(low, cums[0], cums[1])
            fed = stepx * signal
            fed_low = fed.astype(BF16)
            local = []
            for e in range(2):
                head = 2 * i + e
                kernel = jnp.exp(cums[e] - cum_t[head : head + 1, :] + shut)
                local.append(dot((kernel * meet).astype(BF16), fed_low))
            entry = jnp.exp(cumx) * inherits
            out = jnp.where(low, local[0], local[1]) + entry * carried_out[:, lanes]
            o[here, lanes] = out
            last = cumx[SPAN - 1 : SPAN, :]
            tail = jnp.exp((last - cumx) * last_same) * last_same
            state[:, lanes] = entry[SPAN - 1 : SPAN, :] * before[:, lanes] + dot(
                key_side, (tail * fed).astype(BF16), ((0,), (0,))
            )
            mixed = (out + chp[0:1, lanes] * signal) * chp[1:2, lanes]
            gate_in = projm[body, lanes].astype(F32)
            gated = mixed * (gate_in * jax.nn.sigmoid(gate_in))
            squares = squares + gated * gated
            scaled[here, lanes] = (gated * chp[2:3, lanes]).astype(BF16)
        st[0, pl.ds(chunk, 1), :] = lane_sum(squares).T[0:1, :]

    def backward_chunk(
        self, chunk, docs, starts, unit, projm, pre_sig, pre_bc, o, states, step_s, cum_s, dg, st, taps, sel,
        hp, chp, dcom, normed_out, sums, heads, dstate, dnext, projc,
    ):
        nd = self.nd
        first = chunk * SPAN
        here = rows_of(chunk)
        lead = pl.ds(pl.multiple_of(chunk * SPAN, SPAN), SPAN + PAD)
        body = pl.ds(pl.multiple_of(chunk * SPAN + PAD, PAD), SPAN)
        lane = iota((SPAN, TILE), 1)
        row = iota((SPAN, TILE), 0)
        low = lane < HEAD_DIM
        begin_t = begin_at(first + row, starts, docs)
        begin_s = begin_at(first + lane, starts, docs)
        shut = jnp.where((begin_t == begin_s) & (lane <= row), 0.0, NEG)
        inherits = (begin_t < first).astype(F32)
        begin_last = begin_at(jnp.full((SPAN, TILE), first + SPAN - 1, jnp.int32), starts, docs)
        last_same = (begin_t == begin_last).astype(F32)
        lower = (lane <= row).astype(F32)
        key_pre, query_pre = pre_bc[here, :TILE], pre_bc[here, TILE:]
        key_side = (key_pre * jax.nn.sigmoid(key_pre)).astype(BF16)
        query_side = (query_pre * jax.nn.sigmoid(query_pre)).astype(BF16)
        meet = dot(query_side, key_side, ((1,), (1,)))
        step, cum = step_s[here, :], cum_s[here, :]
        cum_t = cum.T
        square = jnp.broadcast_to(st[0, pl.ds(chunk, 1), :], (SPAN, TILE)).T
        cross = jnp.broadcast_to(st[1, pl.ds(chunk, 1), :], (SPAN, TILE)).T
        root = lax.rsqrt(square * unit + EPSILON)
        pull = root * root * root * cross * unit
        before_low = states[chunk]
        before = before_low.astype(F32)
        after = dstate[...]
        after_low = after.astype(BF16)
        carried_out = dot(query_side, before_low)
        from_state = dot(key_side, after_low)
        meet_grad = jnp.zeros((SPAN, SPAN), F32)
        cum_cols = jnp.zeros((SPAN, TILE), F32)
        cum_rows = jnp.zeros((8, SPAN), F32)
        step_cols = jnp.zeros((SPAN, TILE), F32)
        entered, tails = [], []
        head_rows = iota((8, SPAN), 0)
        next_rows = first + iota((SPAN + PAD, TILE), 0)
        next_begin = begin_at(next_rows, starts, docs)
        valid = [next_rows - (KW - 1 - tap) >= next_begin for tap in range(KW)]
        tail_row = row == SPAN - 1

        def conv_back(pre_grad, ext, lanes):
            sums[2:3, lanes] += jnp.sum(pre_grad, axis=0, keepdims=True)
            later = jnp.concatenate([pre_grad, dnext[:, lanes]], axis=0)
            dnext[:, lanes] = pre_grad[0:PAD, :]
            back_grad = jnp.zeros((SPAN, TILE), F32)
            for tap in range(KW):
                back = KW - 1 - tap
                masked = jnp.where(valid[tap], later, 0.0)
                moved = ext if back == 0 else pltpu.roll(ext, back, 0)
                sums[4 + tap : 5 + tap, lanes] += jnp.sum(masked[:SPAN] * moved[PAD:], axis=0, keepdims=True)
                ahead = masked if back == 0 else pltpu.roll(masked, SPAN + PAD - back, 0)
                back_grad = back_grad + ahead[:SPAN] * taps[tap : tap + 1, lanes]
            return back_grad

        for i in range(nd):
            lanes = tile_of(i)
            pre = pre_sig[here, lanes]
            gate_of = jax.nn.sigmoid(pre)
            signal = pre * gate_of
            gate_in = projm[body, lanes].astype(F32)
            gate_sig = jax.nn.sigmoid(gate_in)
            opened = gate_in * gate_sig
            mask = chp[1:2, lanes]
            mixed = (o[here, lanes] + chp[0:1, lanes] * signal) * mask
            gated = mixed * opened
            grad = dg[here, lanes]
            gain = chp[2:3, lanes]
            normed_out[here, lanes] = (gated * root * gain).astype(BF16)
            sums[0:1, lanes] += jnp.sum(grad * gated * root, axis=0, keepdims=True)
            gated_grad = root * grad * gain - gated * pull
            mixed_grad = gated_grad * opened * mask
            projm[body, lanes] = (
                gated_grad * mixed * (gate_sig * (1.0 + gate_in * (1.0 - gate_sig)))
            ).astype(BF16)
            sums[1:2, lanes] += jnp.sum(mixed_grad * signal, axis=0, keepdims=True)
            cums = [head_col(cum, 2 * i), head_col(cum, 2 * i + 1)]
            stepx = jnp.where(low, head_col(step, 2 * i), head_col(step, 2 * i + 1))
            cumx = jnp.where(low, cums[0], cums[1])
            fed = stepx * signal
            fed_low = fed.astype(BF16)
            out_grad = mixed_grad
            out_low = out_grad.astype(BF16)
            entry = jnp.exp(cumx) * inherits
            last = cumx[SPAN - 1 : SPAN, :]
            tail = jnp.exp((last - cumx) * last_same) * last_same
            backs = []
            for e in range(2):
                head = 2 * i + e
                kernel = jnp.exp(cums[e] - cum_t[head : head + 1, :] + shut)
                mix = kernel * meet
                half = low if e == 0 else jnp.logical_not(low)
                mix_grad = dot(jnp.where(half, out_grad, 0.0).astype(BF16), fed_low, ((1,), (1,)))
                meet_grad = meet_grad + kernel * mix_grad
                weight = mix * mix_grad
                cum_cols = cum_cols + jnp.where(lane == head, lane_sum(weight), 0.0)
                cum_rows = cum_rows + jnp.where(
                    head_rows == head, jnp.broadcast_to(jnp.sum(weight, axis=0, keepdims=True), (8, SPAN)), 0.0
                )
                backs.append(dot(mix.astype(BF16), out_low, ((0,), (0,))))
            entry_grad = entry * out_grad
            tail_fed = tail * fed
            entered.append(entry_grad.astype(BF16))
            tails.append(tail_fed.astype(BF16))
            fed_grad = jnp.where(low, backs[0], backs[1]) + tail * from_state[:, lanes]
            moved_in = entry_grad * carried_out[:, lanes]
            moved_out = tail_fed * from_state[:, lanes]
            direct = fed_grad * signal
            end = entry[SPAN - 1 : SPAN, :]
            kept = jnp.sum(after[:, lanes] * before[:, lanes], axis=0, keepdims=True) * end
            at_end = jnp.sum(moved_out, axis=0, keepdims=True) + kept
            local = moved_in - moved_out + jnp.where(tail_row, at_end, 0.0)
            for e in range(2):
                half = low if e == 0 else jnp.logical_not(low)
                place = lane == 2 * i + e
                cum_cols = cum_cols + jnp.where(place, lane_sum(jnp.where(half, local, 0.0)), 0.0)
                step_cols = step_cols + jnp.where(place, lane_sum(jnp.where(half, direct, 0.0)), 0.0)
            dstate[:, lanes] = end * after[:, lanes] + dot(query_side, entry_grad.astype(BF16), ((0,), (0,)))
            signal_grad = stepx * fed_grad + chp[0:1, lanes] * mixed_grad
            pre_grad = signal_grad * (gate_of * (1.0 + pre * (1.0 - gate_of)))
            cols = tile_of(nd + i)
            projm[body, cols] = conv_back(pre_grad, projm[lead, cols].astype(F32), lanes).astype(BF16)
        meet_low = meet_grad.astype(BF16)
        state_rows = ((1,), (1,))
        query_grad = dot(meet_low, key_side) + dot(jnp.concatenate(entered, axis=1), before_low, state_rows)
        key_grad = dot(meet_low, query_side, ((0,), (0,))) + dot(
            jnp.concatenate(tails, axis=1), after_low, state_rows
        )
        for i, (side_grad, side_pre) in enumerate(((key_grad, key_pre), (query_grad, query_pre))):
            back_grad = conv_back(side_grad * silu_slope(side_pre), projc[lead, tile_of(i)].astype(F32), tile_of(nd + i))
            dcom[here, tile_of(i)] = back_grad.astype(BF16)
        rows_t = jnp.concatenate([cum_rows, jnp.zeros((SPAN - 8, SPAN), F32)], axis=0).T
        decay_grad = exact(lower, cum_cols - rows_t, ((0,), (0,)))
        log_decay = step * hp[1:2, :]
        slope = 1.0 - jnp.exp(-step)
        rate_grad = (step_cols + decay_grad * hp[1:2, :]) * slope
        heads[0:1, :] += jnp.sum(rate_grad, axis=0, keepdims=True)
        heads[1:2, :] += jnp.sum(decay_grad * log_decay, axis=0, keepdims=True)
        dcom[here, 2 * TILE :] = dot(rate_grad.astype(BF16), sel[...], ((1,), (1,))).astype(BF16)

    def run(self, docs, *args):
        nd, nc, nz, nm, rows, span, wide = self.nd, self.nc, self.nz, self.nm, self.rows_in, self.span, self.wide
        like = jax.ShapeDtypeStruct
        block = (SPAN, MODEL)
        npar = MODEL // TILE + 8 * (nd + 2) + 8

        def low(*shape):
            return pltpu.VMEM(shape, BF16)

        def full(*shape):
            return pltpu.VMEM(shape, F32)

        pair = lambda *shape: [DMA(shape), DMA(shape)]
        return pl.pallas_call(
            functools.partial(self.kernel, docs),
            out_shape=[
                like(block, BF16),
                like(block, BF16),
                like((nm, rows, 2 * wide), BF16),
                like((rows, COMMON), F32),
                like((TILE, MODEL), BF16),
                like((nm, npar, TILE), F32),
            ],
            in_specs=[SM, SM] + [VM] * 9 + [ANY, ANY],
            out_specs=[VM] * 6,
            scratch_shapes=[
                low(span, MODEL), low(span, MODEL), low(nd, nm * rows, 2 * wide), low(MODEL, COMMON),
                low(nd, TILE, MODEL), low(nm * rows, 2 * wide), low(rows, COMMON), full(8, TILE),
                full(nd, 8, 2 * TILE), full(nm, nd, 8, 2 * TILE), full(8, CONV), low(PAD + span, 2 * wide),
                full(span, wide), full(span, wide), low(nm, STATE, wide),
                full(span, TILE), full(span, TILE), full(span, wide), low(span, wide), low(TILE, TILE),
                full(8, TILE), full(8, wide), full(STATE, wide), full(PAD, wide + 2 * TILE),
                full(nm - 1, 2, nm, TILE), full(2, nm, TILE), full(span, 2 * TILE), low(PAD + span, COMMON),
                full(8, wide + 2 * TILE),
                low(nm, *block), low(nz, *block), low(nz, *block), low(nz + 1, *block), low(nz + 1, *block),
                low(span, COMMON), full(8, wide + 2 * TILE), full(8, TILE), full(8, MODEL),
                low(nd * nc, nz * rows, COMMON), low(4, nz * rows, 2 * TILE),
                low(2, nz * rows, 2 * TILE), low(nz * rows, COMMON), low(nz - 1, rows, COMMON),
                low(4, nm * rows, wide), low(2, nm * rows, wide),
                low(2, TILE, MODEL // 2),
                full(nd - 1, npar, TILE), full(npar, TILE),
                *pair(nd), *pair(nm), *pair(nm), *pair(nz), *pair(4, nm), *pair(4, nz), *pair(4, 1), *pair(nd),
                *pair(nz), *pair(nz), *pair(nz), *pair(nz), *pair(nz), *pair(nz),
                *pair(nm), *pair(nz), *pair(nz), *pair(nz),
                *pair(nz), *pair(nz), *pair(nz), *pair(nd), *pair(1, 4), *pair(1, 2), *pair(nz),
                *pair(2, 4), *pair(2, 2), *pair(1, 4), *pair(1, 2), *pair(nm), *pair(nd), *pair(nm), DMA((4,)),
            ],
            compiler_params=pltpu.CompilerParams(
                collective_id=0, has_side_effects=True, vmem_limit_bytes=63 * 2**20
            ),
            name="first",
        )(*args)

    def finish_kernel(
        self, y, dx, dw, dwc, dwo, pars,
        y_out, dx_out, norm_out, in_out, tap_out, bias_out, step_out, rate_out, skip_out, gain_out, out_out, every, narrow,
    ):
        nd, nm, rows = self.nd, self.nm, self.rows_in
        dp, c, z = self.place()
        owner = dp * nm + c * self.nz + z
        own_conv = CONV // (nd * nm)
        base_row = MODEL // TILE
        y_out[...] = y[...]
        dx_out[...] = dx[...]
        out_out[...] = dwo[...].astype(F32)
        for m in range(nm):
            for i in range(2 * nd):
                in_out[:, tile_of(i * nm + m)] = dw[m, :, tile_of(i)].astype(F32)
        in_out[:, 2 * INNER :] = dwc[:, : EXTENT - 2 * INNER]
        summed = pars[0]
        for m in range(1, nm):
            summed = summed + pars[m]
        narrow[...] = summed[0:base_row, :]
        row = narrow[pl.ds(lax.div(owner, 2), 1), :]
        norm_out[...] = jnp.where(lax.rem(owner, 2) == 0, row[:, :rows], row[:, rows:])
        for i in range(nd):
            for m in range(nm):
                every[:, tile_of(i * nm + m)] = pars[m, base_row + 8 * i : base_row + 8 * i + 8, :]
        for i in range(2):
            at = base_row + 8 * (nd + i)
            every[:, tile_of(nd * nm + i)] = summed[at : at + 8, :]
        start = owner * own_conv
        window = every[:, pl.ds(pl.multiple_of(lax.div(start, TILE) * TILE, TILE), 2 * TILE)]
        window = pltpu.roll(window, lax.rem(2 * TILE - lax.rem(start, TILE), 2 * TILE), 1)
        tap_out[...] = window[4 : 4 + KW, :own_conv]
        bias_out[...] = window[2:3, :own_conv]
        at = base_row + 8 * (nd + 2)
        step_out[...] = summed[at : at + 1, :HEADS]
        rate_out[...] = summed[at + 1 : at + 2, :HEADS]
        skip_out[...] = summed[at + 2 : at + 3, :HEADS]
        mine = pars[lax.rem(owner, nm), pl.ds(pl.multiple_of(base_row + 8 * dp, 8), 8), :]
        gain_out[...] = mine[0:1, :]

    def finish(self, *args):
        nd, nm, rows = self.nd, self.nm, self.rows_in
        own_conv = CONV // (nd * nm)
        like = jax.ShapeDtypeStruct
        return pl.pallas_call(
            self.finish_kernel,
            out_shape=[
                like((SPAN, MODEL), BF16),
                like((SPAN, MODEL), BF16),
                like((1, rows), F32),
                like((rows, EXTENT), F32),
                like((KW, own_conv), F32),
                like((1, own_conv), F32),
                like((1, HEADS), F32),
                like((1, HEADS), F32),
                like((1, HEADS), F32),
                like((1, TILE), F32),
                like((TILE, MODEL), F32),
            ],
            in_specs=[VM] * 6,
            out_specs=[VM] * 11,
            scratch_shapes=[pltpu.VMEM((8, CONV), F32), pltpu.VMEM((MODEL // TILE, TILE), F32)],
            compiler_params=pltpu.CompilerParams(vmem_limit_bytes=63 * 2**20),
            name="finish",
        )(*args)

    def local(
        self, layer_input, out_grad, norm_gain, in_weight, conv_weight, conv_bias, step_bias, log_rate,
        skip_gain, gate_gain, out_weight, nest_level, doc_lengths,
    ):
        docs = doc_lengths.shape[1]
        x = layer_input.reshape(SPAN, MODEL)
        g = out_grad.reshape(SPAN, MODEL)
        parts = self.run(
            docs, doc_lengths, nest_level, x, conv_weight.T, conv_bias[None], norm_gain[None], gate_gain[None],
            step_bias[None], log_rate[None], skip_gain[None], in_weight, g, out_weight,
        )
        y_out, dx_out, norm, in_weight_grad, taps, bias, step, rate, skip, gain, dwo = self.finish(*parts)
        return (
            y_out.reshape(1, SPAN, MODEL),
            dx_out.reshape(1, SPAN, MODEL),
            norm[0],
            in_weight_grad,
            taps.T,
            bias[0],
            step[0],
            rate[0],
            skip[0],
            gain[0],
            dwo,
        )


def solution(mesh):
    shape = dict(mesh.shape)
    head_split = HeadSplit(shape["dp"], shape["seq"], shape["fsdp"])
    return jax.shard_map(
        head_split.local if head_split.fits() else token_split,
        mesh=mesh,
        in_specs=(
            P("dp", ("seq", "fsdp"), None),
            P("dp", ("seq", "fsdp"), None),
            P(("dp", "seq", "fsdp")),
            P(("dp", "seq", "fsdp"), None),
            P(("dp", "seq", "fsdp"), None),
            P(("dp", "seq", "fsdp")),
            P(),
            P(),
            P(),
            P(("dp", "seq", "fsdp")),
            P(("dp", "seq", "fsdp"), None),
            P("dp"),
            P("dp", None),
        ),
        out_specs=(
            P("dp", ("seq", "fsdp"), None),
            P("dp", ("seq", "fsdp"), None),
            P(("dp", "seq", "fsdp")),
            P(("dp", "seq", "fsdp"), None),
            P(("dp", "seq", "fsdp"), None),
            P(("dp", "seq", "fsdp")),
            P(),
            P(),
            P(),
            P(("dp", "seq", "fsdp")),
            P(("dp", "seq", "fsdp"), None),
        ),
        check_vma=False,
    )
```
